32 devices in a mesh: fsdp: 32 (over z, y, x, core).
Axes of the slice: x: 2, y: 2, z: 4, core: 2. Of those that a mesh axis runs over, the one named last changes fastest.
Arguments:
- tokens: bfloat16 [6144, 2048], P('fsdp'), may hold values from -6 to 6
- cotangent: bfloat16 [6144, 2048], P('fsdp'), may hold values from -6 to 6
- norm_gains: bfloat16 [4, 2048], P(None, 'fsdp'), may hold values from 0.5 to 1.5
- attention_in: bfloat16 [2048, 6144], P('fsdp'), may hold values from -0.125 to 0.125
- attention_out: bfloat16 [2048, 2048], P('fsdp'), may hold values from -0.75 to 0.75
- router_weight: bfloat16 [2048, 16], P('fsdp'), may hold values from -0.0625 to 0.0625
- expert_in: bfloat16 [32, 2048, 1024], P('fsdp'), may hold values from -0.125 to 0.125
- expert_out: bfloat16 [32, 512, 2048], P('fsdp'), may hold values from -0.75 to 0.75
- routes: int32 [6144, 8], P('fsdp'), may hold values from 0 to 15, all different within a row; in each aligned block of 192 rows (0 to 191, 192 to 383, ...) at most 128 rows name the same one
- lengths: int32 [32, 3], P('fsdp'), may hold values from 1 to 96, 192 in all within a row
Outputs:
- output: bfloat16 [6144, 2048], P('fsdp')
- input_grad: float32 [6144, 2048], P('fsdp')
- gains_grad: float32 [4, 2048], P(None, 'fsdp')
- attention_in_grad: float32 [2048, 6144], P('fsdp')
- attention_out_grad: float32 [2048, 2048], P('fsdp')
- router_grad: float32 [2048, 16], P('fsdp')
- expert_in_grad: float32 [32, 2048, 1024], P('fsdp')
- expert_out_grad: float32 [32, 512, 2048], P('fsdp')
The draws below stay inside these ranges and needn't reach their ends.
Inputs may be any that keep to these rules, and one draw needn't show every extreme that they name: `routes`: in the rows of one device no expert is named by more than 128 rows, a bound that some block reaches. Each device's lengths add up to 192; its longest sequence has exactly 96 tokens.
All inputs are finite; a program needn't handle non-finite values.
Results may differ from the reference program's by a relative error of at most 0.015.
Values may be sent and summed in bfloat16 or wider, within the bound.
No kernel may reach another device: no remote copies, remote signals or barrier semaphores. Data moves between devices by JAX's collectives and lax.ppermute only.
A program may use at most 320 MiB of HBM per device.

```python
import math
import jax
import jax.numpy as jnp
import numpy as np
from jax import lax

D = 2048
HEADS = 16
HEAD_DIM = 128
FF = 1024
TOP = 8
TOK_DEV = 192
SEQS = 3
MAXLEN = 96
RANKS = 32
EXPERTS = 16
CAP = 128
TOKENS = 6144
N_FSDP = 32


def shard_levels(own_key, dims, split, smallest, largest):
    gain = 1.0
    for axis_at, parts in split:
        steps = jax.random.uniform(jax.random.fold_in(jax.random.fold_in(own_key, 6), axis_at), (parts,), jnp.float32, smallest / len(split), largest / len(split))
        gain = gain * jnp.repeat(jnp.exp(steps), dims[axis_at] // parts).reshape((-1,) + (1,) * (len(dims) - 1 - axis_at))
    return gain


def split_up(count, total, most, slope):
    weights = [(1 << 20) // math.isqrt(rank ** slope) + 1 for rank in range(2, count + 1)]
    rest, holding = total - most - (count - 1), [1] * (count - 1)
    while rest > 0:
        candidates = [i for i in range(count - 1) if holding[i] < most]
        mass, left = sum([weights[i] for i in candidates]), rest
        for i in candidates:
            addition = min(most - holding[i], max(1, left * weights[i] // mass), rest)
            holding[i] = holding[i] + addition
            rest = rest - addition
    return np.array([most] + holding)


def uneven(key, count, total, bound, skew):
    if count == 2:
        one = jax.random.randint(key, (), max(1, total - bound), min(bound, total - 1) + 1)
        return jnp.stack([one, total - one])
    tallies = jnp.asarray(split_up(count, total, bound, skew), jnp.int32)
    twos = (count - 1) // 2
    donor, sink = tallies[1:1 + 2 * twos:2], tallies[2:2 + 2 * twos:2]
    slack = jnp.minimum(donor - 1, bound - sink)
    shifted = jax.random.randint(jax.random.fold_in(key, 1), (twos,), 0, 1 << 20) % (slack + 1)
    tallies = tallies.at[1:1 + 2 * twos:2].set(donor - shifted).at[2:2 + 2 * twos:2].set(sink + shifted)
    return tallies[jax.random.permutation(jax.random.fold_in(key, 2), count)]


def routed_block(key, own, number, rows, number_of, top, most, skew):
    sequence = jax.random.permutation(key, number_of)
    heavy_load, usual = portions_of(number_of, rows * top, most, skew, True), portions_of(number_of, rows * top, most, skew, False)
    places = jnp.arange(number_of)

    def named(sizes, rotation):
        used = int((sizes > 0).sum())
        fixed = max(1, used // 4)
        shifted = fixed + (places - fixed + rotation * (used - fixed)) % max(1, number_of - fixed)
        return jnp.zeros((number_of,), jnp.int32).at[sequence[jnp.where(places < fixed, places, shifted)]].set(jnp.asarray(sizes, jnp.int32))

    sizes = jnp.where(number % 4 == 0, named(heavy_load, number // 4), named(usual, number - number // 4 - 1))
    mixed = jax.random.permutation(jax.random.fold_in(own, 3), number_of)
    donor, receiver = mixed[0:number_of // 2 * 2:2], mixed[1:number_of // 2 * 2:2]
    margin = jnp.minimum(sizes[donor] - 1, most - sizes[receiver]) // 2
    margin = jnp.where((donor == sequence[0]) | (receiver == sequence[0]) | (sizes[receiver] == 0), 0, jnp.maximum(margin, 0))
    shifted = jax.random.randint(jax.random.fold_in(own, 4), (number_of // 2,), 0, 1 << 20) % (margin + 1)
    sizes = sizes.at[donor].add(-shifted).at[receiver].add(shifted)
    labels = jnp.searchsorted(jnp.cumsum(sizes), jnp.arange(rows * top), side="right").astype(jnp.int32)
    table = labels.reshape(top, rows).T
    table = table[jax.random.permutation(jax.random.fold_in(own, 1), rows)]
    rotation = jax.random.randint(jax.random.fold_in(own, 2), (rows, 1), 0, top)
    return jnp.take_along_axis(table, (jnp.arange(top)[None, :] + rotation) % top, axis=1)


def portions_of(count, total, bound, skew, full):
    weights = [(1 << 20) // math.isqrt(grade ** skew) + 1 for grade in range(1, count + 1)]
    largest = bound if full else min(bound, max(-(-total // count), total * weights[0] // sum(weights)))
    least = 1 if total - largest >= count - 1 else 0
    given, rest = [largest] + [least] * (count - 1), total - largest - least * (count - 1)
    while rest > 0:
        movable = [i for i in range(1, count) if given[i] < largest] or [i for i in range(1, count) if given[i] < bound]
        mass, left = sum([weights[i] for i in movable]), rest
        for i in movable:
            extra = min(bound - given[i], max(1, left * weights[i] // mass), rest)
            given[i] = given[i] + extra
            rest = rest - extra
    return np.array(given)


def gaussian(own_key, shape, scale, limit, pieces=(), held_as=jnp.bfloat16):
    loudness = shard_levels(own_key, shape, pieces, -0.22, 0.18) if pieces else 1.0
    entries = jax.random.normal(own_key, shape, jnp.float32) * scale * loudness
    return jnp.minimum(jnp.maximum(entries, -limit), limit).astype(held_as)


def setup_inputs(seed: int = 0) -> dict:
    key_list = jax.random.split(jax.random.key(seed), 11)
    tokens = gaussian(key_list[0], (TOKENS, D), 1.0, 6.0, ((0, 32),))
    cotangent = gaussian(key_list[1], (TOKENS, D), 1.0, 6.0, ((0, 32),))
    norm_gains = jnp.clip(1.0 + 0.1 * jax.random.normal(key_list[2], (4, D), jnp.float32), 0.5, 1.5).astype(jnp.bfloat16)
    attention_in = gaussian(key_list[3], (D, 3 * D), D ** -0.5, 0.125, ((0, 32),))
    attention_out = gaussian(key_list[4], (D, D), (D // 32) ** -0.5, 0.75, ((0, 32),))
    router_weight = gaussian(key_list[5], (D, EXPERTS), (4 * D) ** -0.5, 0.0625, ((0, 32),))
    expert_in = gaussian(key_list[6], (2 * EXPERTS, D, FF), D ** -0.5, 0.125, ((0, 32),))
    expert_out = gaussian(key_list[7], (2 * EXPERTS, FF // 2, D), (FF // 16) ** -0.5, 0.75, ((0, 32),))
    routes_keys = jax.random.split(jax.random.fold_in(key_list[8], 1), TOKENS // TOK_DEV)
    routes_turns = jax.random.permutation(jax.random.fold_in(key_list[8], 3), TOKENS // TOK_DEV)
    routes = jax.vmap(lambda own, number: routed_block(jax.random.fold_in(key_list[8], 2), own, number, TOK_DEV, EXPERTS, TOP, CAP, 1))(routes_keys, routes_turns).reshape((TOKENS, TOP))
    lengths = jax.vmap(lambda own: uneven(own, SEQS, TOK_DEV, MAXLEN, 2))(jax.random.split(key_list[9], RANKS)).reshape((RANKS, SEQS)).astype(jnp.int32)
    return dict(tokens=tokens, cotangent=cotangent, norm_gains=norm_gains, attention_in=attention_in, attention_out=attention_out, router_weight=router_weight, expert_in=expert_in, expert_out=expert_out, routes=routes, lengths=lengths)


EPSILON = 1e-05
ROPE_BASE = 10000.0
MASKED = -1000000000.0

@jax.custom_vjp
def low(v):
    return lax.optimization_barrier(v.astype(jnp.bfloat16)).astype(jnp.float32)

@jax.custom_vjp
def low_back(v):
    return v

def low_keep(v):
    return (low(v), None)

def low_pass(kept, grad):
    return (grad,)

def back_keep(v):
    return (v, None)

def back_low(kept, grad):
    return (low(grad),)
low.defvjp(low_keep, low_pass)
low_back.defvjp(back_keep, back_low)

def product(left, right):
    return jnp.dot(left, right, precision=lax.Precision.HIGHEST, preferred_element_type=jnp.float32)

def root_norm(vector, scaling):
    return vector * lax.rsqrt(lax.optimization_barrier(jnp.mean(vector * vector, axis=-1, keepdims=True)) + EPSILON) * scaling

def rotary(vector, cos_table, sin_table):
    half_dim = vector.shape[-1] // 2
    first = vector[..., :half_dim]
    second = vector[..., half_dim:]
    return jnp.concatenate([first * cos_table - second * sin_table, second * cos_table + first * sin_table], axis=-1)

def layout(lengths, number):
    ends_at = jnp.cumsum(lengths).astype(jnp.int32)
    places = jnp.arange(number, dtype=jnp.int32)
    segment = lax.optimization_barrier(jnp.sum((places[:, None] >= ends_at[None, :]).astype(jnp.int32), axis=1))
    starts = ends_at - lengths
    select_mask = (segment[:, None] == jnp.arange(lengths.shape[0], dtype=jnp.int32)[None, :]).astype(jnp.int32)
    position = places - lax.optimization_barrier(jnp.sum(select_mask * starts[None, :], axis=1))
    return (segment, position)

def tables(position):
    half_dim = HEAD_DIM // 2
    inverse = ROPE_BASE ** (-2.0 * jnp.arange(half_dim, dtype=jnp.float32) / HEAD_DIM)
    angles = position.astype(jnp.float32)[:, None] * inverse[None, :]
    return (jnp.cos(angles)[:, None, :], jnp.sin(angles)[:, None, :])

def prepare(projected, query_gain, key_gain, cos_table, sin_table):
    count_rows = projected.shape[0]
    query_heads = root_norm(projected[:, :D], query_gain).reshape(count_rows, HEADS, HEAD_DIM)
    key_heads = root_norm(projected[:, D:2 * D], key_gain).reshape(count_rows, HEADS, HEAD_DIM)
    value_heads = projected[:, 2 * D:].reshape(count_rows, HEADS, HEAD_DIM)
    return (rotary(query_heads, cos_table, sin_table), rotary(key_heads, cos_table, sin_table), value_heads)

def softmax_rows(logits):
    row_max = lax.optimization_barrier(jnp.max(logits, axis=-1, keepdims=True))
    exponent = jnp.exp(logits - row_max)
    return exponent / lax.optimization_barrier(jnp.sum(exponent, axis=-1, keepdims=True))

def attend_device(member):
    query_heads, key_heads, value_heads, segment = member
    places = jnp.arange(segment.shape[0], dtype=jnp.int32)
    allowed = (segment[:, None] == segment[None, :]) & (places[:, None] >= places[None, :])
    scores = jnp.einsum('qhd,khd->hqk', query_heads, key_heads, precision=lax.Precision.HIGHEST) * HEAD_DIM ** (-0.5)
    scores = low_back(jnp.where(allowed[None], scores, MASKED))
    weights = low(softmax_rows(scores))
    return jnp.einsum('hqk,khd->qhd', weights, value_heads, precision=lax.Precision.HIGHEST)

def forward(inputs, gain_rows, attention_in, attention_out, router_weight, expert_in, expert_out, segment, cos_table, sin_table, routes, sources, occupied, target):
    normed_input = low(root_norm(inputs, gain_rows[0]))
    projected = low_back(product(normed_input, attention_in))
    query_heads, key_heads, value_heads = prepare(projected, gain_rows[1], gain_rows[2], cos_table, sin_table)
    layout_shape = (N_FSDP, TOK_DEV, HEADS, HEAD_DIM)
    attended = lax.map(jax.checkpoint(attend_device), (low(query_heads).reshape(layout_shape), low(key_heads).reshape(layout_shape), low(value_heads).reshape(layout_shape), segment))
    attended = low(low_back(attended.reshape(TOKENS, D)))
    branch_out = low_back(product(attended, attention_out))
    residual = inputs + branch_out
    normed = low(root_norm(residual, gain_rows[3]))
    logits = low_back(product(normed, router_weight))
    router_probs = softmax_rows(logits)
    chosen = jnp.take_along_axis(router_probs, routes, axis=1)
    gate_values = chosen / lax.optimization_barrier(jnp.sum(chosen, axis=1, keepdims=True))
    routed_rows = jnp.broadcast_to(normed[:, None, :], (TOKENS, TOP, D)).reshape(TOKENS * TOP, D)
    half_units = FF // 2

    def run_expert(member):
        source_rows, live_rows, weight_in, weight_out = member
        arrived = low_back(routed_rows[source_rows] * live_rows[:, None])
        gate_up_out = low_back(product(arrived, weight_in))
        hidden = low(jax.nn.silu(gate_up_out[:, :half_units]) * gate_up_out[:, half_units:])
        return low(low_back(product(hidden, weight_out)))
    half_sources = jnp.repeat(sources, 2, axis=0)
    half_occupied = jnp.repeat(occupied, 2, axis=0)
    produced = lax.map(jax.checkpoint(run_expert), (half_sources, half_occupied, expert_in, expert_out))
    produced = lax.optimization_barrier(jnp.sum(produced.reshape(EXPERTS, 2, N_FSDP * CAP, D), axis=1))
    picked = produced.reshape(EXPERTS * N_FSDP * CAP, D)[target].reshape(TOKENS, TOP, D)
    expert_sum = lax.optimization_barrier(jnp.sum(gate_values[:, :, None] * picked, axis=1))
    return residual + expert_sum

def reference(tokens, cotangent, norm_gains, attention_in, attention_out, router_weight, expert_in, expert_out, routes, lengths):
    segment, position = jax.vmap(lambda row_lengths: layout(row_lengths, TOK_DEV))(lengths)
    cos_table, sin_table = tables(position.reshape(-1))
    device_routes = routes.reshape(N_FSDP, TOK_DEV * TOP)
    route_hits = (device_routes[:, :, None] == jnp.arange(EXPERTS, dtype=jnp.int32)[None, None, :]).astype(jnp.int32)
    slot_index = lax.optimization_barrier(jnp.sum((jnp.cumsum(route_hits, axis=1) - route_hits) * route_hits, axis=2))
    device_ids = jnp.arange(N_FSDP, dtype=jnp.int32)[:, None]
    target = (device_routes * (N_FSDP * CAP) + device_ids * CAP + slot_index).reshape(-1).astype(jnp.int32)
    slot_count = EXPERTS * N_FSDP * CAP
    sources = jnp.zeros((slot_count,), jnp.int32).at[target].set(jnp.arange(TOKENS * TOP, dtype=jnp.int32)).reshape(EXPERTS, N_FSDP * CAP)
    occupied = jnp.zeros((slot_count,), jnp.float32).at[target].set(1.0).reshape(EXPERTS, N_FSDP * CAP)
    parameters = tuple((item.astype(jnp.float32) for item in (tokens, norm_gains, attention_in, attention_out, router_weight, expert_in, expert_out)))

    def apply_layer(*values):
        return forward(*values, segment, cos_table, sin_table, routes, sources, occupied, target)
    result, pullback = jax.vjp(apply_layer, *parameters)
    grads = pullback(cotangent.astype(jnp.float32))
    return (result.astype(jnp.bfloat16), grads[0], grads[1], grads[2], grads[3], grads[4], grads[5], grads[6])
```

```python
import functools

import jax
import jax.numpy as jnp
from jax import lax
from jax.experimental import pallas as pl
from jax.experimental.pallas import tpu as pltpu
from jax.sharding import PartitionSpec as P

D = 2048
HEADS = 16
HEAD_DIM = 128


EPSILON = 1e-05
ROPE_BASE = 10000.0
MASKED = -1000000000.0


def root_norm(vector, scaling):
    return vector * lax.rsqrt(jnp.mean(vector * vector, axis=-1, keepdims=True) + EPSILON) * scaling


def rotary(vector, cos_table, sin_table):
    half_dim = vector.shape[-1] // 2
    first = vector[..., :half_dim]
    second = vector[..., half_dim:]
    return jnp.concatenate(
        [first * cos_table - second * sin_table, second * cos_table + first * sin_table], axis=-1
    )


def layout(lengths, number):
    ends_at = jnp.cumsum(lengths)
    places = jnp.arange(number, dtype=jnp.int32)
    segment = jnp.sum((places[:, None] >= ends_at[None, :]).astype(jnp.int32), axis=1)
    starts = ends_at - lengths
    select_mask = (
        segment[:, None] == jnp.arange(lengths.shape[0], dtype=jnp.int32)[None, :]
    ).astype(jnp.int32)
    position = places - jnp.sum(select_mask * starts[None, :], axis=1)
    return (segment, position)


def tables(position):
    half_dim = HEAD_DIM // 2
    inverse = ROPE_BASE ** (-2.0 * jnp.arange(half_dim, dtype=jnp.float32) / HEAD_DIM)
    angles = position.astype(jnp.float32)[:, None] * inverse[None, :]
    return (jnp.cos(angles)[:, None, :], jnp.sin(angles)[:, None, :])


def prepare(projected, query_gain, key_gain, cos_table, sin_table):
    count_rows = projected.shape[0]
    query_heads = root_norm(projected[:, :D], query_gain).reshape(count_rows, HEADS, HEAD_DIM)
    key_heads = root_norm(projected[:, D : 2 * D], key_gain).reshape(count_rows, HEADS, HEAD_DIM)
    value_heads = projected[:, 2 * D :].reshape(count_rows, HEADS, HEAD_DIM)
    return (
        rotary(query_heads, cos_table, sin_table),
        rotary(key_heads, cos_table, sin_table),
        value_heads,
    )


def softmax_rows(logits):
    row_max = jnp.max(logits, axis=-1, keepdims=True)
    exponent = jnp.exp(logits - row_max)
    return exponent / jnp.sum(exponent, axis=-1, keepdims=True)


def dot_first(left, right):
    return lax.dot_general(
        left, right, (((0,), (0,)), ((), ())), preferred_element_type=jnp.float32
    )


def dot_last(left, right):
    return lax.dot_general(
        left, right, (((1,), (1,)), ((), ())), preferred_element_type=jnp.float32
    )


def shards_routed(
    tokens,
    cotangent,
    norm_gains,
    attention_in,
    attention_out,
    router_weight,
    expert_in,
    expert_out,
    routes,
    lengths,
):
    row_count = tokens.shape[0]
    devices_count = lax.axis_size("fsdp")
    experts = devices_count // 2
    choose = routes.shape[1]
    half_units = expert_out.shape[1]
    capacity = 4 * row_count * choose // (3 * experts)
    scaling = HEAD_DIM ** (-0.5)
    gain_full, gathered_in, gathered_out, gathered_router = (
        lax.all_gather(norm_gains, "fsdp", axis=1, tiled=True),
        lax.all_gather(attention_in, "fsdp", axis=0, tiled=True),
        lax.all_gather(attention_out, "fsdp", axis=0, tiled=True),
        lax.all_gather(router_weight, "fsdp", axis=0, tiled=True),
    )
    gain_rows = gain_full.astype(jnp.float32)
    segment, position = layout(lengths[0], row_count)
    cos_table, sin_table = tables(position)
    places = jnp.arange(row_count, dtype=jnp.int32)
    allowed = ((segment[:, None] == segment[None, :]) & (places[:, None] >= places[None, :]))[None]
    inputs = tokens.astype(jnp.float32)
    normed_input = root_norm(inputs, gain_rows[0]).astype(jnp.bfloat16)
    projected = jnp.dot(normed_input, gathered_in, preferred_element_type=jnp.float32)

    def prepare_local(projected_value, query_gain, key_gain):
        return prepare(projected_value, query_gain, key_gain, cos_table, sin_table)

    (query_f, key_f, value_f), prepare_back = jax.vjp(
        prepare_local, projected, gain_rows[1], gain_rows[2]
    )
    query_heads = query_f.astype(jnp.bfloat16)
    key_heads = key_f.astype(jnp.bfloat16)
    value_heads = value_f.astype(jnp.bfloat16)

    def score_block():
        raw_scores = (
            jnp.einsum("qhd,khd->hqk", query_heads, key_heads, preferred_element_type=jnp.float32)
            * scaling
        )
        return jnp.where(allowed, raw_scores, MASKED)

    scores = score_block()
    row_max = jnp.max(scores, axis=-1, keepdims=True)
    exponent = jnp.exp(scores - row_max)
    row_sum = jnp.sum(exponent, axis=-1, keepdims=True)
    log_total = row_max + jnp.log(row_sum)
    attend_probs = (exponent / row_sum).astype(jnp.bfloat16)
    attended = (
        jnp.einsum("hqk,khd->qhd", attend_probs, value_heads, preferred_element_type=jnp.float32)
        .reshape(row_count, D)
        .astype(jnp.bfloat16)
    )
    branch_out = jnp.dot(attended, gathered_out, preferred_element_type=jnp.float32)
    residual = inputs + branch_out
    normed = root_norm(residual, gain_rows[3]).astype(jnp.bfloat16)
    logits = jnp.dot(normed, gathered_router, preferred_element_type=jnp.float32)
    router_probs = softmax_rows(logits)
    chosen = jnp.take_along_axis(router_probs, routes, axis=1)
    gate_total = jnp.sum(chosen, axis=1, keepdims=True)
    gate_values = chosen / gate_total
    flat_routes = routes.reshape(-1)
    route_hits = (flat_routes[:, None] == jnp.arange(experts, dtype=jnp.int32)[None, :]).astype(
        jnp.int32
    )
    slot_index = jnp.sum((jnp.cumsum(route_hits, axis=0) - route_hits) * route_hits, axis=1)
    target = flat_routes * capacity + slot_index
    owner_token = (
        jnp.zeros((experts * capacity,), jnp.int32)
        .at[target]
        .set(jnp.arange(row_count * choose, dtype=jnp.int32) // choose)
    )
    filled = (
        jnp.zeros((experts * capacity,), jnp.bfloat16)
        .at[target]
        .set(jnp.ones((row_count * choose,), jnp.bfloat16))
    )
    outgoing = jnp.repeat(
        (normed[owner_token] * filled[:, None]).reshape(experts, capacity, D), 2, axis=0
    )
    arrived = lax.all_to_all(outgoing, "fsdp", split_axis=0, concat_axis=0, tiled=True).reshape(
        devices_count * capacity, D
    )
    gate_up_out = jnp.dot(arrived, expert_in[0], preferred_element_type=jnp.float32)
    gate_part = gate_up_out[:, :half_units]
    up_part = gate_up_out[:, half_units:]
    hidden_f, swiglu_back = jax.vjp(
        lambda gate_in, up_in: jax.nn.silu(gate_in) * up_in, gate_part, up_part
    )
    hidden = hidden_f.astype(jnp.bfloat16)
    produced = (
        jnp.dot(hidden, expert_out[0], preferred_element_type=jnp.float32)
        .astype(jnp.bfloat16)
        .reshape(devices_count, capacity, D)
    )
    returned = (
        lax.all_to_all(produced, "fsdp", split_axis=0, concat_axis=0, tiled=True)
        .reshape(experts, 2, capacity, D)
        .astype(jnp.float32)
    )
    returned = jnp.sum(returned, axis=1).reshape(experts * capacity, D)
    picked = returned[target].reshape(row_count, choose, D)
    expert_sum = jnp.sum(gate_values[:, :, None] * picked, axis=1)
    output = (residual + expert_sum).astype(jnp.bfloat16)
    back_in, back_out, back_router = (
        lax.all_gather(attention_in, "fsdp", axis=0, tiled=True),
        lax.all_gather(attention_out, "fsdp", axis=0, tiled=True),
        lax.all_gather(router_weight, "fsdp", axis=0, tiled=True),
    )
    upstream = cotangent.astype(jnp.float32)
    gate_grad = jnp.sum(upstream[:, None, :] * picked, axis=2)
    send_grad = (
        (gate_values[:, :, None] * upstream[:, None, :])
        .astype(jnp.bfloat16)
        .reshape(row_count * choose, D)
    )
    grad_buffer = (
        jnp.zeros((experts * capacity, D), jnp.bfloat16)
        .at[target]
        .set(send_grad)
        .reshape(experts, capacity, D)
    )
    grad_buffer = jnp.repeat(grad_buffer, 2, axis=0)
    grad_arrived = lax.all_to_all(
        grad_buffer, "fsdp", split_axis=0, concat_axis=0, tiled=True
    ).reshape(devices_count * capacity, D)
    grad_hidden = dot_last(grad_arrived, expert_out[0])
    expert_out_grad = dot_first(hidden, grad_arrived)
    grad_gate, grad_up = swiglu_back(grad_hidden)
    grad_gate_up = jnp.concatenate([grad_gate, grad_up], axis=1).astype(jnp.bfloat16)
    expert_in_grad = dot_first(arrived, grad_gate_up)
    grad_rows = (
        dot_last(grad_gate_up, expert_in[0])
        .astype(jnp.bfloat16)
        .reshape(devices_count, capacity, D)
    )
    grad_back = (
        lax.all_to_all(grad_rows, "fsdp", split_axis=0, concat_axis=0, tiled=True)
        .reshape(experts, 2, capacity, D)
        .astype(jnp.float32)
    )
    grad_back = jnp.sum(grad_back, axis=1).reshape(experts * capacity, D)
    dispatch_grad = jnp.sum(grad_back[target].reshape(row_count, choose, D), axis=1)
    chosen_grad = (gate_grad - jnp.sum(gate_grad * gate_values, axis=1, keepdims=True)) / gate_total
    expert_match = (
        routes[:, :, None] == jnp.arange(experts, dtype=jnp.int32)[None, None, :]
    ).astype(jnp.float32)
    prob_grad = jnp.sum(expert_match * chosen_grad[:, :, None], axis=1)
    logit_grad = (
        router_probs * (prob_grad - jnp.sum(prob_grad * router_probs, axis=1, keepdims=True))
    ).astype(jnp.bfloat16)
    router_grad = dot_first(normed, logit_grad)
    normed_grad = dispatch_grad + dot_last(logit_grad, back_router)
    _, second_back = jax.vjp(root_norm, residual, gain_rows[3])
    residual_norm_grad, second_gain_grad = second_back(normed_grad)
    residual_grad = upstream + residual_norm_grad
    branch_grad = residual_grad.astype(jnp.bfloat16)
    out_grad = dot_first(attended, branch_grad)
    attended_grad = (
        dot_last(branch_grad, back_out).astype(jnp.bfloat16).reshape(row_count, HEADS, HEAD_DIM)
    )
    recomputed = jnp.exp(score_block() - log_total)
    value_grad = jnp.einsum(
        "hqk,qhd->khd", attend_probs, attended_grad, preferred_element_type=jnp.float32
    )
    attend_grad = jnp.einsum(
        "qhd,khd->hqk", attended_grad, value_heads, preferred_element_type=jnp.float32
    )
    row_delta = jnp.sum(recomputed * attend_grad, axis=-1, keepdims=True)
    score_grad = (recomputed * (attend_grad - row_delta)).astype(jnp.bfloat16)
    query_grad = (
        jnp.einsum("hqk,khd->qhd", score_grad, key_heads, preferred_element_type=jnp.float32)
        * scaling
    )
    key_grad = (
        jnp.einsum("hqk,qhd->khd", score_grad, query_heads, preferred_element_type=jnp.float32)
        * scaling
    )
    projected_grad, query_gain_grad, key_gain_grad = prepare_back(
        (query_grad, key_grad, value_grad)
    )
    projected_grad = projected_grad.astype(jnp.bfloat16)
    attention_in_grad = dot_first(normed_input, projected_grad)
    normed_input_grad = dot_last(projected_grad, back_in)
    _, first_back = jax.vjp(root_norm, inputs, gain_rows[0])
    input_norm_grad, first_gain_grad = first_back(normed_input_grad)
    input_grad = residual_grad + input_norm_grad
    gains_grad = jnp.stack([first_gain_grad, query_gain_grad, key_gain_grad, second_gain_grad])
    gains_share, in_share, out_share, router_share = (
        lax.psum_scatter(gains_grad, "fsdp", scatter_dimension=1, tiled=True),
        lax.psum_scatter(attention_in_grad, "fsdp", scatter_dimension=0, tiled=True),
        lax.psum_scatter(out_grad, "fsdp", scatter_dimension=0, tiled=True),
        lax.psum_scatter(router_grad, "fsdp", scatter_dimension=0, tiled=True),
    )
    return (
        output,
        input_grad,
        gains_share,
        in_share,
        out_share,
        router_share,
        expert_in_grad[None],
        expert_out_grad[None],
    )


def product(left, right):
    return jnp.dot(left, right, preferred_element_type=jnp.float32)


PLANE = 8
WIDE = 128


class Moves:
    def __init__(self, count):
        planes = count // PLANE
        order = list(range(0, planes, 2)) + list(range(1, planes, 2))[::-1]
        after = {order[i]: order[(i + 1) % planes] for i in range(planes)}
        self.planes = planes
        self.ring = [(i, after[i // PLANE] * PLANE + i % PLANE) for i in range(count)]
        self.first = [(i, i ^ (4 if i & 1 else 2)) for i in range(count)]
        self.second = [(i, i ^ (2 if i & 1 else 4)) for i in range(count)]
        self.core = [(i, i ^ 1) for i in range(count)]


def send(value, pairs):
    return lax.ppermute(value, "fsdp", pairs)


def spread(moves, block):
    groups = []
    current = block
    for step in range(moves.planes):
        if step:
            current = send(current, moves.ring)
        near = send(current, moves.first)
        own = [current, near, send(current, moves.second), send(near, moves.second)]
        groups.append(own + [send(item, moves.core) for item in own])
    return groups


def collect_plane(moves, kept, sent):
    kept = kept.astype(jnp.float32) + send(sent, moves.core).astype(jnp.float32)
    kept = kept.astype(jnp.bfloat16)
    back = send(kept[2:], moves.second)
    near = (kept[1].astype(jnp.float32) + back[1].astype(jnp.float32)).astype(jnp.bfloat16)
    home = kept[0].astype(jnp.float32) + back[0].astype(jnp.float32)
    return home + send(near, moves.first).astype(jnp.float32)


def collect_ring(moves, sums):
    total = sums[1]
    for step in range(2, moves.planes):
        total = sums[step] + send(total.astype(jnp.bfloat16), moves.ring).astype(jnp.float32)
    return sums[0] + send(total.astype(jnp.bfloat16), moves.ring).astype(jnp.float32)


def expert_body(per_step, cap, experts, meta, *refs):
    row_refs, grad_refs = refs[:PLANE], refs[PLANE : 2 * PLANE]
    in_hbm, out_hbm = refs[2 * PLANE : 2 * PLANE + 2]
    outputs = refs[2 * PLANE + 6 : 2 * PLANE + 14]
    x_save, dy_save, m_save, du_save, out_keep, out_send, row_keep, row_send = outputs
    rows_v, grads_v, in_v, out_v, row_sem, grad_sem, weight_sem = refs[2 * PLANE + 14 :]
    step = pl.program_id(0)
    count, width, half = rows_v.shape[1], grads_v.shape[2], out_v.shape[0]
    expert, device = meta[0], meta[1]
    bf, f32 = jnp.bfloat16, jnp.float32

    def fetch_rows(j):
        return pltpu.make_async_copy(row_refs[j], rows_v.at[j], row_sem.at[j])

    def fetch_grads(j):
        return pltpu.make_async_copy(grad_refs[j], grads_v.at[j], grad_sem.at[j])

    fetch_in = pltpu.make_async_copy(in_hbm, in_v, weight_sem.at[0])
    fetch_out = pltpu.make_async_copy(out_hbm, out_v, weight_sem.at[1])

    @pl.when(step == 0)
    def _():
        for j in range(per_step):
            fetch_rows(j).start()
        fetch_in.start()
        for j in range(per_step):
            fetch_grads(j).start()
        fetch_out.start()
        for j in range(per_step, PLANE):
            fetch_rows(j).start()
            fetch_grads(j).start()

    members = [step * per_step + j for j in range(per_step)]
    for j in members:
        pltpu.make_async_copy(row_refs[0], rows_v.at[j], row_sem.at[j]).wait()
    lane8 = lax.broadcasted_iota(jnp.int32, (8, WIDE), 1)
    row8 = lax.broadcasted_iota(jnp.int32, (8, WIDE), 0)
    pick = (
        jnp.where((row8 == 0) & (lane8 == expert), 1.0, 0.0)
        + jnp.where((row8 == 1) & (lane8 == experts + expert), 1.0, 0.0)
        + jnp.where((row8 == 1) & (lane8 == 2 * experts + expert), 1.0, 0.0)
    ).astype(bf)
    lanes = lax.broadcasted_iota(jnp.int32, (count, WIDE), 1)
    slots_down = lax.broadcasted_iota(jnp.int32, (cap, count), 0)
    slots_along = lax.broadcasted_iota(jnp.int32, (count, cap), 1)
    gather, scatter, taken, gates = [], [], [], []
    for j in members:
        extra = rows_v[j, :, width:]
        info = dot_last(pick, extra)
        chosen = slots_down == info[0:1].astype(jnp.int32)
        gates.append(jnp.sum(jnp.where(chosen, info[1:2], 0.0), axis=1, keepdims=True))
        gather.append(jnp.where(chosen, 1.0, 0.0).astype(bf))
        slot = jnp.sum(
            jnp.where(lanes == expert, extra.astype(f32), 0.0), axis=1, keepdims=True
        ).astype(jnp.int32)
        scatter.append(jnp.where(slots_along == slot, 1.0, 0.0).astype(bf))
        taken.append(product(gather[-1], rows_v[j, :, :width]).astype(bf))
    x = jnp.concatenate(taken, axis=0)
    gate = jnp.concatenate(gates, axis=0)
    x_save[...] = x

    @pl.when(step == 0)
    def _():
        fetch_in.wait()

    u = product(x, in_v[...])
    gate_part, up_part = u[:, :half], u[:, half:]
    sigmoid = 1.0 / (1.0 + jnp.exp(-gate_part))
    silu = gate_part * sigmoid
    m = (silu * up_part).astype(bf)
    m_save[...] = m

    @pl.when(step == 0)
    def _():
        fetch_out.wait()

    y = product(m, out_v[...])
    for j in members:
        pltpu.make_async_copy(grad_refs[0], grads_v.at[j], grad_sem.at[j]).wait()
    g = jnp.concatenate([product(gather[i], grads_v[j]) for i, j in enumerate(members)], axis=0)
    dgate = jnp.sum(g * y, axis=1, keepdims=True)
    z = (gate * y).astype(bf)
    dy = (gate * g).astype(bf)
    dy_save[...] = dy
    dm = dot_last(dy, out_v[...])
    slope = sigmoid * (1.0 + gate_part * (1.0 - sigmoid))
    du = jnp.concatenate([dm * up_part * slope, dm * silu], axis=1).astype(bf)
    du_save[...] = du
    drows = dot_last(du, in_v[...]).astype(bf)
    upper = dgate.astype(bf).astype(f32)
    lane_m = lax.broadcasted_iota(jnp.int32, (per_step * cap, WIDE), 1)
    pair = jnp.where(
        lane_m == 2 * device,
        upper,
        jnp.where(lane_m == 2 * device + 1, dgate - upper, 0.0),
    ).astype(bf)

    def put(out_ref, row_ref):
        for i in range(per_step):
            own = slice(i * cap, (i + 1) * cap)
            out_ref[i] = product(scatter[i], z[own]).astype(bf)
            row_ref[i, :, :width] = product(scatter[i], drows[own]).astype(bf)
            row_ref[i, :, width:] = product(scatter[i], pair[own]).astype(bf)

    half_way = PLANE // per_step // 2

    @pl.when(step < half_way)
    def _():
        put(out_keep, row_keep)

    @pl.when(step >= half_way)
    def _():
        put(out_send, row_send)


def expert_group(meta, rows, grads, weight_in, weight_out, saved, index, groups, cap, experts):
    per_step = 2
    count, wide = rows[0].shape
    width, half = grads[0].shape[1], weight_out.shape[0]
    steps = PLANE // per_step
    half_way = steps // 2
    bf = jnp.bfloat16

    def shape(*dims):
        return jax.ShapeDtypeStruct(dims, bf)

    def saves(columns):
        return pl.BlockSpec((per_step * cap, columns), lambda i: (index * steps + i, 0))

    def keeps(columns):
        return pl.BlockSpec((per_step, count, columns), lambda i: (jnp.minimum(i, half_way - 1), 0, 0))

    def sends(columns):
        return pl.BlockSpec((per_step, count, columns), lambda i: (jnp.maximum(i - half_way, 0), 0, 0))

    anywhere = pl.BlockSpec(memory_space=pl.ANY)
    aliases = {2 * PLANE + 3 + t: t for t in range(4)}
    if saved is None:
        saved, aliases = [jnp.zeros((16, WIDE), bf)] * 4, {}
    slots = groups * PLANE * cap
    return pl.pallas_call(
        functools.partial(expert_body, per_step, cap, experts),
        grid=(steps,),
        out_shape=[
            shape(slots, width),
            shape(slots, width),
            shape(slots, half),
            shape(slots, 2 * half),
            shape(PLANE // 2, count, width),
            shape(PLANE // 2, count, width),
            shape(PLANE // 2, count, wide),
            shape(PLANE // 2, count, wide),
        ],
        in_specs=[pl.BlockSpec(memory_space=pltpu.SMEM)] + [anywhere] * (2 * PLANE + 6),
        out_specs=[
            saves(width),
            saves(width),
            saves(half),
            saves(2 * half),
            keeps(width),
            sends(width),
            keeps(wide),
            sends(wide),
        ],
        scratch_shapes=[
            pltpu.VMEM((PLANE, count, wide), bf),
            pltpu.VMEM((PLANE, count, width), bf),
            pltpu.VMEM(weight_in.shape, bf),
            pltpu.VMEM(weight_out.shape, bf),
            pltpu.SemaphoreType.DMA((PLANE,)),
            pltpu.SemaphoreType.DMA((PLANE,)),
            pltpu.SemaphoreType.DMA((2,)),
        ],
        input_output_aliases=aliases,
        compiler_params=pltpu.CompilerParams(
            vmem_limit_bytes=58 << 20, dimension_semantics=("arbitrary",)
        ),
        cost_estimate=pl.CostEstimate(
            flops=16 * 10**9, bytes_accessed=60 << 20, transcendentals=PLANE * cap * half
        ),
        name="expert_group",
    )(meta, *rows, *grads, weight_in, weight_out, *saved)


def shards_dense(
    tokens,
    cotangent,
    norm_gains,
    attention_in,
    attention_out,
    router_weight,
    expert_in,
    expert_out,
    routes,
    lengths,
):
    row_count = tokens.shape[0]
    devices_count = lax.axis_size("fsdp")
    moves = Moves(devices_count)
    device = lax.axis_index("fsdp")
    experts = devices_count // 2
    choose = routes.shape[1]
    capacity = 4 * row_count * choose // (3 * experts)
    scaling = HEAD_DIM ** (-0.5)
    bf = jnp.bfloat16
    gain_full, gathered_in, gathered_out, gathered_router = (
        lax.all_gather(norm_gains, "fsdp", axis=1, tiled=True),
        lax.all_gather(attention_in, "fsdp", axis=0, tiled=True),
        lax.all_gather(attention_out, "fsdp", axis=0, tiled=True),
        lax.all_gather(router_weight, "fsdp", axis=0, tiled=True),
    )
    gain_rows = gain_full.astype(jnp.float32)
    grad_groups = spread(moves, cotangent)

    expert_ids = jnp.arange(experts, dtype=jnp.int32)
    match = jnp.sum((routes[:, :, None] == expert_ids[None, None, :]).astype(jnp.float32), axis=1)
    places = jnp.arange(row_count, dtype=jnp.int32)
    before = (places[:, None] > places[None, :]).astype(bf)
    rank = jnp.where(match > 0, product(before, match.astype(bf)), -1.0).astype(bf)

    segment, position = layout(lengths[0], row_count)
    cos_table, sin_table = tables(position)
    allowed = ((segment[:, None] == segment[None, :]) & (places[:, None] >= places[None, :]))[None]
    inputs = tokens.astype(jnp.float32)
    normed_input = root_norm(inputs, gain_rows[0]).astype(bf)
    projected = product(normed_input, gathered_in)

    def prepare_local(projected_value, query_gain, key_gain):
        return prepare(projected_value, query_gain, key_gain, cos_table, sin_table)

    (query_f, key_f, value_f), prepare_back = jax.vjp(
        prepare_local, projected, gain_rows[1], gain_rows[2]
    )
    query_heads = query_f.astype(bf)
    key_heads = key_f.astype(bf)
    value_heads = value_f.astype(bf)

    def score_block():
        raw_scores = (
            jnp.einsum("qhd,khd->hqk", query_heads, key_heads, preferred_element_type=jnp.float32)
            * scaling
        )
        return jnp.where(allowed, raw_scores, MASKED)

    scores = score_block()
    row_max = jnp.max(scores, axis=-1, keepdims=True)
    exponent = jnp.exp(scores - row_max)
    row_sum = jnp.sum(exponent, axis=-1, keepdims=True)
    log_total = row_max + jnp.log(row_sum)
    attend_probs = (exponent / row_sum).astype(bf)
    attended = (
        jnp.einsum("hqk,khd->qhd", attend_probs, value_heads, preferred_element_type=jnp.float32)
        .reshape(row_count, D)
        .astype(bf)
    )
    branch_out = product(attended, gathered_out)
    residual = inputs + branch_out
    normed = root_norm(residual, gain_rows[3]).astype(bf)
    logits = product(normed, gathered_router)
    router_probs = softmax_rows(logits)
    gate_total = jnp.sum(router_probs * match, axis=1, keepdims=True)
    gate_values = router_probs * match / gate_total
    upper = lax.reduce_precision(gate_values, 8, 7)
    extra = jnp.concatenate(
        [
            rank,
            upper.astype(bf),
            (gate_values - upper).astype(bf),
            jnp.zeros((row_count, WIDE - 3 * experts), bf),
        ],
        axis=1,
    )
    row_groups = spread(moves, jnp.concatenate([normed, extra], axis=1))

    meta = jnp.stack([device // 2, device]).astype(jnp.int32)
    saved, out_parts, row_parts = None, [], []
    for index in range(moves.planes):
        *saved, out_keep, out_send, row_keep, row_send = expert_group(
            meta,
            row_groups[index],
            grad_groups[index],
            expert_in[0],
            expert_out[0],
            saved,
            index,
            moves.planes,
            capacity,
            experts,
        )
        out_parts.append((out_keep, out_send))
        row_parts.append((row_keep, row_send))
    row_total = collect_ring(moves, [collect_plane(moves, *part) for part in row_parts])
    x_rows, dy_rows, m_rows, du_rows = saved
    expert_in_grad = dot_first(x_rows, du_rows)
    expert_out_grad = dot_first(m_rows, dy_rows)

    upstream = cotangent.astype(jnp.float32)
    dispatch_grad = row_total[:, :D]
    gate_grad = jnp.sum(
        row_total[:, D : D + 4 * experts].reshape(row_count, experts, 4), axis=2
    )
    chosen_grad = (
        match * (gate_grad - jnp.sum(gate_grad * gate_values, axis=1, keepdims=True)) / gate_total
    )
    logit_grad = (
        router_probs * (chosen_grad - jnp.sum(chosen_grad * router_probs, axis=1, keepdims=True))
    ).astype(bf)
    router_grad = dot_first(normed, logit_grad)
    normed_grad = dispatch_grad + dot_last(logit_grad, gathered_router)
    _, second_back = jax.vjp(root_norm, residual, gain_rows[3])
    residual_norm_grad, second_gain_grad = second_back(normed_grad)
    residual_grad = upstream + residual_norm_grad
    branch_grad = residual_grad.astype(bf)

    out_parts, branch_grad = lax.optimization_barrier((out_parts, branch_grad))
    out_total = collect_ring(moves, [collect_plane(moves, *part) for part in out_parts])
    output = (residual + out_total).astype(bf)

    out_grad = dot_first(attended, branch_grad)
    attended_grad = (
        dot_last(branch_grad, gathered_out).astype(bf).reshape(row_count, HEADS, HEAD_DIM)
    )
    recomputed = jnp.exp(score_block() - log_total)
    value_grad = jnp.einsum(
        "hqk,qhd->khd", attend_probs, attended_grad, preferred_element_type=jnp.float32
    )
    attend_grad = jnp.einsum(
        "qhd,khd->hqk", attended_grad, value_heads, preferred_element_type=jnp.float32
    )
    row_delta = jnp.sum(recomputed * attend_grad, axis=-1, keepdims=True)
    score_grad = (recomputed * (attend_grad - row_delta)).astype(bf)
    query_grad = (
        jnp.einsum("hqk,khd->qhd", score_grad, key_heads, preferred_element_type=jnp.float32)
        * scaling
    )
    key_grad = (
        jnp.einsum("hqk,qhd->khd", score_grad, query_heads, preferred_element_type=jnp.float32)
        * scaling
    )
    projected_grad, query_gain_grad, key_gain_grad = prepare_back(
        (query_grad, key_grad, value_grad)
    )
    projected_grad = projected_grad.astype(bf)
    attention_in_grad = dot_first(normed_input, projected_grad)
    normed_input_grad = dot_last(projected_grad, gathered_in)
    _, first_back = jax.vjp(root_norm, inputs, gain_rows[0])
    input_norm_grad, first_gain_grad = first_back(normed_input_grad)
    input_grad = residual_grad + input_norm_grad
    gains_grad = jnp.stack([first_gain_grad, query_gain_grad, key_gain_grad, second_gain_grad])
    small = jnp.concatenate([gains_grad.T, router_grad], axis=1)
    small_share, in_share, out_share = (
        lax.psum_scatter(small, "fsdp", scatter_dimension=0, tiled=True),
        lax.psum_scatter(attention_in_grad.astype(bf), "fsdp", scatter_dimension=0, tiled=True),
        lax.psum_scatter(out_grad.astype(bf), "fsdp", scatter_dimension=0, tiled=True),
    )
    return (
        output,
        input_grad,
        small_share[:, :4].T,
        in_share.astype(jnp.float32),
        out_share.astype(jnp.float32),
        small_share[:, 4:],
        expert_in_grad[None],
        expert_out_grad[None],
    )


def shards(*arguments):
    routes = arguments[8]
    experts = lax.axis_size("fsdp") // 2
    if 2 * routes.shape[1] >= experts:
        return shards_dense(*arguments)
    return shards_routed(*arguments)


def solution(mesh):
    in_specs = (
        P("fsdp", None),
        P("fsdp", None),
        P(None, "fsdp"),
        P("fsdp", None),
        P("fsdp", None),
        P("fsdp", None),
        P("fsdp", None, None),
        P("fsdp", None, None),
        P("fsdp", None),
        P("fsdp", None),
    )
    out_specs = (
        P("fsdp", None),
        P("fsdp", None),
        P(None, "fsdp"),
        P("fsdp", None),
        P("fsdp", None),
        P("fsdp", None),
        P("fsdp", None, None),
        P("fsdp", None, None),
    )
    return jax.shard_map(shards, mesh=mesh, in_specs=in_specs, out_specs=out_specs, check_vma=False)
```

```python
import functools

import jax
import jax.numpy as jnp
from jax import lax
from jax.experimental import pallas as pl
from jax.experimental.pallas import tpu as pltpu
from jax.sharding import PartitionSpec as P

D = 2048
HEADS = 16
HEAD_DIM = 128


EPSILON = 1e-05
ROPE_BASE = 10000.0
MASKED = -1000000000.0


def root_norm(vector, scaling):
    return vector * lax.rsqrt(jnp.mean(vector * vector, axis=-1, keepdims=True) + EPSILON) * scaling


def rotary(vector, cos_table, sin_table):
    half_dim = vector.shape[-1] // 2
    first = vector[..., :half_dim]
    second = vector[..., half_dim:]
    return jnp.concatenate(
        [first * cos_table - second * sin_table, second * cos_table + first * sin_table], axis=-1
    )


def layout(lengths, number):
    ends_at = jnp.cumsum(lengths)
    places = jnp.arange(number, dtype=jnp.int32)
    segment = jnp.sum((places[:, None] >= ends_at[None, :]).astype(jnp.int32), axis=1)
    starts = ends_at - lengths
    select_mask = (
        segment[:, None] == jnp.arange(lengths.shape[0], dtype=jnp.int32)[None, :]
    ).astype(jnp.int32)
    position = places - jnp.sum(select_mask * starts[None, :], axis=1)
    return (segment, position)


def tables(position):
    half_dim = HEAD_DIM // 2
    inverse = ROPE_BASE ** (-2.0 * jnp.arange(half_dim, dtype=jnp.float32) / HEAD_DIM)
    angles = position.astype(jnp.float32)[:, None] * inverse[None, :]
    return (jnp.cos(angles)[:, None, :], jnp.sin(angles)[:, None, :])


def prepare(projected, query_gain, key_gain, cos_table, sin_table):
    count_rows = projected.shape[0]
    query_heads = root_norm(projected[:, :D], query_gain).reshape(count_rows, HEADS, HEAD_DIM)
    key_heads = root_norm(projected[:, D : 2 * D], key_gain).reshape(count_rows, HEADS, HEAD_DIM)
    value_heads = projected[:, 2 * D :].reshape(count_rows, HEADS, HEAD_DIM)
    return (
        rotary(query_heads, cos_table, sin_table),
        rotary(key_heads, cos_table, sin_table),
        value_heads,
    )


def softmax_rows(logits):
    row_max = jnp.max(logits, axis=-1, keepdims=True)
    exponent = jnp.exp(logits - row_max)
    return exponent / jnp.sum(exponent, axis=-1, keepdims=True)


def dot_first(left, right):
    return lax.dot_general(
        left, right, (((0,), (0,)), ((), ())), preferred_element_type=jnp.float32
    )


def dot_last(left, right):
    return lax.dot_general(
        left, right, (((1,), (1,)), ((), ())), preferred_element_type=jnp.float32
    )


def shards_routed(
    tokens,
    cotangent,
    norm_gains,
    attention_in,
    attention_out,
    router_weight,
    expert_in,
    expert_out,
    routes,
    lengths,
):
    row_count = tokens.shape[0]
    devices_count = lax.axis_size("fsdp")
    experts = devices_count // 2
    choose = routes.shape[1]
    half_units = expert_out.shape[1]
    capacity = 4 * row_count * choose // (3 * experts)
    scaling = HEAD_DIM ** (-0.5)
    gain_full, gathered_in, gathered_out, gathered_router = (
        lax.all_gather(norm_gains, "fsdp", axis=1, tiled=True),
        lax.all_gather(attention_in, "fsdp", axis=0, tiled=True),
        lax.all_gather(attention_out, "fsdp", axis=0, tiled=True),
        lax.all_gather(router_weight, "fsdp", axis=0, tiled=True),
    )
    gain_rows = gain_full.astype(jnp.float32)
    segment, position = layout(lengths[0], row_count)
    cos_table, sin_table = tables(position)
    places = jnp.arange(row_count, dtype=jnp.int32)
    allowed = ((segment[:, None] == segment[None, :]) & (places[:, None] >= places[None, :]))[None]
    inputs = tokens.astype(jnp.float32)
    normed_input = root_norm(inputs, gain_rows[0]).astype(jnp.bfloat16)
    projected = jnp.dot(normed_input, gathered_in, preferred_element_type=jnp.float32)

    def prepare_local(projected_value, query_gain, key_gain):
        return prepare(projected_value, query_gain, key_gain, cos_table, sin_table)

    (query_f, key_f, value_f), prepare_back = jax.vjp(
        prepare_local, projected, gain_rows[1], gain_rows[2]
    )
    query_heads = query_f.astype(jnp.bfloat16)
    key_heads = key_f.astype(jnp.bfloat16)
    value_heads = value_f.astype(jnp.bfloat16)

    def score_block():
        raw_scores = (
            jnp.einsum("qhd,khd->hqk", query_heads, key_heads, preferred_element_type=jnp.float32)
            * scaling
        )
        return jnp.where(allowed, raw_scores, MASKED)

    scores = score_block()
    row_max = jnp.max(scores, axis=-1, keepdims=True)
    exponent = jnp.exp(scores - row_max)
    row_sum = jnp.sum(exponent, axis=-1, keepdims=True)
    log_total = row_max + jnp.log(row_sum)
    attend_probs = (exponent / row_sum).astype(jnp.bfloat16)
    attended = (
        jnp.einsum("hqk,khd->qhd", attend_probs, value_heads, preferred_element_type=jnp.float32)
        .reshape(row_count, D)
        .astype(jnp.bfloat16)
    )
    branch_out = jnp.dot(attended, gathered_out, preferred_element_type=jnp.float32)
    residual = inputs + branch_out
    normed = root_norm(residual, gain_rows[3]).astype(jnp.bfloat16)
    logits = jnp.dot(normed, gathered_router, preferred_element_type=jnp.float32)
    router_probs = softmax_rows(logits)
    chosen = jnp.take_along_axis(router_probs, routes, axis=1)
    gate_total = jnp.sum(chosen, axis=1, keepdims=True)
    gate_values = chosen / gate_total
    flat_routes = routes.reshape(-1)
    route_hits = (flat_routes[:, None] == jnp.arange(experts, dtype=jnp.int32)[None, :]).astype(
        jnp.int32
    )
    slot_index = jnp.sum((jnp.cumsum(route_hits, axis=0) - route_hits) * route_hits, axis=1)
    target = flat_routes * capacity + slot_index
    owner_token = (
        jnp.zeros((experts * capacity,), jnp.int32)
        .at[target]
        .set(jnp.arange(row_count * choose, dtype=jnp.int32) // choose)
    )
    filled = (
        jnp.zeros((experts * capacity,), jnp.bfloat16)
        .at[target]
        .set(jnp.ones((row_count * choose,), jnp.bfloat16))
    )
    outgoing = jnp.repeat(
        (normed[owner_token] * filled[:, None]).reshape(experts, capacity, D), 2, axis=0
    )
    arrived = lax.all_to_all(outgoing, "fsdp", split_axis=0, concat_axis=0, tiled=True).reshape(
        devices_count * capacity, D
    )
    gate_up_out = jnp.dot(arrived, expert_in[0], preferred_element_type=jnp.float32)
    gate_part = gate_up_out[:, :half_units]
    up_part = gate_up_out[:, half_units:]
    hidden_f, swiglu_back = jax.vjp(
        lambda gate_in, up_in: jax.nn.silu(gate_in) * up_in, gate_part, up_part
    )
    hidden = hidden_f.astype(jnp.bfloat16)
    produced = (
        jnp.dot(hidden, expert_out[0], preferred_element_type=jnp.float32)
        .astype(jnp.bfloat16)
        .reshape(devices_count, capacity, D)
    )
    returned = (
        lax.all_to_all(produced, "fsdp", split_axis=0, concat_axis=0, tiled=True)
        .reshape(experts, 2, capacity, D)
        .astype(jnp.float32)
    )
    returned = jnp.sum(returned, axis=1).reshape(experts * capacity, D)
    picked = returned[target].reshape(row_count, choose, D)
    expert_sum = jnp.sum(gate_values[:, :, None] * picked, axis=1)
    output = (residual + expert_sum).astype(jnp.bfloat16)
    back_in, back_out, back_router = (
        lax.all_gather(attention_in, "fsdp", axis=0, tiled=True),
        lax.all_gather(attention_out, "fsdp", axis=0, tiled=True),
        lax.all_gather(router_weight, "fsdp", axis=0, tiled=True),
    )
    upstream = cotangent.astype(jnp.float32)
    gate_grad = jnp.sum(upstream[:, None, :] * picked, axis=2)
    send_grad = (
        (gate_values[:, :, None] * upstream[:, None, :])
        .astype(jnp.bfloat16)
        .reshape(row_count * choose, D)
    )
    grad_buffer = (
        jnp.zeros((experts * capacity, D), jnp.bfloat16)
        .at[target]
        .set(send_grad)
        .reshape(experts, capacity, D)
    )
    grad_buffer = jnp.repeat(grad_buffer, 2, axis=0)
    grad_arrived = lax.all_to_all(
        grad_buffer, "fsdp", split_axis=0, concat_axis=0, tiled=True
    ).reshape(devices_count * capacity, D)
    grad_hidden = dot_last(grad_arrived, expert_out[0])
    expert_out_grad = dot_first(hidden, grad_arrived)
    grad_gate, grad_up = swiglu_back(grad_hidden)
    grad_gate_up = jnp.concatenate([grad_gate, grad_up], axis=1).astype(jnp.bfloat16)
    expert_in_grad = dot_first(arrived, grad_gate_up)
    grad_rows = (
        dot_last(grad_gate_up, expert_in[0])
        .astype(jnp.bfloat16)
        .reshape(devices_count, capacity, D)
    )
    grad_back = (
        lax.all_to_all(grad_rows, "fsdp", split_axis=0, concat_axis=0, tiled=True)
        .reshape(experts, 2, capacity, D)
        .astype(jnp.float32)
    )
    grad_back = jnp.sum(grad_back, axis=1).reshape(experts * capacity, D)
    dispatch_grad = jnp.sum(grad_back[target].reshape(row_count, choose, D), axis=1)
    chosen_grad = (gate_grad - jnp.sum(gate_grad * gate_values, axis=1, keepdims=True)) / gate_total
    expert_match = (
        routes[:, :, None] == jnp.arange(experts, dtype=jnp.int32)[None, None, :]
    ).astype(jnp.float32)
    prob_grad = jnp.sum(expert_match * chosen_grad[:, :, None], axis=1)
    logit_grad = (
        router_probs * (prob_grad - jnp.sum(prob_grad * router_probs, axis=1, keepdims=True))
    ).astype(jnp.bfloat16)
    router_grad = dot_first(normed, logit_grad)
    normed_grad = dispatch_grad + dot_last(logit_grad, back_router)
    _, second_back = jax.vjp(root_norm, residual, gain_rows[3])
    residual_norm_grad, second_gain_grad = second_back(normed_grad)
    residual_grad = upstream + residual_norm_grad
    branch_grad = residual_grad.astype(jnp.bfloat16)
    out_grad = dot_first(attended, branch_grad)
    attended_grad = (
        dot_last(branch_grad, back_out).astype(jnp.bfloat16).reshape(row_count, HEADS, HEAD_DIM)
    )
    recomputed = jnp.exp(score_block() - log_total)
    value_grad = jnp.einsum(
        "hqk,qhd->khd", attend_probs, attended_grad, preferred_element_type=jnp.float32
    )
    attend_grad = jnp.einsum(
        "qhd,khd->hqk", attended_grad, value_heads, preferred_element_type=jnp.float32
    )
    row_delta = jnp.sum(recomputed * attend_grad, axis=-1, keepdims=True)
    score_grad = (recomputed * (attend_grad - row_delta)).astype(jnp.bfloat16)
    query_grad = (
        jnp.einsum("hqk,khd->qhd", score_grad, key_heads, preferred_element_type=jnp.float32)
        * scaling
    )
    key_grad = (
        jnp.einsum("hqk,qhd->khd", score_grad, query_heads, preferred_element_type=jnp.float32)
        * scaling
    )
    projected_grad, query_gain_grad, key_gain_grad = prepare_back(
        (query_grad, key_grad, value_grad)
    )
    projected_grad = projected_grad.astype(jnp.bfloat16)
    attention_in_grad = dot_first(normed_input, projected_grad)
    normed_input_grad = dot_last(projected_grad, back_in)
    _, first_back = jax.vjp(root_norm, inputs, gain_rows[0])
    input_norm_grad, first_gain_grad = first_back(normed_input_grad)
    input_grad = residual_grad + input_norm_grad
    gains_grad = jnp.stack([first_gain_grad, query_gain_grad, key_gain_grad, second_gain_grad])
    gains_share, in_share, out_share, router_share = (
        lax.psum_scatter(gains_grad, "fsdp", scatter_dimension=1, tiled=True),
        lax.psum_scatter(attention_in_grad, "fsdp", scatter_dimension=0, tiled=True),
        lax.psum_scatter(out_grad, "fsdp", scatter_dimension=0, tiled=True),
        lax.psum_scatter(router_grad, "fsdp", scatter_dimension=0, tiled=True),
    )
    return (
        output,
        input_grad,
        gains_share,
        in_share,
        out_share,
        router_share,
        expert_in_grad[None],
        expert_out_grad[None],
    )


def product(left, right):
    return jnp.dot(left, right, preferred_element_type=jnp.float32)


PLANE = 8
WIDE = 128


class Moves:
    def __init__(self, count):
        planes = count // PLANE
        order = list(range(0, planes, 2)) + list(range(1, planes, 2))[::-1]
        after = {order[i]: order[(i + 1) % planes] for i in range(planes)}
        self.planes = planes
        self.ring = [(i, after[i // PLANE] * PLANE + i % PLANE) for i in range(count)]
        self.first = [(i, i ^ (4 if i & 1 else 2)) for i in range(count)]
        self.second = [(i, i ^ (2 if i & 1 else 4)) for i in range(count)]
        self.core = [(i, i ^ 1) for i in range(count)]
        self.flip = [[(i, i ^ mask) for i in range(count)] for mask in range(PLANE)]
        self.masks = ((0, 2, 4, 6, 1, 5, 3, 7), (0, 4, 2, 6, 1, 3, 5, 7))
        device = lax.axis_index("fsdp")
        self.device = device
        self.place, self.plane, self.core_id = device % PLANE, device // PLANE, device % 2
        spots = jnp.asarray([order.index(i) for i in range(planes)], jnp.int32)
        self.planes_back = jnp.asarray(order, jnp.int32)[
            (spots[self.plane] - jnp.arange(planes, dtype=jnp.int32)) % planes
        ]
        self.steps_from = (spots[self.plane] - spots) % planes


def send(value, pairs):
    return lax.ppermute(value, "fsdp", pairs)


def pick(value, index):
    return lax.dynamic_index_in_dim(value, index, 0, keepdims=False)


def spread_plane(moves, block):
    near = send(block, moves.first)
    own = [block, near, send(block, moves.second), send(near, moves.second)]
    return own + [send(item, moves.core) for item in own]


def spread(moves, block):
    groups = []
    for step in range(moves.planes):
        if step:
            block = send(block, moves.ring)
        groups.append(spread_plane(moves, block))
    return groups


def round_ring(moves, block):
    blocks = [block]
    for _ in range(1, moves.planes):
        blocks.append(send(blocks[-1], moves.ring))
    return blocks


def trade(moves, pieces):
    got = [pick(pieces, moves.place)]
    for mask in range(1, PLANE):
        got.append(send(pick(pieces, moves.place ^ mask), moves.flip[mask]))
    return jnp.take(jnp.stack(got), moves.place ^ jnp.arange(PLANE, dtype=jnp.int32), axis=0)


def plane_total(moves, parts):
    even, odd = moves.masks
    swap = moves.core_id == 0
    parts = jnp.where(
        swap,
        jnp.stack([parts[:, even.index(m)] for m in range(PLANE)], axis=1),
        jnp.stack([parts[:, odd.index(m)] for m in range(PLANE)], axis=1),
    )
    for bit in (1, 2, 4):
        other = send(parts, moves.flip[bit])
        parts = parts + jnp.stack([other[:, m ^ bit] for m in range(PLANE)], axis=1)
    return jnp.where(
        swap,
        jnp.stack([parts[:, m] for m in even], axis=1),
        jnp.stack([parts[:, m] for m in odd], axis=1),
    )


def collect_plane(moves, kept, sent):
    kept = kept.astype(jnp.float32) + send(sent, moves.core).astype(jnp.float32)
    kept = kept.astype(jnp.bfloat16)
    back = send(kept[2:], moves.second)
    near = (kept[1].astype(jnp.float32) + back[1].astype(jnp.float32)).astype(jnp.bfloat16)
    home = kept[0].astype(jnp.float32) + back[0].astype(jnp.float32)
    return home + send(near, moves.first).astype(jnp.float32)


def collect_ring(moves, sums, kind=jnp.bfloat16):
    total = sums[1]
    for step in range(2, moves.planes):
        total = sums[step] + send(total.astype(kind), moves.ring).astype(jnp.float32)
    return sums[0] + send(total.astype(kind), moves.ring).astype(jnp.float32)


def expert_body(per_step, cap, experts, meta, *refs):
    row_refs, grad_refs = refs[:PLANE], refs[PLANE : 2 * PLANE]
    in_hbm, out_hbm = refs[2 * PLANE : 2 * PLANE + 2]
    outputs = refs[2 * PLANE + 6 : 2 * PLANE + 14]
    x_save, dy_save, m_save, du_save, out_keep, out_send, row_keep, row_send = outputs
    rows_v, grads_v, in_v, out_v, row_sem, grad_sem, weight_sem = refs[2 * PLANE + 14 :]
    step = pl.program_id(0)
    count, width, half = rows_v.shape[1], grads_v.shape[2], out_v.shape[0]
    expert, device = meta[0], meta[1]
    bf, f32 = jnp.bfloat16, jnp.float32

    def fetch_rows(j):
        return pltpu.make_async_copy(row_refs[j], rows_v.at[j], row_sem.at[j])

    def fetch_grads(j):
        return pltpu.make_async_copy(grad_refs[j], grads_v.at[j], grad_sem.at[j])

    fetch_in = pltpu.make_async_copy(in_hbm, in_v, weight_sem.at[0])
    fetch_out = pltpu.make_async_copy(out_hbm, out_v, weight_sem.at[1])

    @pl.when(step == 0)
    def _():
        for j in range(per_step):
            fetch_rows(j).start()
        fetch_in.start()
        for j in range(per_step):
            fetch_grads(j).start()
        fetch_out.start()
        for j in range(per_step, PLANE):
            fetch_rows(j).start()
            fetch_grads(j).start()

    members = [step * per_step + j for j in range(per_step)]
    for j in members:
        pltpu.make_async_copy(row_refs[0], rows_v.at[j], row_sem.at[j]).wait()
    lane8 = lax.broadcasted_iota(jnp.int32, (8, WIDE), 1)
    row8 = lax.broadcasted_iota(jnp.int32, (8, WIDE), 0)
    pick = (
        jnp.where((row8 == 0) & (lane8 == expert), 1.0, 0.0)
        + jnp.where((row8 == 1) & (lane8 == experts + expert), 1.0, 0.0)
        + jnp.where((row8 == 1) & (lane8 == 2 * experts + expert), 1.0, 0.0)
    ).astype(bf)
    lanes = lax.broadcasted_iota(jnp.int32, (count, WIDE), 1)
    slots_down = lax.broadcasted_iota(jnp.int32, (cap, count), 0)
    slots_along = lax.broadcasted_iota(jnp.int32, (count, cap), 1)
    gather, scatter, taken, gates = [], [], [], []
    for j in members:
        extra = rows_v[j, :, width:]
        info = dot_last(pick, extra)
        chosen = slots_down == info[0:1].astype(jnp.int32)
        gates.append(jnp.sum(jnp.where(chosen, info[1:2], 0.0), axis=1, keepdims=True))
        gather.append(jnp.where(chosen, 1.0, 0.0).astype(bf))
        slot = jnp.sum(
            jnp.where(lanes == expert, extra.astype(f32), 0.0), axis=1, keepdims=True
        ).astype(jnp.int32)
        scatter.append(jnp.where(slots_along == slot, 1.0, 0.0).astype(bf))
        taken.append(product(gather[-1], rows_v[j, :, :width]).astype(bf))
    x = jnp.concatenate(taken, axis=0)
    gate = jnp.concatenate(gates, axis=0)
    x_save[...] = x

    @pl.when(step == 0)
    def _():
        fetch_in.wait()

    u = product(x, in_v[...])
    gate_part, up_part = u[:, :half], u[:, half:]
    sigmoid = 1.0 / (1.0 + jnp.exp(-gate_part))
    silu = gate_part * sigmoid
    m = (silu * up_part).astype(bf)
    m_save[...] = m

    @pl.when(step == 0)
    def _():
        fetch_out.wait()

    y = product(m, out_v[...])
    for j in members:
        pltpu.make_async_copy(grad_refs[0], grads_v.at[j], grad_sem.at[j]).wait()
    g = jnp.concatenate([product(gather[i], grads_v[j]) for i, j in enumerate(members)], axis=0)
    dgate = jnp.sum(g * y, axis=1, keepdims=True)
    z = (gate * y).astype(bf)
    dy = (gate * g).astype(bf)
    dy_save[...] = dy
    dm = dot_last(dy, out_v[...])
    slope = sigmoid * (1.0 + gate_part * (1.0 - sigmoid))
    du = jnp.concatenate([dm * up_part * slope, dm * silu], axis=1).astype(bf)
    du_save[...] = du
    drows = dot_last(du, in_v[...]).astype(bf)
    upper = dgate.astype(bf).astype(f32)
    lane_m = lax.broadcasted_iota(jnp.int32, (per_step * cap, WIDE), 1)
    pair = jnp.where(
        lane_m == 2 * device,
        upper,
        jnp.where(lane_m == 2 * device + 1, dgate - upper, 0.0),
    ).astype(bf)

    def put(out_ref, row_ref):
        for i in range(per_step):
            own = slice(i * cap, (i + 1) * cap)
            out_ref[i] = product(scatter[i], z[own]).astype(bf)
            row_ref[i, :, :width] = product(scatter[i], drows[own]).astype(bf)
            row_ref[i, :, width:] = product(scatter[i], pair[own]).astype(bf)

    half_way = PLANE // per_step // 2

    @pl.when(step < half_way)
    def _():
        put(out_keep, row_keep)

    @pl.when(step >= half_way)
    def _():
        put(out_send, row_send)


def expert_group(meta, rows, grads, weight_in, weight_out, saved, index, groups, cap, experts):
    per_step = 2
    count, wide = rows[0].shape
    width, half = grads[0].shape[1], weight_out.shape[0]
    steps = PLANE // per_step
    half_way = steps // 2
    bf = jnp.bfloat16

    def shape(*dims):
        return jax.ShapeDtypeStruct(dims, bf)

    def saves(columns):
        return pl.BlockSpec((per_step * cap, columns), lambda i: (index * steps + i, 0))

    def keeps(columns):
        return pl.BlockSpec((per_step, count, columns), lambda i: (jnp.minimum(i, half_way - 1), 0, 0))

    def sends(columns):
        return pl.BlockSpec((per_step, count, columns), lambda i: (jnp.maximum(i - half_way, 0), 0, 0))

    anywhere = pl.BlockSpec(memory_space=pl.ANY)
    aliases = {2 * PLANE + 3 + t: t for t in range(4)}
    if saved is None:
        saved, aliases = [jnp.zeros((16, WIDE), bf)] * 4, {}
    slots = groups * PLANE * cap
    return pl.pallas_call(
        functools.partial(expert_body, per_step, cap, experts),
        grid=(steps,),
        out_shape=[
            shape(slots, width),
            shape(slots, width),
            shape(slots, half),
            shape(slots, 2 * half),
            shape(PLANE // 2, count, width),
            shape(PLANE // 2, count, width),
            shape(PLANE // 2, count, wide),
            shape(PLANE // 2, count, wide),
        ],
        in_specs=[pl.BlockSpec(memory_space=pltpu.SMEM)] + [anywhere] * (2 * PLANE + 6),
        out_specs=[
            saves(width),
            saves(width),
            saves(half),
            saves(2 * half),
            keeps(width),
            sends(width),
            keeps(wide),
            sends(wide),
        ],
        scratch_shapes=[
            pltpu.VMEM((PLANE, count, wide), bf),
            pltpu.VMEM((PLANE, count, width), bf),
            pltpu.VMEM(weight_in.shape, bf),
            pltpu.VMEM(weight_out.shape, bf),
            pltpu.SemaphoreType.DMA((PLANE,)),
            pltpu.SemaphoreType.DMA((PLANE,)),
            pltpu.SemaphoreType.DMA((2,)),
        ],
        input_output_aliases=aliases,
        compiler_params=pltpu.CompilerParams(
            vmem_limit_bytes=58 << 20, dimension_semantics=("arbitrary",)
        ),
        cost_estimate=pl.CostEstimate(
            flops=16 * 10**9, bytes_accessed=60 << 20, transcendentals=PLANE * cap * half
        ),
        name="expert_group",
    )(meta, *rows, *grads, weight_in, weight_out, *saved)


def turn(pairs, cos_table, sin_table, way):
    half_dim = HEAD_DIM // 2
    first, second = pairs[..., :half_dim], pairs[..., half_dim:]
    sin_table = way * sin_table
    return jnp.concatenate(
        [first * cos_table - second * sin_table, second * cos_table + first * sin_table], axis=-1
    )


SMALL = 20


def shards_dense(
    tokens,
    cotangent,
    norm_gains,
    attention_in,
    attention_out,
    router_weight,
    expert_in,
    expert_out,
    routes,
    lengths,
):
    row_count = tokens.shape[0]
    devices_count = lax.axis_size("fsdp")
    moves = Moves(devices_count)
    experts = devices_count // 2
    choose = routes.shape[1]
    capacity = 4 * row_count * choose // (3 * experts)
    scaling = HEAD_DIM ** (-0.5)
    bf, f32 = jnp.bfloat16, jnp.float32
    own_rows = attention_in.shape[0]
    heads = HEADS // PLANE
    mine = heads * HEAD_DIM
    columns = HEADS // 4
    core, column = moves.core_id, moves.place // 2

    small = jnp.concatenate([router_weight, norm_gains.T], axis=1).reshape(-1)
    riders = jnp.concatenate([small, lengths[0].astype(bf)])
    riders = jnp.pad(riders, (0, 2 * 3 * mine - riders.shape[0])).reshape(2, 3 * mine)
    pieces = (
        attention_in.reshape(own_rows, 3, 2, heads, columns, HEAD_DIM)
        .transpose(4, 2, 0, 1, 3, 5)
        .reshape(PLANE, own_rows, 3 * mine)
    )
    pieces = jnp.concatenate(
        [pieces, jnp.broadcast_to(jnp.pad(riders, ((0, 6), (0, 0))), (PLANE, 8, 3 * mine))], axis=1
    )
    arrived = trade(moves, pieces)
    token_blocks = spread_plane(moves, tokens)
    rider_ring = round_ring(moves, arrived[:, own_rows : own_rows + 2].reshape(2 * PLANE, 3 * mine))
    in_ring = round_ring(moves, arrived[:, :own_rows].reshape(PLANE * own_rows, 3 * mine))
    out_ring = round_ring(moves, attention_out)
    grad_groups = spread(moves, cotangent)

    riders_all = jnp.stack(rider_ring).reshape(moves.planes, PLANE, 6 * mine)
    lengths_plane = riders_all[0, :, small.shape[0] : small.shape[0] + lengths.shape[1]]
    masks = jnp.where(core == 0, *(jnp.asarray(m, jnp.int32) for m in moves.masks))
    lengths_all = jnp.take(lengths_plane, moves.place ^ masks, axis=0).astype(jnp.int32)
    small_all = jnp.take(riders_all[:, :, : small.shape[0]], moves.steps_from, axis=0)
    small_all = small_all.reshape(D, SMALL).astype(f32)
    router_full, gain_rows = small_all[:, : SMALL - 4].astype(bf), small_all[:, SMALL - 4 :].T

    def own_heads(full):
        return full.reshape(2, heads, columns, HEAD_DIM)[core, :, column].reshape(1, mine)

    query_gain, key_gain = own_heads(gain_rows[1]), own_heads(gain_rows[2])
    in_full = jnp.take(jnp.stack(in_ring), moves.steps_from, axis=0).reshape(D, 3 * mine)
    out_line = jnp.take(jnp.stack(out_ring), moves.steps_from, axis=0)
    out_mine = lax.dynamic_slice_in_dim(out_line, heads * core, heads, 0)
    out_other = send(lax.dynamic_slice_in_dim(out_line, heads * (1 - core), heads, 0), moves.core)
    out_full = jnp.stack(
        [jnp.where(core == 0, out_mine, out_other), jnp.where(core == 0, out_other, out_mine)],
        axis=1,
    ).reshape(mine, D)

    expert_ids = jnp.arange(experts, dtype=jnp.int32)
    match = jnp.sum((routes[:, :, None] == expert_ids[None, None, :]).astype(f32), axis=1)
    places = jnp.arange(row_count, dtype=jnp.int32)
    before = (places[:, None] > places[None, :]).astype(bf)
    rank = jnp.where(match > 0, product(before, match.astype(bf)), -1.0).astype(bf)

    segment, position = jax.vmap(lambda item: layout(item, row_count))(lengths_all)
    cos_table, sin_table = tables(position.reshape(-1))
    allowed = (segment[:, :, None] == segment[:, None, :]) & (
        places[:, None] >= places[None, :]
    )[None]
    allowed = allowed[:, None]
    token_all = jnp.concatenate(token_blocks, axis=0).astype(f32)
    normed_all = root_norm(token_all, gain_rows[0][None]).astype(bf)
    projected = sum(
        product(
            lax.dynamic_slice_in_dim(
                normed_all, moves.planes_back[step] * PLANE * own_rows, PLANE * own_rows, 1
            ),
            in_ring[step],
        )
        for step in range(moves.planes)
    )
    query_raw, key_raw, value_raw = (projected[:, i * mine : (i + 1) * mine] for i in range(3))

    def by_block(value):
        return value.reshape(PLANE, row_count, heads, HEAD_DIM)

    def row_totals(first, second):
        sums = jnp.stack([jnp.sum(first, axis=1), jnp.sum(second, axis=1)])
        sums = plane_total(moves, sums.reshape(2, PLANE, row_count)).reshape(2, -1, 1)
        return sums[0], sums[1]

    query_sum, key_sum = row_totals(query_raw * query_raw, key_raw * key_raw)
    query_root = lax.rsqrt(query_sum / D + EPSILON)
    key_root = lax.rsqrt(key_sum / D + EPSILON)

    def turned(raw, root, gain, way=1.0):
        value = (raw * root * gain).reshape(-1, heads, HEAD_DIM)
        return turn(value, cos_table, sin_table, way)

    query_heads = by_block(turned(query_raw, query_root, query_gain).astype(bf))
    key_heads = by_block(turned(key_raw, key_root, key_gain).astype(bf))
    value_heads = by_block(value_raw.astype(bf))

    def score_block():
        raw_scores = (
            jnp.einsum("bqhd,bkhd->bhqk", query_heads, key_heads, preferred_element_type=f32)
            * scaling
        )
        return jnp.where(allowed, raw_scores, MASKED)

    scores = score_block()
    row_max = jnp.max(scores, axis=-1, keepdims=True)
    exponent = jnp.exp(scores - row_max)
    row_sum = jnp.sum(exponent, axis=-1, keepdims=True)
    log_total = row_max + jnp.log(row_sum)
    attend_probs = (exponent / row_sum).astype(bf)
    attended = (
        jnp.einsum("bhqk,bkhd->bqhd", attend_probs, value_heads, preferred_element_type=f32)
        .reshape(-1, mine)
        .astype(bf)
    )

    def home(partial):
        partial = partial.astype(bf).reshape(PLANE, row_count, D)
        return collect_plane(moves, partial[: PLANE // 2], partial[PLANE // 2 :])

    inputs = tokens.astype(f32)
    residual = inputs + home(product(attended, out_full))
    normed = root_norm(residual, gain_rows[3][None]).astype(bf)
    logits = product(normed, router_full)
    router_probs = softmax_rows(logits)
    gate_total = jnp.sum(router_probs * match, axis=1, keepdims=True)
    gate_values = router_probs * match / gate_total
    upper = lax.reduce_precision(gate_values, 8, 7)
    extra = jnp.concatenate(
        [
            rank,
            upper.astype(bf),
            (gate_values - upper).astype(bf),
            jnp.zeros((row_count, WIDE - 3 * experts), bf),
        ],
        axis=1,
    )
    row_groups = spread(moves, jnp.concatenate([normed, extra], axis=1))

    meta = jnp.stack([moves.device // 2, moves.device]).astype(jnp.int32)
    saved, out_parts, row_parts = None, [], []
    for index in range(moves.planes):
        *saved, out_keep, out_send, row_keep, row_send = expert_group(
            meta,
            row_groups[index],
            grad_groups[index],
            expert_in[0],
            expert_out[0],
            saved,
            index,
            moves.planes,
            capacity,
            experts,
        )
        out_parts.append((out_keep, out_send))
        row_parts.append((row_keep, row_send))
    row_total = collect_ring(moves, [collect_plane(moves, *part) for part in row_parts])
    x_rows, dy_rows, m_rows, du_rows = saved
    expert_in_grad = dot_first(x_rows, du_rows)
    expert_out_grad = dot_first(m_rows, dy_rows)

    upstream = cotangent.astype(f32)
    dispatch_grad = row_total[:, :D]
    gate_grad = jnp.sum(row_total[:, D : D + 4 * experts].reshape(row_count, experts, 4), axis=2)
    chosen_grad = (
        match * (gate_grad - jnp.sum(gate_grad * gate_values, axis=1, keepdims=True)) / gate_total
    )
    logit_grad = (
        router_probs * (chosen_grad - jnp.sum(chosen_grad * router_probs, axis=1, keepdims=True))
    ).astype(bf)
    router_grad = dot_first(normed, logit_grad)
    normed_grad = dispatch_grad + dot_last(logit_grad, router_full)
    _, second_back = jax.vjp(root_norm, residual, gain_rows[3])
    residual_norm_grad, second_gain_grad = second_back(normed_grad)
    residual_grad = upstream + residual_norm_grad
    branch_all = jnp.concatenate(spread_plane(moves, residual_grad.astype(bf)), axis=0)

    out_parts, branch_all = lax.optimization_barrier((out_parts, branch_all))
    out_total = collect_ring(moves, [collect_plane(moves, *part) for part in out_parts])
    output = (residual + out_total).astype(bf)

    out_grad = dot_first(attended, branch_all).astype(bf).reshape(heads, 2, own_rows, D)
    out_grad_mine = jnp.where(core == 0, out_grad[:, 0], out_grad[:, 1])
    out_grad_other = send(jnp.where(core == 0, out_grad[:, 1], out_grad[:, 0]), moves.core)
    out_grad_line = jnp.where(
        core == 0,
        jnp.concatenate([out_grad_mine, out_grad_other]),
        jnp.concatenate([out_grad_other, out_grad_mine]),
    )
    out_share = collect_ring(
        moves,
        [pick(out_grad_line, moves.planes_back[k]).astype(f32) for k in range(moves.planes)],
    )

    attended_grad = by_block(dot_last(branch_all, out_full).astype(bf))
    recomputed = jnp.exp(score_block() - log_total)
    value_grad = jnp.einsum(
        "bhqk,bqhd->bkhd", attend_probs, attended_grad, preferred_element_type=f32
    )
    attend_grad = jnp.einsum(
        "bqhd,bkhd->bhqk", attended_grad, value_heads, preferred_element_type=f32
    )
    row_delta = jnp.sum(recomputed * attend_grad, axis=-1, keepdims=True)
    score_grad = (recomputed * (attend_grad - row_delta)).astype(bf)
    query_grad = (
        jnp.einsum("bhqk,bkhd->bqhd", score_grad, key_heads, preferred_element_type=f32) * scaling
    )
    key_grad = (
        jnp.einsum("bhqk,bqhd->bkhd", score_grad, query_heads, preferred_element_type=f32)
        * scaling
    )

    def back_turned(value):
        value = value.reshape(-1, heads, HEAD_DIM)
        return turn(value, cos_table, sin_table, -1.0).reshape(-1, mine)

    query_grad, key_grad = back_turned(query_grad), back_turned(key_grad)
    query_dot, key_dot = row_totals(
        query_grad * query_gain * query_raw, key_grad * key_gain * key_raw
    )

    def norm_back(grad, raw, root, gain, dots):
        return root * gain * grad - raw * (root * root * root * dots / D)

    projected_grad = jnp.concatenate(
        [
            norm_back(query_grad, query_raw, query_root, query_gain, query_dot),
            norm_back(key_grad, key_raw, key_root, key_gain, key_dot),
            value_grad.reshape(-1, mine),
        ],
        axis=1,
    ).astype(bf)
    in_grad = dot_first(normed_all, projected_grad).astype(bf)
    in_sum = collect_ring(
        moves,
        [
            lax.dynamic_slice_in_dim(
                in_grad, moves.planes_back[k] * PLANE * own_rows, PLANE * own_rows, 0
            ).astype(f32)
            for k in range(moves.planes)
        ],
    )
    in_share = (
        trade(moves, in_sum.astype(bf).reshape(PLANE, own_rows, 3 * mine))
        .reshape(columns, 2, own_rows, 3, heads, HEAD_DIM)
        .transpose(2, 3, 1, 4, 0, 5)
        .reshape(own_rows, 3 * D)
        .astype(f32)
    )
    normed_input_grad = home(dot_last(projected_grad, in_full))
    _, first_back = jax.vjp(root_norm, inputs, gain_rows[0])
    input_norm_grad, first_gain_grad = first_back(normed_input_grad)
    input_grad = residual_grad + input_norm_grad

    def own_gain(grad, raw, root):
        own = jnp.sum(grad * raw * root, axis=0).reshape(1, heads, 1, HEAD_DIM)
        here = (jnp.arange(2) == core)[:, None, None, None] & (jnp.arange(columns) == column)[
            None, None, :, None
        ]
        return jnp.where(here, own, 0.0).reshape(D)

    gains_grad = jnp.stack(
        [
            first_gain_grad,
            own_gain(query_grad, query_raw, query_root),
            own_gain(key_grad, key_raw, key_root),
            second_gain_grad,
        ],
        axis=1,
    )
    small_grad = jnp.concatenate([router_grad, gains_grad], axis=1)
    small_grad = small_grad.reshape(moves.planes, PLANE, own_rows * SMALL)
    small_sum = collect_ring(
        moves, [pick(small_grad, moves.planes_back[k]) for k in range(moves.planes)], f32
    )
    small_share = jnp.sum(trade(moves, small_sum.reshape(PLANE, -1, WIDE)), axis=0)
    small_share = small_share.reshape(own_rows, SMALL)
    return (
        output,
        input_grad,
        small_share[:, SMALL - 4 :].T,
        in_share,
        out_share,
        small_share[:, : SMALL - 4],
        expert_in_grad[None],
        expert_out_grad[None],
    )


def shards(*arguments):
    routes = arguments[8]
    experts = lax.axis_size("fsdp") // 2
    if 2 * routes.shape[1] >= experts and HEADS == experts:
        return shards_dense(*arguments)
    return shards_routed(*arguments)


def solution(mesh):
    in_specs = (
        P("fsdp", None),
        P("fsdp", None),
        P(None, "fsdp"),
        P("fsdp", None),
        P("fsdp", None),
        P("fsdp", None),
        P("fsdp", None, None),
        P("fsdp", None, None),
        P("fsdp", None),
        P("fsdp", None),
    )
    out_specs = (
        P("fsdp", None),
        P("fsdp", None),
        P(None, "fsdp"),
        P("fsdp", None),
        P("fsdp", None),
        P("fsdp", None),
        P("fsdp", None, None),
        P("fsdp", None, None),
    )
    return jax.shard_map(shards, mesh=mesh, in_specs=in_specs, out_specs=out_specs, check_vma=False)
```

```python
import functools

import jax
import jax.numpy as jnp
from jax import lax
from jax.experimental import pallas as pl
from jax.experimental.pallas import tpu as pltpu
from jax.sharding import PartitionSpec as P

D = 2048
HEADS = 16
HEAD_DIM = 128


EPSILON = 1e-05
ROPE_BASE = 10000.0
MASKED = -1000000000.0


def root_norm(vector, scaling):
    return vector * lax.rsqrt(jnp.mean(vector * vector, axis=-1, keepdims=True) + EPSILON) * scaling


def rotary(vector, cos_table, sin_table):
    half_dim = vector.shape[-1] // 2
    first = vector[..., :half_dim]
    second = vector[..., half_dim:]
    return jnp.concatenate(
        [first * cos_table - second * sin_table, second * cos_table + first * sin_table], axis=-1
    )


def layout(lengths, number):
    ends_at = jnp.cumsum(lengths)
    places = jnp.arange(number, dtype=jnp.int32)
    segment = jnp.sum((places[:, None] >= ends_at[None, :]).astype(jnp.int32), axis=1)
    starts = ends_at - lengths
    select_mask = (
        segment[:, None] == jnp.arange(lengths.shape[0], dtype=jnp.int32)[None, :]
    ).astype(jnp.int32)
    position = places - jnp.sum(select_mask * starts[None, :], axis=1)
    return (segment, position)


def tables(position):
    half_dim = HEAD_DIM // 2
    inverse = ROPE_BASE ** (-2.0 * jnp.arange(half_dim, dtype=jnp.float32) / HEAD_DIM)
    angles = position.astype(jnp.float32)[:, None] * inverse[None, :]
    return (jnp.cos(angles)[:, None, :], jnp.sin(angles)[:, None, :])


def prepare(projected, query_gain, key_gain, cos_table, sin_table):
    count_rows = projected.shape[0]
    query_heads = root_norm(projected[:, :D], query_gain).reshape(count_rows, HEADS, HEAD_DIM)
    key_heads = root_norm(projected[:, D : 2 * D], key_gain).reshape(count_rows, HEADS, HEAD_DIM)
    value_heads = projected[:, 2 * D :].reshape(count_rows, HEADS, HEAD_DIM)
    return (
        rotary(query_heads, cos_table, sin_table),
        rotary(key_heads, cos_table, sin_table),
        value_heads,
    )


def softmax_rows(logits):
    row_max = jnp.max(logits, axis=-1, keepdims=True)
    exponent = jnp.exp(logits - row_max)
    return exponent / jnp.sum(exponent, axis=-1, keepdims=True)


def dot_first(left, right):
    return lax.dot_general(
        left, right, (((0,), (0,)), ((), ())), preferred_element_type=jnp.float32
    )


def dot_last(left, right):
    return lax.dot_general(
        left, right, (((1,), (1,)), ((), ())), preferred_element_type=jnp.float32
    )


def shards_routed(
    tokens,
    cotangent,
    norm_gains,
    attention_in,
    attention_out,
    router_weight,
    expert_in,
    expert_out,
    routes,
    lengths,
):
    row_count = tokens.shape[0]
    devices_count = lax.axis_size("fsdp")
    experts = devices_count // 2
    choose = routes.shape[1]
    half_units = expert_out.shape[1]
    capacity = 4 * row_count * choose // (3 * experts)
    scaling = HEAD_DIM ** (-0.5)
    gain_full, gathered_in, gathered_out, gathered_router = (
        lax.all_gather(norm_gains, "fsdp", axis=1, tiled=True),
        lax.all_gather(attention_in, "fsdp", axis=0, tiled=True),
        lax.all_gather(attention_out, "fsdp", axis=0, tiled=True),
        lax.all_gather(router_weight, "fsdp", axis=0, tiled=True),
    )
    gain_rows = gain_full.astype(jnp.float32)
    segment, position = layout(lengths[0], row_count)
    cos_table, sin_table = tables(position)
    places = jnp.arange(row_count, dtype=jnp.int32)
    allowed = ((segment[:, None] == segment[None, :]) & (places[:, None] >= places[None, :]))[None]
    inputs = tokens.astype(jnp.float32)
    normed_input = root_norm(inputs, gain_rows[0]).astype(jnp.bfloat16)
    projected = jnp.dot(normed_input, gathered_in, preferred_element_type=jnp.float32)

    def prepare_local(projected_value, query_gain, key_gain):
        return prepare(projected_value, query_gain, key_gain, cos_table, sin_table)

    (query_f, key_f, value_f), prepare_back = jax.vjp(
        prepare_local, projected, gain_rows[1], gain_rows[2]
    )
    query_heads = query_f.astype(jnp.bfloat16)
    key_heads = key_f.astype(jnp.bfloat16)
    value_heads = value_f.astype(jnp.bfloat16)

    def score_block():
        raw_scores = (
            jnp.einsum("qhd,khd->hqk", query_heads, key_heads, preferred_element_type=jnp.float32)
            * scaling
        )
        return jnp.where(allowed, raw_scores, MASKED)

    scores = score_block()
    row_max = jnp.max(scores, axis=-1, keepdims=True)
    exponent = jnp.exp(scores - row_max)
    row_sum = jnp.sum(exponent, axis=-1, keepdims=True)
    log_total = row_max + jnp.log(row_sum)
    attend_probs = (exponent / row_sum).astype(jnp.bfloat16)
    attended = (
        jnp.einsum("hqk,khd->qhd", attend_probs, value_heads, preferred_element_type=jnp.float32)
        .reshape(row_count, D)
        .astype(jnp.bfloat16)
    )
    branch_out = jnp.dot(attended, gathered_out, preferred_element_type=jnp.float32)
    residual = inputs + branch_out
    normed = root_norm(residual, gain_rows[3]).astype(jnp.bfloat16)
    logits = jnp.dot(normed, gathered_router, preferred_element_type=jnp.float32)
    router_probs = softmax_rows(logits)
    chosen = jnp.take_along_axis(router_probs, routes, axis=1)
    gate_total = jnp.sum(chosen, axis=1, keepdims=True)
    gate_values = chosen / gate_total
    flat_routes = routes.reshape(-1)
    route_hits = (flat_routes[:, None] == jnp.arange(experts, dtype=jnp.int32)[None, :]).astype(
        jnp.int32
    )
    slot_index = jnp.sum((jnp.cumsum(route_hits, axis=0) - route_hits) * route_hits, axis=1)
    target = flat_routes * capacity + slot_index
    owner_token = (
        jnp.zeros((experts * capacity,), jnp.int32)
        .at[target]
        .set(jnp.arange(row_count * choose, dtype=jnp.int32) // choose)
    )
    filled = (
        jnp.zeros((experts * capacity,), jnp.bfloat16)
        .at[target]
        .set(jnp.ones((row_count * choose,), jnp.bfloat16))
    )
    outgoing = jnp.repeat(
        (normed[owner_token] * filled[:, None]).reshape(experts, capacity, D), 2, axis=0
    )
    arrived = lax.all_to_all(outgoing, "fsdp", split_axis=0, concat_axis=0, tiled=True).reshape(
        devices_count * capacity, D
    )
    gate_up_out = jnp.dot(arrived, expert_in[0], preferred_element_type=jnp.float32)
    gate_part = gate_up_out[:, :half_units]
    up_part = gate_up_out[:, half_units:]
    hidden_f, swiglu_back = jax.vjp(
        lambda gate_in, up_in: jax.nn.silu(gate_in) * up_in, gate_part, up_part
    )
    hidden = hidden_f.astype(jnp.bfloat16)
    produced = (
        jnp.dot(hidden, expert_out[0], preferred_element_type=jnp.float32)
        .astype(jnp.bfloat16)
        .reshape(devices_count, capacity, D)
    )
    returned = (
        lax.all_to_all(produced, "fsdp", split_axis=0, concat_axis=0, tiled=True)
        .reshape(experts, 2, capacity, D)
        .astype(jnp.float32)
    )
    returned = jnp.sum(returned, axis=1).reshape(experts * capacity, D)
    picked = returned[target].reshape(row_count, choose, D)
    expert_sum = jnp.sum(gate_values[:, :, None] * picked, axis=1)
    output = (residual + expert_sum).astype(jnp.bfloat16)
    back_in, back_out, back_router = (
        lax.all_gather(attention_in, "fsdp", axis=0, tiled=True),
        lax.all_gather(attention_out, "fsdp", axis=0, tiled=True),
        lax.all_gather(router_weight, "fsdp", axis=0, tiled=True),
    )
    upstream = cotangent.astype(jnp.float32)
    gate_grad = jnp.sum(upstream[:, None, :] * picked, axis=2)
    send_grad = (
        (gate_values[:, :, None] * upstream[:, None, :])
        .astype(jnp.bfloat16)
        .reshape(row_count * choose, D)
    )
    grad_buffer = (
        jnp.zeros((experts * capacity, D), jnp.bfloat16)
        .at[target]
        .set(send_grad)
        .reshape(experts, capacity, D)
    )
    grad_buffer = jnp.repeat(grad_buffer, 2, axis=0)
    grad_arrived = lax.all_to_all(
        grad_buffer, "fsdp", split_axis=0, concat_axis=0, tiled=True
    ).reshape(devices_count * capacity, D)
    grad_hidden = dot_last(grad_arrived, expert_out[0])
    expert_out_grad = dot_first(hidden, grad_arrived)
    grad_gate, grad_up = swiglu_back(grad_hidden)
    grad_gate_up = jnp.concatenate([grad_gate, grad_up], axis=1).astype(jnp.bfloat16)
    expert_in_grad = dot_first(arrived, grad_gate_up)
    grad_rows = (
        dot_last(grad_gate_up, expert_in[0])
        .astype(jnp.bfloat16)
        .reshape(devices_count, capacity, D)
    )
    grad_back = (
        lax.all_to_all(grad_rows, "fsdp", split_axis=0, concat_axis=0, tiled=True)
        .reshape(experts, 2, capacity, D)
        .astype(jnp.float32)
    )
    grad_back = jnp.sum(grad_back, axis=1).reshape(experts * capacity, D)
    dispatch_grad = jnp.sum(grad_back[target].reshape(row_count, choose, D), axis=1)
    chosen_grad = (gate_grad - jnp.sum(gate_grad * gate_values, axis=1, keepdims=True)) / gate_total
    expert_match = (
        routes[:, :, None] == jnp.arange(experts, dtype=jnp.int32)[None, None, :]
    ).astype(jnp.float32)
    prob_grad = jnp.sum(expert_match * chosen_grad[:, :, None], axis=1)
    logit_grad = (
        router_probs * (prob_grad - jnp.sum(prob_grad * router_probs, axis=1, keepdims=True))
    ).astype(jnp.bfloat16)
    router_grad = dot_first(normed, logit_grad)
    normed_grad = dispatch_grad + dot_last(logit_grad, back_router)
    _, second_back = jax.vjp(root_norm, residual, gain_rows[3])
    residual_norm_grad, second_gain_grad = second_back(normed_grad)
    residual_grad = upstream + residual_norm_grad
    branch_grad = residual_grad.astype(jnp.bfloat16)
    out_grad = dot_first(attended, branch_grad)
    attended_grad = (
        dot_last(branch_grad, back_out).astype(jnp.bfloat16).reshape(row_count, HEADS, HEAD_DIM)
    )
    recomputed = jnp.exp(score_block() - log_total)
    value_grad = jnp.einsum(
        "hqk,qhd->khd", attend_probs, attended_grad, preferred_element_type=jnp.float32
    )
    attend_grad = jnp.einsum(
        "qhd,khd->hqk", attended_grad, value_heads, preferred_element_type=jnp.float32
    )
    row_delta = jnp.sum(recomputed * attend_grad, axis=-1, keepdims=True)
    score_grad = (recomputed * (attend_grad - row_delta)).astype(jnp.bfloat16)
    query_grad = (
        jnp.einsum("hqk,khd->qhd", score_grad, key_heads, preferred_element_type=jnp.float32)
        * scaling
    )
    key_grad = (
        jnp.einsum("hqk,qhd->khd", score_grad, query_heads, preferred_element_type=jnp.float32)
        * scaling
    )
    projected_grad, query_gain_grad, key_gain_grad = prepare_back(
        (query_grad, key_grad, value_grad)
    )
    projected_grad = projected_grad.astype(jnp.bfloat16)
    attention_in_grad = dot_first(normed_input, projected_grad)
    normed_input_grad = dot_last(projected_grad, back_in)
    _, first_back = jax.vjp(root_norm, inputs, gain_rows[0])
    input_norm_grad, first_gain_grad = first_back(normed_input_grad)
    input_grad = residual_grad + input_norm_grad
    gains_grad = jnp.stack([first_gain_grad, query_gain_grad, key_gain_grad, second_gain_grad])
    gains_share, in_share, out_share, router_share = (
        lax.psum_scatter(gains_grad, "fsdp", scatter_dimension=1, tiled=True),
        lax.psum_scatter(attention_in_grad, "fsdp", scatter_dimension=0, tiled=True),
        lax.psum_scatter(out_grad, "fsdp", scatter_dimension=0, tiled=True),
        lax.psum_scatter(router_grad, "fsdp", scatter_dimension=0, tiled=True),
    )
    return (
        output,
        input_grad,
        gains_share,
        in_share,
        out_share,
        router_share,
        expert_in_grad[None],
        expert_out_grad[None],
    )


def product(left, right):
    return jnp.dot(left, right, preferred_element_type=jnp.float32)


def widen(value):
    return value.astype(jnp.float32)


PLANE = 8
SPOTS = 4
WIDE = 128


class Moves:
    def __init__(self, count):
        planes = count // PLANE
        order = list(range(0, planes, 2)) + list(range(1, planes, 2))[::-1]
        after = {order[i]: order[(i + 1) % planes] for i in range(planes)}
        self.planes = planes
        self.ring = [(i, after[i // PLANE] * PLANE + i % PLANE) for i in range(count)]
        self.first = [(i, i ^ (4 if i & 1 else 2)) for i in range(count)]
        self.second = [(i, i ^ (2 if i & 1 else 4)) for i in range(count)]
        self.core = [(i, i ^ 1) for i in range(count)]
        self.spots = [[(i, i ^ (2 * mask)) for i in range(count)] for mask in range(SPOTS)]
        device = lax.axis_index("fsdp")
        self.device = device
        self.plane, self.spot, self.core_id = device // PLANE, device % PLANE // 2, device % 2
        rank = jnp.asarray([order.index(i) for i in range(planes)], jnp.int32)
        self.planes_back = jnp.asarray(order, jnp.int32)[
            (rank[self.plane] - jnp.arange(planes, dtype=jnp.int32)) % planes
        ]
        self.steps_from = (rank[self.plane] - rank) % planes
        self.group_spots = self.spot ^ jnp.where(
            self.core_id == 0, jnp.asarray([0, 1, 2, 3]), jnp.asarray([0, 2, 1, 3])
        )


def send(value, pairs):
    return lax.ppermute(value, "fsdp", pairs)


def tie(*values):
    return lax.optimization_barrier(values)


def plane_total(moves, parts):
    def swapped(value):
        return jnp.where(moves.core_id == 0, value, value[:, jnp.asarray([0, 2, 1, 3])])

    parts = swapped(parts)
    for bit in (1, 2):
        other = send(parts, moves.spots[bit])
        parts = parts + jnp.stack([other[:, m ^ bit] for m in range(SPOTS)], axis=1)
    return swapped(parts)


def full_spec(*dims):
    return pl.BlockSpec(dims, lambda *_: (0,) * len(dims))


SCALARS = pl.BlockSpec(memory_space=pltpu.SMEM)
ANYWHERE = pl.BlockSpec(memory_space=pl.ANY)


def params(mebibytes):
    return pltpu.CompilerParams(vmem_limit_bytes=mebibytes << 20)


def cost(flops, moved, special=0):
    return pl.CostEstimate(flops=flops, bytes_accessed=moved, transcendentals=special)


def column_places(spot, mask, lines):
    for part in range(3):
        for line in range(lines):
            piece = (part * lines + line) * HEAD_DIM
            whole = ((part * lines + line) * SPOTS + (spot ^ mask)) * HEAD_DIM
            yield pl.ds(pl.multiple_of(whole, HEAD_DIM), HEAD_DIM), pl.ds(piece, HEAD_DIM)


def split_body(lines, meta, whole_ref, *pieces):
    for mask, piece in enumerate(pieces):
        for whole_at, piece_at in column_places(meta[0], mask, lines):
            piece[:, piece_at] = whole_ref[:, whole_at]


def split_columns(spot, whole):
    rows, columns = whole.shape
    return pl.pallas_call(
        functools.partial(split_body, HEADS // SPOTS),
        out_shape=[jax.ShapeDtypeStruct((rows, columns // SPOTS), whole.dtype)] * SPOTS,
        in_specs=[SCALARS, full_spec(rows, columns)],
        out_specs=[full_spec(rows, columns // SPOTS)] * SPOTS,
        compiler_params=params(16),
        name="split_columns",
    )(spot.reshape(1), whole)


def join_body(lines, meta, *refs):
    *pieces, whole_ref = refs
    for mask, piece in enumerate(pieces):
        for whole_at, piece_at in column_places(meta[0], mask, lines):
            whole_ref[:, whole_at] = widen(piece[:, piece_at])


def join_columns(spot, pieces):
    rows, columns = pieces[0].shape
    return pl.pallas_call(
        functools.partial(join_body, HEADS // SPOTS),
        out_shape=jax.ShapeDtypeStruct((rows, columns * SPOTS), jnp.float32),
        in_specs=[SCALARS] + [full_spec(rows, columns)] * SPOTS,
        out_specs=full_spec(rows, columns * SPOTS),
        compiler_params=params(16),
        name="join_columns",
    )(spot.reshape(1), *pieces)


def expert_body(index, cap, experts, blocks, meta, *refs):
    row_refs, grad_refs, weights = refs[:blocks], refs[blocks : 2 * blocks], refs[2 * blocks :][:4]
    refs = refs[2 * blocks + 4 + 6 :]
    saves, out_parts, row_parts = refs[:6], refs[6 : 6 + blocks], refs[6 + blocks :][:blocks]
    rows_v, grads_v, in_v, out_v, x_v, dy_v, m_v, du_v, part_v, back_v, sem, done = refs[
        6 + 2 * blocks :
    ]
    bf, f32 = jnp.bfloat16, jnp.float32
    count, width, half = rows_v.shape[1], grads_v.shape[2], out_v.shape[1]
    expert = meta[0]

    def fetch(ref, place, n):
        copy = pltpu.make_async_copy(ref, place, sem.at[n])
        copy.start()
        return copy

    fetch_rows = [fetch(ref, rows_v.at[j], j) for j, ref in enumerate(row_refs)]
    fetch_in = [fetch(weights[h], in_v.at[h], blocks + h) for h in range(2)]
    fetch_out = [fetch(weights[2 + h], out_v.at[h], blocks + 2 + h) for h in range(2)]
    fetch_grads = [fetch(ref, grads_v.at[j], blocks + 4 + j) for j, ref in enumerate(grad_refs)]
    leaving = []

    def leave(place, ref):
        leaving.append(pltpu.make_async_copy(place, ref, done.at[len(leaving)]))
        leaving[-1].start()

    def save(place, n):
        leave(place, saves[n].at[pl.ds(index * cap, blocks * cap)])

    lane8 = lax.broadcasted_iota(jnp.int32, (8, WIDE), 1)
    row8 = lax.broadcasted_iota(jnp.int32, (8, WIDE), 0)
    picker = (
        jnp.where((row8 == 0) & (lane8 == expert), 1.0, 0.0)
        + jnp.where((row8 == 1) & (lane8 == experts + expert), 1.0, 0.0)
        + jnp.where((row8 == 1) & (lane8 == 2 * experts + expert), 1.0, 0.0)
    ).astype(bf)
    lanes = lax.broadcasted_iota(jnp.int32, (count, WIDE), 1)
    slots_down = lax.broadcasted_iota(jnp.int32, (cap, count), 0)
    slots_along = lax.broadcasted_iota(jnp.int32, (count, cap), 1)
    gather, scatter, gates = [], [], []
    slots = [slice(j * cap, (j + 1) * cap) for j in range(blocks)]
    for j in range(blocks):
        fetch_rows[j].wait()
        extra = rows_v[j, :, width:]
        info = dot_last(picker, extra)
        chosen = slots_down == info[0:1].astype(jnp.int32)
        gates.append(jnp.sum(jnp.where(chosen, info[1:2], 0.0), axis=1, keepdims=True))
        gather.append(jnp.where(chosen, 1.0, 0.0).astype(bf))
        slot = jnp.sum(
            jnp.where(lanes == expert, widen(extra), 0.0), axis=1, keepdims=True
        ).astype(jnp.int32)
        scatter.append(jnp.where(slots_along == slot, 1.0, 0.0).astype(bf))
        x_v[slots[j], :] = product(gather[j], rows_v[j, :, :width]).astype(bf)
    gate = jnp.concatenate(gates, axis=0)
    save(x_v, 0)
    x = x_v[...]
    inner = []
    for h in range(2):
        fetch_in[h].wait()
        u = product(x, in_v[h])
        gate_part, up_part = u[:, :half], u[:, half:]
        sigmoid = 1.0 / (1.0 + jnp.exp(-gate_part))
        silu = gate_part * sigmoid
        inner.append((gate_part, up_part, sigmoid, silu))
        m_v[h] = (silu * up_part).astype(bf)
        save(m_v.at[h], 2 + h)
    for copy in fetch_out:
        copy.wait()
    y = product(m_v[0], out_v[0]) + product(m_v[1], out_v[1])
    for copy in fetch_grads:
        copy.wait()
    g = jnp.concatenate([product(gather[j], grads_v[j]) for j in range(blocks)], axis=0)
    dgate = jnp.sum(g * y, axis=1, keepdims=True)
    z = (gate * y).astype(bf)
    dy_v[...] = (gate * g).astype(bf)
    save(dy_v, 1)
    for j in range(blocks):
        part_v[j] = product(scatter[j], z[slots[j]]).astype(bf)
        leave(part_v.at[j], out_parts[j])
    dy = dy_v[...]
    for h in range(2):
        gate_part, up_part, sigmoid, silu = inner[h]
        dm = dot_last(dy, out_v[h])
        slope = sigmoid * (1.0 + gate_part * (1.0 - sigmoid))
        du_v[h, :, :half] = (dm * up_part * slope).astype(bf)
        du_v[h, :, half:] = (dm * silu).astype(bf)
        save(du_v.at[h], 4 + h)
    drows = (dot_last(du_v[0], in_v[0]) + dot_last(du_v[1], in_v[1])).astype(bf)
    upper = widen(dgate.astype(bf))
    lane_m = lax.broadcasted_iota(jnp.int32, (blocks * cap, WIDE), 1)
    pair = jnp.where(
        lane_m == 2 * expert, upper, jnp.where(lane_m == 2 * expert + 1, dgate - upper, 0.0)
    ).astype(bf)
    for j in range(blocks):
        back_v[j, :, :width] = product(scatter[j], drows[slots[j]]).astype(bf)
        back_v[j, :, width:] = product(scatter[j], pair[slots[j]]).astype(bf)
        leave(back_v.at[j], row_parts[j])
    for copy in leaving:
        copy.wait()


def expert_blocks(meta, rows, grads, weights, saved, index, total, cap, experts):
    blocks = len(rows)
    count, wide = rows[0].shape
    width, half = grads[0].shape[1], weights[2].shape[0]
    bf = jnp.bfloat16
    used = blocks * cap

    def shape(*dims):
        return jax.ShapeDtypeStruct(dims, bf)

    aliases = {2 * blocks + 5 + t: t for t in range(6)}
    if saved is None:
        saved, aliases = [jnp.zeros((16, WIDE), bf)] * 6, {}
    save_columns = (width, width, half, half, 2 * half, 2 * half)
    results = pl.pallas_call(
        functools.partial(expert_body, index, cap, experts, blocks),
        out_shape=[shape(total * cap, columns) for columns in save_columns]
        + [shape(count, width)] * blocks
        + [shape(count, wide)] * blocks,
        in_specs=[SCALARS] + [ANYWHERE] * (2 * blocks + 10),
        out_specs=[ANYWHERE] * (6 + 2 * blocks),
        scratch_shapes=[
            pltpu.VMEM((blocks, count, wide), bf),
            pltpu.VMEM((blocks, count, width), bf),
            pltpu.VMEM((2, width, 2 * half), bf),
            pltpu.VMEM((2, half, width), bf),
            pltpu.VMEM((used, width), bf),
            pltpu.VMEM((used, width), bf),
            pltpu.VMEM((2, used, half), bf),
            pltpu.VMEM((2, used, 2 * half), bf),
            pltpu.VMEM((blocks, count, width), bf),
            pltpu.VMEM((blocks, count, wide), bf),
            pltpu.SemaphoreType.DMA((2 * blocks + 4,)),
            pltpu.SemaphoreType.DMA((6 + 2 * blocks,)),
        ],
        input_output_aliases=aliases,
        compiler_params=params(58),
        cost_estimate=cost(blocks * 38 * 10**8, 30 << 20, 2 * used * half),
        name="expert_blocks",
    )(meta, *rows, *grads, *weights, *saved)
    return results[:6], results[6 : 6 + blocks], results[6 + blocks :]


def eye(count):
    return lax.broadcasted_iota(jnp.int32, (count, count), 0) == lax.broadcasted_iota(
        jnp.int32, (count, count), 1
    )


def as_column(row):
    return jnp.sum(jnp.where(eye(row.shape[1]), row, 0.0), axis=1, keepdims=True)


def as_row(column):
    return jnp.sum(jnp.where(eye(column.shape[0]), column, 0.0), axis=0, keepdims=True)


def rolled(value):
    return pltpu.roll(value, HEAD_DIM // 2, 1)


def root_of(total):
    return lax.rsqrt(total / D + EPSILON)


def weights_of(query, key, start):
    count = query.shape[0]
    rows = lax.broadcasted_iota(jnp.int32, (count, count), 0)
    columns = lax.broadcasted_iota(jnp.int32, (count, count), 1)
    allowed = (columns <= rows) & (columns >= start.astype(jnp.int32))
    scores = jnp.where(allowed, dot_last(query, key) * HEAD_DIM ** (-0.5), MASKED)
    exponent = jnp.exp(scores - jnp.max(scores, axis=1, keepdims=True))
    return exponent / jnp.sum(exponent, axis=1, keepdims=True)


def spans(mine):
    return [slice(h, h + HEAD_DIM) for h in range(0, mine, HEAD_DIM)]


def project_body(planes, own_rows, meta, gain, *refs):
    blocks, own, other = refs[:SPOTS], refs[SPOTS : SPOTS + planes], refs[SPOTS + planes :][:planes]
    proj_ref, a_ref, in_ref, sums_ref = refs[SPOTS + 2 * planes :][:4]
    x_v, a_v, in_v, proj_v, sem, in_sem, done = refs[SPOTS + 2 * planes + 4 :]
    spot, core = meta[0], meta[1]
    count = x_v.shape[1]
    mine = proj_v.shape[1] // 3
    fetch_x = [pltpu.make_async_copy(ref, x_v.at[j], sem.at[j]) for j, ref in enumerate(blocks)]
    for copy in fetch_x:
        copy.start()
    fetch_in = []
    for k in range(planes):
        for mask in range(SPOTS):
            chunk = meta[2 + k] * PLANE + (spot ^ mask) * 2
            for n, (refs_k, c) in enumerate(((own, core), (other, 1 - core))):
                at = pl.multiple_of((chunk + c) * own_rows, own_rows)
                fetch_in.append(
                    pltpu.make_async_copy(
                        refs_k[k].at[mask],
                        in_v.at[pl.ds(at, own_rows)],
                        in_sem.at[(k * SPOTS + mask) * 2 + n],
                    )
                )
                fetch_in[-1].start()
    for j in range(SPOTS):
        fetch_x[j].wait()
        x = widen(x_v[j])
        root = lax.rsqrt(jnp.mean(x * x, axis=1, keepdims=True) + EPSILON)
        a_v[j * count : (j + 1) * count, :] = (x * root * gain[...]).astype(jnp.bfloat16)
    leaving = [pltpu.make_async_copy(a_v, a_ref, done.at[0])]
    leaving[0].start()
    for copy in fetch_in:
        copy.wait()
    leaving.append(pltpu.make_async_copy(in_v, in_ref, done.at[1]))
    leaving[1].start()
    for n in range(3):
        part = slice(n * mine, (n + 1) * mine)
        value = product(a_v[...], in_v[:, part])
        proj_v[:, part] = value
        leaving.append(
            pltpu.make_async_copy(proj_v.at[:, part], proj_ref.at[:, part], done.at[2 + n])
        )
        leaving[-1].start()
        if n < 2:
            squares = jnp.sum(value * value, axis=1, keepdims=True)
            for j in range(SPOTS):
                sums_ref[n, j : j + 1, :] = as_row(squares[j * count : (j + 1) * count])
    for copy in leaving:
        copy.wait()


def project(moves, gain, blocks, own, other):
    planes, own_rows, width = len(own), own[0].shape[1], own[0].shape[2]
    count, depth = blocks[0].shape
    bf, f32 = jnp.bfloat16, jnp.float32
    rows = SPOTS * count
    meta = jnp.concatenate([jnp.stack([moves.spot, moves.core_id]), moves.planes_back])
    shape = jax.ShapeDtypeStruct
    return pl.pallas_call(
        functools.partial(project_body, planes, own_rows),
        out_shape=[
            shape((rows, width), f32),
            shape((rows, depth), bf),
            shape((depth, width), bf),
            shape((2, SPOTS, count), f32),
        ],
        in_specs=[SCALARS, full_spec(1, depth)] + [ANYWHERE] * (SPOTS + 2 * planes),
        out_specs=[ANYWHERE] * 3 + [full_spec(2, SPOTS, count)],
        scratch_shapes=[
            pltpu.VMEM((SPOTS, count, depth), bf),
            pltpu.VMEM((rows, depth), bf),
            pltpu.VMEM((depth, width), bf),
            pltpu.VMEM((rows, width), f32),
            pltpu.SemaphoreType.DMA((SPOTS,)),
            pltpu.SemaphoreType.DMA((2 * SPOTS * planes,)),
            pltpu.SemaphoreType.DMA((5,)),
        ],
        compiler_params=params(40),
        cost_estimate=cost(5 * 10**9, 20 << 20),
        name="project",
    )(meta.astype(jnp.int32), gain, *blocks, *own, *other)


def by_block(count, width):
    return [pl.BlockSpec((count, width), lambda i: (0, 0))] * SPOTS


def put_by_block(step, refs, value):
    for n, ref in enumerate(refs):

        @pl.when(step == n)
        def _(ref=ref):
            ref[...] = value


def forward_body(planes, own_rows, meta, totals, starts, gains, proj_ref, cos_ref, sin_ref, *refs):
    own, other = refs[:planes], refs[planes : 2 * planes]
    q_ref, k_ref, v_ref, o_ref, out_w, *parts = refs[2 * planes :][: 5 + SPOTS]
    sem = refs[-1]
    step = pl.program_id(0)
    bf = jnp.bfloat16
    mine = q_ref.shape[1]
    fetches = []
    for k in range(planes):
        for n, (refs_k, c) in enumerate(((own, meta[1]), (other, 1 - meta[1]))):
            at = pl.multiple_of((meta[2 + k] * 2 + c) * own_rows, own_rows)
            fetches.append(
                pltpu.make_async_copy(
                    refs_k[k], out_w.at[pl.ds(at, own_rows)], sem.at[2 * k + n]
                )
            )

    @pl.when(step == 0)
    def _():
        for copy in fetches:
            copy.start()

    query_root = root_of(as_column(totals[0, pl.ds(step, 1), :]))
    key_root = root_of(as_column(totals[1, pl.ds(step, 1), :]))
    start = as_column(starts[pl.ds(step, 1), :])
    cos, sin = cos_ref[...], sin_ref[...]
    for own_span in spans(mine):
        at = own_span.start
        query = proj_ref[:, at : at + HEAD_DIM] * query_root * gains[0:1, own_span]
        key = proj_ref[:, mine + at : mine + at + HEAD_DIM] * key_root * gains[1:2, own_span]
        value = proj_ref[:, 2 * mine + at : 2 * mine + at + HEAD_DIM].astype(bf)
        query = (query * cos + rolled(query) * sin).astype(bf)
        key = (key * cos + rolled(key) * sin).astype(bf)
        weights = weights_of(query, key, start).astype(bf)
        q_ref[:, own_span] = query
        k_ref[:, own_span] = key
        v_ref[:, own_span] = value
        o_ref[:, own_span] = product(weights, value).astype(bf)

    @pl.when(step == 0)
    def _():
        for copy in fetches:
            copy.wait()

    put_by_block(step, parts, product(o_ref[...], out_w[...]).astype(bf))


def block_spec(count, columns):
    return pl.BlockSpec((count, columns), lambda i: (i, 0))


def attend_forward(moves, totals, starts, gains, projected, cos_all, sin_all, own, other):
    planes, own_rows = len(own), own[0].shape[0]
    rows, mine = projected.shape[0], gains.shape[1]
    count = rows // SPOTS
    bf = jnp.bfloat16
    meta = jnp.concatenate([jnp.stack([moves.spot, moves.core_id]), moves.planes_back])
    return pl.pallas_call(
        functools.partial(forward_body, planes, own_rows),
        grid=(SPOTS,),
        out_shape=[jax.ShapeDtypeStruct((rows, mine), bf)] * 4
        + [jax.ShapeDtypeStruct((mine, D), bf)]
        + [jax.ShapeDtypeStruct((count, D), bf)] * SPOTS,
        in_specs=[
            SCALARS,
            full_spec(*totals.shape),
            full_spec(*starts.shape),
            full_spec(*gains.shape),
            block_spec(count, 3 * mine),
            block_spec(count, HEAD_DIM),
            block_spec(count, HEAD_DIM),
        ]
        + [ANYWHERE] * (2 * planes),
        out_specs=[block_spec(count, mine)] * 4 + [full_spec(mine, D)] + by_block(count, D),
        scratch_shapes=[pltpu.SemaphoreType.DMA((2 * planes,))],
        compiler_params=params(40),
        cost_estimate=cost(5 * 10**9, 20 << 20),
        name="attend_forward",
    )(meta.astype(jnp.int32), totals, starts, gains, projected, cos_all, sin_all, *own, *other)


def backward_body(
    meta, totals, starts, gains, proj_ref, cos_ref, sin_ref, q_ref, k_ref, v_ref, o_ref, out_w, *refs
):
    blocks = refs[:SPOTS]
    dq_ref, dk_ref, dv_ref, sums_ref, own_grad, other_grad, gain_grad = refs[SPOTS : SPOTS + 7]
    grads_v, total_v, sem = refs[SPOTS + 7 :]
    step = pl.program_id(0)
    bf = jnp.bfloat16
    mine = q_ref.shape[1]

    @pl.when(step == 0)
    def _():
        for n in range(SPOTS):
            pltpu.make_async_copy(blocks[n], grads_v.at[n], sem.at[n]).start()
        total_v[...] = jnp.zeros_like(total_v)
        gain_grad[...] = jnp.zeros_like(gain_grad)

    pltpu.make_async_copy(blocks[0], grads_v.at[step], sem.at[step]).wait()
    grads = grads_v[step]
    total_v[...] += dot_first(o_ref[...], grads)
    do = dot_last(grads, out_w[...]).astype(bf)
    roots = [root_of(as_column(totals[n, pl.ds(step, 1), :])) for n in range(2)]
    start = as_column(starts[pl.ds(step, 1), :])
    cos, sin = cos_ref[...], sin_ref[...]
    sums = [0.0, 0.0]
    for own in spans(mine):
        query, key, value = q_ref[:, own], k_ref[:, own], v_ref[:, own]
        weights = weights_of(query, key, start)
        dv_ref[:, own] = dot_first(weights.astype(bf), do[:, own]).astype(bf)
        dweights = dot_last(do[:, own], value)
        inner = jnp.sum(weights * dweights, axis=1, keepdims=True)
        dscores = (weights * (dweights - inner)).astype(bf)
        for n, (grad, ref) in enumerate(
            ((product(dscores, key), dq_ref), (dot_first(dscores, query), dk_ref))
        ):
            grad = grad * HEAD_DIM ** (-0.5)
            grad = grad * cos - rolled(grad) * sin
            ref[:, own] = grad
            at = n * mine + own.start
            raw = grad * proj_ref[:, at : at + HEAD_DIM]
            sums[n] += jnp.sum(raw * gains[n : n + 1, own], axis=1, keepdims=True)
            gain_grad[n : n + 1, own] += jnp.sum(raw * roots[n], axis=0, keepdims=True)
    for n in range(2):
        sums_ref[n, pl.ds(step, 1), :] = as_row(sums[n])

    @pl.when(step == SPOTS - 1)
    def _():
        planes, own_rows = own_grad.shape[:2]
        for k in range(planes):
            for ref, c in ((own_grad, meta[1]), (other_grad, 1 - meta[1])):
                at = pl.multiple_of((meta[2 + k] * 2 + c) * own_rows, own_rows)
                ref[k] = total_v[pl.ds(at, own_rows), :].astype(bf)


def attend_backward(
    moves, totals, starts, gains, projected, cos_all, sin_all, heads, out_full, blocks
):
    rows, mine = projected.shape[0], gains.shape[1]
    count = rows // SPOTS
    planes = moves.planes
    own_rows = mine // (2 * planes)
    bf, f32 = jnp.bfloat16, jnp.float32
    meta = jnp.concatenate([jnp.stack([moves.spot, moves.core_id]), moves.planes_back])
    shape = jax.ShapeDtypeStruct
    return pl.pallas_call(
        backward_body,
        grid=(SPOTS,),
        out_shape=[
            shape((rows, mine), f32),
            shape((rows, mine), f32),
            shape((rows, mine), bf),
            shape((2, SPOTS, count), f32),
            shape((planes, own_rows, D), bf),
            shape((planes, own_rows, D), bf),
            shape((8, mine), f32),
        ],
        in_specs=[
            SCALARS,
            full_spec(*totals.shape),
            full_spec(*starts.shape),
            full_spec(*gains.shape),
            block_spec(count, 3 * mine),
            block_spec(count, HEAD_DIM),
            block_spec(count, HEAD_DIM),
        ]
        + [block_spec(count, mine)] * 4
        + [full_spec(*out_full.shape)]
        + [ANYWHERE] * SPOTS,
        out_specs=[block_spec(count, mine)] * 3
        + [full_spec(2, SPOTS, count)]
        + [full_spec(planes, own_rows, D)] * 2
        + [full_spec(8, mine)],
        scratch_shapes=[
            pltpu.VMEM((SPOTS, count, D), bf),
            pltpu.VMEM((mine, D), f32),
            pltpu.SemaphoreType.DMA((SPOTS,)),
        ],
        compiler_params=params(48),
        cost_estimate=cost(7 * 10**9, 25 << 20),
        name="attend_backward",
    )(
        meta.astype(jnp.int32),
        totals,
        starts,
        gains,
        projected,
        cos_all,
        sin_all,
        *heads,
        out_full,
        *blocks,
    )


def project_back_body(
    planes, own_rows, meta, totals, dots, gains, proj_ref, dq_ref, dk_ref, dv_ref, a_ref, *refs
):
    dp_ref, own, other, total_v = refs[0], refs[1 : 1 + planes], refs[1 + planes : -1], refs[-1]
    step = pl.program_id(0)
    bf = jnp.bfloat16
    mine = dv_ref.shape[1]
    count = dv_ref.shape[0] // 2
    for n, ref in enumerate((dq_ref, dk_ref)):
        columns = slice(n * mine, (n + 1) * mine)
        for j in range(2):
            rows = slice(j * count, (j + 1) * count)
            root = root_of(as_column(totals[n, pl.ds(2 * step + j, 1), :]))
            inner = as_column(dots[n, pl.ds(2 * step + j, 1), :])
            grad = root * gains[n : n + 1, :] * ref[rows, :]
            grad = grad - proj_ref[rows, columns] * (root * root * root * inner / D)
            dp_ref[rows, columns] = grad.astype(bf)
    dp_ref[:, 2 * mine :] = dv_ref[...]

    @pl.when(step == 0)
    def _():
        total_v[...] = dot_first(a_ref[...], dp_ref[...])

    @pl.when(step == 1)
    def _():
        total_v[...] += dot_first(a_ref[...], dp_ref[...])
        for k in range(planes):
            for mask in range(SPOTS):
                chunk = meta[2 + k] * PLANE + (meta[0] ^ mask) * 2
                for refs_k, c in ((own, meta[1]), (other, 1 - meta[1])):
                    at = pl.multiple_of((chunk + c) * own_rows, own_rows)
                    refs_k[k][mask] = total_v[pl.ds(at, own_rows), :].astype(bf)


def project_back(moves, totals, dots, gains, projected, dq, dk, dv, normed_all):
    rows, mine = dv.shape
    planes = moves.planes
    own_rows = D // (planes * PLANE)
    bf = jnp.bfloat16
    meta = jnp.concatenate([jnp.stack([moves.spot, moves.core_id]), moves.planes_back])
    half = rows // 2
    pieces = (SPOTS, own_rows, 3 * mine)
    return pl.pallas_call(
        functools.partial(project_back_body, planes, own_rows),
        grid=(2,),
        out_shape=[jax.ShapeDtypeStruct((rows, 3 * mine), bf)]
        + [jax.ShapeDtypeStruct(pieces, bf)] * (2 * planes),
        in_specs=[
            SCALARS,
            full_spec(*totals.shape),
            full_spec(*dots.shape),
            full_spec(*gains.shape),
            block_spec(half, 3 * mine),
            block_spec(half, mine),
            block_spec(half, mine),
            block_spec(half, mine),
            block_spec(half, D),
        ],
        out_specs=[block_spec(half, 3 * mine)] + [full_spec(*pieces)] * (2 * planes),
        scratch_shapes=[pltpu.VMEM((D, 3 * mine), jnp.float32)],
        compiler_params=params(60),
        cost_estimate=cost(5 * 10**9, 30 << 20),
        name="project_back",
    )(meta.astype(jnp.int32), totals, dots, gains, projected, dq, dk, dv, normed_all)


def rows_back_body(dp_ref, in_w, *refs):
    blocks, parts, gain_grad, (x_v, sem) = (
        refs[:SPOTS],
        refs[SPOTS : 2 * SPOTS],
        refs[2 * SPOTS],
        refs[2 * SPOTS + 1 :],
    )
    step = pl.program_id(0)

    @pl.when(step == 0)
    def _():
        for n in range(SPOTS):
            pltpu.make_async_copy(blocks[n], x_v.at[n], sem.at[n]).start()
        gain_grad[...] = jnp.zeros_like(gain_grad)

    value = dot_last(dp_ref[...], in_w[...])
    put_by_block(step, parts, value.astype(jnp.bfloat16))
    pltpu.make_async_copy(blocks[0], x_v.at[step], sem.at[step]).wait()
    x = widen(x_v[step])
    root = lax.rsqrt(jnp.mean(x * x, axis=1, keepdims=True) + EPSILON)
    gain_grad[...] += jnp.sum(value * (x * root), axis=0, keepdims=True)


def rows_back(projected_grad, in_full, blocks):
    rows, columns = projected_grad.shape
    count = rows // SPOTS
    bf = jnp.bfloat16
    return pl.pallas_call(
        rows_back_body,
        grid=(SPOTS,),
        out_shape=[jax.ShapeDtypeStruct((count, D), bf)] * SPOTS
        + [jax.ShapeDtypeStruct((1, D), jnp.float32)],
        in_specs=[block_spec(count, columns), full_spec(*in_full.shape)] + [ANYWHERE] * SPOTS,
        out_specs=by_block(count, D) + [full_spec(1, D)],
        scratch_shapes=[
            pltpu.VMEM((SPOTS, count, D), bf),
            pltpu.SemaphoreType.DMA((SPOTS,)),
        ],
        compiler_params=params(48),
        cost_estimate=cost(5 * 10**9, 12 << 20),
        name="rows_back",
    )(projected_grad, in_full, *blocks)


SMALL = 20


def shards_dense(
    tokens,
    cotangent,
    norm_gains,
    attention_in,
    attention_out,
    router_weight,
    expert_in,
    expert_out,
    routes,
    lengths,
):
    row_count = tokens.shape[0]
    devices_count = lax.axis_size("fsdp")
    moves = Moves(devices_count)
    planes, core, spot = moves.planes, moves.core_id, moves.spot
    ring, first, second, cores = moves.ring, moves.first, moves.second, moves.core
    experts = devices_count // 2
    choose = routes.shape[1]
    capacity = 4 * row_count * choose // (3 * experts)
    bf, f32 = jnp.bfloat16, jnp.float32
    own_rows = attention_in.shape[0]
    lines = HEADS // SPOTS
    mine = lines * HEAD_DIM

    def low(value):
        return value.astype(bf)

    flat = jnp.concatenate(
        [router_weight.T.reshape(-1), norm_gains.reshape(-1), lengths[0].astype(bf)]
    )
    riders = [jnp.pad(flat, (0, -flat.shape[0] % WIDE)).reshape(-1, WIDE)]
    pieces = split_columns(spot, attention_in)
    near_x = send(tokens, first)
    riders.append(send(riders[0], ring))
    out_own = [attention_out, send(attention_out, ring)]
    weights = [expert_in[0], send(expert_in[0], cores), expert_out[0], send(expert_out[0], cores)]
    riders, out_own, pieces = tie(riders, out_own, pieces)

    riders.append(send(riders[1], ring))
    out_own.append(send(out_own[1], ring))
    traded = [pieces[0]] + [send(pieces[m], moves.spots[m]) for m in range(1, SPOTS)]
    riders, out_own, traded, near_x = tie(riders, out_own, traded, near_x)

    in_own = [jnp.stack(traded)]
    riders.append(send(riders[2], ring))
    out_own.append(send(out_own[2], ring))
    in_own.append(send(in_own[0], ring))
    blocks_x = [tokens, near_x, send(tokens, second), send(near_x, second)]
    riders_all = jnp.stack(riders)
    for pairs in (moves.spots[1], moves.spots[2], cores):
        riders_all = jnp.concatenate([riders_all, send(riders_all, pairs)])
    in_own, blocks_x, riders_all, out_own = tie(in_own, blocks_x, riders_all, out_own)

    in_own.append(send(in_own[1], ring))
    in_other = [send(item, cores) for item in in_own[:2]]
    out_other = [send(item, cores) for item in out_own]
    grads = {(0, 0): [cotangent, send(cotangent, first)]}
    in_own, in_other, grads = tie(in_own, in_other, grads)

    in_own.append(send(in_own[2], ring))
    in_other.append(send(in_own[2], cores))
    grads[0, 1] = [send(item, second) for item in grads[0, 0]]

    ids = jnp.arange(devices_count, dtype=jnp.int32)
    source = (
        ((ids % 2) ^ core) * (SPOTS * planes)
        + ((ids % PLANE // 2) ^ spot) * planes
        + moves.steps_from[ids // PLANE]
    )
    arrived = jnp.take(riders_all, source, axis=0).reshape(devices_count, -1)
    small_all = arrived[:, : SMALL * own_rows].reshape(devices_count, SMALL, own_rows)
    small_all = small_all.transpose(1, 0, 2).reshape(SMALL, D)
    router_full, gain_rows = small_all[: SMALL - 4], widen(small_all[SMALL - 4 :])
    lengths_all = arrived[:, SMALL * own_rows : SMALL * own_rows + lengths.shape[1]]
    lengths_all = jnp.take(
        lengths_all, moves.plane * PLANE + moves.group_spots * 2 + core, axis=0
    ).astype(jnp.int32)
    gains = jnp.stack(
        [
            lax.dynamic_index_in_dim(
                gain_rows[n].reshape(lines, SPOTS, HEAD_DIM), spot, 1, keepdims=False
            ).reshape(mine)
            for n in (1, 2)
        ]
    )
    places = jnp.arange(row_count, dtype=jnp.int32)
    _, position = jax.vmap(lambda item: layout(item, row_count))(lengths_all)
    starts = (places[None] - position).astype(f32)
    cos_half, sin_half = (table[:, 0] for table in tables(position.reshape(-1)))
    cos_all = jnp.concatenate([cos_half, cos_half], axis=1)
    sin_all = jnp.concatenate([-sin_half, sin_half], axis=1)

    expert_ids = jnp.arange(experts, dtype=jnp.int32)
    match = jnp.sum((routes[:, :, None] == expert_ids[None, None, :]).astype(f32), axis=1)
    before = (places[:, None] > places[None, :]).astype(bf)
    rank = jnp.where(match > 0, product(before, match.astype(bf)), -1.0).astype(bf)

    in_own, in_other, grads, starts, cos_all, sin_all, gains, rank = tie(
        in_own, in_other, grads, starts, cos_all, sin_all, gains, rank
    )
    in_other.append(send(in_own[3], cores))
    own_1 = send(cotangent, ring)
    projected, normed_all, in_full, sums = project(
        moves, gain_rows[0:1], blocks_x, in_own, in_other
    )
    totals = plane_total(moves, sums)
    totals, own_1 = tie(totals, own_1)

    near_1 = send(grads[0, 0][1], ring)
    across_1 = send(own_1, second)
    attention = (moves, totals, starts, gains, projected, cos_all, sin_all)
    results = attend_forward(*attention, out_own, out_other)
    heads, out_full, parts = results[:4], results[4], results[5:]
    parts, near_1, across_1 = tie(parts, near_1, across_1)

    def cross(parts):
        return [send(parts[2], second), send(parts[3], second)]

    def gather_near(parts, backs):
        near = low(widen(parts[1]) + widen(backs[1]))
        return widen(parts[0]) + widen(backs[0]), send(near, first)

    own_2 = send(own_1, ring)
    backs = cross(parts)
    backs, own_2 = tie(backs, own_2)
    near_2 = send(near_1, ring)
    home, near = gather_near(parts, backs)
    home, near, near_2 = tie(home, near, near_2)

    grads[1, 0] = [own_1, near_1]
    grads[1, 1] = [across_1, send(near_1, second)]
    grads[2, 0] = [own_2, near_2]
    inputs = widen(tokens)
    residual = inputs + (home + widen(near))
    normed = low(root_norm(residual, gain_rows[3][None]))
    logits = dot_last(normed, router_full)
    router_probs = softmax_rows(logits)
    gate_total = jnp.sum(router_probs * match, axis=1, keepdims=True)
    gate_values = router_probs * match / gate_total
    upper = lax.reduce_precision(gate_values, 8, 7)
    extra = jnp.concatenate(
        [
            rank,
            upper.astype(bf),
            (gate_values - upper).astype(bf),
            jnp.zeros((row_count, WIDE - 3 * experts), bf),
        ],
        axis=1,
    )
    rows = jnp.concatenate([normed, extra], axis=1)
    rows, grads = tie(rows, grads)

    meta = (moves.device // 2).reshape(1).astype(jnp.int32)
    saved, done = None, 0
    row_parts, out_parts = {}, {}

    def run_expert(group, which, blocks):
        nonlocal saved, done
        saved, outs, backs = expert_blocks(
            meta,
            blocks,
            grads[group, which],
            weights,
            saved,
            done,
            planes * SPOTS,
            capacity,
            experts,
        )
        done += len(blocks)
        out_parts.setdefault(group, []).extend(outs)
        row_parts.setdefault(group, []).extend(backs)

    row_near = send(rows, first)
    row_1 = send(rows, ring)
    (row_near,) = tie(row_near)

    near_row_1 = send(row_near, ring)
    across = [send(rows, second), send(row_near, second)]
    run_expert(0, 0, [rows, row_near])
    saved, across, row_1 = tie(saved, across, row_1)

    row_2 = send(row_1, ring)
    across_row_1 = send(row_1, second)
    grads[2, 1] = [send(item, second) for item in grads[2, 0]]
    run_expert(0, 1, across)
    saved, near_row_1, across_row_1, grads[2, 1] = tie(
        saved, near_row_1, across_row_1, grads[2, 1]
    )

    near_row_2 = send(near_row_1, ring)
    own_3 = send(own_2, ring)
    across = [across_row_1, send(near_row_1, second)]
    run_expert(1, 0, [row_1, near_row_1])
    saved, across, row_2 = tie(saved, across, row_2)

    row_3 = send(row_2, ring)
    across_row_2 = send(row_2, second)
    run_expert(1, 1, across)
    saved, near_row_2, own_3, across_row_2 = tie(saved, near_row_2, own_3, across_row_2)

    near_row_3 = send(near_row_2, ring)
    across = [across_row_2, send(near_row_2, second)]
    grads[3, 0] = [own_3, send(own_3, first)]
    across_3 = send(own_3, second)
    backs_1 = cross(row_parts[1])
    run_expert(2, 0, [row_2, near_row_2])
    saved, across, row_3, grads[3, 0], across_3 = tie(
        saved, across, row_3, grads[3, 0], across_3
    )

    across_row_3 = send(row_3, second)
    grads[3, 1] = [across_3, send(grads[3, 0][1], second)]
    run_expert(2, 1, across)
    saved, near_row_3, across_row_3, backs_1 = tie(saved, near_row_3, across_row_3, backs_1)

    across = [across_row_3, send(near_row_3, second)]
    home_1, near_1 = gather_near(row_parts[1], backs_1)
    backs_2 = cross(row_parts[2])
    run_expert(3, 0, [row_3, near_row_3])
    saved, across, grads[3, 1], home_1, near_1, backs_2 = tie(
        saved, across, grads[3, 1], home_1, near_1, backs_2
    )

    total = send(low(home_1 + widen(near_1)), ring)
    home_2, near_2 = gather_near(row_parts[2], backs_2)
    backs_0 = cross(row_parts[0])
    run_expert(3, 1, across)
    saved, total, home_2, near_2 = tie(saved, total, home_2, near_2)

    total = send(low(widen(total) + (home_2 + widen(near_2))), ring)
    backs_3 = cross(row_parts[3])
    x_rows, dy_rows, m_own, m_other, du_own, du_other = saved
    in_theirs = dot_first(x_rows, du_other)
    total, backs_3, backs_0, in_theirs = tie(total, backs_3, backs_0, in_theirs)

    home_3, near_3 = gather_near(row_parts[3], backs_3)
    home_0, near_0 = gather_near(row_parts[0], backs_0)
    in_theirs = send(in_theirs, cores)
    out_theirs = dot_first(m_other, dy_rows)
    home_3, near_3, home_0, near_0, out_theirs = tie(home_3, near_3, home_0, near_0, out_theirs)

    total = send(low(widen(total) + (home_3 + widen(near_3))), ring)
    out_theirs = send(out_theirs, cores)
    out_backs = {1: cross(out_parts[1])}
    (total,) = tie(total)
    row_total = widen(total) + (home_0 + widen(near_0))

    upstream = widen(cotangent)
    dispatch_grad = row_total[:, :D]
    gate_grad = jnp.sum(row_total[:, D : D + 2 * experts].reshape(row_count, experts, 2), axis=2)
    chosen_grad = (
        match * (gate_grad - jnp.sum(gate_grad * gate_values, axis=1, keepdims=True)) / gate_total
    )
    logit_grad = low(
        router_probs * (chosen_grad - jnp.sum(chosen_grad * router_probs, axis=1, keepdims=True))
    )
    normed_grad = dispatch_grad + product(logit_grad, router_full)
    _, second_back = jax.vjp(root_norm, residual, gain_rows[3])
    residual_norm_grad, second_gain_grad = second_back(normed_grad)
    residual_grad = upstream + residual_norm_grad
    branch_grad = low(residual_grad)
    branch_near = send(branch_grad, first)
    branch_near, out_backs = tie(branch_near, out_backs)

    branch_blocks = [
        branch_grad,
        branch_near,
        send(branch_grad, second),
        send(branch_near, second),
    ]
    expert_in_grad = dot_first(x_rows, du_own) + in_theirs
    expert_out_grad = dot_first(m_own, dy_rows) + out_theirs
    router_grad = dot_first(logit_grad, normed)
    branch_blocks, expert_in_grad, expert_out_grad, router_grad = tie(
        branch_blocks, expert_in_grad, expert_out_grad, router_grad
    )

    out_homes = {1: gather_near(out_parts[1], out_backs[1])}
    out_backs[2] = cross(out_parts[2])
    dq, dk, dv, dots, own_grad, other_grad, gain_grads = attend_backward(
        *attention, heads, out_full, branch_blocks
    )
    dots, out_homes, out_backs = tie(dots, out_homes, out_backs)

    out_total = send(low(out_homes[1][0] + widen(out_homes[1][1])), ring)
    other_grad = send(other_grad, cores)
    out_homes[2] = gather_near(out_parts[2], out_backs[2])
    out_backs[3] = cross(out_parts[3])
    dots = plane_total(moves, dots)
    projected_grad, *in_grads = project_back(
        moves, totals, dots, gains, projected, dq, dk, dv, normed_all
    )
    in_grads, out_total, out_homes, out_backs, other_grad = tie(
        in_grads, out_total, out_homes, out_backs, other_grad
    )

    others = [send(in_grads[planes + k], cores) for k in range(planes)]
    in_sums = [widen(in_grads[k]) + widen(others[k]) for k in range(planes)]
    out_sums = [widen(own_grad[k]) + widen(other_grad[k]) for k in range(planes)]
    in_total = send(low(in_sums[1]), ring)
    out_share = send(low(out_sums[1]), ring)
    *parts, first_gain_grad = rows_back(projected_grad, in_full, blocks_x)
    in_total, out_share, parts = tie(in_total, out_share, parts)

    backs = cross(parts)
    in_total = send(low(widen(in_total) + in_sums[2]), ring)
    out_share = send(low(widen(out_share) + out_sums[2]), ring)
    out_total = send(low(widen(out_total) + out_homes[2][0] + widen(out_homes[2][1])), ring)
    in_total, out_share, backs = tie(in_total, out_share, backs)

    home, near = gather_near(parts, backs)
    in_total = send(low(widen(in_total) + in_sums[3]), ring)
    out_share = widen(send(low(widen(out_share) + out_sums[3]), ring)) + out_sums[0]
    out_homes[3] = gather_near(out_parts[3], out_backs[3])
    out_backs[0] = cross(out_parts[0])
    in_total, home, near, out_total, out_homes, out_backs = tie(
        in_total, home, near, out_total, out_homes, out_backs
    )

    out_total = send(low(widen(out_total) + out_homes[3][0] + widen(out_homes[3][1])), ring)
    in_total = low(widen(in_total) + in_sums[0])
    traded = [in_total[0]] + [send(in_total[m], moves.spots[m]) for m in range(1, SPOTS)]
    in_share = join_columns(spot, traded)
    out_homes[0] = gather_near(out_parts[0], out_backs[0])
    output = low(residual + (widen(out_total) + (out_homes[0][0] + widen(out_homes[0][1]))))
    _, first_back = jax.vjp(lambda value: root_norm(value, gain_rows[0]), inputs)
    (input_norm_grad,) = first_back(home + widen(near))
    input_grad = residual_grad + input_norm_grad

    here = (jnp.arange(SPOTS, dtype=jnp.int32) == spot)[None, :, None]

    def own_gain(row):
        return jnp.where(here, row.reshape(lines, 1, HEAD_DIM), 0.0).reshape(1, D)

    small_grad = jnp.concatenate(
        [
            router_grad,
            first_gain_grad,
            own_gain(gain_grads[0]),
            own_gain(gain_grads[1]),
            second_gain_grad[None],
        ]
    )
    span = PLANE * own_rows

    def plane_part(step):
        return lax.dynamic_slice_in_dim(small_grad, moves.planes_back[step] * span, span, 1)

    small_total = plane_part(1)
    for step in (*range(2, planes), 0):
        small_total = plane_part(step) + send(small_total, ring)
    for bit, pairs in ((spot // 2, moves.spots[2]), (spot % 2, moves.spots[1])):
        span //= 2
        kept = lax.dynamic_slice_in_dim(small_total, bit * span, span, 1)
        given = lax.dynamic_slice_in_dim(small_total, (1 - bit) * span, span, 1)
        small_total = kept + send(given, pairs)
    left, right = small_total[:, :own_rows], small_total[:, own_rows:]
    small_share = jnp.where(core == 0, left, right) + send(
        jnp.where(core == 0, right, left), cores
    )
    return (
        output,
        input_grad,
        small_share[SMALL - 4 :],
        in_share,
        out_share,
        small_share[: SMALL - 4].T,
        expert_in_grad[None],
        expert_out_grad[None],
    )


def shards(*arguments):
    routes = arguments[8]
    experts = lax.axis_size("fsdp") // 2
    if 2 * routes.shape[1] >= experts and HEADS == experts:
        return shards_dense(*arguments)
    return shards_routed(*arguments)


def solution(mesh):
    in_specs = (
        P("fsdp", None),
        P("fsdp", None),
        P(None, "fsdp"),
        P("fsdp", None),
        P("fsdp", None),
        P("fsdp", None),
        P("fsdp", None, None),
        P("fsdp", None, None),
        P("fsdp", None),
        P("fsdp", None),
    )
    out_specs = (
        P("fsdp", None),
        P("fsdp", None),
        P(None, "fsdp"),
        P("fsdp", None),
        P("fsdp", None),
        P("fsdp", None),
        P("fsdp", None, None),
        P("fsdp", None, None),
    )
    return jax.shard_map(shards, mesh=mesh, in_specs=in_specs, out_specs=out_specs, check_vma=False)
```

```python
import functools

import jax
import jax.numpy as jnp
from jax import lax
from jax.experimental import pallas as pl
from jax.experimental.pallas import tpu as pltpu
from jax.sharding import PartitionSpec as P

D = 2048
HEADS = 16
HEAD_DIM = 128


EPSILON = 1e-05
ROPE_BASE = 10000.0
MASKED = -1000000000.0


def root_norm(vector, scaling):
    return vector * lax.rsqrt(jnp.mean(vector * vector, axis=-1, keepdims=True) + EPSILON) * scaling


def rotary(vector, cos_table, sin_table):
    half_dim = vector.shape[-1] // 2
    first = vector[..., :half_dim]
    second = vector[..., half_dim:]
    return jnp.concatenate(
        [first * cos_table - second * sin_table, second * cos_table + first * sin_table], axis=-1
    )


def layout(lengths, number):
    ends_at = jnp.cumsum(lengths)
    places = jnp.arange(number, dtype=jnp.int32)
    segment = jnp.sum((places[:, None] >= ends_at[None, :]).astype(jnp.int32), axis=1)
    starts = ends_at - lengths
    select_mask = (
        segment[:, None] == jnp.arange(lengths.shape[0], dtype=jnp.int32)[None, :]
    ).astype(jnp.int32)
    position = places - jnp.sum(select_mask * starts[None, :], axis=1)
    return (segment, position)


def tables(position):
    half_dim = HEAD_DIM // 2
    inverse = ROPE_BASE ** (-2.0 * jnp.arange(half_dim, dtype=jnp.float32) / HEAD_DIM)
    angles = position.astype(jnp.float32)[:, None] * inverse[None, :]
    return (jnp.cos(angles)[:, None, :], jnp.sin(angles)[:, None, :])


def prepare(projected, query_gain, key_gain, cos_table, sin_table):
    count_rows = projected.shape[0]
    query_heads = root_norm(projected[:, :D], query_gain).reshape(count_rows, HEADS, HEAD_DIM)
    key_heads = root_norm(projected[:, D : 2 * D], key_gain).reshape(count_rows, HEADS, HEAD_DIM)
    value_heads = projected[:, 2 * D :].reshape(count_rows, HEADS, HEAD_DIM)
    return (
        rotary(query_heads, cos_table, sin_table),
        rotary(key_heads, cos_table, sin_table),
        value_heads,
    )


def softmax_rows(logits):
    row_max = jnp.max(logits, axis=-1, keepdims=True)
    exponent = jnp.exp(logits - row_max)
    return exponent / jnp.sum(exponent, axis=-1, keepdims=True)


def dot_first(left, right):
    return lax.dot_general(
        left, right, (((0,), (0,)), ((), ())), preferred_element_type=jnp.float32
    )


def dot_last(left, right):
    return lax.dot_general(
        left, right, (((1,), (1,)), ((), ())), preferred_element_type=jnp.float32
    )


def shards_routed(
    tokens,
    cotangent,
    norm_gains,
    attention_in,
    attention_out,
    router_weight,
    expert_in,
    expert_out,
    routes,
    lengths,
):
    row_count = tokens.shape[0]
    devices_count = lax.axis_size("fsdp")
    experts = devices_count // 2
    choose = routes.shape[1]
    half_units = expert_out.shape[1]
    capacity = 4 * row_count * choose // (3 * experts)
    scaling = HEAD_DIM ** (-0.5)
    gain_full, gathered_in, gathered_out, gathered_router = (
        lax.all_gather(norm_gains, "fsdp", axis=1, tiled=True),
        lax.all_gather(attention_in, "fsdp", axis=0, tiled=True),
        lax.all_gather(attention_out, "fsdp", axis=0, tiled=True),
        lax.all_gather(router_weight, "fsdp", axis=0, tiled=True),
    )
    gain_rows = gain_full.astype(jnp.float32)
    segment, position = layout(lengths[0], row_count)
    cos_table, sin_table = tables(position)
    places = jnp.arange(row_count, dtype=jnp.int32)
    allowed = ((segment[:, None] == segment[None, :]) & (places[:, None] >= places[None, :]))[None]
    inputs = tokens.astype(jnp.float32)
    normed_input = root_norm(inputs, gain_rows[0]).astype(jnp.bfloat16)
    projected = jnp.dot(normed_input, gathered_in, preferred_element_type=jnp.float32)

    def prepare_local(projected_value, query_gain, key_gain):
        return prepare(projected_value, query_gain, key_gain, cos_table, sin_table)

    (query_f, key_f, value_f), prepare_back = jax.vjp(
        prepare_local, projected, gain_rows[1], gain_rows[2]
    )
    query_heads = query_f.astype(jnp.bfloat16)
    key_heads = key_f.astype(jnp.bfloat16)
    value_heads = value_f.astype(jnp.bfloat16)

    def score_block():
        raw_scores = (
            jnp.einsum("qhd,khd->hqk", query_heads, key_heads, preferred_element_type=jnp.float32)
            * scaling
        )
        return jnp.where(allowed, raw_scores, MASKED)

    scores = score_block()
    row_max = jnp.max(scores, axis=-1, keepdims=True)
    exponent = jnp.exp(scores - row_max)
    row_sum = jnp.sum(exponent, axis=-1, keepdims=True)
    log_total = row_max + jnp.log(row_sum)
    attend_probs = (exponent / row_sum).astype(jnp.bfloat16)
    attended = (
        jnp.einsum("hqk,khd->qhd", attend_probs, value_heads, preferred_element_type=jnp.float32)
        .reshape(row_count, D)
        .astype(jnp.bfloat16)
    )
    branch_out = jnp.dot(attended, gathered_out, preferred_element_type=jnp.float32)
    residual = inputs + branch_out
    normed = root_norm(residual, gain_rows[3]).astype(jnp.bfloat16)
    logits = jnp.dot(normed, gathered_router, preferred_element_type=jnp.float32)
    router_probs = softmax_rows(logits)
    chosen = jnp.take_along_axis(router_probs, routes, axis=1)
    gate_total = jnp.sum(chosen, axis=1, keepdims=True)
    gate_values = chosen / gate_total
    flat_routes = routes.reshape(-1)
    route_hits = (flat_routes[:, None] == jnp.arange(experts, dtype=jnp.int32)[None, :]).astype(
        jnp.int32
    )
    slot_index = jnp.sum((jnp.cumsum(route_hits, axis=0) - route_hits) * route_hits, axis=1)
    target = flat_routes * capacity + slot_index
    owner_token = (
        jnp.zeros((experts * capacity,), jnp.int32)
        .at[target]
        .set(jnp.arange(row_count * choose, dtype=jnp.int32) // choose)
    )
    filled = (
        jnp.zeros((experts * capacity,), jnp.bfloat16)
        .at[target]
        .set(jnp.ones((row_count * choose,), jnp.bfloat16))
    )
    outgoing = jnp.repeat(
        (normed[owner_token] * filled[:, None]).reshape(experts, capacity, D), 2, axis=0
    )
    arrived = lax.all_to_all(outgoing, "fsdp", split_axis=0, concat_axis=0, tiled=True).reshape(
        devices_count * capacity, D
    )
    gate_up_out = jnp.dot(arrived, expert_in[0], preferred_element_type=jnp.float32)
    gate_part = gate_up_out[:, :half_units]
    up_part = gate_up_out[:, half_units:]
    hidden_f, swiglu_back = jax.vjp(
        lambda gate_in, up_in: jax.nn.silu(gate_in) * up_in, gate_part, up_part
    )
    hidden = hidden_f.astype(jnp.bfloat16)
    produced = (
        jnp.dot(hidden, expert_out[0], preferred_element_type=jnp.float32)
        .astype(jnp.bfloat16)
        .reshape(devices_count, capacity, D)
    )
    returned = (
        lax.all_to_all(produced, "fsdp", split_axis=0, concat_axis=0, tiled=True)
        .reshape(experts, 2, capacity, D)
        .astype(jnp.float32)
    )
    returned = jnp.sum(returned, axis=1).reshape(experts * capacity, D)
    picked = returned[target].reshape(row_count, choose, D)
    expert_sum = jnp.sum(gate_values[:, :, None] * picked, axis=1)
    output = (residual + expert_sum).astype(jnp.bfloat16)
    back_in, back_out, back_router = (
        lax.all_gather(attention_in, "fsdp", axis=0, tiled=True),
        lax.all_gather(attention_out, "fsdp", axis=0, tiled=True),
        lax.all_gather(router_weight, "fsdp", axis=0, tiled=True),
    )
    upstream = cotangent.astype(jnp.float32)
    gate_grad = jnp.sum(upstream[:, None, :] * picked, axis=2)
    send_grad = (
        (gate_values[:, :, None] * upstream[:, None, :])
        .astype(jnp.bfloat16)
        .reshape(row_count * choose, D)
    )
    grad_buffer = (
        jnp.zeros((experts * capacity, D), jnp.bfloat16)
        .at[target]
        .set(send_grad)
        .reshape(experts, capacity, D)
    )
    grad_buffer = jnp.repeat(grad_buffer, 2, axis=0)
    grad_arrived = lax.all_to_all(
        grad_buffer, "fsdp", split_axis=0, concat_axis=0, tiled=True
    ).reshape(devices_count * capacity, D)
    grad_hidden = dot_last(grad_arrived, expert_out[0])
    expert_out_grad = dot_first(hidden, grad_arrived)
    grad_gate, grad_up = swiglu_back(grad_hidden)
    grad_gate_up = jnp.concatenate([grad_gate, grad_up], axis=1).astype(jnp.bfloat16)
    expert_in_grad = dot_first(arrived, grad_gate_up)
    grad_rows = (
        dot_last(grad_gate_up, expert_in[0])
        .astype(jnp.bfloat16)
        .reshape(devices_count, capacity, D)
    )
    grad_back = (
        lax.all_to_all(grad_rows, "fsdp", split_axis=0, concat_axis=0, tiled=True)
        .reshape(experts, 2, capacity, D)
        .astype(jnp.float32)
    )
    grad_back = jnp.sum(grad_back, axis=1).reshape(experts * capacity, D)
    dispatch_grad = jnp.sum(grad_back[target].reshape(row_count, choose, D), axis=1)
    chosen_grad = (gate_grad - jnp.sum(gate_grad * gate_values, axis=1, keepdims=True)) / gate_total
    expert_match = (
        routes[:, :, None] == jnp.arange(experts, dtype=jnp.int32)[None, None, :]
    ).astype(jnp.float32)
    prob_grad = jnp.sum(expert_match * chosen_grad[:, :, None], axis=1)
    logit_grad = (
        router_probs * (prob_grad - jnp.sum(prob_grad * router_probs, axis=1, keepdims=True))
    ).astype(jnp.bfloat16)
    router_grad = dot_first(normed, logit_grad)
    normed_grad = dispatch_grad + dot_last(logit_grad, back_router)
    _, second_back = jax.vjp(root_norm, residual, gain_rows[3])
    residual_norm_grad, second_gain_grad = second_back(normed_grad)
    residual_grad = upstream + residual_norm_grad
    branch_grad = residual_grad.astype(jnp.bfloat16)
    out_grad = dot_first(attended, branch_grad)
    attended_grad = (
        dot_last(branch_grad, back_out).astype(jnp.bfloat16).reshape(row_count, HEADS, HEAD_DIM)
    )
    recomputed = jnp.exp(score_block() - log_total)
    value_grad = jnp.einsum(
        "hqk,qhd->khd", attend_probs, attended_grad, preferred_element_type=jnp.float32
    )
    attend_grad = jnp.einsum(
        "qhd,khd->hqk", attended_grad, value_heads, preferred_element_type=jnp.float32
    )
    row_delta = jnp.sum(recomputed * attend_grad, axis=-1, keepdims=True)
    score_grad = (recomputed * (attend_grad - row_delta)).astype(jnp.bfloat16)
    query_grad = (
        jnp.einsum("hqk,khd->qhd", score_grad, key_heads, preferred_element_type=jnp.float32)
        * scaling
    )
    key_grad = (
        jnp.einsum("hqk,qhd->khd", score_grad, query_heads, preferred_element_type=jnp.float32)
        * scaling
    )
    projected_grad, query_gain_grad, key_gain_grad = prepare_back(
        (query_grad, key_grad, value_grad)
    )
    projected_grad = projected_grad.astype(jnp.bfloat16)
    attention_in_grad = dot_first(normed_input, projected_grad)
    normed_input_grad = dot_last(projected_grad, back_in)
    _, first_back = jax.vjp(root_norm, inputs, gain_rows[0])
    input_norm_grad, first_gain_grad = first_back(normed_input_grad)
    input_grad = residual_grad + input_norm_grad
    gains_grad = jnp.stack([first_gain_grad, query_gain_grad, key_gain_grad, second_gain_grad])
    gains_share, in_share, out_share, router_share = (
        lax.psum_scatter(gains_grad, "fsdp", scatter_dimension=1, tiled=True),
        lax.psum_scatter(attention_in_grad, "fsdp", scatter_dimension=0, tiled=True),
        lax.psum_scatter(out_grad, "fsdp", scatter_dimension=0, tiled=True),
        lax.psum_scatter(router_grad, "fsdp", scatter_dimension=0, tiled=True),
    )
    return (
        output,
        input_grad,
        gains_share,
        in_share,
        out_share,
        router_share,
        expert_in_grad[None],
        expert_out_grad[None],
    )


def product(left, right):
    return jnp.dot(left, right, preferred_element_type=jnp.float32)


def widen(value):
    return value.astype(jnp.float32)


PLANE = 8
SPOTS = 4
WIDE = 128
SMALL = 20
FIRST_GAIN = SMALL - 4


class Moves:
    def __init__(self, count):
        planes = count // PLANE
        order = list(range(0, planes, 2)) + list(range(1, planes, 2))[::-1]
        after = {order[i]: order[(i + 1) % planes] for i in range(planes)}
        self.planes = planes
        self.ring = [(i, after[i // PLANE] * PLANE + i % PLANE) for i in range(count)]
        self.first = [(i, i ^ (4 if i & 1 else 2)) for i in range(count)]
        self.second = [(i, i ^ (2 if i & 1 else 4)) for i in range(count)]
        self.core = [(i, i ^ 1) for i in range(count)]
        self.spots = [[(i, i ^ (2 * mask)) for i in range(count)] for mask in range(SPOTS)]
        device = lax.axis_index("fsdp")
        self.device = device
        self.plane, self.spot, self.core_id = device // PLANE, device % PLANE // 2, device % 2
        rank = jnp.asarray([order.index(i) for i in range(planes)], jnp.int32)
        self.planes_back = jnp.asarray(order, jnp.int32)[
            (rank[self.plane] - jnp.arange(planes, dtype=jnp.int32)) % planes
        ]
        self.steps_from = (rank[self.plane] - rank) % planes
        self.group_spots = self.spot ^ jnp.where(
            self.core_id == 0, jnp.asarray([0, 1, 2, 3]), jnp.asarray([0, 2, 1, 3])
        )


def send(value, pairs):
    return lax.ppermute(value, "fsdp", pairs)


def tie(*values):
    return lax.optimization_barrier(values)


def by_spot(moves, parts):
    return jnp.where(moves.core_id == 0, parts, parts[:, jnp.asarray([0, 2, 1, 3])])


def plane_step(moves, parts, bit):
    other = send(parts, moves.spots[bit])
    return parts + jnp.stack([other[:, m ^ bit] for m in range(SPOTS)], axis=1)


def full_spec(*dims):
    return pl.BlockSpec(dims, lambda *_: (0,) * len(dims))


SCALARS = pl.BlockSpec(memory_space=pltpu.SMEM)
ANYWHERE = pl.BlockSpec(memory_space=pl.ANY)


def params(mebibytes):
    return pltpu.CompilerParams(vmem_limit_bytes=mebibytes << 20)


def cost(flops, moved, special=0):
    return pl.CostEstimate(flops=flops, bytes_accessed=moved, transcendentals=special)


def column_places(spot, mask, lines):
    for part in range(3):
        for line in range(lines):
            piece = (part * lines + line) * HEAD_DIM
            whole = ((part * lines + line) * SPOTS + (spot ^ mask)) * HEAD_DIM
            yield pl.ds(pl.multiple_of(whole, HEAD_DIM), HEAD_DIM), pl.ds(piece, HEAD_DIM)


def split_body(lines, spot, lengths, whole_ref, router_ref, gains_ref, *pieces):
    rows, columns = pieces[0].shape[0], pieces[0].shape[1] - WIDE
    routers = router_ref.shape[1]
    lane = lax.broadcasted_iota(jnp.int32, (rows, WIDE), 1)
    row = lax.broadcasted_iota(jnp.int32, (rows, WIDE), 0)
    spread = lax.broadcasted_iota(jnp.int32, (routers, WIDE), 0) == lax.broadcasted_iota(
        jnp.int32, (routers, WIDE), 1
    )
    riding = product(router_ref[...], jnp.where(spread, 1.0, 0.0).astype(jnp.bfloat16))
    for n in range(gains_ref.shape[0]):
        column = as_column(widen(gains_ref[...])[n : n + 1, :])
        riding = jnp.where(lane == FIRST_GAIN + n, column, riding)
    for n in range(lengths.shape[1]):
        riding = jnp.where((lane == SMALL) & (row == n), lengths[0, n].astype(jnp.float32), riding)
    for mask, piece in enumerate(pieces):
        for whole_at, piece_at in column_places(spot[0], mask, lines):
            piece[:, piece_at] = whole_ref[:, whole_at]
        piece[:, columns:] = riding.astype(jnp.bfloat16)


def split_columns(spot, whole, router, gains, lengths):
    rows, columns = whole.shape
    columns = columns // SPOTS + WIDE
    return pl.pallas_call(
        functools.partial(split_body, HEADS // SPOTS),
        out_shape=[jax.ShapeDtypeStruct((rows, columns), whole.dtype)] * SPOTS,
        in_specs=[
            SCALARS,
            SCALARS,
            full_spec(*whole.shape),
            full_spec(*router.shape),
            full_spec(*gains.shape),
        ],
        out_specs=[full_spec(rows, columns)] * SPOTS,
        compiler_params=params(60),
        name="split_columns",
    )(spot.reshape(1), lengths, whole, router, gains)


def join_body(lines, meta, *refs):
    *pieces, whole_ref, small_ref = refs
    for mask, piece in enumerate(pieces):
        for whole_at, piece_at in column_places(meta[0], mask, lines):
            whole_ref[:, whole_at] = widen(piece[:, piece_at])
    small_ref[...] = sum(widen(piece[:, piece.shape[1] - WIDE :]) for piece in pieces)


def join_columns(spot, pieces):
    rows, wide = pieces[0].shape
    columns = wide - WIDE
    return pl.pallas_call(
        functools.partial(join_body, HEADS // SPOTS),
        out_shape=[
            jax.ShapeDtypeStruct((rows, columns * SPOTS), jnp.float32),
            jax.ShapeDtypeStruct((rows, WIDE), jnp.float32),
        ],
        in_specs=[SCALARS] + [full_spec(rows, wide)] * SPOTS,
        out_specs=[full_spec(rows, columns * SPOTS), full_spec(rows, WIDE)],
        compiler_params=params(60),
        name="join_columns",
    )(spot.reshape(1), *pieces)


def expert_body(index, cap, experts, blocks, meta, *refs):
    row_refs, grad_refs, weights = refs[:blocks], refs[blocks : 2 * blocks], refs[2 * blocks :][:4]
    refs = refs[2 * blocks + 4 + 6 :]
    saves, out_parts, row_parts = refs[:6], refs[6 : 6 + blocks], refs[6 + blocks :][:blocks]
    rows_v, grads_v, in_v, out_v, x_v, dy_v, m_v, du_v, part_v, back_v, sem, done = refs[
        6 + 2 * blocks :
    ]
    bf, f32 = jnp.bfloat16, jnp.float32
    count, width, half = rows_v.shape[1], grads_v.shape[2], out_v.shape[1]
    expert = meta[0]

    def fetch(ref, place, n):
        copy = pltpu.make_async_copy(ref, place, sem.at[n])
        copy.start()
        return copy

    fetch_rows = [fetch(ref, rows_v.at[j], j) for j, ref in enumerate(row_refs)]
    fetch_in = [fetch(weights[h], in_v.at[h], blocks + h) for h in range(2)]
    fetch_out = [fetch(weights[2 + h], out_v.at[h], blocks + 2 + h) for h in range(2)]
    fetch_grads = [fetch(ref, grads_v.at[j], blocks + 4 + j) for j, ref in enumerate(grad_refs)]
    leaving = []

    def leave(place, ref):
        leaving.append(pltpu.make_async_copy(place, ref, done.at[len(leaving)]))
        leaving[-1].start()

    def save(place, n):
        leave(place, saves[n].at[pl.ds(index * cap, blocks * cap)])

    lane8 = lax.broadcasted_iota(jnp.int32, (8, WIDE), 1)
    row8 = lax.broadcasted_iota(jnp.int32, (8, WIDE), 0)
    picker = (
        jnp.where((row8 == 0) & (lane8 == expert), 1.0, 0.0)
        + jnp.where((row8 == 1) & (lane8 == experts + expert), 1.0, 0.0)
        + jnp.where((row8 == 1) & (lane8 == 2 * experts + expert), 1.0, 0.0)
    ).astype(bf)
    lanes = lax.broadcasted_iota(jnp.int32, (count, WIDE), 1)
    slots_down = lax.broadcasted_iota(jnp.int32, (cap, count), 0)
    slots_along = lax.broadcasted_iota(jnp.int32, (count, cap), 1)
    gather, scatter, gates = [], [], []
    slots = [slice(j * cap, (j + 1) * cap) for j in range(blocks)]
    for j in range(blocks):
        fetch_rows[j].wait()
        extra = rows_v[j, :, width:]
        info = dot_last(picker, extra)
        chosen = slots_down == info[0:1].astype(jnp.int32)
        gates.append(jnp.sum(jnp.where(chosen, info[1:2], 0.0), axis=1, keepdims=True))
        gather.append(jnp.where(chosen, 1.0, 0.0).astype(bf))
        slot = jnp.sum(
            jnp.where(lanes == expert, widen(extra), 0.0), axis=1, keepdims=True
        ).astype(jnp.int32)
        scatter.append(jnp.where(slots_along == slot, 1.0, 0.0).astype(bf))
        x_v[slots[j], :] = product(gather[j], rows_v[j, :, :width]).astype(bf)
    gate = jnp.concatenate(gates, axis=0)
    save(x_v, 0)
    x = x_v[...]
    inner = []
    for h in range(2):
        fetch_in[h].wait()
        u = product(x, in_v[h])
        gate_part, up_part = u[:, :half], u[:, half:]
        sigmoid = 1.0 / (1.0 + jnp.exp(-gate_part))
        silu = gate_part * sigmoid
        inner.append((gate_part, up_part, sigmoid, silu))
        m_v[h] = (silu * up_part).astype(bf)
        save(m_v.at[h], 2 + h)
    for copy in fetch_out:
        copy.wait()
    y = product(m_v[0], out_v[0]) + product(m_v[1], out_v[1])
    for copy in fetch_grads:
        copy.wait()
    g = jnp.concatenate([product(gather[j], grads_v[j]) for j in range(blocks)], axis=0)
    dgate = jnp.sum(g * y, axis=1, keepdims=True)
    z = (gate * y).astype(bf)
    dy_v[...] = (gate * g).astype(bf)
    save(dy_v, 1)
    for j in range(blocks):
        part_v[j] = product(scatter[j], z[slots[j]]).astype(bf)
        leave(part_v.at[j], out_parts[j])
    dy = dy_v[...]
    for h in range(2):
        gate_part, up_part, sigmoid, silu = inner[h]
        dm = dot_last(dy, out_v[h])
        slope = sigmoid * (1.0 + gate_part * (1.0 - sigmoid))
        du_v[h, :, :half] = (dm * up_part * slope).astype(bf)
        du_v[h, :, half:] = (dm * silu).astype(bf)
        save(du_v.at[h], 4 + h)
    drows = (dot_last(du_v[0], in_v[0]) + dot_last(du_v[1], in_v[1])).astype(bf)
    upper = widen(dgate.astype(bf))
    lane_m = lax.broadcasted_iota(jnp.int32, (blocks * cap, WIDE), 1)
    pair = jnp.where(
        lane_m == 2 * expert, upper, jnp.where(lane_m == 2 * expert + 1, dgate - upper, 0.0)
    ).astype(bf)
    for j in range(blocks):
        back_v[j, :, :width] = product(scatter[j], drows[slots[j]]).astype(bf)
        back_v[j, :, width:] = product(scatter[j], pair[slots[j]]).astype(bf)
        leave(back_v.at[j], row_parts[j])
    for copy in leaving:
        copy.wait()


def expert_blocks(meta, rows, grads, weights, saved, index, total, cap, experts):
    blocks = len(rows)
    count, wide = rows[0].shape
    width, half = grads[0].shape[1], weights[2].shape[0]
    bf = jnp.bfloat16
    used = blocks * cap

    def shape(*dims):
        return jax.ShapeDtypeStruct(dims, bf)

    aliases = {2 * blocks + 5 + t: t for t in range(6)}
    if saved is None:
        saved, aliases = [jnp.zeros((16, WIDE), bf)] * 6, {}
    save_columns = (width, width, half, half, 2 * half, 2 * half)
    results = pl.pallas_call(
        functools.partial(expert_body, index, cap, experts, blocks),
        out_shape=[shape(total * cap, columns) for columns in save_columns]
        + [shape(count, width)] * blocks
        + [shape(count, wide)] * blocks,
        in_specs=[SCALARS] + [ANYWHERE] * (2 * blocks + 10),
        out_specs=[ANYWHERE] * (6 + 2 * blocks),
        scratch_shapes=[
            pltpu.VMEM((blocks, count, wide), bf),
            pltpu.VMEM((blocks, count, width), bf),
            pltpu.VMEM((2, width, 2 * half), bf),
            pltpu.VMEM((2, half, width), bf),
            pltpu.VMEM((used, width), bf),
            pltpu.VMEM((used, width), bf),
            pltpu.VMEM((2, used, half), bf),
            pltpu.VMEM((2, used, 2 * half), bf),
            pltpu.VMEM((blocks, count, width), bf),
            pltpu.VMEM((blocks, count, wide), bf),
            pltpu.SemaphoreType.DMA((2 * blocks + 4,)),
            pltpu.SemaphoreType.DMA((6 + 2 * blocks,)),
        ],
        input_output_aliases=aliases,
        compiler_params=params(60),
        cost_estimate=cost(blocks * 38 * 10**8, 30 << 20, 2 * used * half),
        name="expert_blocks",
    )(meta, *rows, *grads, *weights, *saved)
    return results[:6], results[6 : 6 + blocks], results[6 + blocks :]


def eye(count):
    return lax.broadcasted_iota(jnp.int32, (count, count), 0) == lax.broadcasted_iota(
        jnp.int32, (count, count), 1
    )


def as_column(row):
    return jnp.sum(jnp.where(eye(row.shape[1]), row, 0.0), axis=1, keepdims=True)


def as_row(column):
    return jnp.sum(jnp.where(eye(column.shape[0]), column, 0.0), axis=0, keepdims=True)


def rolled(value):
    return pltpu.roll(value, HEAD_DIM // 2, 1)


def root_of(total):
    return lax.rsqrt(total / D + EPSILON)


def weights_of(query, key, start):
    count = query.shape[0]
    rows = lax.broadcasted_iota(jnp.int32, (count, count), 0)
    columns = lax.broadcasted_iota(jnp.int32, (count, count), 1)
    allowed = (columns <= rows) & (columns >= start.astype(jnp.int32))
    scores = jnp.where(allowed, dot_last(query, key) * HEAD_DIM ** (-0.5), MASKED)
    exponent = jnp.exp(scores - jnp.max(scores, axis=1, keepdims=True))
    return exponent / jnp.sum(exponent, axis=1, keepdims=True)


def spans(mine):
    return [slice(h, h + HEAD_DIM) for h in range(0, mine, HEAD_DIM)]


def project_body(planes, own_rows, meta, *refs):
    blocks, own, other = refs[:SPOTS], refs[SPOTS : SPOTS + planes], refs[SPOTS + planes :][:planes]
    proj_ref, a_ref, in_ref, sums_ref, small_ref, gains_ref = refs[SPOTS + 2 * planes :][:6]
    x_v, a_v, in_v, proj_v, sem, in_sem, done = refs[SPOTS + 2 * planes + 6 :]
    spot, core = meta[0], meta[1]
    count = x_v.shape[1]
    mine = proj_v.shape[1] // 3
    fetch_x = [pltpu.make_async_copy(ref, x_v.at[j], sem.at[j]) for j, ref in enumerate(blocks)]
    for copy in fetch_x:
        copy.start()
    fetch_in = []
    for k in range(planes):
        for mask in range(SPOTS):
            chunk = meta[2 + k] * PLANE + (spot ^ mask) * 2
            for n, (refs_k, c) in enumerate(((own, core), (other, 1 - core))):
                at = pl.multiple_of((chunk + c) * own_rows, own_rows)
                fetch_in.append(
                    pltpu.make_async_copy(
                        refs_k[k].at[mask],
                        in_v.at[pl.ds(at, own_rows)],
                        in_sem.at[(k * SPOTS + mask) * 2 + n],
                    )
                )
                fetch_in[-1].start()
    roots = []
    for j in range(SPOTS):
        fetch_x[j].wait()
        x = widen(x_v[j])
        roots.append(lax.rsqrt(jnp.mean(x * x, axis=1, keepdims=True) + EPSILON))
    for copy in fetch_in:
        copy.wait()
    leaving = [pltpu.make_async_copy(in_v, in_ref, done.at[0])]
    leaving[0].start()
    turn_by = lax.broadcasted_iota(jnp.int32, (small_ref.shape[0], WIDE), 0) == (
        lax.broadcasted_iota(jnp.int32, (small_ref.shape[0], WIDE), 1)
    )
    small = dot_last(jnp.where(turn_by, 1.0, 0.0).astype(jnp.bfloat16), in_v[:, 3 * mine :])
    small_ref[...] = small
    for line in range(mine // HEAD_DIM):
        at = pl.multiple_of((line * SPOTS + spot) * HEAD_DIM, HEAD_DIM)
        for n in range(2):
            gains_ref[n : n + 1, line * HEAD_DIM : (line + 1) * HEAD_DIM] = small_ref[
                FIRST_GAIN + 1 + n : FIRST_GAIN + 2 + n, pl.ds(at, HEAD_DIM)
            ]
    gain = small[FIRST_GAIN : FIRST_GAIN + 1, :]
    for j in range(SPOTS):
        a_v[j * count : (j + 1) * count, :] = (widen(x_v[j]) * roots[j] * gain).astype(jnp.bfloat16)
    leaving.append(pltpu.make_async_copy(a_v, a_ref, done.at[1]))
    leaving[1].start()
    for n in range(3):
        part = slice(n * mine, (n + 1) * mine)
        value = product(a_v[...], in_v[:, part])
        proj_v[:, part] = value
        leaving.append(
            pltpu.make_async_copy(proj_v.at[:, part], proj_ref.at[:, part], done.at[2 + n])
        )
        leaving[-1].start()
        if n < 2:
            squares = jnp.sum(value * value, axis=1, keepdims=True)
            for j in range(SPOTS):
                sums_ref[n, j : j + 1, :] = as_row(squares[j * count : (j + 1) * count])
    for copy in leaving:
        copy.wait()


def project(moves, blocks, own, other):
    planes, own_rows, wide = len(own), own[0].shape[1], own[0].shape[2]
    width = wide - WIDE
    count, depth = blocks[0].shape
    bf, f32 = jnp.bfloat16, jnp.float32
    rows = SPOTS * count
    meta = jnp.concatenate([jnp.stack([moves.spot, moves.core_id]), moves.planes_back])
    shape = jax.ShapeDtypeStruct
    return pl.pallas_call(
        functools.partial(project_body, planes, own_rows),
        out_shape=[
            shape((rows, width), f32),
            shape((rows, depth), bf),
            shape((depth, wide), bf),
            shape((2, SPOTS, count), f32),
            shape((32, depth), f32),
            shape((2, width // 3), f32),
        ],
        in_specs=[SCALARS] + [ANYWHERE] * (SPOTS + 2 * planes),
        out_specs=[ANYWHERE] * 3
        + [full_spec(2, SPOTS, count), full_spec(32, depth), full_spec(2, width // 3)],
        scratch_shapes=[
            pltpu.VMEM((SPOTS, count, depth), bf),
            pltpu.VMEM((rows, depth), bf),
            pltpu.VMEM((depth, wide), bf),
            pltpu.VMEM((rows, width), f32),
            pltpu.SemaphoreType.DMA((SPOTS,)),
            pltpu.SemaphoreType.DMA((2 * SPOTS * planes,)),
            pltpu.SemaphoreType.DMA((5,)),
        ],
        compiler_params=params(60),
        cost_estimate=cost(5 * 10**9, 20 << 20),
        name="project",
    )(meta.astype(jnp.int32), *blocks, *own, *other)


def by_block(count, width):
    return [pl.BlockSpec((count, width), lambda i: (0, 0))] * SPOTS


def put_by_block(step, refs, value):
    for n, ref in enumerate(refs):

        @pl.when(step == n)
        def _(ref=ref):
            ref[...] = value


def forward_body(planes, own_rows, meta, totals, starts, gains, proj_ref, cos_ref, sin_ref, *refs):
    own, other = refs[:planes], refs[planes : 2 * planes]
    q_ref, k_ref, v_ref, o_ref, out_w, *parts = refs[2 * planes :][: 5 + SPOTS]
    sem = refs[-1]
    step = pl.program_id(0)
    bf = jnp.bfloat16
    mine = q_ref.shape[1]
    fetches = []
    for k in range(planes):
        for n, (refs_k, c) in enumerate(((own, meta[1]), (other, 1 - meta[1]))):
            at = pl.multiple_of((meta[2 + k] * 2 + c) * own_rows, own_rows)
            fetches.append(
                pltpu.make_async_copy(
                    refs_k[k], out_w.at[pl.ds(at, own_rows)], sem.at[2 * k + n]
                )
            )

    @pl.when(step == 0)
    def _():
        for copy in fetches:
            copy.start()

    query_root = root_of(as_column(totals[0, pl.ds(step, 1), :]))
    key_root = root_of(as_column(totals[1, pl.ds(step, 1), :]))
    start = as_column(starts[pl.ds(step, 1), :])
    cos, sin = cos_ref[...], sin_ref[...]
    for own_span in spans(mine):
        at = own_span.start
        query = proj_ref[:, at : at + HEAD_DIM] * query_root * gains[0:1, own_span]
        key = proj_ref[:, mine + at : mine + at + HEAD_DIM] * key_root * gains[1:2, own_span]
        value = proj_ref[:, 2 * mine + at : 2 * mine + at + HEAD_DIM].astype(bf)
        query = (query * cos + rolled(query) * sin).astype(bf)
        key = (key * cos + rolled(key) * sin).astype(bf)
        weights = weights_of(query, key, start).astype(bf)
        q_ref[:, own_span] = query
        k_ref[:, own_span] = key
        v_ref[:, own_span] = value
        o_ref[:, own_span] = product(weights, value).astype(bf)

    @pl.when(step == 0)
    def _():
        for copy in fetches:
            copy.wait()

    put_by_block(step, parts, product(o_ref[...], out_w[...]).astype(bf))


def block_spec(count, columns):
    return pl.BlockSpec((count, columns), lambda i: (i, 0))


def attend_forward(moves, totals, starts, gains, projected, cos_all, sin_all, own, other):
    planes, own_rows = len(own), own[0].shape[0]
    rows, mine = projected.shape[0], gains.shape[1]
    count = rows // SPOTS
    bf = jnp.bfloat16
    meta = jnp.concatenate([jnp.stack([moves.spot, moves.core_id]), moves.planes_back])
    return pl.pallas_call(
        functools.partial(forward_body, planes, own_rows),
        grid=(SPOTS,),
        out_shape=[jax.ShapeDtypeStruct((rows, mine), bf)] * 4
        + [jax.ShapeDtypeStruct((mine, D), bf)]
        + [jax.ShapeDtypeStruct((count, D), bf)] * SPOTS,
        in_specs=[
            SCALARS,
            full_spec(*totals.shape),
            full_spec(*starts.shape),
            full_spec(*gains.shape),
            block_spec(count, 3 * mine),
            block_spec(count, HEAD_DIM),
            block_spec(count, HEAD_DIM),
        ]
        + [ANYWHERE] * (2 * planes),
        out_specs=[block_spec(count, mine)] * 4 + [full_spec(mine, D)] + by_block(count, D),
        scratch_shapes=[pltpu.SemaphoreType.DMA((2 * planes,))],
        compiler_params=params(60),
        cost_estimate=cost(5 * 10**9, 20 << 20),
        name="attend_forward",
    )(meta.astype(jnp.int32), totals, starts, gains, projected, cos_all, sin_all, *own, *other)


def backward_body(
    meta, totals, starts, gains, proj_ref, cos_ref, sin_ref, q_ref, k_ref, v_ref, o_ref, out_w, *refs
):
    blocks = refs[:SPOTS]
    dq_ref, dk_ref, dv_ref, sums_ref, own_grad, other_grad, gain_grad = refs[SPOTS : SPOTS + 7]
    grads_v, o_v, total_v, sem = refs[SPOTS + 7 :]
    step = pl.program_id(0)
    bf = jnp.bfloat16
    mine = q_ref.shape[1]

    @pl.when(step == 0)
    def _():
        for n in range(SPOTS):
            pltpu.make_async_copy(blocks[n], grads_v.at[n], sem.at[n]).start()
        gain_grad[...] = jnp.zeros_like(gain_grad)

    pltpu.make_async_copy(blocks[0], grads_v.at[step], sem.at[step]).wait()
    grads = grads_v[step]
    count = grads.shape[0]
    o_v[pl.ds(pl.multiple_of(step * count, 64), count), :] = o_ref[...]
    do = dot_last(grads, out_w[...]).astype(bf)
    roots = [root_of(as_column(totals[n, pl.ds(step, 1), :])) for n in range(2)]
    start = as_column(starts[pl.ds(step, 1), :])
    cos, sin = cos_ref[...], sin_ref[...]
    sums = [0.0, 0.0]
    for own in spans(mine):
        query, key, value = q_ref[:, own], k_ref[:, own], v_ref[:, own]
        weights = weights_of(query, key, start)
        dv_ref[:, own] = dot_first(weights.astype(bf), do[:, own]).astype(bf)
        dweights = dot_last(do[:, own], value)
        inner = jnp.sum(weights * dweights, axis=1, keepdims=True)
        dscores = (weights * (dweights - inner)).astype(bf)
        for n, (grad, ref) in enumerate(
            ((product(dscores, key), dq_ref), (dot_first(dscores, query), dk_ref))
        ):
            grad = grad * HEAD_DIM ** (-0.5)
            grad = grad * cos - rolled(grad) * sin
            ref[:, own] = grad
            at = n * mine + own.start
            raw = grad * proj_ref[:, at : at + HEAD_DIM]
            sums[n] += jnp.sum(raw * gains[n : n + 1, own], axis=1, keepdims=True)
            line = pl.multiple_of((own.start // HEAD_DIM * SPOTS + meta[0]) * HEAD_DIM, HEAD_DIM)
            gain_grad[n : n + 1, pl.ds(line, HEAD_DIM)] += jnp.sum(
                raw * roots[n], axis=0, keepdims=True
            )
    for n in range(2):
        sums_ref[n, pl.ds(step, 1), :] = as_row(sums[n])

    @pl.when(step == SPOTS - 1)
    def _():
        planes, own_rows = own_grad.shape[:2]
        total = sum(
            dot_first(o_v[j * count : (j + 1) * count, :], grads_v[j]) for j in range(SPOTS)
        )
        total_v[...] = total.astype(bf)
        for k in range(planes):
            for ref, c in ((own_grad, meta[1]), (other_grad, 1 - meta[1])):
                at = pl.multiple_of((meta[2 + k] * 2 + c) * own_rows, own_rows)
                ref[k] = total_v[pl.ds(at, own_rows), :]


def attend_backward(
    moves, totals, starts, gains, projected, cos_all, sin_all, heads, out_full, blocks
):
    rows, mine = projected.shape[0], gains.shape[1]
    count = rows // SPOTS
    planes = moves.planes
    own_rows = mine // (2 * planes)
    bf, f32 = jnp.bfloat16, jnp.float32
    meta = jnp.concatenate([jnp.stack([moves.spot, moves.core_id]), moves.planes_back])
    shape = jax.ShapeDtypeStruct
    return pl.pallas_call(
        backward_body,
        grid=(SPOTS,),
        out_shape=[
            shape((rows, mine), f32),
            shape((rows, mine), f32),
            shape((rows, mine), bf),
            shape((2, SPOTS, count), f32),
            shape((planes, own_rows, D), bf),
            shape((planes, own_rows, D), bf),
            shape((2, D), f32),
        ],
        in_specs=[
            SCALARS,
            full_spec(*totals.shape),
            full_spec(*starts.shape),
            full_spec(*gains.shape),
            block_spec(count, 3 * mine),
            block_spec(count, HEAD_DIM),
            block_spec(count, HEAD_DIM),
        ]
        + [block_spec(count, mine)] * 4
        + [full_spec(*out_full.shape)]
        + [ANYWHERE] * SPOTS,
        out_specs=[block_spec(count, mine)] * 3
        + [full_spec(2, SPOTS, count)]
        + [full_spec(planes, own_rows, D)] * 2
        + [full_spec(2, D)],
        scratch_shapes=[
            pltpu.VMEM((SPOTS, count, D), bf),
            pltpu.VMEM((rows, mine), bf),
            pltpu.VMEM((mine, D), bf),
            pltpu.SemaphoreType.DMA((SPOTS,)),
        ],
        compiler_params=params(60),
        cost_estimate=cost(7 * 10**9, 25 << 20),
        name="attend_backward",
    )(
        meta.astype(jnp.int32),
        totals,
        starts,
        gains,
        projected,
        cos_all,
        sin_all,
        *heads,
        out_full,
        *blocks,
    )


def project_back_body(
    planes,
    own_rows,
    meta,
    totals,
    dots,
    gains,
    router_grad,
    small_rows,
    gain_grads,
    second_grad,
    proj_ref,
    dq_ref,
    dk_ref,
    dv_ref,
    a_ref,
    in_w,
    *refs,
):
    dp_ref, own, other, rest = refs[0], refs[1 : 1 + planes], refs[1 + planes], refs[2 + planes]
    a_v, in_v, own_v, other_v, riding_v, small, sem, done = refs[3 + planes :]
    bf = jnp.bfloat16
    rows, mine = dv_ref.shape
    count = rows // SPOTS
    fetches = [
        pltpu.make_async_copy(a_ref, a_v, sem.at[0]),
        pltpu.make_async_copy(in_w, in_v, sem.at[1]),
    ]
    for copy in fetches:
        copy.start()
    for n, ref in enumerate((dq_ref, dk_ref)):
        columns = slice(n * mine, (n + 1) * mine)
        for j in range(SPOTS):
            block = slice(j * count, (j + 1) * count)
            root = root_of(as_column(totals[n, j : j + 1, :]))
            inner = as_column(dots[n, j : j + 1, :])
            grad = root * gains[n : n + 1, :] * ref[block, :]
            grad = grad - proj_ref[block, columns] * (root * root * root * inner / D)
            dp_ref[block, columns] = grad.astype(bf)
    dp_ref[:, 2 * mine :] = dv_ref[...]
    small[...] = jnp.zeros_like(small)
    small[:FIRST_GAIN, :] = router_grad[...]
    small[FIRST_GAIN : FIRST_GAIN + 1, :] = small_rows[FIRST_GAIN : FIRST_GAIN + 1, :]
    small[FIRST_GAIN + 1 : FIRST_GAIN + 3, :] = gain_grads[...]
    small[FIRST_GAIN + 3 : SMALL, :] = second_grad[...]
    turn_by = lax.broadcasted_iota(jnp.int32, (small.shape[0], WIDE), 0) == (
        lax.broadcasted_iota(jnp.int32, (small.shape[0], WIDE), 1)
    )
    riding_v[...] = dot_first(small[...].astype(bf), jnp.where(turn_by, 1.0, 0.0).astype(bf))
    lane = lax.broadcasted_iota(jnp.int32, (own_rows, WIDE), 1)
    for copy in fetches:
        copy.wait()
    leaving = []
    span = PLANE * own_rows
    for k in [*range(1, planes), 0]:
        plane = meta[2 + k]
        first_row = pl.multiple_of(plane * span, span)
        grads = dot_first(a_v[:, pl.ds(first_row, span)], dp_ref[...])
        for spot in range(SPOTS):
            for c in range(2):
                at = (spot * 2 + c) * own_rows
                grad = grads[at : at + own_rows, :]
                rows_at = pl.ds(pl.multiple_of(first_row + at, own_rows), own_rows)
                gain_grad = jnp.sum(grad * widen(in_v[rows_at, : 3 * mine]), axis=1, keepdims=True)
                riding = riding_v[rows_at, :]
                riding = jnp.where(lane == FIRST_GAIN, gain_grad / riding, riding).astype(bf)

                def put(place, grad=grad, riding=riding):
                    place[:, : 3 * mine] = grad.astype(bf)
                    place[:, 3 * mine :] = riding

                @pl.when(meta[1] == c)
                def _():
                    put(own_v.at[k, spot ^ meta[0]])

                @pl.when(meta[1] != c)
                def _():
                    put(other_v.at[k, spot ^ meta[0]])

        target = other if k == 1 else rest.at[(k - 2) % planes]
        for place, ref in ((own_v, own[k]), (other_v, target)):
            leaving.append(pltpu.make_async_copy(place.at[k], ref, done.at[len(leaving)]))
            leaving[-1].start()
    for copy in leaving:
        copy.wait()


def project_back(moves, totals, dots, gains, small, in_full, projected, dq, dk, dv, normed_all):
    rows, mine = dv.shape
    planes = moves.planes
    own_rows = D // (planes * PLANE)
    bf = jnp.bfloat16
    meta = jnp.concatenate([jnp.stack([moves.spot, moves.core_id]), moves.planes_back])
    pieces = (SPOTS, own_rows, 3 * mine + WIDE)
    inputs = (totals, dots, gains, *small, projected, dq, dk, dv)
    return pl.pallas_call(
        functools.partial(project_back_body, planes, own_rows),
        out_shape=[jax.ShapeDtypeStruct((rows, 3 * mine), bf)]
        + [jax.ShapeDtypeStruct(pieces, bf)] * (planes + 1)
        + [jax.ShapeDtypeStruct((planes - 1, *pieces), bf)],
        in_specs=[SCALARS] + [full_spec(*item.shape) for item in inputs] + [ANYWHERE] * 2,
        out_specs=[full_spec(rows, 3 * mine)] + [ANYWHERE] * (planes + 2),
        scratch_shapes=[
            pltpu.VMEM((rows, D), bf),
            pltpu.VMEM(in_full.shape, bf),
            pltpu.VMEM((planes, *pieces), bf),
            pltpu.VMEM((planes, *pieces), bf),
            pltpu.VMEM((D, WIDE), jnp.float32),
            pltpu.VMEM((32, D), jnp.float32),
            pltpu.SemaphoreType.DMA((2,)),
            pltpu.SemaphoreType.DMA((2 * planes,)),
        ],
        compiler_params=params(60),
        cost_estimate=cost(5 * 10**9, 30 << 20),
        name="project_back",
    )(meta.astype(jnp.int32), *inputs, normed_all, in_full)


def rows_back_body(dp_ref, in_w, *parts):
    value = dot_last(dp_ref[...], in_w[:, : dp_ref.shape[1]]).astype(jnp.bfloat16)
    put_by_block(pl.program_id(0), parts, value)


def rows_back(projected_grad, in_full):
    rows, columns = projected_grad.shape
    count = rows // SPOTS
    return pl.pallas_call(
        rows_back_body,
        grid=(SPOTS,),
        out_shape=[jax.ShapeDtypeStruct((count, D), jnp.bfloat16)] * SPOTS,
        in_specs=[block_spec(count, columns), full_spec(*in_full.shape)],
        out_specs=by_block(count, D),
        compiler_params=params(60),
        cost_estimate=cost(5 * 10**9, 12 << 20),
        name="rows_back",
    )(projected_grad, in_full)


def route_body(tokens, home, back, near, match, rank, small, residual_ref, rows_ref, probs_ref):
    bf = jnp.bfloat16
    residual = widen(tokens[...]) + (widen(home[...]) + widen(back[...]) + widen(near[...]))
    residual_ref[...] = residual
    root = lax.rsqrt(jnp.mean(residual * residual, axis=1, keepdims=True) + EPSILON)
    normed = (residual * root * small[FIRST_GAIN + 3 : FIRST_GAIN + 4, :]).astype(bf)
    rows_ref[:, :D] = normed
    experts = match.shape[1]
    logits = dot_last(normed, small[:experts, :].astype(bf))
    exponent = jnp.exp(logits - jnp.max(logits, axis=1, keepdims=True))
    probs = exponent / jnp.sum(exponent, axis=1, keepdims=True)
    chosen = probs * match[...]
    total = jnp.sum(chosen, axis=1, keepdims=True)
    gates = chosen / total
    upper = widen(gates.astype(bf))
    behind = 0.0
    for n, part in enumerate((rank[...], upper.astype(bf), (gates - upper).astype(bf))):
        places = lax.broadcasted_iota(jnp.int32, (experts, WIDE), 0) + n * experts == (
            lax.broadcasted_iota(jnp.int32, (experts, WIDE), 1)
        )
        behind += product(part, jnp.where(places, 1.0, 0.0).astype(bf))
    rows_ref[:, D:] = behind.astype(bf)
    probs_ref[0] = probs
    probs_ref[1] = gates
    probs_ref[2] = jnp.broadcast_to(total, probs.shape)


def route(tokens, home, back, near, match, rank, small):
    count, width = tokens.shape
    experts = match.shape[1]
    inputs = (tokens, home, back, near, match, rank, small)
    shape = jax.ShapeDtypeStruct
    return pl.pallas_call(
        route_body,
        out_shape=[
            shape((count, width), jnp.float32),
            shape((count, width + WIDE), jnp.bfloat16),
            shape((3, count, experts), jnp.float32),
        ],
        in_specs=[full_spec(*item.shape) for item in inputs],
        out_specs=[
            full_spec(count, width),
            full_spec(count, width + WIDE),
            full_spec(3, count, experts),
        ],
        compiler_params=params(60),
        cost_estimate=cost(10**8, 8 << 20),
        name="route",
    )(*inputs)


def route_back_body(total, home, back, near, match, probs_ref, small, residual, upstream, *results):
    grad_ref, branch_ref, router_ref, gain_ref = results
    bf = jnp.bfloat16
    rows = widen(total[...]) + (widen(home[...]) + widen(back[...]) + widen(near[...]))
    experts = match.shape[1]
    probs, gates, gate_total = probs_ref[0], probs_ref[1], probs_ref[2]
    pairs = lax.broadcasted_iota(jnp.int32, (WIDE, experts), 0) // 2 == (
        lax.broadcasted_iota(jnp.int32, (WIDE, experts), 1)
    )
    gate_grad = product(rows[:, D:].astype(bf), jnp.where(pairs, 1.0, 0.0).astype(bf))
    inner = jnp.sum(gate_grad * gates, axis=1, keepdims=True)
    chosen_grad = match[...] * (gate_grad - inner) / gate_total
    inner = jnp.sum(chosen_grad * probs, axis=1, keepdims=True)
    logit_grad = (probs * (chosen_grad - inner)).astype(bf)
    normed_grad = rows[:, :D] + product(logit_grad, small[:experts, :].astype(bf))
    gain = small[FIRST_GAIN + 3 : FIRST_GAIN + 4, :]
    value = residual[...]
    root = lax.rsqrt(jnp.mean(value * value, axis=1, keepdims=True) + EPSILON)
    normed = (value * root * gain).astype(bf)
    router_ref[...] = dot_first(logit_grad, normed)
    scaled = normed_grad * value
    gain_ref[...] = jnp.sum(scaled * root, axis=0, keepdims=True)
    inner = jnp.mean(scaled * gain, axis=1, keepdims=True)
    grad = widen(upstream[...]) + root * gain * normed_grad - value * (root * root * root * inner)
    grad_ref[...] = grad
    branch_ref[...] = grad.astype(bf)


def route_back(total, home, back, near, match, probs, small, residual, upstream):
    count, width = residual.shape
    experts = match.shape[1]
    inputs = (total, home, back, near, match, probs, small, residual, upstream)
    shape = jax.ShapeDtypeStruct
    return pl.pallas_call(
        route_back_body,
        out_shape=[
            shape((count, width), jnp.float32),
            shape((count, width), jnp.bfloat16),
            shape((experts, width), jnp.float32),
            shape((1, width), jnp.float32),
        ],
        in_specs=[full_spec(*item.shape) for item in inputs],
        out_specs=[
            full_spec(count, width),
            full_spec(count, width),
            full_spec(experts, width),
            full_spec(1, width),
        ],
        compiler_params=params(60),
        cost_estimate=cost(10**8, 10 << 20),
        name="route_back",
    )(*inputs)


def shards_dense(
    tokens,
    cotangent,
    norm_gains,
    attention_in,
    attention_out,
    router_weight,
    expert_in,
    expert_out,
    routes,
    lengths,
):
    row_count = tokens.shape[0]
    devices_count = lax.axis_size("fsdp")
    moves = Moves(devices_count)
    planes, core, spot = moves.planes, moves.core_id, moves.spot
    ring, first, second, cores = moves.ring, moves.first, moves.second, moves.core
    experts = devices_count // 2
    choose = routes.shape[1]
    capacity = 4 * row_count * choose // (3 * experts)
    bf, f32 = jnp.bfloat16, jnp.float32
    own_rows = attention_in.shape[0]
    lines = HEADS // SPOTS
    mine = lines * HEAD_DIM

    def low(value):
        return value.astype(bf)

    pieces = split_columns(spot, attention_in, router_weight, norm_gains, lengths)
    traded = [pieces[0]] + [send(pieces[m], moves.spots[m]) for m in range(1, SPOTS)]
    own_1 = send(cotangent, ring)
    tokens_then, traded, own_1 = tie(tokens, traded, own_1)

    in_own = [jnp.stack(traded)]
    in_own.append(send(in_own[0], ring))
    in_other = [send(in_own[0], cores)]
    near_x = send(tokens_then, first)
    near_0 = send(cotangent, first)
    in_own, in_other, near_x = tie(in_own, in_other, near_x)

    in_own.append(send(in_own[1], ring))
    in_other.append(send(in_own[1], cores))
    blocks_x = [tokens, near_x, send(tokens, second), send(near_x, second)]
    in_own, in_other, blocks_x, near_0 = tie(in_own, in_other, blocks_x, near_0)

    in_own.append(send(in_own[2], ring))
    in_other.append(send(in_own[2], cores))
    out_own = [attention_out, send(attention_out, ring)]
    out_other = [send(attention_out, cores)]
    grads = {(0, 0): [cotangent, near_0], (1, 0): [own_1, send(own_1, first)]}
    grads[0, 1] = [send(item, second) for item in grads[0, 0]]
    columns = 3 * mine
    lengths_all = jnp.stack([piece[: lengths.shape[1], columns + SMALL] for piece in traded])
    lengths_all = jnp.where(core == 0, lengths_all, lengths_all[jnp.asarray([0, 2, 1, 3])])
    places = jnp.arange(row_count, dtype=jnp.int32)
    _, position = jax.vmap(lambda item: layout(item, row_count))(lengths_all.astype(jnp.int32))
    starts = (places[None] - position).astype(f32)
    cos_half, sin_half = (table[:, 0] for table in tables(position.reshape(-1)))
    cos_all = jnp.concatenate([cos_half, cos_half], axis=1)
    sin_all = jnp.concatenate([-sin_half, sin_half], axis=1)

    expert_ids = jnp.arange(experts, dtype=jnp.int32)
    match = jnp.sum((routes[:, :, None] == expert_ids[None, None, :]).astype(f32), axis=1)
    before = (places[:, None] > places[None, :]).astype(bf)
    rank = jnp.where(match > 0, product(before, match.astype(bf)), -1.0).astype(bf)
    in_own, in_other, out_other, grads[1, 0], starts, cos_all, sin_all, rank = tie(
        in_own, in_other, out_other, grads[1, 0], starts, cos_all, sin_all, rank
    )

    in_other.append(send(in_own[3], cores))
    in_other, out_own, grads = tie(in_other, out_own, grads)
    out_own.append(send(out_own[1], ring))
    out_other.append(send(out_own[1], cores))
    own_2 = send(own_1, ring)
    grads[1, 1] = [send(item, second) for item in grads[1, 0]]
    projected, normed_all, in_full, sums, small_rows, gains = project(
        moves, blocks_x, in_own, in_other
    )
    sums, out_own, out_other, own_2, grads = tie(sums, out_own, out_other, own_2, grads)
    out_own.append(send(out_own[2], ring))
    out_other.append(send(out_own[2], cores))
    sums = plane_step(moves, by_spot(moves, sums), 1)
    sums, own_2 = tie(sums, own_2)
    own_3 = send(own_2, ring)
    totals = by_spot(moves, plane_step(moves, sums, 2))
    totals, out_own, out_other = tie(totals, out_own, out_other)
    out_other.append(send(out_own[3], cores))
    totals, out_other, own_2 = tie(totals, out_other, own_2)

    across_2 = send(own_2, second)
    weights = [expert_in[0], send(expert_in[0], cores), expert_out[0], send(expert_out[0], cores)]
    attention = (moves, totals, starts, gains, projected, cos_all, sin_all)
    results = attend_forward(*attention, out_own, out_other)
    heads, out_full, parts = results[:4], results[4], results[5:]
    parts, weights, own_3, across_2 = tie(parts, weights, own_3, across_2)

    def cross(parts):
        return [send(parts[2], second), send(parts[3], second)]

    def gather_near(parts, backs):
        near = low(widen(parts[1]) + widen(backs[1]))
        return widen(parts[0]) + widen(backs[0]), send(near, first)

    backs = cross(parts)
    near_2 = send(grads[1, 0][1], ring)
    backs, parts, near_2 = tie(backs, parts, near_2)
    near = send(low(widen(parts[1]) + widen(backs[1])), first)
    near_3 = send(near_2, ring)
    (near,) = tie(near)
    grads[2, 0] = [own_2, near_2]
    residual, rows, probs = route(tokens, parts[0], backs[0], near, match, rank, small_rows)
    rows, near_3 = tie(rows, near_3)

    meta = (moves.device // 2).reshape(1).astype(jnp.int32)
    saved, done = None, 0
    row_parts, out_parts = {}, {}

    def run_expert(group, which, blocks):
        nonlocal saved, done
        saved, outs, backs = expert_blocks(
            meta,
            blocks,
            grads[group, which],
            weights,
            saved,
            done,
            planes * SPOTS,
            capacity,
            experts,
        )
        done += len(blocks)
        out_parts.setdefault(group, []).extend(outs)
        row_parts.setdefault(group, []).extend(backs)

    row_near = send(rows, first)
    row_1 = send(rows, ring)
    rows, row_near = tie(rows, row_near)

    near_row_1 = send(row_near, ring)
    across = [send(rows, second), send(row_near, second)]
    run_expert(0, 0, [rows, row_near])
    saved, across, row_1 = tie(saved, across, row_1)

    row_2 = send(row_1, ring)
    across_row_1 = send(row_1, second)
    grads[2, 1] = [across_2, send(near_2, second)]
    grads[3, 0] = [own_3, near_3]
    run_expert(0, 1, across)
    saved, near_row_1, across_row_1 = tie(saved, near_row_1, across_row_1)

    near_row_2 = send(near_row_1, ring)
    across = [across_row_1, send(near_row_1, second)]
    across_3 = send(own_3, second)
    run_expert(1, 0, [row_1, near_row_1])
    saved, across, row_2, row_parts[0], grads[2, 1], near_3 = tie(
        saved, across, row_2, row_parts[0], grads[2, 1], near_3
    )

    row_3 = send(row_2, ring)
    across_row_2 = send(row_2, second)
    grads[3, 1] = [across_3, send(near_3, second)]
    run_expert(1, 1, across)
    saved, near_row_2, across_row_2, row_parts[0], grads[3, 1] = tie(
        saved, near_row_2, across_row_2, row_parts[0], grads[3, 1]
    )

    near_row_3 = send(near_row_2, ring)
    across = [across_row_2, send(near_row_2, second)]
    backs_0 = cross(row_parts[0])
    run_expert(2, 0, [row_2, near_row_2])
    saved, across, row_3, row_parts[1] = tie(saved, across, row_3, row_parts[1])

    across_row_3 = send(row_3, second)
    backs_1 = cross(row_parts[1])
    run_expert(2, 1, across)
    saved, near_row_3, across_row_3, backs_0 = tie(saved, near_row_3, across_row_3, backs_0)

    across = [across_row_3, send(near_row_3, second)]
    run_expert(3, 0, [row_3, near_row_3])
    saved, across, backs_1, row_parts[2] = tie(saved, across, backs_1, row_parts[2])

    pair = [send(low(widen(row_parts[1][n]) + widen(backs_1[n])), ring) for n in range(2)]
    backs_2 = cross(row_parts[2])
    run_expert(3, 1, across)
    saved, pair, backs_2 = tie(saved, pair, backs_2)

    near = send(low(widen(pair[1]) + widen(row_parts[2][1]) + widen(backs_2[1])), first)
    home = widen(pair[0]) + (widen(row_parts[2][0]) + widen(backs_2[0]))
    backs_3 = cross(row_parts[3])
    x_rows, dy_rows, m_own, m_other, du_own, du_other = saved
    in_theirs = dot_first(x_rows, du_other)
    home, near, backs_3, in_theirs = tie(home, near, backs_3, in_theirs)

    total = send(low(home + widen(near)), ring)
    home, near = gather_near(row_parts[3], backs_3)
    in_theirs = send(in_theirs, cores)
    out_theirs = dot_first(m_other, dy_rows)
    total, home, near, out_theirs = tie(total, home, near, out_theirs)

    total = send(low(widen(total) + (home + widen(near))), ring)
    _, near_0 = gather_near(row_parts[0], backs_0)
    out_theirs = send(out_theirs, cores)
    out_backs = {1: cross(out_parts[1])}
    total, near_0 = tie(total, near_0)
    residual_grad, branch_grad, router_grad, second_gain_grad = route_back(
        total, row_parts[0][0], backs_0[0], near_0, match, probs, small_rows, residual, cotangent
    )
    branch_near = send(branch_grad, first)
    branch_grad, branch_near, out_backs, out_parts = tie(
        branch_grad, branch_near, out_backs, out_parts
    )

    branch_blocks = [
        branch_grad,
        branch_near,
        send(branch_grad, second),
        send(branch_near, second),
    ]
    out_pair = [
        send(low(widen(out_parts[1][n]) + widen(out_backs[1][n])), ring) for n in range(2)
    ]
    expert_out_grad = dot_first(m_own, dy_rows) + out_theirs
    branch_blocks, expert_out_grad, out_parts = tie(branch_blocks, expert_out_grad, out_parts)

    out_backs[2] = cross(out_parts[2])
    dq, dk, dv, dots, own_grad, other_grad, gain_grads = attend_backward(
        *attention, heads, out_full, branch_blocks
    )
    dots, out_backs, out_parts, out_pair, other_grad = tie(
        dots, out_backs, out_parts, out_pair, other_grad
    )

    other_grad = send(other_grad, cores)
    out_pair = [
        send(low(widen(out_pair[n]) + widen(out_parts[2][n]) + widen(out_backs[2][n])), ring)
        for n in range(2)
    ]
    dots = plane_step(moves, by_spot(moves, dots), 1)
    dots = by_spot(moves, plane_step(moves, dots, 2))
    dots, other_grad, out_parts = tie(dots, other_grad, out_parts)
    out_sums = [widen(own_grad[k]) + widen(other_grad[k]) for k in range(planes)]
    out_backs[3] = cross(out_parts[3])
    small = (router_grad, small_rows, gain_grads, second_gain_grad)
    projected_grad, *in_grads = project_back(
        moves, totals, dots, gains, small, in_full, projected, dq, dk, dv, normed_all
    )
    in_grads, projected_grad, out_pair, out_backs, out_parts, out_sums = tie(
        in_grads, projected_grad, out_pair, out_backs, out_parts, out_sums
    )

    *in_grads, others, others_rest = in_grads
    others = send(others, cores)
    projected_grad, in_full, others, out_backs = tie(projected_grad, in_full, others, out_backs)
    in_total = send(low(widen(in_grads[1]) + widen(others)), ring)
    others_rest = send(others_rest, cores)
    out_near = send(
        low(widen(out_pair[1]) + widen(out_parts[3][1]) + widen(out_backs[3][1])), first
    )
    out_share = send(low(out_sums[1]), ring)
    parts = rows_back(projected_grad, in_full)
    in_total, others_rest, parts, out_near, x_rows, out_parts = tie(
        in_total, others_rest, parts, out_near, x_rows, out_parts
    )

    in_total = send(low(widen(in_total) + (widen(in_grads[2]) + widen(others_rest[0]))), ring)
    backs = cross(parts)
    out_total = low(
        widen(out_pair[0])
        + (widen(out_parts[3][0]) + widen(out_backs[3][0]))
        + widen(out_near)
    )
    expert_in_grad = dot_first(x_rows, du_own) + in_theirs
    in_total, backs, expert_in_grad, out_parts, out_total, out_share = tie(
        in_total, backs, expert_in_grad, out_parts, out_total, out_share
    )

    home, near = gather_near(parts, backs)
    in_total = send(low(widen(in_total) + (widen(in_grads[3]) + widen(others_rest[1]))), ring)
    out_backs[0] = cross(out_parts[0])
    out_share = send(low(widen(out_share) + out_sums[2]), ring)
    out_total = send(out_total, ring)
    in_total, home, near = tie(in_total, home, near)

    in_total = low(widen(in_total) + (widen(in_grads[0]) + widen(others_rest[2])))
    traded = [in_total[0]] + [send(in_total[m], moves.spots[m]) for m in range(1, SPOTS)]
    _, first_back = jax.vjp(
        lambda value: root_norm(value, small_rows[FIRST_GAIN]), widen(tokens)
    )
    (input_norm_grad,) = first_back(home + widen(near))
    input_grad = residual_grad + input_norm_grad
    traded, input_grad, out_backs, out_share, out_total = tie(
        traded, input_grad, out_backs, out_share, out_total
    )
    out_share = send(low(widen(out_share) + out_sums[3]), ring)

    out_home, out_near = gather_near(out_parts[0], out_backs[0])
    in_share, small_share = join_columns(spot, traded)
    out_share = widen(out_share) + out_sums[0]
    output = low(residual + (widen(out_total) + (out_home + widen(out_near))))
    return (
        output,
        input_grad,
        small_share[:, FIRST_GAIN:SMALL].T,
        in_share,
        out_share,
        small_share[:, :FIRST_GAIN],
        expert_in_grad[None],
        expert_out_grad[None],
    )


def shards(*arguments):
    routes = arguments[8]
    experts = lax.axis_size("fsdp") // 2
    if 2 * routes.shape[1] >= experts and HEADS == experts:
        return shards_dense(*arguments)
    return shards_routed(*arguments)


def solution(mesh):
    in_specs = (
        P("fsdp", None),
        P("fsdp", None),
        P(None, "fsdp"),
        P("fsdp", None),
        P("fsdp", None),
        P("fsdp", None),
        P("fsdp", None, None),
        P("fsdp", None, None),
        P("fsdp", None),
        P("fsdp", None),
    )
    out_specs = (
        P("fsdp", None),
        P("fsdp", None),
        P(None, "fsdp"),
        P("fsdp", None),
        P("fsdp", None),
        P("fsdp", None),
        P("fsdp", None, None),
        P("fsdp", None, None),
    )
    return jax.shard_map(shards, mesh=mesh, in_specs=in_specs, out_specs=out_specs, check_vma=False)
```

```python
import functools

import jax
import jax.numpy as jnp
from jax import lax
from jax.experimental import pallas as pl
from jax.experimental.pallas import tpu as pltpu
from jax.sharding import PartitionSpec as P

D = 2048
HEADS = 16
HEAD_DIM = 128


EPSILON = 1e-05
ROPE_BASE = 10000.0
MASKED = -1000000000.0


def root_norm(vector, scaling):
    return vector * lax.rsqrt(jnp.mean(vector * vector, axis=-1, keepdims=True) + EPSILON) * scaling


def rotary(vector, cos_table, sin_table):
    half_dim = vector.shape[-1] // 2
    first = vector[..., :half_dim]
    second = vector[..., half_dim:]
    return jnp.concatenate(
        [first * cos_table - second * sin_table, second * cos_table + first * sin_table], axis=-1
    )


def layout(lengths, number):
    ends_at = jnp.cumsum(lengths)
    places = jnp.arange(number, dtype=jnp.int32)
    segment = jnp.sum((places[:, None] >= ends_at[None, :]).astype(jnp.int32), axis=1)
    starts = ends_at - lengths
    select_mask = (
        segment[:, None] == jnp.arange(lengths.shape[0], dtype=jnp.int32)[None, :]
    ).astype(jnp.int32)
    position = places - jnp.sum(select_mask * starts[None, :], axis=1)
    return (segment, position)


def tables(position):
    half_dim = HEAD_DIM // 2
    inverse = ROPE_BASE ** (-2.0 * jnp.arange(half_dim, dtype=jnp.float32) / HEAD_DIM)
    angles = position.astype(jnp.float32)[:, None] * inverse[None, :]
    return (jnp.cos(angles)[:, None, :], jnp.sin(angles)[:, None, :])


def prepare(projected, query_gain, key_gain, cos_table, sin_table):
    count_rows = projected.shape[0]
    query_heads = root_norm(projected[:, :D], query_gain).reshape(count_rows, HEADS, HEAD_DIM)
    key_heads = root_norm(projected[:, D : 2 * D], key_gain).reshape(count_rows, HEADS, HEAD_DIM)
    value_heads = projected[:, 2 * D :].reshape(count_rows, HEADS, HEAD_DIM)
    return (
        rotary(query_heads, cos_table, sin_table),
        rotary(key_heads, cos_table, sin_table),
        value_heads,
    )


def softmax_rows(logits):
    row_max = jnp.max(logits, axis=-1, keepdims=True)
    exponent = jnp.exp(logits - row_max)
    return exponent / jnp.sum(exponent, axis=-1, keepdims=True)


def dot_first(left, right):
    return lax.dot_general(
        left, right, (((0,), (0,)), ((), ())), preferred_element_type=jnp.float32
    )


def dot_last(left, right):
    return lax.dot_general(
        left, right, (((1,), (1,)), ((), ())), preferred_element_type=jnp.float32
    )


def shards_routed(
    tokens,
    cotangent,
    norm_gains,
    attention_in,
    attention_out,
    router_weight,
    expert_in,
    expert_out,
    routes,
    lengths,
):
    row_count = tokens.shape[0]
    devices_count = lax.axis_size("fsdp")
    experts = devices_count // 2
    choose = routes.shape[1]
    half_units = expert_out.shape[1]
    capacity = 4 * row_count * choose // (3 * experts)
    scaling = HEAD_DIM ** (-0.5)
    gain_full, gathered_in, gathered_out, gathered_router = (
        lax.all_gather(norm_gains, "fsdp", axis=1, tiled=True),
        lax.all_gather(attention_in, "fsdp", axis=0, tiled=True),
        lax.all_gather(attention_out, "fsdp", axis=0, tiled=True),
        lax.all_gather(router_weight, "fsdp", axis=0, tiled=True),
    )
    gain_rows = gain_full.astype(jnp.float32)
    segment, position = layout(lengths[0], row_count)
    cos_table, sin_table = tables(position)
    places = jnp.arange(row_count, dtype=jnp.int32)
    allowed = ((segment[:, None] == segment[None, :]) & (places[:, None] >= places[None, :]))[None]
    inputs = tokens.astype(jnp.float32)
    normed_input = root_norm(inputs, gain_rows[0]).astype(jnp.bfloat16)
    projected = jnp.dot(normed_input, gathered_in, preferred_element_type=jnp.float32)

    def prepare_local(projected_value, query_gain, key_gain):
        return prepare(projected_value, query_gain, key_gain, cos_table, sin_table)

    (query_f, key_f, value_f), prepare_back = jax.vjp(
        prepare_local, projected, gain_rows[1], gain_rows[2]
    )
    query_heads = query_f.astype(jnp.bfloat16)
    key_heads = key_f.astype(jnp.bfloat16)
    value_heads = value_f.astype(jnp.bfloat16)

    def score_block():
        raw_scores = (
            jnp.einsum("qhd,khd->hqk", query_heads, key_heads, preferred_element_type=jnp.float32)
            * scaling
        )
        return jnp.where(allowed, raw_scores, MASKED)

    scores = score_block()
    row_max = jnp.max(scores, axis=-1, keepdims=True)
    exponent = jnp.exp(scores - row_max)
    row_sum = jnp.sum(exponent, axis=-1, keepdims=True)
    log_total = row_max + jnp.log(row_sum)
    attend_probs = (exponent / row_sum).astype(jnp.bfloat16)
    attended = (
        jnp.einsum("hqk,khd->qhd", attend_probs, value_heads, preferred_element_type=jnp.float32)
        .reshape(row_count, D)
        .astype(jnp.bfloat16)
    )
    branch_out = jnp.dot(attended, gathered_out, preferred_element_type=jnp.float32)
    residual = inputs + branch_out
    normed = root_norm(residual, gain_rows[3]).astype(jnp.bfloat16)
    logits = jnp.dot(normed, gathered_router, preferred_element_type=jnp.float32)
    router_probs = softmax_rows(logits)
    chosen = jnp.take_along_axis(router_probs, routes, axis=1)
    gate_total = jnp.sum(chosen, axis=1, keepdims=True)
    gate_values = chosen / gate_total
    flat_routes = routes.reshape(-1)
    route_hits = (flat_routes[:, None] == jnp.arange(experts, dtype=jnp.int32)[None, :]).astype(
        jnp.int32
    )
    slot_index = jnp.sum((jnp.cumsum(route_hits, axis=0) - route_hits) * route_hits, axis=1)
    target = flat_routes * capacity + slot_index
    owner_token = (
        jnp.zeros((experts * capacity,), jnp.int32)
        .at[target]
        .set(jnp.arange(row_count * choose, dtype=jnp.int32) // choose)
    )
    filled = (
        jnp.zeros((experts * capacity,), jnp.bfloat16)
        .at[target]
        .set(jnp.ones((row_count * choose,), jnp.bfloat16))
    )
    outgoing = jnp.repeat(
        (normed[owner_token] * filled[:, None]).reshape(experts, capacity, D), 2, axis=0
    )
    arrived = lax.all_to_all(outgoing, "fsdp", split_axis=0, concat_axis=0, tiled=True).reshape(
        devices_count * capacity, D
    )
    gate_up_out = jnp.dot(arrived, expert_in[0], preferred_element_type=jnp.float32)
    gate_part = gate_up_out[:, :half_units]
    up_part = gate_up_out[:, half_units:]
    hidden_f, swiglu_back = jax.vjp(
        lambda gate_in, up_in: jax.nn.silu(gate_in) * up_in, gate_part, up_part
    )
    hidden = hidden_f.astype(jnp.bfloat16)
    produced = (
        jnp.dot(hidden, expert_out[0], preferred_element_type=jnp.float32)
        .astype(jnp.bfloat16)
        .reshape(devices_count, capacity, D)
    )
    returned = (
        lax.all_to_all(produced, "fsdp", split_axis=0, concat_axis=0, tiled=True)
        .reshape(experts, 2, capacity, D)
        .astype(jnp.float32)
    )
    returned = jnp.sum(returned, axis=1).reshape(experts * capacity, D)
    picked = returned[target].reshape(row_count, choose, D)
    expert_sum = jnp.sum(gate_values[:, :, None] * picked, axis=1)
    output = (residual + expert_sum).astype(jnp.bfloat16)
    back_in, back_out, back_router = (
        lax.all_gather(attention_in, "fsdp", axis=0, tiled=True),
        lax.all_gather(attention_out, "fsdp", axis=0, tiled=True),
        lax.all_gather(router_weight, "fsdp", axis=0, tiled=True),
    )
    upstream = cotangent.astype(jnp.float32)
    gate_grad = jnp.sum(upstream[:, None, :] * picked, axis=2)
    send_grad = (
        (gate_values[:, :, None] * upstream[:, None, :])
        .astype(jnp.bfloat16)
        .reshape(row_count * choose, D)
    )
    grad_buffer = (
        jnp.zeros((experts * capacity, D), jnp.bfloat16)
        .at[target]
        .set(send_grad)
        .reshape(experts, capacity, D)
    )
    grad_buffer = jnp.repeat(grad_buffer, 2, axis=0)
    grad_arrived = lax.all_to_all(
        grad_buffer, "fsdp", split_axis=0, concat_axis=0, tiled=True
    ).reshape(devices_count * capacity, D)
    grad_hidden = dot_last(grad_arrived, expert_out[0])
    expert_out_grad = dot_first(hidden, grad_arrived)
    grad_gate, grad_up = swiglu_back(grad_hidden)
    grad_gate_up = jnp.concatenate([grad_gate, grad_up], axis=1).astype(jnp.bfloat16)
    expert_in_grad = dot_first(arrived, grad_gate_up)
    grad_rows = (
        dot_last(grad_gate_up, expert_in[0])
        .astype(jnp.bfloat16)
        .reshape(devices_count, capacity, D)
    )
    grad_back = (
        lax.all_to_all(grad_rows, "fsdp", split_axis=0, concat_axis=0, tiled=True)
        .reshape(experts, 2, capacity, D)
        .astype(jnp.float32)
    )
    grad_back = jnp.sum(grad_back, axis=1).reshape(experts * capacity, D)
    dispatch_grad = jnp.sum(grad_back[target].reshape(row_count, choose, D), axis=1)
    chosen_grad = (gate_grad - jnp.sum(gate_grad * gate_values, axis=1, keepdims=True)) / gate_total
    expert_match = (
        routes[:, :, None] == jnp.arange(experts, dtype=jnp.int32)[None, None, :]
    ).astype(jnp.float32)
    prob_grad = jnp.sum(expert_match * chosen_grad[:, :, None], axis=1)
    logit_grad = (
        router_probs * (prob_grad - jnp.sum(prob_grad * router_probs, axis=1, keepdims=True))
    ).astype(jnp.bfloat16)
    router_grad = dot_first(normed, logit_grad)
    normed_grad = dispatch_grad + dot_last(logit_grad, back_router)
    _, second_back = jax.vjp(root_norm, residual, gain_rows[3])
    residual_norm_grad, second_gain_grad = second_back(normed_grad)
    residual_grad = upstream + residual_norm_grad
    branch_grad = residual_grad.astype(jnp.bfloat16)
    out_grad = dot_first(attended, branch_grad)
    attended_grad = (
        dot_last(branch_grad, back_out).astype(jnp.bfloat16).reshape(row_count, HEADS, HEAD_DIM)
    )
    recomputed = jnp.exp(score_block() - log_total)
    value_grad = jnp.einsum(
        "hqk,qhd->khd", attend_probs, attended_grad, preferred_element_type=jnp.float32
    )
    attend_grad = jnp.einsum(
        "qhd,khd->hqk", attended_grad, value_heads, preferred_element_type=jnp.float32
    )
    row_delta = jnp.sum(recomputed * attend_grad, axis=-1, keepdims=True)
    score_grad = (recomputed * (attend_grad - row_delta)).astype(jnp.bfloat16)
    query_grad = (
        jnp.einsum("hqk,khd->qhd", score_grad, key_heads, preferred_element_type=jnp.float32)
        * scaling
    )
    key_grad = (
        jnp.einsum("hqk,qhd->khd", score_grad, query_heads, preferred_element_type=jnp.float32)
        * scaling
    )
    projected_grad, query_gain_grad, key_gain_grad = prepare_back(
        (query_grad, key_grad, value_grad)
    )
    projected_grad = projected_grad.astype(jnp.bfloat16)
    attention_in_grad = dot_first(normed_input, projected_grad)
    normed_input_grad = dot_last(projected_grad, back_in)
    _, first_back = jax.vjp(root_norm, inputs, gain_rows[0])
    input_norm_grad, first_gain_grad = first_back(normed_input_grad)
    input_grad = residual_grad + input_norm_grad
    gains_grad = jnp.stack([first_gain_grad, query_gain_grad, key_gain_grad, second_gain_grad])
    gains_share, in_share, out_share, router_share = (
        lax.psum_scatter(gains_grad, "fsdp", scatter_dimension=1, tiled=True),
        lax.psum_scatter(attention_in_grad, "fsdp", scatter_dimension=0, tiled=True),
        lax.psum_scatter(out_grad, "fsdp", scatter_dimension=0, tiled=True),
        lax.psum_scatter(router_grad, "fsdp", scatter_dimension=0, tiled=True),
    )
    return (
        output,
        input_grad,
        gains_share,
        in_share,
        out_share,
        router_share,
        expert_in_grad[None],
        expert_out_grad[None],
    )


def product(left, right):
    return jnp.dot(left, right, preferred_element_type=jnp.float32)


def widen(value):
    return value.astype(jnp.float32)


PLANE = 8
SPOTS = 4
WIDE = 128
SMALL = 20
FIRST_GAIN = SMALL - 4


class Moves:
    def __init__(self, count):
        planes = count // PLANE
        order = list(range(0, planes, 2)) + list(range(1, planes, 2))[::-1]
        after = {order[i]: order[(i + 1) % planes] for i in range(planes)}
        self.planes = planes
        self.ring = [(i, after[i // PLANE] * PLANE + i % PLANE) for i in range(count)]
        self.first = [(i, i ^ (4 if i & 1 else 2)) for i in range(count)]
        self.second = [(i, i ^ (2 if i & 1 else 4)) for i in range(count)]
        self.core = [(i, i ^ 1) for i in range(count)]
        self.spots = [[(i, i ^ (2 * mask)) for i in range(count)] for mask in range(SPOTS)]
        device = lax.axis_index("fsdp")
        self.device = device
        self.plane, self.spot, self.core_id = device // PLANE, device % PLANE // 2, device % 2
        rank = jnp.asarray([order.index(i) for i in range(planes)], jnp.int32)
        self.planes_back = jnp.asarray(order, jnp.int32)[
            (rank[self.plane] - jnp.arange(planes, dtype=jnp.int32)) % planes
        ]
        self.steps_from = (rank[self.plane] - rank) % planes
        self.group_spots = self.spot ^ jnp.where(
            self.core_id == 0, jnp.asarray([0, 1, 2, 3]), jnp.asarray([0, 2, 1, 3])
        )


def send(value, pairs):
    return lax.ppermute(value, "fsdp", pairs)


def tie(*values):
    return lax.optimization_barrier(values)


def by_spot(moves, parts):
    return jnp.where(moves.core_id == 0, parts, parts[:, jnp.asarray([0, 2, 1, 3])])


def plane_step(moves, parts, bit):
    other = send(parts, moves.spots[bit])
    return parts + jnp.stack([other[:, m ^ bit] for m in range(SPOTS)], axis=1)


def full_spec(*dims):
    return pl.BlockSpec(dims, lambda *_: (0,) * len(dims))


SCALARS = pl.BlockSpec(memory_space=pltpu.SMEM)
ANYWHERE = pl.BlockSpec(memory_space=pl.ANY)


def params(mebibytes):
    return pltpu.CompilerParams(vmem_limit_bytes=mebibytes << 20)


def cost(flops, moved, special=0):
    return pl.CostEstimate(flops=flops, bytes_accessed=moved, transcendentals=special)


def column_places(spot, mask, lines):
    for part in range(3):
        for line in range(lines):
            piece = (part * lines + line) * HEAD_DIM
            whole = ((part * lines + line) * SPOTS + (spot ^ mask)) * HEAD_DIM
            yield pl.ds(pl.multiple_of(whole, HEAD_DIM), HEAD_DIM), pl.ds(piece, HEAD_DIM)


def split_body(lines, spot, lengths, whole_ref, router_ref, gains_ref, *pieces):
    rows, columns = pieces[0].shape[0], pieces[0].shape[1] - WIDE
    routers = router_ref.shape[1]
    lane = lax.broadcasted_iota(jnp.int32, (rows, WIDE), 1)
    row = lax.broadcasted_iota(jnp.int32, (rows, WIDE), 0)
    spread = lax.broadcasted_iota(jnp.int32, (routers, WIDE), 0) == lax.broadcasted_iota(
        jnp.int32, (routers, WIDE), 1
    )
    riding = product(router_ref[...], jnp.where(spread, 1.0, 0.0).astype(jnp.bfloat16))
    for n in range(gains_ref.shape[0]):
        column = as_column(widen(gains_ref[...])[n : n + 1, :])
        riding = jnp.where(lane == FIRST_GAIN + n, column, riding)
    for n in range(lengths.shape[1]):
        riding = jnp.where((lane == SMALL) & (row == n), lengths[0, n].astype(jnp.float32), riding)
    for mask, piece in enumerate(pieces):
        for whole_at, piece_at in column_places(spot[0], mask, lines):
            piece[:, piece_at] = whole_ref[:, whole_at]
        piece[:, columns:] = riding.astype(jnp.bfloat16)


def split_columns(spot, whole, router, gains, lengths):
    rows, columns = whole.shape
    columns = columns // SPOTS + WIDE
    return pl.pallas_call(
        functools.partial(split_body, HEADS // SPOTS),
        out_shape=[jax.ShapeDtypeStruct((rows, columns), whole.dtype)] * SPOTS,
        in_specs=[
            SCALARS,
            SCALARS,
            full_spec(*whole.shape),
            full_spec(*router.shape),
            full_spec(*gains.shape),
        ],
        out_specs=[full_spec(rows, columns)] * SPOTS,
        compiler_params=params(60),
        name="split_columns",
    )(spot.reshape(1), lengths, whole, router, gains)


def join_body(lines, meta, *refs):
    *pieces, weights, gains, whole_ref, small_ref = refs
    for mask, piece in enumerate(pieces):
        for whole_at, piece_at in column_places(meta[0], mask, lines):
            whole_ref[:, whole_at] = widen(piece[:, piece_at])
    small = sum(widen(piece[:, piece.shape[1] - WIDE :]) for piece in pieces)
    lane = lax.broadcasted_iota(jnp.int32, small.shape, 1)
    gain = as_column(widen(gains[...])[0:1, :])
    gain_grad = jnp.sum(whole_ref[...] * widen(weights[...]), axis=1, keepdims=True)
    small_ref[...] = jnp.where(lane == FIRST_GAIN, gain_grad / gain, small)


def join_columns(spot, pieces, weights, gains):
    rows, wide = pieces[0].shape
    columns = wide - WIDE
    return pl.pallas_call(
        functools.partial(join_body, HEADS // SPOTS),
        out_shape=[
            jax.ShapeDtypeStruct((rows, columns * SPOTS), jnp.float32),
            jax.ShapeDtypeStruct((rows, WIDE), jnp.float32),
        ],
        in_specs=[SCALARS] + [full_spec(rows, wide)] * SPOTS
        + [full_spec(*weights.shape), full_spec(*gains.shape)],
        out_specs=[full_spec(rows, columns * SPOTS), full_spec(rows, WIDE)],
        compiler_params=params(60),
        name="join_columns",
    )(spot.reshape(1), *pieces, weights, gains)


def expert_body(index, cap, experts, blocks, meta, *refs):
    row_refs, grad_refs, weights = refs[:blocks], refs[blocks : 2 * blocks], refs[2 * blocks :][:4]
    refs = refs[2 * blocks + 4 + 6 :]
    saves, out_parts, row_parts = refs[:6], refs[6 : 6 + blocks], refs[6 + blocks :][:blocks]
    rows_v, grads_v, in_v, out_v, x_v, dy_v, m_v, du_v, part_v, back_v, sem, done = refs[
        6 + 2 * blocks :
    ]
    bf, f32 = jnp.bfloat16, jnp.float32
    count, width, half = rows_v.shape[1], grads_v.shape[2], out_v.shape[1]
    expert = meta[0]

    def fetch(ref, place, n):
        copy = pltpu.make_async_copy(ref, place, sem.at[n])
        copy.start()
        return copy

    fetch_rows = [fetch(ref, rows_v.at[j], j) for j, ref in enumerate(row_refs)]
    fetch_in = [fetch(weights[h], in_v.at[h], blocks + h) for h in range(2)]
    fetch_out = [fetch(weights[2 + h], out_v.at[h], blocks + 2 + h) for h in range(2)]
    fetch_grads = [fetch(ref, grads_v.at[j], blocks + 4 + j) for j, ref in enumerate(grad_refs)]
    leaving = []

    def leave(place, ref):
        leaving.append(pltpu.make_async_copy(place, ref, done.at[len(leaving)]))
        leaving[-1].start()

    def save(place, n):
        leave(place, saves[n].at[pl.ds(index * cap, blocks * cap)])

    lane8 = lax.broadcasted_iota(jnp.int32, (8, WIDE), 1)
    row8 = lax.broadcasted_iota(jnp.int32, (8, WIDE), 0)
    picker = (
        jnp.where((row8 == 0) & (lane8 == expert), 1.0, 0.0)
        + jnp.where((row8 == 1) & (lane8 == experts + expert), 1.0, 0.0)
        + jnp.where((row8 == 1) & (lane8 == 2 * experts + expert), 1.0, 0.0)
    ).astype(bf)
    lanes = lax.broadcasted_iota(jnp.int32, (count, WIDE), 1)
    slots_down = lax.broadcasted_iota(jnp.int32, (cap, count), 0)
    slots_along = lax.broadcasted_iota(jnp.int32, (count, cap), 1)
    gather, scatter, gates = [], [], []
    slots = [slice(j * cap, (j + 1) * cap) for j in range(blocks)]
    for j in range(blocks):
        fetch_rows[j].wait()
        extra = rows_v[j, :, width:]
        info = dot_last(picker, extra)
        chosen = slots_down == info[0:1].astype(jnp.int32)
        gates.append(jnp.sum(jnp.where(chosen, info[1:2], 0.0), axis=1, keepdims=True))
        gather.append(jnp.where(chosen, 1.0, 0.0).astype(bf))
        slot = jnp.sum(
            jnp.where(lanes == expert, widen(extra), 0.0), axis=1, keepdims=True
        ).astype(jnp.int32)
        scatter.append(jnp.where(slots_along == slot, 1.0, 0.0).astype(bf))
        x_v[slots[j], :] = product(gather[j], rows_v[j, :, :width]).astype(bf)
    gate = jnp.concatenate(gates, axis=0)
    save(x_v, 0)
    x = x_v[...]
    inner = []
    for h in range(2):
        fetch_in[h].wait()
        u = product(x, in_v[h])
        gate_part, up_part = u[:, :half], u[:, half:]
        sigmoid = 1.0 / (1.0 + jnp.exp(-gate_part))
        silu = gate_part * sigmoid
        inner.append((gate_part, up_part, sigmoid, silu))
        m_v[h] = (silu * up_part).astype(bf)
        save(m_v.at[h], 2 + h)
    for copy in fetch_out:
        copy.wait()
    y = product(m_v[0], out_v[0]) + product(m_v[1], out_v[1])
    for copy in fetch_grads:
        copy.wait()
    g = jnp.concatenate([product(gather[j], grads_v[j]) for j in range(blocks)], axis=0)
    dgate = jnp.sum(g * y, axis=1, keepdims=True)
    z = (gate * y).astype(bf)
    dy_v[...] = (gate * g).astype(bf)
    save(dy_v, 1)
    for j in range(blocks):
        part_v[j] = product(scatter[j], z[slots[j]]).astype(bf)
        leave(part_v.at[j], out_parts[j])
    dy = dy_v[...]
    for h in range(2):
        gate_part, up_part, sigmoid, silu = inner[h]
        dm = dot_last(dy, out_v[h])
        slope = sigmoid * (1.0 + gate_part * (1.0 - sigmoid))
        du_v[h, :, :half] = (dm * up_part * slope).astype(bf)
        du_v[h, :, half:] = (dm * silu).astype(bf)
        save(du_v.at[h], 4 + h)
    drows = (dot_last(du_v[0], in_v[0]) + dot_last(du_v[1], in_v[1])).astype(bf)
    upper = widen(dgate.astype(bf))
    lane_m = lax.broadcasted_iota(jnp.int32, (blocks * cap, WIDE), 1)
    pair = jnp.where(
        lane_m == 2 * expert, upper, jnp.where(lane_m == 2 * expert + 1, dgate - upper, 0.0)
    ).astype(bf)
    for j in range(blocks):
        back_v[j, :, :width] = product(scatter[j], drows[slots[j]]).astype(bf)
        back_v[j, :, width:] = product(scatter[j], pair[slots[j]]).astype(bf)
        leave(back_v.at[j], row_parts[j])
    for copy in leaving:
        copy.wait()


def expert_blocks(meta, rows, grads, weights, saved, index, total, cap, experts):
    blocks = len(rows)
    count, wide = rows[0].shape
    width, half = grads[0].shape[1], weights[2].shape[0]
    bf = jnp.bfloat16
    used = blocks * cap

    def shape(*dims):
        return jax.ShapeDtypeStruct(dims, bf)

    aliases = {2 * blocks + 5 + t: t for t in range(6)}
    if saved is None:
        saved, aliases = [jnp.zeros((16, WIDE), bf)] * 6, {}
    save_columns = (width, width, half, half, 2 * half, 2 * half)
    results = pl.pallas_call(
        functools.partial(expert_body, index, cap, experts, blocks),
        out_shape=[shape(total * cap, columns) for columns in save_columns]
        + [shape(count, width)] * blocks
        + [shape(count, wide)] * blocks,
        in_specs=[SCALARS] + [ANYWHERE] * (2 * blocks + 10),
        out_specs=[ANYWHERE] * (6 + 2 * blocks),
        scratch_shapes=[
            pltpu.VMEM((blocks, count, wide), bf),
            pltpu.VMEM((blocks, count, width), bf),
            pltpu.VMEM((2, width, 2 * half), bf),
            pltpu.VMEM((2, half, width), bf),
            pltpu.VMEM((used, width), bf),
            pltpu.VMEM((used, width), bf),
            pltpu.VMEM((2, used, half), bf),
            pltpu.VMEM((2, used, 2 * half), bf),
            pltpu.VMEM((blocks, count, width), bf),
            pltpu.VMEM((blocks, count, wide), bf),
            pltpu.SemaphoreType.DMA((2 * blocks + 4,)),
            pltpu.SemaphoreType.DMA((6 + 2 * blocks,)),
        ],
        input_output_aliases=aliases,
        compiler_params=params(60),
        cost_estimate=cost(blocks * 38 * 10**8, 30 << 20, 2 * used * half),
        name="expert_blocks",
    )(meta, *rows, *grads, *weights, *saved)
    return results[:6], results[6 : 6 + blocks], results[6 + blocks :]


def eye(count):
    return lax.broadcasted_iota(jnp.int32, (count, count), 0) == lax.broadcasted_iota(
        jnp.int32, (count, count), 1
    )


def as_column(row):
    return jnp.sum(jnp.where(eye(row.shape[1]), row, 0.0), axis=1, keepdims=True)


def as_row(column):
    return jnp.sum(jnp.where(eye(column.shape[0]), column, 0.0), axis=0, keepdims=True)


def rolled(value):
    return pltpu.roll(value, HEAD_DIM // 2, 1)


def root_of(total):
    return lax.rsqrt(total / D + EPSILON)


def weights_of(query, key, start):
    count = query.shape[0]
    rows = lax.broadcasted_iota(jnp.int32, (count, count), 0)
    columns = lax.broadcasted_iota(jnp.int32, (count, count), 1)
    allowed = (columns <= rows) & (columns >= start.astype(jnp.int32))
    scores = jnp.where(allowed, dot_last(query, key) * HEAD_DIM ** (-0.5), MASKED)
    exponent = jnp.exp(scores - jnp.max(scores, axis=1, keepdims=True))
    return exponent / jnp.sum(exponent, axis=1, keepdims=True)


def spans(mine):
    return [slice(h, h + HEAD_DIM) for h in range(0, mine, HEAD_DIM)]


def project_body(planes, own_rows, meta, *refs):
    blocks, own, other = refs[:SPOTS], refs[SPOTS : SPOTS + planes], refs[SPOTS + planes :][:planes]
    proj_ref, a_ref, in_ref, sums_ref, small_ref, gains_ref = refs[SPOTS + 2 * planes :][:6]
    x_v, a_v, in_v, proj_v, sem, in_sem, done = refs[SPOTS + 2 * planes + 6 :]
    spot, core = meta[0], meta[1]
    count = x_v.shape[1]
    mine = proj_v.shape[1] // 3
    fetch_x = [pltpu.make_async_copy(ref, x_v.at[j], sem.at[j]) for j, ref in enumerate(blocks)]
    for copy in fetch_x:
        copy.start()
    fetch_in = []
    for k in range(planes):
        for mask in range(SPOTS):
            chunk = meta[2 + k] * PLANE + (spot ^ mask) * 2
            for n, (refs_k, c) in enumerate(((own, core), (other, 1 - core))):
                at = pl.multiple_of((chunk + c) * own_rows, own_rows)
                fetch_in.append(
                    pltpu.make_async_copy(
                        refs_k[k].at[mask],
                        in_v.at[pl.ds(at, own_rows)],
                        in_sem.at[(k * SPOTS + mask) * 2 + n],
                    )
                )
                fetch_in[-1].start()
    roots = []
    for j in range(SPOTS):
        fetch_x[j].wait()
        x = widen(x_v[j])
        roots.append(lax.rsqrt(jnp.mean(x * x, axis=1, keepdims=True) + EPSILON))
    for copy in fetch_in:
        copy.wait()
    leaving = [pltpu.make_async_copy(in_v, in_ref, done.at[0])]
    leaving[0].start()
    turn_by = lax.broadcasted_iota(jnp.int32, (small_ref.shape[0], WIDE), 0) == (
        lax.broadcasted_iota(jnp.int32, (small_ref.shape[0], WIDE), 1)
    )
    small = dot_last(jnp.where(turn_by, 1.0, 0.0).astype(jnp.bfloat16), in_v[:, 3 * mine :])
    small_ref[...] = small
    for line in range(mine // HEAD_DIM):
        at = pl.multiple_of((line * SPOTS + spot) * HEAD_DIM, HEAD_DIM)
        for n in range(2):
            gains_ref[n : n + 1, line * HEAD_DIM : (line + 1) * HEAD_DIM] = small_ref[
                FIRST_GAIN + 1 + n : FIRST_GAIN + 2 + n, pl.ds(at, HEAD_DIM)
            ]
    gain = small[FIRST_GAIN : FIRST_GAIN + 1, :]
    for j in range(SPOTS):
        a_v[j * count : (j + 1) * count, :] = (widen(x_v[j]) * roots[j] * gain).astype(jnp.bfloat16)
    leaving.append(pltpu.make_async_copy(a_v, a_ref, done.at[1]))
    leaving[1].start()
    for n in range(3):
        part = slice(n * mine, (n + 1) * mine)
        value = product(a_v[...], in_v[:, part])
        proj_v[:, part] = value
        leaving.append(
            pltpu.make_async_copy(proj_v.at[:, part], proj_ref.at[:, part], done.at[2 + n])
        )
        leaving[-1].start()
        if n < 2:
            squares = jnp.sum(value * value, axis=1, keepdims=True)
            for j in range(SPOTS):
                sums_ref[n, j : j + 1, :] = as_row(squares[j * count : (j + 1) * count])
    for copy in leaving:
        copy.wait()


def project(moves, blocks, own, other):
    planes, own_rows, wide = len(own), own[0].shape[1], own[0].shape[2]
    width = wide - WIDE
    count, depth = blocks[0].shape
    bf, f32 = jnp.bfloat16, jnp.float32
    rows = SPOTS * count
    meta = jnp.concatenate([jnp.stack([moves.spot, moves.core_id]), moves.planes_back])
    shape = jax.ShapeDtypeStruct
    return pl.pallas_call(
        functools.partial(project_body, planes, own_rows),
        out_shape=[
            shape((rows, width), f32),
            shape((rows, depth), bf),
            shape((depth, wide), bf),
            shape((2, SPOTS, count), f32),
            shape((32, depth), f32),
            shape((2, width // 3), f32),
        ],
        in_specs=[SCALARS] + [ANYWHERE] * (SPOTS + 2 * planes),
        out_specs=[ANYWHERE] * 3
        + [full_spec(2, SPOTS, count), full_spec(32, depth), full_spec(2, width // 3)],
        scratch_shapes=[
            pltpu.VMEM((SPOTS, count, depth), bf),
            pltpu.VMEM((rows, depth), bf),
            pltpu.VMEM((depth, wide), bf),
            pltpu.VMEM((rows, width), f32),
            pltpu.SemaphoreType.DMA((SPOTS,)),
            pltpu.SemaphoreType.DMA((2 * SPOTS * planes,)),
            pltpu.SemaphoreType.DMA((5,)),
        ],
        compiler_params=params(60),
        cost_estimate=cost(5 * 10**9, 20 << 20),
        name="project",
    )(meta.astype(jnp.int32), *blocks, *own, *other)


def by_block(count, width):
    return [pl.BlockSpec((count, width), lambda i: (0, 0))] * SPOTS


def put_by_block(step, refs, value):
    for n, ref in enumerate(refs):

        @pl.when(step == n)
        def _(ref=ref):
            ref[...] = value


def forward_body(planes, own_rows, meta, totals, starts, gains, proj_ref, cos_ref, sin_ref, *refs):
    own, other = refs[:planes], refs[planes : 2 * planes]
    q_ref, k_ref, v_ref, o_ref, out_w, *parts = refs[2 * planes :][: 5 + SPOTS]
    sem = refs[-1]
    step = pl.program_id(0)
    bf = jnp.bfloat16
    mine = q_ref.shape[1]
    fetches = []
    for k in range(planes):
        for n, (refs_k, c) in enumerate(((own, meta[1]), (other, 1 - meta[1]))):
            at = pl.multiple_of((meta[2 + k] * 2 + c) * own_rows, own_rows)
            fetches.append(
                pltpu.make_async_copy(
                    refs_k[k], out_w.at[pl.ds(at, own_rows)], sem.at[2 * k + n]
                )
            )

    @pl.when(step == 0)
    def _():
        for copy in fetches:
            copy.start()

    query_root = root_of(as_column(totals[0, pl.ds(step, 1), :]))
    key_root = root_of(as_column(totals[1, pl.ds(step, 1), :]))
    start = as_column(starts[pl.ds(step, 1), :])
    cos, sin = cos_ref[...], sin_ref[...]
    for own_span in spans(mine):
        at = own_span.start
        query = proj_ref[:, at : at + HEAD_DIM] * query_root * gains[0:1, own_span]
        key = proj_ref[:, mine + at : mine + at + HEAD_DIM] * key_root * gains[1:2, own_span]
        value = proj_ref[:, 2 * mine + at : 2 * mine + at + HEAD_DIM].astype(bf)
        query = (query * cos + rolled(query) * sin).astype(bf)
        key = (key * cos + rolled(key) * sin).astype(bf)
        weights = weights_of(query, key, start).astype(bf)
        q_ref[:, own_span] = query
        k_ref[:, own_span] = key
        v_ref[:, own_span] = value
        o_ref[:, own_span] = product(weights, value).astype(bf)

    @pl.when(step == 0)
    def _():
        for copy in fetches:
            copy.wait()

    put_by_block(step, parts, product(o_ref[...], out_w[...]).astype(bf))


def block_spec(count, columns):
    return pl.BlockSpec((count, columns), lambda i: (i, 0))


def attend_forward(moves, totals, starts, gains, projected, cos_all, sin_all, own, other):
    planes, own_rows = len(own), own[0].shape[0]
    rows, mine = projected.shape[0], gains.shape[1]
    count = rows // SPOTS
    bf = jnp.bfloat16
    meta = jnp.concatenate([jnp.stack([moves.spot, moves.core_id]), moves.planes_back])
    return pl.pallas_call(
        functools.partial(forward_body, planes, own_rows),
        grid=(SPOTS,),
        out_shape=[jax.ShapeDtypeStruct((rows, mine), bf)] * 4
        + [jax.ShapeDtypeStruct((mine, D), bf)]
        + [jax.ShapeDtypeStruct((count, D), bf)] * SPOTS,
        in_specs=[
            SCALARS,
            full_spec(*totals.shape),
            full_spec(*starts.shape),
            full_spec(*gains.shape),
            block_spec(count, 3 * mine),
            block_spec(count, HEAD_DIM),
            block_spec(count, HEAD_DIM),
        ]
        + [ANYWHERE] * (2 * planes),
        out_specs=[block_spec(count, mine)] * 4 + [full_spec(mine, D)] + by_block(count, D),
        scratch_shapes=[pltpu.SemaphoreType.DMA((2 * planes,))],
        compiler_params=params(40),
        cost_estimate=cost(5 * 10**9, 20 << 20),
        name="attend_forward",
    )(meta.astype(jnp.int32), totals, starts, gains, projected, cos_all, sin_all, *own, *other)


def backward_body(
    meta, totals, starts, gains, proj_ref, cos_ref, sin_ref, q_ref, k_ref, v_ref, o_ref, out_w, *refs
):
    blocks = refs[:SPOTS]
    dq_ref, dk_ref, dv_ref, sums_ref, own_grad, other_grad, gain_grad = refs[SPOTS : SPOTS + 7]
    grads_v, o_v, total_v, sem = refs[SPOTS + 7 :]
    step = pl.program_id(0)
    bf = jnp.bfloat16
    mine = q_ref.shape[1]

    @pl.when(step == 0)
    def _():
        for n in range(SPOTS):
            pltpu.make_async_copy(blocks[n], grads_v.at[n], sem.at[n]).start()
        gain_grad[...] = jnp.zeros_like(gain_grad)

    pltpu.make_async_copy(blocks[0], grads_v.at[step], sem.at[step]).wait()
    grads = grads_v[step]
    count = grads.shape[0]
    o_v[pl.ds(pl.multiple_of(step * count, 64), count), :] = o_ref[...]
    do = dot_last(grads, out_w[...]).astype(bf)
    roots = [root_of(as_column(totals[n, pl.ds(step, 1), :])) for n in range(2)]
    start = as_column(starts[pl.ds(step, 1), :])
    cos, sin = cos_ref[...], sin_ref[...]
    sums = [0.0, 0.0]
    for own in spans(mine):
        query, key, value = q_ref[:, own], k_ref[:, own], v_ref[:, own]
        weights = weights_of(query, key, start)
        dv_ref[:, own] = dot_first(weights.astype(bf), do[:, own]).astype(bf)
        dweights = dot_last(do[:, own], value)
        inner = jnp.sum(weights * dweights, axis=1, keepdims=True)
        dscores = (weights * (dweights - inner)).astype(bf)
        for n, (grad, ref) in enumerate(
            ((product(dscores, key), dq_ref), (dot_first(dscores, query), dk_ref))
        ):
            grad = grad * HEAD_DIM ** (-0.5)
            grad = grad * cos - rolled(grad) * sin
            ref[:, own] = grad
            at = n * mine + own.start
            raw = grad * proj_ref[:, at : at + HEAD_DIM]
            sums[n] += jnp.sum(raw * gains[n : n + 1, own], axis=1, keepdims=True)
            line = pl.multiple_of((own.start // HEAD_DIM * SPOTS + meta[0]) * HEAD_DIM, HEAD_DIM)
            gain_grad[n : n + 1, pl.ds(line, HEAD_DIM)] += jnp.sum(
                raw * roots[n], axis=0, keepdims=True
            )
    for n in range(2):
        sums_ref[n, pl.ds(step, 1), :] = as_row(sums[n])

    @pl.when(step == SPOTS - 1)
    def _():
        planes, own_rows = own_grad.shape[:2]
        total = sum(
            dot_first(o_v[j * count : (j + 1) * count, :], grads_v[j]) for j in range(SPOTS)
        )
        total_v[...] = total.astype(bf)
        for k in range(planes):
            for ref, c in ((own_grad, meta[1]), (other_grad, 1 - meta[1])):
                at = pl.multiple_of((meta[2 + k] * 2 + c) * own_rows, own_rows)
                ref[k] = total_v[pl.ds(at, own_rows), :]


def attend_backward(
    moves, totals, starts, gains, projected, cos_all, sin_all, heads, out_full, blocks
):
    rows, mine = projected.shape[0], gains.shape[1]
    count = rows // SPOTS
    planes = moves.planes
    own_rows = mine // (2 * planes)
    bf, f32 = jnp.bfloat16, jnp.float32
    meta = jnp.concatenate([jnp.stack([moves.spot, moves.core_id]), moves.planes_back])
    shape = jax.ShapeDtypeStruct
    return pl.pallas_call(
        backward_body,
        grid=(SPOTS,),
        out_shape=[
            shape((rows, mine), f32),
            shape((rows, mine), f32),
            shape((rows, mine), bf),
            shape((2, SPOTS, count), f32),
            shape((planes, own_rows, D), bf),
            shape((planes, own_rows, D), bf),
            shape((2, D), f32),
        ],
        in_specs=[
            SCALARS,
            full_spec(*totals.shape),
            full_spec(*starts.shape),
            full_spec(*gains.shape),
            block_spec(count, 3 * mine),
            block_spec(count, HEAD_DIM),
            block_spec(count, HEAD_DIM),
        ]
        + [block_spec(count, mine)] * 4
        + [full_spec(*out_full.shape)]
        + [ANYWHERE] * SPOTS,
        out_specs=[block_spec(count, mine)] * 3
        + [full_spec(2, SPOTS, count)]
        + [full_spec(planes, own_rows, D)] * 2
        + [full_spec(2, D)],
        scratch_shapes=[
            pltpu.VMEM((SPOTS, count, D), bf),
            pltpu.VMEM((rows, mine), bf),
            pltpu.VMEM((mine, D), bf),
            pltpu.SemaphoreType.DMA((SPOTS,)),
        ],
        compiler_params=params(48),
        cost_estimate=cost(7 * 10**9, 25 << 20),
        name="attend_backward",
    )(
        meta.astype(jnp.int32),
        totals,
        starts,
        gains,
        projected,
        cos_all,
        sin_all,
        *heads,
        out_full,
        *blocks,
    )


def project_back_body(
    planes,
    own_rows,
    meta,
    totals,
    dots,
    gains,
    router_grad,
    small_rows,
    gain_grads,
    second_grad,
    proj_ref,
    dq_ref,
    dk_ref,
    dv_ref,
    a_ref,
    *refs,
):
    dp_ref, own, other, rest = refs[0], refs[1 : 1 + planes], refs[1 + planes], refs[2 + planes]
    a_v, own_v, other_v, riding_v, small, sem, done = refs[3 + planes :]
    bf = jnp.bfloat16
    rows, mine = dv_ref.shape
    count = rows // SPOTS
    fetch = pltpu.make_async_copy(a_ref, a_v, sem.at[0])
    fetch.start()
    for n, ref in enumerate((dq_ref, dk_ref)):
        columns = slice(n * mine, (n + 1) * mine)
        for j in range(SPOTS):
            block = slice(j * count, (j + 1) * count)
            root = root_of(as_column(totals[n, j : j + 1, :]))
            inner = as_column(dots[n, j : j + 1, :])
            grad = root * gains[n : n + 1, :] * ref[block, :]
            grad = grad - proj_ref[block, columns] * (root * root * root * inner / D)
            dp_ref[block, columns] = grad.astype(bf)
    dp_ref[:, 2 * mine :] = dv_ref[...]
    small[...] = jnp.zeros_like(small)
    small[:FIRST_GAIN, :] = router_grad[...]
    small[FIRST_GAIN : FIRST_GAIN + 1, :] = small_rows[FIRST_GAIN : FIRST_GAIN + 1, :]
    small[FIRST_GAIN + 1 : FIRST_GAIN + 3, :] = gain_grads[...]
    small[FIRST_GAIN + 3 : SMALL, :] = second_grad[...]
    turn_by = lax.broadcasted_iota(jnp.int32, (small.shape[0], WIDE), 0) == (
        lax.broadcasted_iota(jnp.int32, (small.shape[0], WIDE), 1)
    )
    riding_v[...] = dot_first(small[...].astype(bf), jnp.where(turn_by, 1.0, 0.0).astype(bf))
    fetch.wait()
    leaving = []
    span = PLANE * own_rows
    for k in [*range(1, planes), 0]:
        plane = meta[2 + k]
        first_row = pl.multiple_of(plane * span, span)
        grads = dot_first(a_v[:, pl.ds(first_row, span)], dp_ref[...])
        for spot in range(SPOTS):
            for c in range(2):
                at = (spot * 2 + c) * own_rows
                grad = grads[at : at + own_rows, :]
                rows_at = pl.ds(pl.multiple_of(first_row + at, own_rows), own_rows)
                riding = riding_v[rows_at, :].astype(bf)

                def put(place, grad=grad, riding=riding):
                    place[:, : 3 * mine] = grad.astype(bf)
                    place[:, 3 * mine :] = riding

                @pl.when(meta[1] == c)
                def _():
                    put(own_v.at[k, spot ^ meta[0]])

                @pl.when(meta[1] != c)
                def _():
                    put(other_v.at[k, spot ^ meta[0]])

        target = other if k == 1 else rest.at[(k - 2) % planes]
        for place, ref in ((own_v, own[k]), (other_v, target)):
            leaving.append(pltpu.make_async_copy(place.at[k], ref, done.at[len(leaving)]))
            leaving[-1].start()
    for copy in leaving:
        copy.wait()


def project_back(moves, totals, dots, gains, small, projected, dq, dk, dv, normed_all):
    rows, mine = dv.shape
    planes = moves.planes
    own_rows = D // (planes * PLANE)
    bf = jnp.bfloat16
    meta = jnp.concatenate([jnp.stack([moves.spot, moves.core_id]), moves.planes_back])
    pieces = (SPOTS, own_rows, 3 * mine + WIDE)
    inputs = (totals, dots, gains, *small, projected, dq, dk, dv)
    return pl.pallas_call(
        functools.partial(project_back_body, planes, own_rows),
        out_shape=[jax.ShapeDtypeStruct((rows, 3 * mine), bf)]
        + [jax.ShapeDtypeStruct(pieces, bf)] * (planes + 1)
        + [jax.ShapeDtypeStruct((planes - 1, *pieces), bf)],
        in_specs=[SCALARS] + [full_spec(*item.shape) for item in inputs] + [ANYWHERE],
        out_specs=[full_spec(rows, 3 * mine)] + [ANYWHERE] * (planes + 2),
        scratch_shapes=[
            pltpu.VMEM((rows, D), bf),
            pltpu.VMEM((planes, *pieces), bf),
            pltpu.VMEM((planes, *pieces), bf),
            pltpu.VMEM((D, WIDE), jnp.float32),
            pltpu.VMEM((32, D), jnp.float32),
            pltpu.SemaphoreType.DMA((2,)),
            pltpu.SemaphoreType.DMA((2 * planes,)),
        ],
        compiler_params=params(60),
        cost_estimate=cost(5 * 10**9, 30 << 20),
        name="project_back",
    )(meta.astype(jnp.int32), *inputs, normed_all)


def rows_back_body(dp_ref, in_w, *parts):
    value = dot_last(dp_ref[...], in_w[:, : dp_ref.shape[1]]).astype(jnp.bfloat16)
    put_by_block(pl.program_id(0), parts, value)


def rows_back(projected_grad, in_full):
    rows, columns = projected_grad.shape
    count = rows // SPOTS
    return pl.pallas_call(
        rows_back_body,
        grid=(SPOTS,),
        out_shape=[jax.ShapeDtypeStruct((count, D), jnp.bfloat16)] * SPOTS,
        in_specs=[block_spec(count, columns), full_spec(*in_full.shape)],
        out_specs=by_block(count, D),
        compiler_params=params(40),
        cost_estimate=cost(5 * 10**9, 12 << 20),
        name="rows_back",
    )(projected_grad, in_full)


def route_body(tokens, home, back, near, match, rank, small, residual_ref, rows_ref, probs_ref):
    bf = jnp.bfloat16
    residual = widen(tokens[...]) + (widen(home[...]) + widen(back[...]) + widen(near[...]))
    residual_ref[...] = residual
    root = lax.rsqrt(jnp.mean(residual * residual, axis=1, keepdims=True) + EPSILON)
    normed = (residual * root * small[FIRST_GAIN + 3 : FIRST_GAIN + 4, :]).astype(bf)
    rows_ref[:, :D] = normed
    experts = match.shape[1]
    logits = dot_last(normed, small[:experts, :].astype(bf))
    exponent = jnp.exp(logits - jnp.max(logits, axis=1, keepdims=True))
    probs = exponent / jnp.sum(exponent, axis=1, keepdims=True)
    chosen = probs * match[...]
    total = jnp.sum(chosen, axis=1, keepdims=True)
    gates = chosen / total
    upper = widen(gates.astype(bf))
    behind = 0.0
    for n, part in enumerate((rank[...], upper.astype(bf), (gates - upper).astype(bf))):
        places = lax.broadcasted_iota(jnp.int32, (experts, WIDE), 0) + n * experts == (
            lax.broadcasted_iota(jnp.int32, (experts, WIDE), 1)
        )
        behind += product(part, jnp.where(places, 1.0, 0.0).astype(bf))
    rows_ref[:, D:] = behind.astype(bf)
    probs_ref[0] = probs
    probs_ref[1] = gates
    probs_ref[2] = jnp.broadcast_to(total, probs.shape)


def route(tokens, home, back, near, match, rank, small):
    count, width = tokens.shape
    experts = match.shape[1]
    inputs = (tokens, home, back, near, match, rank, small)
    shape = jax.ShapeDtypeStruct
    return pl.pallas_call(
        route_body,
        out_shape=[
            shape((count, width), jnp.float32),
            shape((count, width + WIDE), jnp.bfloat16),
            shape((3, count, experts), jnp.float32),
        ],
        in_specs=[full_spec(*item.shape) for item in inputs],
        out_specs=[
            full_spec(count, width),
            full_spec(count, width + WIDE),
            full_spec(3, count, experts),
        ],
        compiler_params=params(40),
        cost_estimate=cost(10**8, 8 << 20),
        name="route",
    )(*inputs)


def route_back_body(total, home, back, near, match, probs_ref, small, residual, upstream, *results):
    grad_ref, branch_ref, router_ref, gain_ref = results
    bf = jnp.bfloat16
    rows = widen(total[...]) + (widen(home[...]) + widen(back[...]) + widen(near[...]))
    experts = match.shape[1]
    probs, gates, gate_total = probs_ref[0], probs_ref[1], probs_ref[2]
    pairs = lax.broadcasted_iota(jnp.int32, (WIDE, experts), 0) // 2 == (
        lax.broadcasted_iota(jnp.int32, (WIDE, experts), 1)
    )
    gate_grad = product(rows[:, D:].astype(bf), jnp.where(pairs, 1.0, 0.0).astype(bf))
    inner = jnp.sum(gate_grad * gates, axis=1, keepdims=True)
    chosen_grad = match[...] * (gate_grad - inner) / gate_total
    inner = jnp.sum(chosen_grad * probs, axis=1, keepdims=True)
    logit_grad = (probs * (chosen_grad - inner)).astype(bf)
    normed_grad = rows[:, :D] + product(logit_grad, small[:experts, :].astype(bf))
    gain = small[FIRST_GAIN + 3 : FIRST_GAIN + 4, :]
    value = residual[...]
    root = lax.rsqrt(jnp.mean(value * value, axis=1, keepdims=True) + EPSILON)
    normed = (value * root * gain).astype(bf)
    router_ref[...] = dot_first(logit_grad, normed)
    scaled = normed_grad * value
    gain_ref[...] = jnp.sum(scaled * root, axis=0, keepdims=True)
    inner = jnp.mean(scaled * gain, axis=1, keepdims=True)
    grad = widen(upstream[...]) + root * gain * normed_grad - value * (root * root * root * inner)
    grad_ref[...] = grad
    branch_ref[...] = grad.astype(bf)


def route_back(total, home, back, near, match, probs, small, residual, upstream):
    count, width = residual.shape
    experts = match.shape[1]
    inputs = (total, home, back, near, match, probs, small, residual, upstream)
    shape = jax.ShapeDtypeStruct
    return pl.pallas_call(
        route_back_body,
        out_shape=[
            shape((count, width), jnp.float32),
            shape((count, width), jnp.bfloat16),
            shape((experts, width), jnp.float32),
            shape((1, width), jnp.float32),
        ],
        in_specs=[full_spec(*item.shape) for item in inputs],
        out_specs=[
            full_spec(count, width),
            full_spec(count, width),
            full_spec(experts, width),
            full_spec(1, width),
        ],
        compiler_params=params(40),
        cost_estimate=cost(10**8, 10 << 20),
        name="route_back",
    )(*inputs)


def shards_dense(
    tokens,
    cotangent,
    norm_gains,
    attention_in,
    attention_out,
    router_weight,
    expert_in,
    expert_out,
    routes,
    lengths,
):
    row_count = tokens.shape[0]
    devices_count = lax.axis_size("fsdp")
    moves = Moves(devices_count)
    planes, core, spot = moves.planes, moves.core_id, moves.spot
    ring, first, second, cores = moves.ring, moves.first, moves.second, moves.core
    experts = devices_count // 2
    choose = routes.shape[1]
    capacity = 4 * row_count * choose // (3 * experts)
    bf, f32 = jnp.bfloat16, jnp.float32
    own_rows = attention_in.shape[0]
    lines = HEADS // SPOTS
    mine = lines * HEAD_DIM

    def low(value):
        return value.astype(bf)

    pieces = split_columns(spot, attention_in, router_weight, norm_gains, lengths)
    traded = [pieces[0]] + [send(pieces[m], moves.spots[m]) for m in range(1, SPOTS)]
    own_1 = send(cotangent, ring)
    tokens_then, traded, own_1 = tie(tokens, traded, own_1)

    in_own = [jnp.stack(traded)]
    in_own.append(send(in_own[0], ring))
    in_other = [send(in_own[0], cores)]
    near_x = send(tokens_then, first)
    near_0 = send(cotangent, first)
    in_own, in_other, near_x = tie(in_own, in_other, near_x)

    in_own.append(send(in_own[1], ring))
    in_other.append(send(in_own[1], cores))
    blocks_x = [tokens, near_x, send(tokens, second), send(near_x, second)]
    in_own, in_other, blocks_x, near_0 = tie(in_own, in_other, blocks_x, near_0)

    in_own.append(send(in_own[2], ring))
    in_other.append(send(in_own[2], cores))
    out_own = [attention_out, send(attention_out, ring)]
    out_other = [send(attention_out, cores)]
    grads = {(0, 0): [cotangent, near_0], (1, 0): [own_1, send(own_1, first)]}
    columns = 3 * mine
    lengths_all = jnp.stack([piece[: lengths.shape[1], columns + SMALL] for piece in traded])
    lengths_all = jnp.where(core == 0, lengths_all, lengths_all[jnp.asarray([0, 2, 1, 3])])
    places = jnp.arange(row_count, dtype=jnp.int32)
    _, position = jax.vmap(lambda item: layout(item, row_count))(lengths_all.astype(jnp.int32))
    starts = (places[None] - position).astype(f32)
    cos_half, sin_half = (table[:, 0] for table in tables(position.reshape(-1)))
    cos_all = jnp.concatenate([cos_half, cos_half], axis=1)
    sin_all = jnp.concatenate([-sin_half, sin_half], axis=1)

    expert_ids = jnp.arange(experts, dtype=jnp.int32)
    match = jnp.sum((routes[:, :, None] == expert_ids[None, None, :]).astype(f32), axis=1)
    before = (places[:, None] > places[None, :]).astype(bf)
    rank = jnp.where(match > 0, product(before, match.astype(bf)), -1.0).astype(bf)
    in_own, in_other, out_other, grads[1, 0], starts, cos_all, sin_all, rank = tie(
        in_own, in_other, out_other, grads[1, 0], starts, cos_all, sin_all, rank
    )

    in_other.append(send(in_own[3], cores))
    (in_other,) = tie(in_other)
    grads[0, 1] = [send(item, second) for item in grads[0, 0]]
    projected, normed_all, in_full, sums, small_rows, gains = project(
        moves, blocks_x, in_own, in_other
    )
    sums, out_own, grads = tie(sums, out_own, grads)
    out_own.append(send(out_own[1], ring))
    out_other.append(send(out_own[1], cores))
    sums = plane_step(moves, by_spot(moves, sums), 1)
    sums, out_own, own_1 = tie(sums, out_own, own_1)
    out_own.append(send(out_own[2], ring))
    out_other.append(send(out_own[2], cores))
    totals = by_spot(moves, plane_step(moves, sums, 2))
    totals, out_own, out_other = tie(totals, out_own, out_other)
    out_other.append(send(out_own[3], cores))
    totals, out_other, grads, own_1 = tie(totals, out_other, grads, own_1)

    own_2 = send(own_1, ring)
    grads[1, 1] = [send(item, second) for item in grads[1, 0]]
    weights = [expert_in[0], send(expert_in[0], cores), expert_out[0], send(expert_out[0], cores)]
    attention = (moves, totals, starts, gains, projected, cos_all, sin_all)
    results = attend_forward(*attention, out_own, out_other)
    heads, out_full, parts = results[:4], results[4], results[5:]
    parts, weights, own_2, grads = tie(parts, weights, own_2, grads)

    def cross(parts):
        return [send(parts[2], second), send(parts[3], second)]

    def gather_near(parts, backs):
        near = low(widen(parts[1]) + widen(backs[1]))
        return widen(parts[0]) + widen(backs[0]), send(near, first)

    backs = cross(parts)
    own_3 = send(own_2, ring)
    backs, parts, near_1 = tie(backs, parts, grads[1, 0][1])
    near = send(low(widen(parts[1]) + widen(backs[1])), first)
    near_2 = send(near_1, ring)
    near, own_3 = tie(near, own_3)
    grads[2, 0] = [own_2, near_2]
    residual, rows, probs = route(tokens, parts[0], backs[0], near, match, rank, small_rows)
    rows, near_2 = tie(rows, near_2)

    meta = (moves.device // 2).reshape(1).astype(jnp.int32)
    saved, done = None, 0
    row_parts, out_parts = {}, {}

    def run_expert(group, which, blocks):
        nonlocal saved, done
        saved, outs, backs = expert_blocks(
            meta,
            blocks,
            grads[group, which],
            weights,
            saved,
            done,
            planes * SPOTS,
            capacity,
            experts,
        )
        done += len(blocks)
        out_parts.setdefault(group, []).extend(outs)
        row_parts.setdefault(group, []).extend(backs)

    row_near = send(rows, first)
    row_1 = send(rows, ring)
    rows, row_near = tie(rows, row_near)

    near_row_1 = send(row_near, ring)
    across = [send(rows, second), send(row_near, second)]
    run_expert(0, 0, [rows, row_near])
    saved, across, row_1 = tie(saved, across, row_1)

    row_2 = send(row_1, ring)
    across_row_1 = send(row_1, second)
    across_2 = send(own_2, second)
    near_3 = send(near_2, ring)
    run_expert(0, 1, across)
    saved, near_row_1, across_row_1, across_2 = tie(saved, near_row_1, across_row_1, across_2)

    near_row_2 = send(near_row_1, ring)
    across = [across_row_1, send(near_row_1, second)]
    grads[2, 0], grads[2, 1] = [own_2, near_2], [across_2, send(near_2, second)]
    run_expert(1, 0, [row_1, near_row_1])
    saved, across, row_2, grads[2, 1] = tie(saved, across, row_2, grads[2, 1])

    row_3 = send(row_2, ring)
    across_row_2 = send(row_2, second)
    across_3 = send(own_3, second)
    run_expert(1, 1, across)
    saved, near_row_2, across_row_2, across_3 = tie(saved, near_row_2, across_row_2, across_3)

    near_row_3 = send(near_row_2, ring)
    across = [across_row_2, send(near_row_2, second)]
    backs_1 = cross(row_parts[1])
    run_expert(2, 0, [row_2, near_row_2])
    saved, across, row_3, near_3 = tie(saved, across, row_3, near_3)

    grads[3, 0] = [own_3, near_3]
    across_row_3 = send(row_3, second)
    grads[3, 1] = [across_3, send(near_3, second)]
    run_expert(2, 1, across)
    saved, near_row_3, across_row_3, backs_1 = tie(saved, near_row_3, across_row_3, backs_1)

    across = [across_row_3, send(near_row_3, second)]
    run_expert(3, 0, [row_3, near_row_3])
    saved, across, grads[3, 1], row_parts = tie(saved, across, grads[3, 1], row_parts)

    pair = [send(low(widen(row_parts[1][n]) + widen(backs_1[n])), ring) for n in range(2)]
    backs_2 = cross(row_parts[2])
    run_expert(3, 1, across)
    saved, pair, backs_2 = tie(saved, pair, backs_2)

    near = send(low(widen(pair[1]) + widen(row_parts[2][1]) + widen(backs_2[1])), first)
    home = widen(pair[0]) + (widen(row_parts[2][0]) + widen(backs_2[0]))
    backs_3 = cross(row_parts[3])
    x_rows, dy_rows, m_own, m_other, du_own, du_other = saved
    in_theirs = dot_first(x_rows, du_other)
    home, near, backs_3, in_theirs, row_parts[0] = tie(
        home, near, backs_3, in_theirs, row_parts[0]
    )

    total = send(low(home + widen(near)), ring)
    home, near = gather_near(row_parts[3], backs_3)
    in_theirs = send(in_theirs, cores)
    backs_0 = cross(row_parts[0])
    out_theirs = dot_first(m_other, dy_rows)
    total, home, near, out_theirs = tie(total, home, near, out_theirs)

    total = send(low(widen(total) + (home + widen(near))), ring)
    _, near_0 = gather_near(row_parts[0], backs_0)
    out_theirs = send(out_theirs, cores)
    out_backs = {1: cross(out_parts[1])}
    total, near_0 = tie(total, near_0)
    residual_grad, branch_grad, router_grad, second_gain_grad = route_back(
        total, row_parts[0][0], backs_0[0], near_0, match, probs, small_rows, residual, cotangent
    )
    branch_near = send(branch_grad, first)
    branch_grad, branch_near, out_parts = tie(branch_grad, branch_near, out_parts)

    branch_blocks = [
        branch_grad,
        branch_near,
        send(branch_grad, second),
        send(branch_near, second),
    ]
    out_pair = [
        send(low(widen(out_parts[1][n]) + widen(out_backs[1][n])), ring) for n in range(2)
    ]
    expert_out_grad = dot_first(m_own, dy_rows) + out_theirs
    branch_blocks, expert_out_grad, out_parts = tie(branch_blocks, expert_out_grad, out_parts)

    out_backs[2] = cross(out_parts[2])
    dq, dk, dv, dots, own_grad, other_grad, gain_grads = attend_backward(
        *attention, heads, out_full, branch_blocks
    )
    dots, out_backs, out_parts, out_pair, other_grad = tie(
        dots, out_backs, out_parts, out_pair, other_grad
    )

    other_grad = send(other_grad, cores)
    out_near = send(
        low(widen(out_pair[1]) + widen(out_parts[2][1]) + widen(out_backs[2][1])), first
    )
    dots = plane_step(moves, by_spot(moves, dots), 1)
    dots, other_grad = tie(dots, other_grad)

    def out_sum(step):
        return widen(own_grad[step]) + widen(other_grad[step])

    out_share = send(low(out_sum(1)), ring)
    dots = by_spot(moves, plane_step(moves, dots, 2))
    dots, out_share, out_near, out_parts, out_pair = tie(
        dots, out_share, out_near, out_parts, out_pair
    )
    out_total = low(
        widen(out_pair[0])
        + (widen(out_parts[2][0]) + widen(out_backs[2][0]))
        + widen(out_near)
    )
    out_total = send(out_total, ring)
    out_backs[3] = cross(out_parts[3])
    small = (router_grad, small_rows, gain_grads, second_gain_grad)
    projected_grad, *in_grads = project_back(
        moves, totals, dots, gains, small, projected, dq, dk, dv, normed_all
    )
    in_grads, projected_grad, out_share, out_parts, out_total, out_backs[3] = tie(
        in_grads, projected_grad, out_share, out_parts, out_total, out_backs[3]
    )

    *in_grads, others, others_rest = in_grads
    others = send(others, cores)
    projected_grad, in_full, others = tie(projected_grad, in_full, others)
    in_total = send(low(widen(in_grads[1]) + widen(others)), ring)
    others_rest = send(others_rest, cores)
    out_share = send(low(widen(out_share) + out_sum(2)), ring)
    out_backs[0] = cross(out_parts[0])
    parts = rows_back(projected_grad, in_full)
    in_total, others_rest, parts, x_rows, out_share, out_parts, out_backs = tie(
        in_total, others_rest, parts, x_rows, out_share, out_parts, out_backs
    )

    in_total = send(low(widen(in_total) + (widen(in_grads[2]) + widen(others_rest[0]))), ring)
    backs = cross(parts)
    expert_in_grad = dot_first(x_rows, du_own) + in_theirs
    out_home, out_near = gather_near(out_parts[3], out_backs[3])
    in_total, backs, expert_in_grad, out_parts, out_home, out_near, out_share = tie(
        in_total, backs, expert_in_grad, out_parts, out_home, out_near, out_share
    )

    in_total = send(low(widen(in_total) + (widen(in_grads[3]) + widen(others_rest[1]))), ring)
    home, near = gather_near(parts, backs)
    out_total = low(widen(out_total) + (out_home + widen(out_near)))
    out_share = send(low(widen(out_share) + out_sum(3)), ring)
    out_home, out_near = gather_near(out_parts[0], out_backs[0])
    in_total, home, near, out_total, out_share = tie(in_total, home, near, out_total, out_share)

    in_total = low(widen(in_total) + (widen(in_grads[0]) + widen(others_rest[2])))
    traded = [in_total[0]] + [send(in_total[m], moves.spots[m]) for m in range(1, SPOTS)]
    out_total = send(out_total, ring)
    out_share = widen(out_share) + out_sum(0)
    _, first_back = jax.vjp(
        lambda value: root_norm(value, small_rows[FIRST_GAIN]), widen(tokens)
    )
    (input_norm_grad,) = first_back(home + widen(near))
    input_grad = residual_grad + input_norm_grad
    traded, input_grad, out_share, out_home, out_near = tie(
        traded, input_grad, out_share, out_home, out_near
    )
    in_share, small_share = join_columns(spot, traded, attention_in, norm_gains)
    out_total, in_share, out_near = tie(out_total, in_share, out_near)
    output = low(residual + (widen(out_total) + (out_home + widen(out_near))))
    return (
        output,
        input_grad,
        small_share[:, FIRST_GAIN:SMALL].T,
        in_share,
        out_share,
        small_share[:, :FIRST_GAIN],
        expert_in_grad[None],
        expert_out_grad[None],
    )


def shards(*arguments):
    routes = arguments[8]
    experts = lax.axis_size("fsdp") // 2
    if 2 * routes.shape[1] >= experts and HEADS == experts:
        return shards_dense(*arguments)
    return shards_routed(*arguments)


def solution(mesh):
    in_specs = (
        P("fsdp", None),
        P("fsdp", None),
        P(None, "fsdp"),
        P("fsdp", None),
        P("fsdp", None),
        P("fsdp", None),
        P("fsdp", None, None),
        P("fsdp", None, None),
        P("fsdp", None),
        P("fsdp", None),
    )
    out_specs = (
        P("fsdp", None),
        P("fsdp", None),
        P(None, "fsdp"),
        P("fsdp", None),
        P("fsdp", None),
        P("fsdp", None),
        P("fsdp", None, None),
        P("fsdp", None, None),
    )
    return jax.shard_map(shards, mesh=mesh, in_specs=in_specs, out_specs=out_specs, check_vma=False)
```

```python
import functools

import jax
import jax.numpy as jnp
from jax import lax
from jax.experimental import pallas as pl
from jax.experimental.pallas import tpu as pltpu
from jax.sharding import PartitionSpec as P

D = 2048
HEADS = 16
HEAD_DIM = 128


EPSILON = 1e-05
ROPE_BASE = 10000.0
MASKED = -1000000000.0


def root_norm(vector, scaling):
    return vector * lax.rsqrt(jnp.mean(vector * vector, axis=-1, keepdims=True) + EPSILON) * scaling


def rotary(vector, cos_table, sin_table):
    half_dim = vector.shape[-1] // 2
    first = vector[..., :half_dim]
    second = vector[..., half_dim:]
    return jnp.concatenate(
        [first * cos_table - second * sin_table, second * cos_table + first * sin_table], axis=-1
    )


def layout(lengths, number):
    ends_at = jnp.cumsum(lengths)
    places = jnp.arange(number, dtype=jnp.int32)
    segment = jnp.sum((places[:, None] >= ends_at[None, :]).astype(jnp.int32), axis=1)
    starts = ends_at - lengths
    select_mask = (
        segment[:, None] == jnp.arange(lengths.shape[0], dtype=jnp.int32)[None, :]
    ).astype(jnp.int32)
    position = places - jnp.sum(select_mask * starts[None, :], axis=1)
    return (segment, position)


def tables(position):
    half_dim = HEAD_DIM // 2
    inverse = ROPE_BASE ** (-2.0 * jnp.arange(half_dim, dtype=jnp.float32) / HEAD_DIM)
    angles = position.astype(jnp.float32)[:, None] * inverse[None, :]
    return (jnp.cos(angles)[:, None, :], jnp.sin(angles)[:, None, :])


def prepare(projected, query_gain, key_gain, cos_table, sin_table):
    count_rows = projected.shape[0]
    query_heads = root_norm(projected[:, :D], query_gain).reshape(count_rows, HEADS, HEAD_DIM)
    key_heads = root_norm(projected[:, D : 2 * D], key_gain).reshape(count_rows, HEADS, HEAD_DIM)
    value_heads = projected[:, 2 * D :].reshape(count_rows, HEADS, HEAD_DIM)
    return (
        rotary(query_heads, cos_table, sin_table),
        rotary(key_heads, cos_table, sin_table),
        value_heads,
    )


def softmax_rows(logits):
    row_max = jnp.max(logits, axis=-1, keepdims=True)
    exponent = jnp.exp(logits - row_max)
    return exponent / jnp.sum(exponent, axis=-1, keepdims=True)


def dot_first(left, right):
    return lax.dot_general(
        left, right, (((0,), (0,)), ((), ())), preferred_element_type=jnp.float32
    )


def dot_last(left, right):
    return lax.dot_general(
        left, right, (((1,), (1,)), ((), ())), preferred_element_type=jnp.float32
    )


def shards_routed(
    tokens,
    cotangent,
    norm_gains,
    attention_in,
    attention_out,
    router_weight,
    expert_in,
    expert_out,
    routes,
    lengths,
):
    row_count = tokens.shape[0]
    devices_count = lax.axis_size("fsdp")
    experts = devices_count // 2
    choose = routes.shape[1]
    half_units = expert_out.shape[1]
    capacity = 4 * row_count * choose // (3 * experts)
    scaling = HEAD_DIM ** (-0.5)
    gain_full, gathered_in, gathered_out, gathered_router = (
        lax.all_gather(norm_gains, "fsdp", axis=1, tiled=True),
        lax.all_gather(attention_in, "fsdp", axis=0, tiled=True),
        lax.all_gather(attention_out, "fsdp", axis=0, tiled=True),
        lax.all_gather(router_weight, "fsdp", axis=0, tiled=True),
    )
    gain_rows = gain_full.astype(jnp.float32)
    segment, position = layout(lengths[0], row_count)
    cos_table, sin_table = tables(position)
    places = jnp.arange(row_count, dtype=jnp.int32)
    allowed = ((segment[:, None] == segment[None, :]) & (places[:, None] >= places[None, :]))[None]
    inputs = tokens.astype(jnp.float32)
    normed_input = root_norm(inputs, gain_rows[0]).astype(jnp.bfloat16)
    projected = jnp.dot(normed_input, gathered_in, preferred_element_type=jnp.float32)

    def prepare_local(projected_value, query_gain, key_gain):
        return prepare(projected_value, query_gain, key_gain, cos_table, sin_table)

    (query_f, key_f, value_f), prepare_back = jax.vjp(
        prepare_local, projected, gain_rows[1], gain_rows[2]
    )
    query_heads = query_f.astype(jnp.bfloat16)
    key_heads = key_f.astype(jnp.bfloat16)
    value_heads = value_f.astype(jnp.bfloat16)

    def score_block():
        raw_scores = (
            jnp.einsum("qhd,khd->hqk", query_heads, key_heads, preferred_element_type=jnp.float32)
            * scaling
        )
        return jnp.where(allowed, raw_scores, MASKED)

    scores = score_block()
    row_max = jnp.max(scores, axis=-1, keepdims=True)
    exponent = jnp.exp(scores - row_max)
    row_sum = jnp.sum(exponent, axis=-1, keepdims=True)
    log_total = row_max + jnp.log(row_sum)
    attend_probs = (exponent / row_sum).astype(jnp.bfloat16)
    attended = (
        jnp.einsum("hqk,khd->qhd", attend_probs, value_heads, preferred_element_type=jnp.float32)
        .reshape(row_count, D)
        .astype(jnp.bfloat16)
    )
    branch_out = jnp.dot(attended, gathered_out, preferred_element_type=jnp.float32)
    residual = inputs + branch_out
    normed = root_norm(residual, gain_rows[3]).astype(jnp.bfloat16)
    logits = jnp.dot(normed, gathered_router, preferred_element_type=jnp.float32)
    router_probs = softmax_rows(logits)
    chosen = jnp.take_along_axis(router_probs, routes, axis=1)
    gate_total = jnp.sum(chosen, axis=1, keepdims=True)
    gate_values = chosen / gate_total
    flat_routes = routes.reshape(-1)
    route_hits = (flat_routes[:, None] == jnp.arange(experts, dtype=jnp.int32)[None, :]).astype(
        jnp.int32
    )
    slot_index = jnp.sum((jnp.cumsum(route_hits, axis=0) - route_hits) * route_hits, axis=1)
    target = flat_routes * capacity + slot_index
    owner_token = (
        jnp.zeros((experts * capacity,), jnp.int32)
        .at[target]
        .set(jnp.arange(row_count * choose, dtype=jnp.int32) // choose)
    )
    filled = (
        jnp.zeros((experts * capacity,), jnp.bfloat16)
        .at[target]
        .set(jnp.ones((row_count * choose,), jnp.bfloat16))
    )
    outgoing = jnp.repeat(
        (normed[owner_token] * filled[:, None]).reshape(experts, capacity, D), 2, axis=0
    )
    arrived = lax.all_to_all(outgoing, "fsdp", split_axis=0, concat_axis=0, tiled=True).reshape(
        devices_count * capacity, D
    )
    gate_up_out = jnp.dot(arrived, expert_in[0], preferred_element_type=jnp.float32)
    gate_part = gate_up_out[:, :half_units]
    up_part = gate_up_out[:, half_units:]
    hidden_f, swiglu_back = jax.vjp(
        lambda gate_in, up_in: jax.nn.silu(gate_in) * up_in, gate_part, up_part
    )
    hidden = hidden_f.astype(jnp.bfloat16)
    produced = (
        jnp.dot(hidden, expert_out[0], preferred_element_type=jnp.float32)
        .astype(jnp.bfloat16)
        .reshape(devices_count, capacity, D)
    )
    returned = (
        lax.all_to_all(produced, "fsdp", split_axis=0, concat_axis=0, tiled=True)
        .reshape(experts, 2, capacity, D)
        .astype(jnp.float32)
    )
    returned = jnp.sum(returned, axis=1).reshape(experts * capacity, D)
    picked = returned[target].reshape(row_count, choose, D)
    expert_sum = jnp.sum(gate_values[:, :, None] * picked, axis=1)
    output = (residual + expert_sum).astype(jnp.bfloat16)
    back_in, back_out, back_router = (
        lax.all_gather(attention_in, "fsdp", axis=0, tiled=True),
        lax.all_gather(attention_out, "fsdp", axis=0, tiled=True),
        lax.all_gather(router_weight, "fsdp", axis=0, tiled=True),
    )
    upstream = cotangent.astype(jnp.float32)
    gate_grad = jnp.sum(upstream[:, None, :] * picked, axis=2)
    send_grad = (
        (gate_values[:, :, None] * upstream[:, None, :])
        .astype(jnp.bfloat16)
        .reshape(row_count * choose, D)
    )
    grad_buffer = (
        jnp.zeros((experts * capacity, D), jnp.bfloat16)
        .at[target]
        .set(send_grad)
        .reshape(experts, capacity, D)
    )
    grad_buffer = jnp.repeat(grad_buffer, 2, axis=0)
    grad_arrived = lax.all_to_all(
        grad_buffer, "fsdp", split_axis=0, concat_axis=0, tiled=True
    ).reshape(devices_count * capacity, D)
    grad_hidden = dot_last(grad_arrived, expert_out[0])
    expert_out_grad = dot_first(hidden, grad_arrived)
    grad_gate, grad_up = swiglu_back(grad_hidden)
    grad_gate_up = jnp.concatenate([grad_gate, grad_up], axis=1).astype(jnp.bfloat16)
    expert_in_grad = dot_first(arrived, grad_gate_up)
    grad_rows = (
        dot_last(grad_gate_up, expert_in[0])
        .astype(jnp.bfloat16)
        .reshape(devices_count, capacity, D)
    )
    grad_back = (
        lax.all_to_all(grad_rows, "fsdp", split_axis=0, concat_axis=0, tiled=True)
        .reshape(experts, 2, capacity, D)
        .astype(jnp.float32)
    )
    grad_back = jnp.sum(grad_back, axis=1).reshape(experts * capacity, D)
    dispatch_grad = jnp.sum(grad_back[target].reshape(row_count, choose, D), axis=1)
    chosen_grad = (gate_grad - jnp.sum(gate_grad * gate_values, axis=1, keepdims=True)) / gate_total
    expert_match = (
        routes[:, :, None] == jnp.arange(experts, dtype=jnp.int32)[None, None, :]
    ).astype(jnp.float32)
    prob_grad = jnp.sum(expert_match * chosen_grad[:, :, None], axis=1)
    logit_grad = (
        router_probs * (prob_grad - jnp.sum(prob_grad * router_probs, axis=1, keepdims=True))
    ).astype(jnp.bfloat16)
    router_grad = dot_first(normed, logit_grad)
    normed_grad = dispatch_grad + dot_last(logit_grad, back_router)
    _, second_back = jax.vjp(root_norm, residual, gain_rows[3])
    residual_norm_grad, second_gain_grad = second_back(normed_grad)
    residual_grad = upstream + residual_norm_grad
    branch_grad = residual_grad.astype(jnp.bfloat16)
    out_grad = dot_first(attended, branch_grad)
    attended_grad = (
        dot_last(branch_grad, back_out).astype(jnp.bfloat16).reshape(row_count, HEADS, HEAD_DIM)
    )
    recomputed = jnp.exp(score_block() - log_total)
    value_grad = jnp.einsum(
        "hqk,qhd->khd", attend_probs, attended_grad, preferred_element_type=jnp.float32
    )
    attend_grad = jnp.einsum(
        "qhd,khd->hqk", attended_grad, value_heads, preferred_element_type=jnp.float32
    )
    row_delta = jnp.sum(recomputed * attend_grad, axis=-1, keepdims=True)
    score_grad = (recomputed * (attend_grad - row_delta)).astype(jnp.bfloat16)
    query_grad = (
        jnp.einsum("hqk,khd->qhd", score_grad, key_heads, preferred_element_type=jnp.float32)
        * scaling
    )
    key_grad = (
        jnp.einsum("hqk,qhd->khd", score_grad, query_heads, preferred_element_type=jnp.float32)
        * scaling
    )
    projected_grad, query_gain_grad, key_gain_grad = prepare_back(
        (query_grad, key_grad, value_grad)
    )
    projected_grad = projected_grad.astype(jnp.bfloat16)
    attention_in_grad = dot_first(normed_input, projected_grad)
    normed_input_grad = dot_last(projected_grad, back_in)
    _, first_back = jax.vjp(root_norm, inputs, gain_rows[0])
    input_norm_grad, first_gain_grad = first_back(normed_input_grad)
    input_grad = residual_grad + input_norm_grad
    gains_grad = jnp.stack([first_gain_grad, query_gain_grad, key_gain_grad, second_gain_grad])
    gains_share, in_share, out_share, router_share = (
        lax.psum_scatter(gains_grad, "fsdp", scatter_dimension=1, tiled=True),
        lax.psum_scatter(attention_in_grad, "fsdp", scatter_dimension=0, tiled=True),
        lax.psum_scatter(out_grad, "fsdp", scatter_dimension=0, tiled=True),
        lax.psum_scatter(router_grad, "fsdp", scatter_dimension=0, tiled=True),
    )
    return (
        output,
        input_grad,
        gains_share,
        in_share,
        out_share,
        router_share,
        expert_in_grad[None],
        expert_out_grad[None],
    )


def product(left, right):
    return jnp.dot(left, right, preferred_element_type=jnp.float32)


def widen(value):
    return value.astype(jnp.float32)


PLANE = 8
SPOTS = 4
WIDE = 128
SMALL = 20
FIRST_GAIN = SMALL - 4


class Moves:
    def __init__(self, count):
        planes = count // PLANE
        order = list(range(0, planes, 2)) + list(range(1, planes, 2))[::-1]
        after = {order[i]: order[(i + 1) % planes] for i in range(planes)}
        self.planes = planes
        self.ring = [(i, after[i // PLANE] * PLANE + i % PLANE) for i in range(count)]
        self.first = [(i, i ^ (4 if i & 1 else 2)) for i in range(count)]
        self.second = [(i, i ^ (2 if i & 1 else 4)) for i in range(count)]
        self.core = [(i, i ^ 1) for i in range(count)]
        self.spots = [[(i, i ^ (2 * mask)) for i in range(count)] for mask in range(SPOTS)]
        device = lax.axis_index("fsdp")
        self.device = device
        self.plane, self.spot, self.core_id = device // PLANE, device % PLANE // 2, device % 2
        rank = jnp.asarray([order.index(i) for i in range(planes)], jnp.int32)
        self.planes_back = jnp.asarray(order, jnp.int32)[
            (rank[self.plane] - jnp.arange(planes, dtype=jnp.int32)) % planes
        ]
        self.steps_from = (rank[self.plane] - rank) % planes
        self.group_spots = self.spot ^ jnp.where(
            self.core_id == 0, jnp.asarray([0, 1, 2, 3]), jnp.asarray([0, 2, 1, 3])
        )


def send(value, pairs):
    return lax.ppermute(value, "fsdp", pairs)


def tie(*values):
    return lax.optimization_barrier(values)


def by_spot(moves, parts):
    return jnp.where(moves.core_id == 0, parts, parts[:, jnp.asarray([0, 2, 1, 3])])


def plane_step(moves, parts, bit):
    other = send(parts, moves.spots[bit])
    return parts + jnp.stack([other[:, m ^ bit] for m in range(SPOTS)], axis=1)


def full_spec(*dims):
    return pl.BlockSpec(dims, lambda *_: (0,) * len(dims))


SCALARS = pl.BlockSpec(memory_space=pltpu.SMEM)
ANYWHERE = pl.BlockSpec(memory_space=pl.ANY)


def params(mebibytes):
    return pltpu.CompilerParams(vmem_limit_bytes=mebibytes << 20)


def cost(flops, moved, special=0):
    return pl.CostEstimate(flops=flops, bytes_accessed=moved, transcendentals=special)


def column_places(spot, mask, lines):
    for part in range(3):
        for line in range(lines):
            piece = (part * lines + line) * HEAD_DIM
            whole = ((part * lines + line) * SPOTS + (spot ^ mask)) * HEAD_DIM
            yield pl.ds(pl.multiple_of(whole, HEAD_DIM), HEAD_DIM), pl.ds(piece, HEAD_DIM)


def split_body(lines, spot, lengths, whole_ref, router_ref, gains_ref, *pieces):
    rows, columns = pieces[0].shape[0], pieces[0].shape[1] - WIDE
    routers = router_ref.shape[1]
    lane = lax.broadcasted_iota(jnp.int32, (rows, WIDE), 1)
    row = lax.broadcasted_iota(jnp.int32, (rows, WIDE), 0)
    spread = lax.broadcasted_iota(jnp.int32, (routers, WIDE), 0) == lax.broadcasted_iota(
        jnp.int32, (routers, WIDE), 1
    )
    riding = product(router_ref[...], jnp.where(spread, 1.0, 0.0).astype(jnp.bfloat16))
    for n in range(gains_ref.shape[0]):
        column = as_column(widen(gains_ref[...])[n : n + 1, :])
        riding = jnp.where(lane == FIRST_GAIN + n, column, riding)
    for n in range(lengths.shape[1]):
        riding = jnp.where((lane == SMALL) & (row == n), lengths[0, n].astype(jnp.float32), riding)
    for mask, piece in enumerate(pieces):
        for whole_at, piece_at in column_places(spot[0], mask, lines):
            piece[:, piece_at] = whole_ref[:, whole_at]
        piece[:, columns:] = riding.astype(jnp.bfloat16)


def split_columns(spot, whole, router, gains, lengths):
    rows, columns = whole.shape
    columns = columns // SPOTS + WIDE
    return pl.pallas_call(
        functools.partial(split_body, HEADS // SPOTS),
        out_shape=[jax.ShapeDtypeStruct((rows, columns), whole.dtype)] * SPOTS,
        in_specs=[
            SCALARS,
            SCALARS,
            full_spec(*whole.shape),
            full_spec(*router.shape),
            full_spec(*gains.shape),
        ],
        out_specs=[full_spec(rows, columns)] * SPOTS,
        compiler_params=params(60),
        name="split_columns",
    )(spot.reshape(1), lengths, whole, router, gains)


def join_body(lines, meta, *refs):
    *pieces, weights, gains, whole_ref, small_ref = refs
    for mask, piece in enumerate(pieces):
        for whole_at, piece_at in column_places(meta[0], mask, lines):
            whole_ref[:, whole_at] = widen(piece[:, piece_at])
    small = sum(widen(piece[:, piece.shape[1] - WIDE :]) for piece in pieces)
    lane = lax.broadcasted_iota(jnp.int32, small.shape, 1)
    gain = as_column(widen(gains[...])[0:1, :])
    gain_grad = jnp.sum(whole_ref[...] * widen(weights[...]), axis=1, keepdims=True)
    small_ref[...] = jnp.where(lane == FIRST_GAIN, gain_grad / gain, small)


def join_columns(spot, pieces, weights, gains):
    rows, wide = pieces[0].shape
    columns = wide - WIDE
    return pl.pallas_call(
        functools.partial(join_body, HEADS // SPOTS),
        out_shape=[
            jax.ShapeDtypeStruct((rows, columns * SPOTS), jnp.float32),
            jax.ShapeDtypeStruct((rows, WIDE), jnp.float32),
        ],
        in_specs=[SCALARS] + [full_spec(rows, wide)] * SPOTS
        + [full_spec(*weights.shape), full_spec(*gains.shape)],
        out_specs=[full_spec(rows, columns * SPOTS), full_spec(rows, WIDE)],
        compiler_params=params(60),
        name="join_columns",
    )(spot.reshape(1), *pieces, weights, gains)


def expert_body(index, cap, experts, blocks, meta, *refs):
    row_refs, grad_refs, weights = refs[:blocks], refs[blocks : 2 * blocks], refs[2 * blocks :][:4]
    refs = refs[2 * blocks + 4 + 6 :]
    saves, out_parts, row_parts = refs[:6], refs[6 : 6 + blocks], refs[6 + blocks :][:blocks]
    rows_v, grads_v, in_v, out_v, x_v, dy_v, m_v, du_v, part_v, back_v, sem, done = refs[
        6 + 2 * blocks :
    ]
    bf, f32 = jnp.bfloat16, jnp.float32
    count, width, half = rows_v.shape[1], grads_v.shape[2], out_v.shape[1]
    expert = meta[0]

    def fetch(ref, place, n):
        copy = pltpu.make_async_copy(ref, place, sem.at[n])
        copy.start()
        return copy

    fetch_rows = [fetch(ref, rows_v.at[j], j) for j, ref in enumerate(row_refs)]
    fetch_in = [fetch(weights[h], in_v.at[h], blocks + h) for h in range(2)]
    fetch_out = [fetch(weights[2 + h], out_v.at[h], blocks + 2 + h) for h in range(2)]
    fetch_grads = [fetch(ref, grads_v.at[j], blocks + 4 + j) for j, ref in enumerate(grad_refs)]
    leaving = []

    def leave(place, ref):
        leaving.append(pltpu.make_async_copy(place, ref, done.at[len(leaving)]))
        leaving[-1].start()

    def save(place, n):
        leave(place, saves[n].at[pl.ds(index * cap, blocks * cap)])

    lane8 = lax.broadcasted_iota(jnp.int32, (8, WIDE), 1)
    row8 = lax.broadcasted_iota(jnp.int32, (8, WIDE), 0)
    picker = (
        jnp.where((row8 == 0) & (lane8 == expert), 1.0, 0.0)
        + jnp.where((row8 == 1) & (lane8 == experts + expert), 1.0, 0.0)
        + jnp.where((row8 == 1) & (lane8 == 2 * experts + expert), 1.0, 0.0)
    ).astype(bf)
    lanes = lax.broadcasted_iota(jnp.int32, (count, WIDE), 1)
    slots_down = lax.broadcasted_iota(jnp.int32, (cap, count), 0)
    slots_along = lax.broadcasted_iota(jnp.int32, (count, cap), 1)
    gather, scatter, gates = [], [], []
    slots = [slice(j * cap, (j + 1) * cap) for j in range(blocks)]
    for j in range(blocks):
        fetch_rows[j].wait()
        extra = rows_v[j, :, width:]
        info = dot_last(picker, extra)
        chosen = slots_down == info[0:1].astype(jnp.int32)
        gates.append(jnp.sum(jnp.where(chosen, info[1:2], 0.0), axis=1, keepdims=True))
        gather.append(jnp.where(chosen, 1.0, 0.0).astype(bf))
        slot = jnp.sum(
            jnp.where(lanes == expert, widen(extra), 0.0), axis=1, keepdims=True
        ).astype(jnp.int32)
        scatter.append(jnp.where(slots_along == slot, 1.0, 0.0).astype(bf))
        x_v[slots[j], :] = product(gather[j], rows_v[j, :, :width]).astype(bf)
    gate = jnp.concatenate(gates, axis=0)
    save(x_v, 0)
    x = x_v[...]
    inner = []
    for h in range(2):
        fetch_in[h].wait()
        u = product(x, in_v[h])
        gate_part, up_part = u[:, :half], u[:, half:]
        sigmoid = 1.0 / (1.0 + jnp.exp(-gate_part))
        silu = gate_part * sigmoid
        inner.append((gate_part, up_part, sigmoid, silu))
        m_v[h] = (silu * up_part).astype(bf)
        save(m_v.at[h], 2 + h)
    for copy in fetch_out:
        copy.wait()
    y = product(m_v[0], out_v[0]) + product(m_v[1], out_v[1])
    for copy in fetch_grads:
        copy.wait()
    g = jnp.concatenate([product(gather[j], grads_v[j]) for j in range(blocks)], axis=0)
    dgate = jnp.sum(g * y, axis=1, keepdims=True)
    z = (gate * y).astype(bf)
    dy_v[...] = (gate * g).astype(bf)
    save(dy_v, 1)
    for j in range(blocks):
        part_v[j] = product(scatter[j], z[slots[j]]).astype(bf)
        leave(part_v.at[j], out_parts[j])
    dy = dy_v[...]
    for h in range(2):
        gate_part, up_part, sigmoid, silu = inner[h]
        dm = dot_last(dy, out_v[h])
        slope = sigmoid * (1.0 + gate_part * (1.0 - sigmoid))
        du_v[h, :, :half] = (dm * up_part * slope).astype(bf)
        du_v[h, :, half:] = (dm * silu).astype(bf)
        save(du_v.at[h], 4 + h)
    drows = (dot_last(du_v[0], in_v[0]) + dot_last(du_v[1], in_v[1])).astype(bf)
    upper = widen(dgate.astype(bf))
    lane_m = lax.broadcasted_iota(jnp.int32, (blocks * cap, WIDE), 1)
    pair = jnp.where(
        lane_m == 2 * expert, upper, jnp.where(lane_m == 2 * expert + 1, dgate - upper, 0.0)
    ).astype(bf)
    for j in range(blocks):
        back_v[j, :, :width] = product(scatter[j], drows[slots[j]]).astype(bf)
        back_v[j, :, width:] = product(scatter[j], pair[slots[j]]).astype(bf)
        leave(back_v.at[j], row_parts[j])
    for copy in leaving:
        copy.wait()


def expert_blocks(meta, rows, grads, weights, saved, index, total, cap, experts):
    blocks = len(rows)
    count, wide = rows[0].shape
    width, half = grads[0].shape[1], weights[2].shape[0]
    bf = jnp.bfloat16
    used = blocks * cap

    def shape(*dims):
        return jax.ShapeDtypeStruct(dims, bf)

    aliases = {2 * blocks + 5 + t: t for t in range(6)}
    if saved is None:
        saved, aliases = [jnp.zeros((16, WIDE), bf)] * 6, {}
    save_columns = (width, width, half, half, 2 * half, 2 * half)
    results = pl.pallas_call(
        functools.partial(expert_body, index, cap, experts, blocks),
        out_shape=[shape(total * cap, columns) for columns in save_columns]
        + [shape(count, width)] * blocks
        + [shape(count, wide)] * blocks,
        in_specs=[SCALARS] + [ANYWHERE] * (2 * blocks + 10),
        out_specs=[ANYWHERE] * (6 + 2 * blocks),
        scratch_shapes=[
            pltpu.VMEM((blocks, count, wide), bf),
            pltpu.VMEM((blocks, count, width), bf),
            pltpu.VMEM((2, width, 2 * half), bf),
            pltpu.VMEM((2, half, width), bf),
            pltpu.VMEM((used, width), bf),
            pltpu.VMEM((used, width), bf),
            pltpu.VMEM((2, used, half), bf),
            pltpu.VMEM((2, used, 2 * half), bf),
            pltpu.VMEM((blocks, count, width), bf),
            pltpu.VMEM((blocks, count, wide), bf),
            pltpu.SemaphoreType.DMA((2 * blocks + 4,)),
            pltpu.SemaphoreType.DMA((6 + 2 * blocks,)),
        ],
        input_output_aliases=aliases,
        compiler_params=params(60),
        cost_estimate=cost(blocks * 38 * 10**8, 30 << 20, 2 * used * half),
        name="expert_blocks",
    )(meta, *rows, *grads, *weights, *saved)
    return results[:6], results[6 : 6 + blocks], results[6 + blocks :]


def eye(count):
    return lax.broadcasted_iota(jnp.int32, (count, count), 0) == lax.broadcasted_iota(
        jnp.int32, (count, count), 1
    )


def as_column(row):
    return jnp.sum(jnp.where(eye(row.shape[1]), row, 0.0), axis=1, keepdims=True)


def as_row(column):
    return jnp.sum(jnp.where(eye(column.shape[0]), column, 0.0), axis=0, keepdims=True)


def rolled(value):
    return pltpu.roll(value, HEAD_DIM // 2, 1)


def root_of(total):
    return lax.rsqrt(total / D + EPSILON)


def weights_of(query, key, start):
    count = query.shape[0]
    rows = lax.broadcasted_iota(jnp.int32, (count, count), 0)
    columns = lax.broadcasted_iota(jnp.int32, (count, count), 1)
    allowed = (columns <= rows) & (columns >= start.astype(jnp.int32))
    scores = jnp.where(allowed, dot_last(query, key) * HEAD_DIM ** (-0.5), MASKED)
    exponent = jnp.exp(scores - jnp.max(scores, axis=1, keepdims=True))
    return exponent / jnp.sum(exponent, axis=1, keepdims=True)


def spans(mine):
    return [slice(h, h + HEAD_DIM) for h in range(0, mine, HEAD_DIM)]


def project_body(planes, own_rows, meta, *refs):
    blocks, own, other = refs[:SPOTS], refs[SPOTS : SPOTS + planes], refs[SPOTS + planes :][:planes]
    proj_ref, a_ref, in_ref, sums_ref, small_ref, gains_ref = refs[SPOTS + 2 * planes :][:6]
    x_v, a_v, in_v, proj_v, sem, in_sem, done = refs[SPOTS + 2 * planes + 6 :]
    spot, core = meta[0], meta[1]
    count = x_v.shape[1]
    mine = proj_v.shape[1] // 3
    fetch_x = [pltpu.make_async_copy(ref, x_v.at[j], sem.at[j]) for j, ref in enumerate(blocks)]
    for copy in fetch_x:
        copy.start()
    fetch_in = []
    for k in range(planes):
        for mask in range(SPOTS):
            chunk = meta[2 + k] * PLANE + (spot ^ mask) * 2
            for n, (refs_k, c) in enumerate(((own, core), (other, 1 - core))):
                at = pl.multiple_of((chunk + c) * own_rows, own_rows)
                fetch_in.append(
                    pltpu.make_async_copy(
                        refs_k[k].at[mask],
                        in_v.at[pl.ds(at, own_rows)],
                        in_sem.at[(k * SPOTS + mask) * 2 + n],
                    )
                )
                fetch_in[-1].start()
    roots = []
    for j in range(SPOTS):
        fetch_x[j].wait()
        x = widen(x_v[j])
        roots.append(lax.rsqrt(jnp.mean(x * x, axis=1, keepdims=True) + EPSILON))
    for copy in fetch_in:
        copy.wait()
    leaving = [pltpu.make_async_copy(in_v, in_ref, done.at[0])]
    leaving[0].start()
    turn_by = lax.broadcasted_iota(jnp.int32, (small_ref.shape[0], WIDE), 0) == (
        lax.broadcasted_iota(jnp.int32, (small_ref.shape[0], WIDE), 1)
    )
    small = dot_last(jnp.where(turn_by, 1.0, 0.0).astype(jnp.bfloat16), in_v[:, 3 * mine :])
    small_ref[...] = small
    for line in range(mine // HEAD_DIM):
        at = pl.multiple_of((line * SPOTS + spot) * HEAD_DIM, HEAD_DIM)
        for n in range(2):
            gains_ref[n : n + 1, line * HEAD_DIM : (line + 1) * HEAD_DIM] = small_ref[
                FIRST_GAIN + 1 + n : FIRST_GAIN + 2 + n, pl.ds(at, HEAD_DIM)
            ]
    gain = small[FIRST_GAIN : FIRST_GAIN + 1, :]
    for j in range(SPOTS):
        a_v[j * count : (j + 1) * count, :] = (widen(x_v[j]) * roots[j] * gain).astype(jnp.bfloat16)
    leaving.append(pltpu.make_async_copy(a_v, a_ref, done.at[1]))
    leaving[1].start()
    for n in range(3):
        part = slice(n * mine, (n + 1) * mine)
        value = product(a_v[...], in_v[:, part])
        proj_v[:, part] = value
        leaving.append(
            pltpu.make_async_copy(proj_v.at[:, part], proj_ref.at[:, part], done.at[2 + n])
        )
        leaving[-1].start()
        if n < 2:
            squares = jnp.sum(value * value, axis=1, keepdims=True)
            for j in range(SPOTS):
                sums_ref[n, j : j + 1, :] = as_row(squares[j * count : (j + 1) * count])
    for copy in leaving:
        copy.wait()


def project(moves, blocks, own, other):
    planes, own_rows, wide = len(own), own[0].shape[1], own[0].shape[2]
    width = wide - WIDE
    count, depth = blocks[0].shape
    bf, f32 = jnp.bfloat16, jnp.float32
    rows = SPOTS * count
    meta = jnp.concatenate([jnp.stack([moves.spot, moves.core_id]), moves.planes_back])
    shape = jax.ShapeDtypeStruct
    return pl.pallas_call(
        functools.partial(project_body, planes, own_rows),
        out_shape=[
            shape((rows, width), f32),
            shape((rows, depth), bf),
            shape((depth, wide), bf),
            shape((2, SPOTS, count), f32),
            shape((32, depth), f32),
            shape((2, width // 3), f32),
        ],
        in_specs=[SCALARS] + [ANYWHERE] * (SPOTS + 2 * planes),
        out_specs=[ANYWHERE] * 3
        + [full_spec(2, SPOTS, count), full_spec(32, depth), full_spec(2, width // 3)],
        scratch_shapes=[
            pltpu.VMEM((SPOTS, count, depth), bf),
            pltpu.VMEM((rows, depth), bf),
            pltpu.VMEM((depth, wide), bf),
            pltpu.VMEM((rows, width), f32),
            pltpu.SemaphoreType.DMA((SPOTS,)),
            pltpu.SemaphoreType.DMA((2 * SPOTS * planes,)),
            pltpu.SemaphoreType.DMA((5,)),
        ],
        compiler_params=params(60),
        cost_estimate=cost(5 * 10**9, 20 << 20),
        name="project",
    )(meta.astype(jnp.int32), *blocks, *own, *other)


def by_block(count, width):
    return [pl.BlockSpec((count, width), lambda i: (0, 0))] * SPOTS


def put_by_block(step, refs, value):
    for n, ref in enumerate(refs):

        @pl.when(step == n)
        def _(ref=ref):
            ref[...] = value


def forward_body(planes, own_rows, meta, totals, starts, gains, proj_ref, cos_ref, sin_ref, *refs):
    own, other = refs[:planes], refs[planes : 2 * planes]
    q_ref, k_ref, v_ref, o_ref, out_w, *parts = refs[2 * planes :][: 5 + SPOTS]
    sem = refs[-1]
    step = pl.program_id(0)
    bf = jnp.bfloat16
    mine = q_ref.shape[1]
    fetches = []
    for k in range(planes):
        for n, (refs_k, c) in enumerate(((own, meta[1]), (other, 1 - meta[1]))):
            at = pl.multiple_of((meta[2 + k] * 2 + c) * own_rows, own_rows)
            fetches.append(
                pltpu.make_async_copy(
                    refs_k[k], out_w.at[pl.ds(at, own_rows)], sem.at[2 * k + n]
                )
            )

    @pl.when(step == 0)
    def _():
        for copy in fetches:
            copy.start()

    query_root = root_of(as_column(totals[0, pl.ds(step, 1), :]))
    key_root = root_of(as_column(totals[1, pl.ds(step, 1), :]))
    start = as_column(starts[pl.ds(step, 1), :])
    cos, sin = cos_ref[...], sin_ref[...]
    for own_span in spans(mine):
        at = own_span.start
        query = proj_ref[:, at : at + HEAD_DIM] * query_root * gains[0:1, own_span]
        key = proj_ref[:, mine + at : mine + at + HEAD_DIM] * key_root * gains[1:2, own_span]
        value = proj_ref[:, 2 * mine + at : 2 * mine + at + HEAD_DIM].astype(bf)
        query = (query * cos + rolled(query) * sin).astype(bf)
        key = (key * cos + rolled(key) * sin).astype(bf)
        weights = weights_of(query, key, start).astype(bf)
        q_ref[:, own_span] = query
        k_ref[:, own_span] = key
        v_ref[:, own_span] = value
        o_ref[:, own_span] = product(weights, value).astype(bf)

    @pl.when(step == 0)
    def _():
        for copy in fetches:
            copy.wait()

    put_by_block(step, parts, product(o_ref[...], out_w[...]).astype(bf))


def block_spec(count, columns):
    return pl.BlockSpec((count, columns), lambda i: (i, 0))


def attend_forward(moves, totals, starts, gains, projected, cos_all, sin_all, own, other):
    planes, own_rows = len(own), own[0].shape[0]
    rows, mine = projected.shape[0], gains.shape[1]
    count = rows // SPOTS
    bf = jnp.bfloat16
    meta = jnp.concatenate([jnp.stack([moves.spot, moves.core_id]), moves.planes_back])
    return pl.pallas_call(
        functools.partial(forward_body, planes, own_rows),
        grid=(SPOTS,),
        out_shape=[jax.ShapeDtypeStruct((rows, mine), bf)] * 4
        + [jax.ShapeDtypeStruct((mine, D), bf)]
        + [jax.ShapeDtypeStruct((count, D), bf)] * SPOTS,
        in_specs=[
            SCALARS,
            full_spec(*totals.shape),
            full_spec(*starts.shape),
            full_spec(*gains.shape),
            block_spec(count, 3 * mine),
            block_spec(count, HEAD_DIM),
            block_spec(count, HEAD_DIM),
        ]
        + [ANYWHERE] * (2 * planes),
        out_specs=[block_spec(count, mine)] * 4 + [full_spec(mine, D)] + by_block(count, D),
        scratch_shapes=[pltpu.SemaphoreType.DMA((2 * planes,))],
        compiler_params=params(40),
        cost_estimate=cost(5 * 10**9, 20 << 20),
        name="attend_forward",
    )(meta.astype(jnp.int32), totals, starts, gains, projected, cos_all, sin_all, *own, *other)


def backward_body(
    meta, totals, starts, gains, proj_ref, cos_ref, sin_ref, q_ref, k_ref, v_ref, o_ref, out_w, *refs
):
    blocks = refs[:SPOTS]
    dq_ref, dk_ref, dv_ref, sums_ref, own_grad, other_grad, gain_grad = refs[SPOTS : SPOTS + 7]
    grads_v, o_v, total_v, sem = refs[SPOTS + 7 :]
    step = pl.program_id(0)
    bf = jnp.bfloat16
    mine = q_ref.shape[1]

    @pl.when(step == 0)
    def _():
        for n in range(SPOTS):
            pltpu.make_async_copy(blocks[n], grads_v.at[n], sem.at[n]).start()
        gain_grad[...] = jnp.zeros_like(gain_grad)

    pltpu.make_async_copy(blocks[0], grads_v.at[step], sem.at[step]).wait()
    grads = grads_v[step]
    count = grads.shape[0]
    o_v[pl.ds(pl.multiple_of(step * count, 64), count), :] = o_ref[...]
    do = dot_last(grads, out_w[...]).astype(bf)
    roots = [root_of(as_column(totals[n, pl.ds(step, 1), :])) for n in range(2)]
    start = as_column(starts[pl.ds(step, 1), :])
    cos, sin = cos_ref[...], sin_ref[...]
    sums = [0.0, 0.0]
    for own in spans(mine):
        query, key, value = q_ref[:, own], k_ref[:, own], v_ref[:, own]
        weights = weights_of(query, key, start)
        dv_ref[:, own] = dot_first(weights.astype(bf), do[:, own]).astype(bf)
        dweights = dot_last(do[:, own], value)
        inner = jnp.sum(weights * dweights, axis=1, keepdims=True)
        dscores = (weights * (dweights - inner)).astype(bf)
        for n, (grad, ref) in enumerate(
            ((product(dscores, key), dq_ref), (dot_first(dscores, query), dk_ref))
        ):
            grad = grad * HEAD_DIM ** (-0.5)
            grad = grad * cos - rolled(grad) * sin
            ref[:, own] = grad
            at = n * mine + own.start
            raw = grad * proj_ref[:, at : at + HEAD_DIM]
            sums[n] += jnp.sum(raw * gains[n : n + 1, own], axis=1, keepdims=True)
            line = pl.multiple_of((own.start // HEAD_DIM * SPOTS + meta[0]) * HEAD_DIM, HEAD_DIM)
            gain_grad[n : n + 1, pl.ds(line, HEAD_DIM)] += jnp.sum(
                raw * roots[n], axis=0, keepdims=True
            )
    for n in range(2):
        sums_ref[n, pl.ds(step, 1), :] = as_row(sums[n])

    @pl.when(step == SPOTS - 1)
    def _():
        planes, own_rows = own_grad.shape[:2]
        total = sum(
            dot_first(o_v[j * count : (j + 1) * count, :], grads_v[j]) for j in range(SPOTS)
        )
        total_v[...] = total.astype(bf)
        for k in range(planes):
            for ref, c in ((own_grad, meta[1]), (other_grad, 1 - meta[1])):
                at = pl.multiple_of((meta[2 + k] * 2 + c) * own_rows, own_rows)
                ref[k] = total_v[pl.ds(at, own_rows), :]


def attend_backward(
    moves, totals, starts, gains, projected, cos_all, sin_all, heads, out_full, blocks
):
    rows, mine = projected.shape[0], gains.shape[1]
    count = rows // SPOTS
    planes = moves.planes
    own_rows = mine // (2 * planes)
    bf, f32 = jnp.bfloat16, jnp.float32
    meta = jnp.concatenate([jnp.stack([moves.spot, moves.core_id]), moves.planes_back])
    shape = jax.ShapeDtypeStruct
    return pl.pallas_call(
        backward_body,
        grid=(SPOTS,),
        out_shape=[
            shape((rows, mine), f32),
            shape((rows, mine), f32),
            shape((rows, mine), bf),
            shape((2, SPOTS, count), f32),
            shape((planes, own_rows, D), bf),
            shape((planes, own_rows, D), bf),
            shape((2, D), f32),
        ],
        in_specs=[
            SCALARS,
            full_spec(*totals.shape),
            full_spec(*starts.shape),
            full_spec(*gains.shape),
            block_spec(count, 3 * mine),
            block_spec(count, HEAD_DIM),
            block_spec(count, HEAD_DIM),
        ]
        + [block_spec(count, mine)] * 4
        + [full_spec(*out_full.shape)]
        + [ANYWHERE] * SPOTS,
        out_specs=[block_spec(count, mine)] * 3
        + [full_spec(2, SPOTS, count)]
        + [full_spec(planes, own_rows, D)] * 2
        + [full_spec(2, D)],
        scratch_shapes=[
            pltpu.VMEM((SPOTS, count, D), bf),
            pltpu.VMEM((rows, mine), bf),
            pltpu.VMEM((mine, D), bf),
            pltpu.SemaphoreType.DMA((SPOTS,)),
        ],
        compiler_params=params(48),
        cost_estimate=cost(7 * 10**9, 25 << 20),
        name="attend_backward",
    )(
        meta.astype(jnp.int32),
        totals,
        starts,
        gains,
        projected,
        cos_all,
        sin_all,
        *heads,
        out_full,
        *blocks,
    )


def project_back_body(
    planes,
    own_rows,
    meta,
    totals,
    dots,
    gains,
    router_grad,
    small_rows,
    gain_grads,
    second_grad,
    proj_ref,
    dq_ref,
    dk_ref,
    dv_ref,
    a_ref,
    *refs,
):
    dp_ref, own, other, rest = refs[0], refs[1 : 1 + planes], refs[1 + planes], refs[2 + planes]
    a_v, own_v, other_v, riding_v, small, sem, done = refs[3 + planes :]
    bf = jnp.bfloat16
    rows, mine = dv_ref.shape
    count = rows // SPOTS
    fetch = pltpu.make_async_copy(a_ref, a_v, sem.at[0])
    fetch.start()
    for n, ref in enumerate((dq_ref, dk_ref)):
        columns = slice(n * mine, (n + 1) * mine)
        for j in range(SPOTS):
            block = slice(j * count, (j + 1) * count)
            root = root_of(as_column(totals[n, j : j + 1, :]))
            inner = as_column(dots[n, j : j + 1, :])
            grad = root * gains[n : n + 1, :] * ref[block, :]
            grad = grad - proj_ref[block, columns] * (root * root * root * inner / D)
            dp_ref[block, columns] = grad.astype(bf)
    dp_ref[:, 2 * mine :] = dv_ref[...]
    small[...] = jnp.zeros_like(small)
    small[:FIRST_GAIN, :] = router_grad[...]
    small[FIRST_GAIN : FIRST_GAIN + 1, :] = small_rows[FIRST_GAIN : FIRST_GAIN + 1, :]
    small[FIRST_GAIN + 1 : FIRST_GAIN + 3, :] = gain_grads[...]
    small[FIRST_GAIN + 3 : SMALL, :] = second_grad[...]
    turn_by = lax.broadcasted_iota(jnp.int32, (small.shape[0], WIDE), 0) == (
        lax.broadcasted_iota(jnp.int32, (small.shape[0], WIDE), 1)
    )
    riding_v[...] = dot_first(small[...].astype(bf), jnp.where(turn_by, 1.0, 0.0).astype(bf))
    fetch.wait()
    leaving = []
    span = PLANE * own_rows
    for k in [*range(1, planes), 0]:
        plane = meta[2 + k]
        first_row = pl.multiple_of(plane * span, span)
        grads = dot_first(a_v[:, pl.ds(first_row, span)], dp_ref[...])
        for spot in range(SPOTS):
            for c in range(2):
                at = (spot * 2 + c) * own_rows
                grad = grads[at : at + own_rows, :]
                rows_at = pl.ds(pl.multiple_of(first_row + at, own_rows), own_rows)
                riding = riding_v[rows_at, :].astype(bf)

                def put(place, grad=grad, riding=riding):
                    place[:, : 3 * mine] = grad.astype(bf)
                    place[:, 3 * mine :] = riding

                @pl.when(meta[1] == c)
                def _():
                    put(own_v.at[k, spot ^ meta[0]])

                @pl.when(meta[1] != c)
                def _():
                    put(other_v.at[k, spot ^ meta[0]])

        target = other if k == 1 else rest.at[(k - 2) % planes]
        for place, ref in ((own_v, own[k]), (other_v, target)):
            leaving.append(pltpu.make_async_copy(place.at[k], ref, done.at[len(leaving)]))
            leaving[-1].start()
    for copy in leaving:
        copy.wait()


def project_back(moves, totals, dots, gains, small, projected, dq, dk, dv, normed_all):
    rows, mine = dv.shape
    planes = moves.planes
    own_rows = D // (planes * PLANE)
    bf = jnp.bfloat16
    meta = jnp.concatenate([jnp.stack([moves.spot, moves.core_id]), moves.planes_back])
    pieces = (SPOTS, own_rows, 3 * mine + WIDE)
    inputs = (totals, dots, gains, *small, projected, dq, dk, dv)
    return pl.pallas_call(
        functools.partial(project_back_body, planes, own_rows),
        out_shape=[jax.ShapeDtypeStruct((rows, 3 * mine), bf)]
        + [jax.ShapeDtypeStruct(pieces, bf)] * (planes + 1)
        + [jax.ShapeDtypeStruct((planes - 1, *pieces), bf)],
        in_specs=[SCALARS] + [full_spec(*item.shape) for item in inputs] + [ANYWHERE],
        out_specs=[full_spec(rows, 3 * mine)] + [ANYWHERE] * (planes + 2),
        scratch_shapes=[
            pltpu.VMEM((rows, D), bf),
            pltpu.VMEM((planes, *pieces), bf),
            pltpu.VMEM((planes, *pieces), bf),
            pltpu.VMEM((D, WIDE), jnp.float32),
            pltpu.VMEM((32, D), jnp.float32),
            pltpu.SemaphoreType.DMA((2,)),
            pltpu.SemaphoreType.DMA((2 * planes,)),
        ],
        compiler_params=params(60),
        cost_estimate=cost(5 * 10**9, 30 << 20),
        name="project_back",
    )(meta.astype(jnp.int32), *inputs, normed_all)


def rows_back_body(dp_ref, in_w, *parts):
    value = dot_last(dp_ref[...], in_w[:, : dp_ref.shape[1]]).astype(jnp.bfloat16)
    put_by_block(pl.program_id(0), parts, value)


def rows_back(projected_grad, in_full):
    rows, columns = projected_grad.shape
    count = rows // SPOTS
    return pl.pallas_call(
        rows_back_body,
        grid=(SPOTS,),
        out_shape=[jax.ShapeDtypeStruct((count, D), jnp.bfloat16)] * SPOTS,
        in_specs=[block_spec(count, columns), full_spec(*in_full.shape)],
        out_specs=by_block(count, D),
        compiler_params=params(40),
        cost_estimate=cost(5 * 10**9, 12 << 20),
        name="rows_back",
    )(projected_grad, in_full)


def route_body(tokens, home, back, near, match, rank, small, residual_ref, rows_ref, probs_ref):
    bf = jnp.bfloat16
    residual = widen(tokens[...]) + (widen(home[...]) + widen(back[...]) + widen(near[...]))
    residual_ref[...] = residual
    root = lax.rsqrt(jnp.mean(residual * residual, axis=1, keepdims=True) + EPSILON)
    normed = (residual * root * small[FIRST_GAIN + 3 : FIRST_GAIN + 4, :]).astype(bf)
    rows_ref[:, :D] = normed
    experts = match.shape[1]
    logits = dot_last(normed, small[:experts, :].astype(bf))
    exponent = jnp.exp(logits - jnp.max(logits, axis=1, keepdims=True))
    probs = exponent / jnp.sum(exponent, axis=1, keepdims=True)
    chosen = probs * match[...]
    total = jnp.sum(chosen, axis=1, keepdims=True)
    gates = chosen / total
    upper = widen(gates.astype(bf))
    behind = 0.0
    for n, part in enumerate((rank[...], upper.astype(bf), (gates - upper).astype(bf))):
        places = lax.broadcasted_iota(jnp.int32, (experts, WIDE), 0) + n * experts == (
            lax.broadcasted_iota(jnp.int32, (experts, WIDE), 1)
        )
        behind += product(part, jnp.where(places, 1.0, 0.0).astype(bf))
    rows_ref[:, D:] = behind.astype(bf)
    probs_ref[0] = probs
    probs_ref[1] = gates
    probs_ref[2] = jnp.broadcast_to(total, probs.shape)


def route(tokens, home, back, near, match, rank, small):
    count, width = tokens.shape
    experts = match.shape[1]
    inputs = (tokens, home, back, near, match, rank, small)
    shape = jax.ShapeDtypeStruct
    return pl.pallas_call(
        route_body,
        out_shape=[
            shape((count, width), jnp.float32),
            shape((count, width + WIDE), jnp.bfloat16),
            shape((3, count, experts), jnp.float32),
        ],
        in_specs=[full_spec(*item.shape) for item in inputs],
        out_specs=[
            full_spec(count, width),
            full_spec(count, width + WIDE),
            full_spec(3, count, experts),
        ],
        compiler_params=params(40),
        cost_estimate=cost(10**8, 8 << 20),
        name="route",
    )(*inputs)


def route_back_body(total, home, back, near, match, probs_ref, small, residual, upstream, *results):
    grad_ref, branch_ref, router_ref, gain_ref = results
    bf = jnp.bfloat16
    rows = widen(total[...]) + (widen(home[...]) + widen(back[...]) + widen(near[...]))
    experts = match.shape[1]
    probs, gates, gate_total = probs_ref[0], probs_ref[1], probs_ref[2]
    pairs = lax.broadcasted_iota(jnp.int32, (WIDE, experts), 0) // 2 == (
        lax.broadcasted_iota(jnp.int32, (WIDE, experts), 1)
    )
    gate_grad = product(rows[:, D:].astype(bf), jnp.where(pairs, 1.0, 0.0).astype(bf))
    inner = jnp.sum(gate_grad * gates, axis=1, keepdims=True)
    chosen_grad = match[...] * (gate_grad - inner) / gate_total
    inner = jnp.sum(chosen_grad * probs, axis=1, keepdims=True)
    logit_grad = (probs * (chosen_grad - inner)).astype(bf)
    normed_grad = rows[:, :D] + product(logit_grad, small[:experts, :].astype(bf))
    gain = small[FIRST_GAIN + 3 : FIRST_GAIN + 4, :]
    value = residual[...]
    root = lax.rsqrt(jnp.mean(value * value, axis=1, keepdims=True) + EPSILON)
    normed = (value * root * gain).astype(bf)
    router_ref[...] = dot_first(logit_grad, normed)
    scaled = normed_grad * value
    gain_ref[...] = jnp.sum(scaled * root, axis=0, keepdims=True)
    inner = jnp.mean(scaled * gain, axis=1, keepdims=True)
    grad = widen(upstream[...]) + root * gain * normed_grad - value * (root * root * root * inner)
    grad_ref[...] = grad
    branch_ref[...] = grad.astype(bf)


def route_back(total, home, back, near, match, probs, small, residual, upstream):
    count, width = residual.shape
    experts = match.shape[1]
    inputs = (total, home, back, near, match, probs, small, residual, upstream)
    shape = jax.ShapeDtypeStruct
    return pl.pallas_call(
        route_back_body,
        out_shape=[
            shape((count, width), jnp.float32),
            shape((count, width), jnp.bfloat16),
            shape((experts, width), jnp.float32),
            shape((1, width), jnp.float32),
        ],
        in_specs=[full_spec(*item.shape) for item in inputs],
        out_specs=[
            full_spec(count, width),
            full_spec(count, width),
            full_spec(experts, width),
            full_spec(1, width),
        ],
        compiler_params=params(40),
        cost_estimate=cost(10**8, 10 << 20),
        name="route_back",
    )(*inputs)


def shards_dense(
    tokens,
    cotangent,
    norm_gains,
    attention_in,
    attention_out,
    router_weight,
    expert_in,
    expert_out,
    routes,
    lengths,
):
    row_count = tokens.shape[0]
    devices_count = lax.axis_size("fsdp")
    moves = Moves(devices_count)
    planes, core, spot = moves.planes, moves.core_id, moves.spot
    ring, first, second, cores = moves.ring, moves.first, moves.second, moves.core
    experts = devices_count // 2
    choose = routes.shape[1]
    capacity = 4 * row_count * choose // (3 * experts)
    bf, f32 = jnp.bfloat16, jnp.float32
    own_rows = attention_in.shape[0]
    lines = HEADS // SPOTS
    mine = lines * HEAD_DIM

    def low(value):
        return value.astype(bf)

    pieces = split_columns(spot, attention_in, router_weight, norm_gains, lengths)
    traded = [pieces[0]] + [send(pieces[m], moves.spots[m]) for m in range(1, SPOTS)]
    own_1 = send(cotangent, ring)
    tokens_then, traded, own_1 = tie(tokens, traded, own_1)

    in_own = [jnp.stack(traded)]
    in_own.append(send(in_own[0], ring))
    in_other = [send(in_own[0], cores)]
    near_x = send(tokens_then, first)
    near_0 = send(cotangent, first)
    in_own, in_other, near_x = tie(in_own, in_other, near_x)

    in_own.append(send(in_own[1], ring))
    in_other.append(send(in_own[1], cores))
    blocks_x = [tokens, near_x, send(tokens, second), send(near_x, second)]
    in_own, in_other, blocks_x, near_0 = tie(in_own, in_other, blocks_x, near_0)

    in_own.append(send(in_own[2], ring))
    in_other.append(send(in_own[2], cores))
    out_own = [attention_out, send(attention_out, ring)]
    out_other = [send(attention_out, cores)]
    grads = {(0, 0): [cotangent, near_0], (1, 0): [own_1, send(own_1, first)]}
    columns = 3 * mine
    lengths_all = jnp.stack([piece[: lengths.shape[1], columns + SMALL] for piece in traded])
    lengths_all = jnp.where(core == 0, lengths_all, lengths_all[jnp.asarray([0, 2, 1, 3])])
    places = jnp.arange(row_count, dtype=jnp.int32)
    _, position = jax.vmap(lambda item: layout(item, row_count))(lengths_all.astype(jnp.int32))
    starts = (places[None] - position).astype(f32)
    cos_half, sin_half = (table[:, 0] for table in tables(position.reshape(-1)))
    cos_all = jnp.concatenate([cos_half, cos_half], axis=1)
    sin_all = jnp.concatenate([-sin_half, sin_half], axis=1)

    expert_ids = jnp.arange(experts, dtype=jnp.int32)
    match = jnp.sum((routes[:, :, None] == expert_ids[None, None, :]).astype(f32), axis=1)
    before = (places[:, None] > places[None, :]).astype(bf)
    rank = jnp.where(match > 0, product(before, match.astype(bf)), -1.0).astype(bf)
    in_own, in_other, out_other, grads[1, 0], starts, cos_all, sin_all, rank = tie(
        in_own, in_other, out_other, grads[1, 0], starts, cos_all, sin_all, rank
    )

    in_other.append(send(in_own[3], cores))
    in_other, out_own = tie(in_other, out_own)
    out_own.append(send(out_own[1], ring))
    out_other.append(send(out_own[1], cores))
    grads[0, 1] = [send(item, second) for item in grads[0, 0]]
    projected, normed_all, in_full, sums, small_rows, gains = project(
        moves, blocks_x, in_own, in_other
    )
    sums, out_own, out_other, grads = tie(sums, out_own, out_other, grads)
    out_own.append(send(out_own[2], ring))
    out_other.append(send(out_own[2], cores))
    sums = plane_step(moves, by_spot(moves, sums), 1)
    sums, own_1 = tie(sums, own_1)
    totals = by_spot(moves, plane_step(moves, sums, 2))
    totals, out_own, out_other = tie(totals, out_own, out_other)
    out_other.append(send(out_own[3], cores))
    totals, out_other, grads, own_1 = tie(totals, out_other, grads, own_1)

    own_2 = send(own_1, ring)
    grads[1, 1] = [send(item, second) for item in grads[1, 0]]
    weights = [expert_in[0], send(expert_in[0], cores), expert_out[0], send(expert_out[0], cores)]
    attention = (moves, totals, starts, gains, projected, cos_all, sin_all)
    results = attend_forward(*attention, out_own, out_other)
    heads, out_full, parts = results[:4], results[4], results[5:]
    parts, weights, own_2, grads = tie(parts, weights, own_2, grads)

    def cross(parts):
        return [send(parts[2], second), send(parts[3], second)]

    def gather_near(parts, backs):
        near = low(widen(parts[1]) + widen(backs[1]))
        return widen(parts[0]) + widen(backs[0]), send(near, first)

    backs = cross(parts)
    own_3 = send(own_2, ring)
    backs, parts, near_1 = tie(backs, parts, grads[1, 0][1])
    near = send(low(widen(parts[1]) + widen(backs[1])), first)
    near_2 = send(near_1, ring)
    near, own_3 = tie(near, own_3)
    grads[2, 0] = [own_2, near_2]
    residual, rows, probs = route(tokens, parts[0], backs[0], near, match, rank, small_rows)
    rows, near_2 = tie(rows, near_2)

    meta = (moves.device // 2).reshape(1).astype(jnp.int32)
    saved, done = None, 0
    row_parts, out_parts = {}, {}

    def run_expert(group, which, blocks):
        nonlocal saved, done
        saved, outs, backs = expert_blocks(
            meta,
            blocks,
            grads[group, which],
            weights,
            saved,
            done,
            planes * SPOTS,
            capacity,
            experts,
        )
        done += len(blocks)
        out_parts.setdefault(group, []).extend(outs)
        row_parts.setdefault(group, []).extend(backs)

    row_near = send(rows, first)
    row_1 = send(rows, ring)
    rows, row_near = tie(rows, row_near)

    near_row_1 = send(row_near, ring)
    across = [send(rows, second), send(row_near, second)]
    run_expert(0, 0, [rows, row_near])
    saved, across, row_1 = tie(saved, across, row_1)

    row_2 = send(row_1, ring)
    across_row_1 = send(row_1, second)
    across_2 = send(own_2, second)
    near_3 = send(near_2, ring)
    run_expert(0, 1, across)
    saved, near_row_1, across_row_1, across_2 = tie(saved, near_row_1, across_row_1, across_2)

    near_row_2 = send(near_row_1, ring)
    across = [across_row_1, send(near_row_1, second)]
    grads[2, 0], grads[2, 1] = [own_2, near_2], [across_2, send(near_2, second)]
    run_expert(1, 0, [row_1, near_row_1])
    saved, across, row_2, grads[2, 1] = tie(saved, across, row_2, grads[2, 1])

    row_3 = send(row_2, ring)
    across_row_2 = send(row_2, second)
    across_3 = send(own_3, second)
    run_expert(1, 1, across)
    saved, near_row_2, across_row_2, across_3 = tie(saved, near_row_2, across_row_2, across_3)

    near_row_3 = send(near_row_2, ring)
    across = [across_row_2, send(near_row_2, second)]
    backs_1 = cross(row_parts[1])
    run_expert(2, 0, [row_2, near_row_2])
    saved, across, row_3, near_3 = tie(saved, across, row_3, near_3)

    grads[3, 0] = [own_3, near_3]
    across_row_3 = send(row_3, second)
    grads[3, 1] = [across_3, send(near_3, second)]
    run_expert(2, 1, across)
    saved, near_row_3, across_row_3, backs_1 = tie(saved, near_row_3, across_row_3, backs_1)

    across = [across_row_3, send(near_row_3, second)]
    run_expert(3, 0, [row_3, near_row_3])
    saved, across, grads[3, 1], row_parts = tie(saved, across, grads[3, 1], row_parts)

    pair = [send(low(widen(row_parts[1][n]) + widen(backs_1[n])), ring) for n in range(2)]
    backs_2 = cross(row_parts[2])
    run_expert(3, 1, across)
    saved, pair, backs_2 = tie(saved, pair, backs_2)

    near = send(low(widen(pair[1]) + widen(row_parts[2][1]) + widen(backs_2[1])), first)
    home = widen(pair[0]) + (widen(row_parts[2][0]) + widen(backs_2[0]))
    backs_3 = cross(row_parts[3])
    x_rows, dy_rows, m_own, m_other, du_own, du_other = saved
    in_theirs = dot_first(x_rows, du_other)
    home, near, backs_3, in_theirs, row_parts[0] = tie(
        home, near, backs_3, in_theirs, row_parts[0]
    )

    total = send(low(home + widen(near)), ring)
    home, near = gather_near(row_parts[3], backs_3)
    in_theirs = send(in_theirs, cores)
    backs_0 = cross(row_parts[0])
    out_theirs = dot_first(m_other, dy_rows)
    total, home, near, out_theirs = tie(total, home, near, out_theirs)

    total = send(low(widen(total) + (home + widen(near))), ring)
    _, near_0 = gather_near(row_parts[0], backs_0)
    out_theirs = send(out_theirs, cores)
    out_backs = {1: cross(out_parts[1])}
    total, near_0 = tie(total, near_0)
    residual_grad, branch_grad, router_grad, second_gain_grad = route_back(
        total, row_parts[0][0], backs_0[0], near_0, match, probs, small_rows, residual, cotangent
    )
    branch_near = send(branch_grad, first)
    branch_grad, branch_near, out_parts = tie(branch_grad, branch_near, out_parts)

    branch_blocks = [
        branch_grad,
        branch_near,
        send(branch_grad, second),
        send(branch_near, second),
    ]
    out_pair = [
        send(low(widen(out_parts[1][n]) + widen(out_backs[1][n])), ring) for n in range(2)
    ]
    expert_out_grad = dot_first(m_own, dy_rows) + out_theirs
    branch_blocks, expert_out_grad, out_parts = tie(branch_blocks, expert_out_grad, out_parts)

    out_backs[2] = cross(out_parts[2])
    dq, dk, dv, dots, own_grad, other_grad, gain_grads = attend_backward(
        *attention, heads, out_full, branch_blocks
    )
    dots, out_backs, out_parts, out_pair, other_grad = tie(
        dots, out_backs, out_parts, out_pair, other_grad
    )

    other_grad = send(other_grad, cores)
    out_near = send(
        low(widen(out_pair[1]) + widen(out_parts[2][1]) + widen(out_backs[2][1])), first
    )
    dots = plane_step(moves, by_spot(moves, dots), 1)
    dots, other_grad = tie(dots, other_grad)

    def out_sum(step):
        return widen(own_grad[step]) + widen(other_grad[step])

    out_share = send(low(out_sum(1)), ring)
    dots = by_spot(moves, plane_step(moves, dots, 2))
    dots, out_share, out_near, out_parts, out_pair = tie(
        dots, out_share, out_near, out_parts, out_pair
    )
    out_total = low(
        widen(out_pair[0])
        + (widen(out_parts[2][0]) + widen(out_backs[2][0]))
        + widen(out_near)
    )
    out_total = send(out_total, ring)
    out_backs[3] = cross(out_parts[3])
    small = (router_grad, small_rows, gain_grads, second_gain_grad)
    projected_grad, *in_grads = project_back(
        moves, totals, dots, gains, small, projected, dq, dk, dv, normed_all
    )
    in_grads, projected_grad, out_share, out_parts, out_total, out_backs[3] = tie(
        in_grads, projected_grad, out_share, out_parts, out_total, out_backs[3]
    )

    *in_grads, others, others_rest = in_grads
    others = send(others, cores)
    projected_grad, in_full, others = tie(projected_grad, in_full, others)
    in_total = send(low(widen(in_grads[1]) + widen(others)), ring)
    others_rest = send(others_rest, cores)
    out_share = send(low(widen(out_share) + out_sum(2)), ring)
    out_backs[0] = cross(out_parts[0])
    parts = rows_back(projected_grad, in_full)
    in_total, others_rest, parts, x_rows, out_share, out_parts, out_backs = tie(
        in_total, others_rest, parts, x_rows, out_share, out_parts, out_backs
    )

    in_total = send(low(widen(in_total) + (widen(in_grads[2]) + widen(others_rest[0]))), ring)
    backs = cross(parts)
    expert_in_grad = dot_first(x_rows, du_own) + in_theirs
    in_total, backs, expert_in_grad, out_parts, out_share = tie(
        in_total, backs, expert_in_grad, out_parts, out_share
    )

    in_total = send(low(widen(in_total) + (widen(in_grads[3]) + widen(others_rest[1]))), ring)
    home, near = gather_near(parts, backs)
    out_home_3, out_near_3 = gather_near(out_parts[3], out_backs[3])
    out_share = send(low(widen(out_share) + out_sum(3)), ring)
    out_home, out_near = gather_near(out_parts[0], out_backs[0])
    in_total, home, near, out_home_3, out_near_3, out_share = tie(
        in_total, home, near, out_home_3, out_near_3, out_share
    )

    in_total = low(widen(in_total) + (widen(in_grads[0]) + widen(others_rest[2])))
    traded = [in_total[0]] + [send(in_total[m], moves.spots[m]) for m in range(1, SPOTS)]
    out_total = send(low(widen(out_total) + (out_home_3 + widen(out_near_3))), ring)
    out_share = widen(out_share) + out_sum(0)
    _, first_back = jax.vjp(
        lambda value: root_norm(value, small_rows[FIRST_GAIN]), widen(tokens)
    )
    (input_norm_grad,) = first_back(home + widen(near))
    input_grad = residual_grad + input_norm_grad
    traded, input_grad, out_share, out_home, out_near = tie(
        traded, input_grad, out_share, out_home, out_near
    )
    in_share, small_share = join_columns(spot, traded, attention_in, norm_gains)
    out_total, in_share, out_near = tie(out_total, in_share, out_near)
    output = low(residual + (widen(out_total) + (out_home + widen(out_near))))
    return (
        output,
        input_grad,
        small_share[:, FIRST_GAIN:SMALL].T,
        in_share,
        out_share,
        small_share[:, :FIRST_GAIN],
        expert_in_grad[None],
        expert_out_grad[None],
    )


def shards(*arguments):
    routes = arguments[8]
    experts = lax.axis_size("fsdp") // 2
    if 2 * routes.shape[1] >= experts and HEADS == experts:
        return shards_dense(*arguments)
    return shards_routed(*arguments)


def solution(mesh):
    in_specs = (
        P("fsdp", None),
        P("fsdp", None),
        P(None, "fsdp"),
        P("fsdp", None),
        P("fsdp", None),
        P("fsdp", None),
        P("fsdp", None, None),
        P("fsdp", None, None),
        P("fsdp", None),
        P("fsdp", None),
    )
    out_specs = (
        P("fsdp", None),
        P("fsdp", None),
        P(None, "fsdp"),
        P("fsdp", None),
        P("fsdp", None),
        P("fsdp", None),
        P("fsdp", None, None),
        P("fsdp", None, None),
    )
    return jax.shard_map(shards, mesh=mesh, in_specs=in_specs, out_specs=out_specs, check_vma=False)
```

```python
import functools

import jax
import jax.numpy as jnp
from jax import lax
from jax.experimental import pallas as pl
from jax.experimental.pallas import tpu as pltpu
from jax.sharding import PartitionSpec as P

D = 2048
HEADS = 16
HEAD_DIM = 128


EPSILON = 1e-05
ROPE_BASE = 10000.0
MASKED = -1000000000.0


def root_norm(vector, scaling):
    return vector * lax.rsqrt(jnp.mean(vector * vector, axis=-1, keepdims=True) + EPSILON) * scaling


def rotary(vector, cos_table, sin_table):
    half_dim = vector.shape[-1] // 2
    first = vector[..., :half_dim]
    second = vector[..., half_dim:]
    return jnp.concatenate(
        [first * cos_table - second * sin_table, second * cos_table + first * sin_table], axis=-1
    )


def layout(lengths, number):
    ends_at = jnp.cumsum(lengths)
    places = jnp.arange(number, dtype=jnp.int32)
    segment = jnp.sum((places[:, None] >= ends_at[None, :]).astype(jnp.int32), axis=1)
    starts = ends_at - lengths
    select_mask = (
        segment[:, None] == jnp.arange(lengths.shape[0], dtype=jnp.int32)[None, :]
    ).astype(jnp.int32)
    position = places - jnp.sum(select_mask * starts[None, :], axis=1)
    return (segment, position)


def tables(position):
    half_dim = HEAD_DIM // 2
    inverse = ROPE_BASE ** (-2.0 * jnp.arange(half_dim, dtype=jnp.float32) / HEAD_DIM)
    angles = position.astype(jnp.float32)[:, None] * inverse[None, :]
    return (jnp.cos(angles)[:, None, :], jnp.sin(angles)[:, None, :])


def prepare(projected, query_gain, key_gain, cos_table, sin_table):
    count_rows = projected.shape[0]
    query_heads = root_norm(projected[:, :D], query_gain).reshape(count_rows, HEADS, HEAD_DIM)
    key_heads = root_norm(projected[:, D : 2 * D], key_gain).reshape(count_rows, HEADS, HEAD_DIM)
    value_heads = projected[:, 2 * D :].reshape(count_rows, HEADS, HEAD_DIM)
    return (
        rotary(query_heads, cos_table, sin_table),
        rotary(key_heads, cos_table, sin_table),
        value_heads,
    )


def softmax_rows(logits):
    row_max = jnp.max(logits, axis=-1, keepdims=True)
    exponent = jnp.exp(logits - row_max)
    return exponent / jnp.sum(exponent, axis=-1, keepdims=True)


def dot_first(left, right):
    return lax.dot_general(
        left, right, (((0,), (0,)), ((), ())), preferred_element_type=jnp.float32
    )


def dot_last(left, right):
    return lax.dot_general(
        left, right, (((1,), (1,)), ((), ())), preferred_element_type=jnp.float32
    )


def shards_routed(
    tokens,
    cotangent,
    norm_gains,
    attention_in,
    attention_out,
    router_weight,
    expert_in,
    expert_out,
    routes,
    lengths,
):
    row_count = tokens.shape[0]
    devices_count = lax.axis_size("fsdp")
    experts = devices_count // 2
    choose = routes.shape[1]
    half_units = expert_out.shape[1]
    capacity = 4 * row_count * choose // (3 * experts)
    scaling = HEAD_DIM ** (-0.5)
    gain_full, gathered_in, gathered_out, gathered_router = (
        lax.all_gather(norm_gains, "fsdp", axis=1, tiled=True),
        lax.all_gather(attention_in, "fsdp", axis=0, tiled=True),
        lax.all_gather(attention_out, "fsdp", axis=0, tiled=True),
        lax.all_gather(router_weight, "fsdp", axis=0, tiled=True),
    )
    gain_rows = gain_full.astype(jnp.float32)
    segment, position = layout(lengths[0], row_count)
    cos_table, sin_table = tables(position)
    places = jnp.arange(row_count, dtype=jnp.int32)
    allowed = ((segment[:, None] == segment[None, :]) & (places[:, None] >= places[None, :]))[None]
    inputs = tokens.astype(jnp.float32)
    normed_input = root_norm(inputs, gain_rows[0]).astype(jnp.bfloat16)
    projected = jnp.dot(normed_input, gathered_in, preferred_element_type=jnp.float32)

    def prepare_local(projected_value, query_gain, key_gain):
        return prepare(projected_value, query_gain, key_gain, cos_table, sin_table)

    (query_f, key_f, value_f), prepare_back = jax.vjp(
        prepare_local, projected, gain_rows[1], gain_rows[2]
    )
    query_heads = query_f.astype(jnp.bfloat16)
    key_heads = key_f.astype(jnp.bfloat16)
    value_heads = value_f.astype(jnp.bfloat16)

    def score_block():
        raw_scores = (
            jnp.einsum("qhd,khd->hqk", query_heads, key_heads, preferred_element_type=jnp.float32)
            * scaling
        )
        return jnp.where(allowed, raw_scores, MASKED)

    scores = score_block()
    row_max = jnp.max(scores, axis=-1, keepdims=True)
    exponent = jnp.exp(scores - row_max)
    row_sum = jnp.sum(exponent, axis=-1, keepdims=True)
    log_total = row_max + jnp.log(row_sum)
    attend_probs = (exponent / row_sum).astype(jnp.bfloat16)
    attended = (
        jnp.einsum("hqk,khd->qhd", attend_probs, value_heads, preferred_element_type=jnp.float32)
        .reshape(row_count, D)
        .astype(jnp.bfloat16)
    )
    branch_out = jnp.dot(attended, gathered_out, preferred_element_type=jnp.float32)
    residual = inputs + branch_out
    normed = root_norm(residual, gain_rows[3]).astype(jnp.bfloat16)
    logits = jnp.dot(normed, gathered_router, preferred_element_type=jnp.float32)
    router_probs = softmax_rows(logits)
    chosen = jnp.take_along_axis(router_probs, routes, axis=1)
    gate_total = jnp.sum(chosen, axis=1, keepdims=True)
    gate_values = chosen / gate_total
    flat_routes = routes.reshape(-1)
    route_hits = (flat_routes[:, None] == jnp.arange(experts, dtype=jnp.int32)[None, :]).astype(
        jnp.int32
    )
    slot_index = jnp.sum((jnp.cumsum(route_hits, axis=0) - route_hits) * route_hits, axis=1)
    target = flat_routes * capacity + slot_index
    owner_token = (
        jnp.zeros((experts * capacity,), jnp.int32)
        .at[target]
        .set(jnp.arange(row_count * choose, dtype=jnp.int32) // choose)
    )
    filled = (
        jnp.zeros((experts * capacity,), jnp.bfloat16)
        .at[target]
        .set(jnp.ones((row_count * choose,), jnp.bfloat16))
    )
    outgoing = jnp.repeat(
        (normed[owner_token] * filled[:, None]).reshape(experts, capacity, D), 2, axis=0
    )
    arrived = lax.all_to_all(outgoing, "fsdp", split_axis=0, concat_axis=0, tiled=True).reshape(
        devices_count * capacity, D
    )
    gate_up_out = jnp.dot(arrived, expert_in[0], preferred_element_type=jnp.float32)
    gate_part = gate_up_out[:, :half_units]
    up_part = gate_up_out[:, half_units:]
    hidden_f, swiglu_back = jax.vjp(
        lambda gate_in, up_in: jax.nn.silu(gate_in) * up_in, gate_part, up_part
    )
    hidden = hidden_f.astype(jnp.bfloat16)
    produced = (
        jnp.dot(hidden, expert_out[0], preferred_element_type=jnp.float32)
        .astype(jnp.bfloat16)
        .reshape(devices_count, capacity, D)
    )
    returned = (
        lax.all_to_all(produced, "fsdp", split_axis=0, concat_axis=0, tiled=True)
        .reshape(experts, 2, capacity, D)
        .astype(jnp.float32)
    )
    returned = jnp.sum(returned, axis=1).reshape(experts * capacity, D)
    picked = returned[target].reshape(row_count, choose, D)
    expert_sum = jnp.sum(gate_values[:, :, None] * picked, axis=1)
    output = (residual + expert_sum).astype(jnp.bfloat16)
    back_in, back_out, back_router = (
        lax.all_gather(attention_in, "fsdp", axis=0, tiled=True),
        lax.all_gather(attention_out, "fsdp", axis=0, tiled=True),
        lax.all_gather(router_weight, "fsdp", axis=0, tiled=True),
    )
    upstream = cotangent.astype(jnp.float32)
    gate_grad = jnp.sum(upstream[:, None, :] * picked, axis=2)
    send_grad = (
        (gate_values[:, :, None] * upstream[:, None, :])
        .astype(jnp.bfloat16)
        .reshape(row_count * choose, D)
    )
    grad_buffer = (
        jnp.zeros((experts * capacity, D), jnp.bfloat16)
        .at[target]
        .set(send_grad)
        .reshape(experts, capacity, D)
    )
    grad_buffer = jnp.repeat(grad_buffer, 2, axis=0)
    grad_arrived = lax.all_to_all(
        grad_buffer, "fsdp", split_axis=0, concat_axis=0, tiled=True
    ).reshape(devices_count * capacity, D)
    grad_hidden = dot_last(grad_arrived, expert_out[0])
    expert_out_grad = dot_first(hidden, grad_arrived)
    grad_gate, grad_up = swiglu_back(grad_hidden)
    grad_gate_up = jnp.concatenate([grad_gate, grad_up], axis=1).astype(jnp.bfloat16)
    expert_in_grad = dot_first(arrived, grad_gate_up)
    grad_rows = (
        dot_last(grad_gate_up, expert_in[0])
        .astype(jnp.bfloat16)
        .reshape(devices_count, capacity, D)
    )
    grad_back = (
        lax.all_to_all(grad_rows, "fsdp", split_axis=0, concat_axis=0, tiled=True)
        .reshape(experts, 2, capacity, D)
        .astype(jnp.float32)
    )
    grad_back = jnp.sum(grad_back, axis=1).reshape(experts * capacity, D)
    dispatch_grad = jnp.sum(grad_back[target].reshape(row_count, choose, D), axis=1)
    chosen_grad = (gate_grad - jnp.sum(gate_grad * gate_values, axis=1, keepdims=True)) / gate_total
    expert_match = (
        routes[:, :, None] == jnp.arange(experts, dtype=jnp.int32)[None, None, :]
    ).astype(jnp.float32)
    prob_grad = jnp.sum(expert_match * chosen_grad[:, :, None], axis=1)
    logit_grad = (
        router_probs * (prob_grad - jnp.sum(prob_grad * router_probs, axis=1, keepdims=True))
    ).astype(jnp.bfloat16)
    router_grad = dot_first(normed, logit_grad)
    normed_grad = dispatch_grad + dot_last(logit_grad, back_router)
    _, second_back = jax.vjp(root_norm, residual, gain_rows[3])
    residual_norm_grad, second_gain_grad = second_back(normed_grad)
    residual_grad = upstream + residual_norm_grad
    branch_grad = residual_grad.astype(jnp.bfloat16)
    out_grad = dot_first(attended, branch_grad)
    attended_grad = (
        dot_last(branch_grad, back_out).astype(jnp.bfloat16).reshape(row_count, HEADS, HEAD_DIM)
    )
    recomputed = jnp.exp(score_block() - log_total)
    value_grad = jnp.einsum(
        "hqk,qhd->khd", attend_probs, attended_grad, preferred_element_type=jnp.float32
    )
    attend_grad = jnp.einsum(
        "qhd,khd->hqk", attended_grad, value_heads, preferred_element_type=jnp.float32
    )
    row_delta = jnp.sum(recomputed * attend_grad, axis=-1, keepdims=True)
    score_grad = (recomputed * (attend_grad - row_delta)).astype(jnp.bfloat16)
    query_grad = (
        jnp.einsum("hqk,khd->qhd", score_grad, key_heads, preferred_element_type=jnp.float32)
        * scaling
    )
    key_grad = (
        jnp.einsum("hqk,qhd->khd", score_grad, query_heads, preferred_element_type=jnp.float32)
        * scaling
    )
    projected_grad, query_gain_grad, key_gain_grad = prepare_back(
        (query_grad, key_grad, value_grad)
    )
    projected_grad = projected_grad.astype(jnp.bfloat16)
    attention_in_grad = dot_first(normed_input, projected_grad)
    normed_input_grad = dot_last(projected_grad, back_in)
    _, first_back = jax.vjp(root_norm, inputs, gain_rows[0])
    input_norm_grad, first_gain_grad = first_back(normed_input_grad)
    input_grad = residual_grad + input_norm_grad
    gains_grad = jnp.stack([first_gain_grad, query_gain_grad, key_gain_grad, second_gain_grad])
    gains_share, in_share, out_share, router_share = (
        lax.psum_scatter(gains_grad, "fsdp", scatter_dimension=1, tiled=True),
        lax.psum_scatter(attention_in_grad, "fsdp", scatter_dimension=0, tiled=True),
        lax.psum_scatter(out_grad, "fsdp", scatter_dimension=0, tiled=True),
        lax.psum_scatter(router_grad, "fsdp", scatter_dimension=0, tiled=True),
    )
    return (
        output,
        input_grad,
        gains_share,
        in_share,
        out_share,
        router_share,
        expert_in_grad[None],
        expert_out_grad[None],
    )


def product(left, right):
    return jnp.dot(left, right, preferred_element_type=jnp.float32)


def widen(value):
    return value.astype(jnp.float32)


PLANE = 8
SPOTS = 4
WIDE = 128
SMALL = 20
FIRST_GAIN = SMALL - 4


class Moves:
    def __init__(self, count):
        planes = count // PLANE
        order = list(range(0, planes, 2)) + list(range(1, planes, 2))[::-1]
        after = {order[i]: order[(i + 1) % planes] for i in range(planes)}
        self.planes = planes
        self.ring = [(i, after[i // PLANE] * PLANE + i % PLANE) for i in range(count)]
        self.first = [(i, i ^ (4 if i & 1 else 2)) for i in range(count)]
        self.second = [(i, i ^ (2 if i & 1 else 4)) for i in range(count)]
        self.core = [(i, i ^ 1) for i in range(count)]
        self.spots = [[(i, i ^ (2 * mask)) for i in range(count)] for mask in range(SPOTS)]
        device = lax.axis_index("fsdp")
        self.device = device
        self.plane, self.spot, self.core_id = device // PLANE, device % PLANE // 2, device % 2
        rank = jnp.asarray([order.index(i) for i in range(planes)], jnp.int32)
        self.planes_back = jnp.asarray(order, jnp.int32)[
            (rank[self.plane] - jnp.arange(planes, dtype=jnp.int32)) % planes
        ]
        self.steps_from = (rank[self.plane] - rank) % planes
        self.group_spots = self.spot ^ jnp.where(
            self.core_id == 0, jnp.asarray([0, 1, 2, 3]), jnp.asarray([0, 2, 1, 3])
        )


def send(value, pairs):
    return lax.ppermute(value, "fsdp", pairs)


def tie(*values):
    return lax.optimization_barrier(values)


def by_spot(moves, parts):
    return jnp.where(moves.core_id == 0, parts, parts[:, jnp.asarray([0, 2, 1, 3])])


def plane_step(moves, parts, bit):
    other = send(parts, moves.spots[bit])
    return parts + jnp.stack([other[:, m ^ bit] for m in range(SPOTS)], axis=1)


def full_spec(*dims):
    return pl.BlockSpec(dims, lambda *_: (0,) * len(dims))


SCALARS = pl.BlockSpec(memory_space=pltpu.SMEM)
ANYWHERE = pl.BlockSpec(memory_space=pl.ANY)


def params(mebibytes):
    return pltpu.CompilerParams(vmem_limit_bytes=mebibytes << 20)


def cost(flops, moved, special=0):
    return pl.CostEstimate(
        flops=flops // 2, bytes_accessed=moved // 2, transcendentals=special // 2
    )


def column_places(spot, mask, lines):
    for part in range(3):
        for line in range(lines):
            piece = (part * lines + line) * HEAD_DIM
            whole = ((part * lines + line) * SPOTS + (spot ^ mask)) * HEAD_DIM
            yield pl.ds(pl.multiple_of(whole, HEAD_DIM), HEAD_DIM), pl.ds(piece, HEAD_DIM)


def split_body(lines, spot, lengths, whole_ref, router_ref, gains_ref, *pieces):
    rows, columns = pieces[0].shape[0], pieces[0].shape[1] - WIDE
    routers = router_ref.shape[1]
    lane = lax.broadcasted_iota(jnp.int32, (rows, WIDE), 1)
    row = lax.broadcasted_iota(jnp.int32, (rows, WIDE), 0)
    spread = lax.broadcasted_iota(jnp.int32, (routers, WIDE), 0) == lax.broadcasted_iota(
        jnp.int32, (routers, WIDE), 1
    )
    riding = product(router_ref[...], jnp.where(spread, 1.0, 0.0).astype(jnp.bfloat16))
    for n in range(gains_ref.shape[0]):
        column = as_column(widen(gains_ref[...])[n : n + 1, :])
        riding = jnp.where(lane == FIRST_GAIN + n, column, riding)
    for n in range(lengths.shape[1]):
        riding = jnp.where((lane == SMALL) & (row == n), lengths[0, n].astype(jnp.float32), riding)
    for mask, piece in enumerate(pieces):
        for whole_at, piece_at in column_places(spot[0], mask, lines):
            piece[:, piece_at] = whole_ref[:, whole_at]
        piece[:, columns:] = riding.astype(jnp.bfloat16)


def split_columns(spot, whole, router, gains, lengths):
    rows, columns = whole.shape
    columns = columns // SPOTS + WIDE
    return pl.pallas_call(
        functools.partial(split_body, HEADS // SPOTS),
        out_shape=[jax.ShapeDtypeStruct((rows, columns), whole.dtype)] * SPOTS,
        in_specs=[
            SCALARS,
            SCALARS,
            full_spec(*whole.shape),
            full_spec(*router.shape),
            full_spec(*gains.shape),
        ],
        out_specs=[full_spec(rows, columns)] * SPOTS,
        compiler_params=params(60),
        name="split_columns",
    )(spot.reshape(1), lengths, whole, router, gains)


def join_body(lines, meta, *refs):
    *pieces, weights, gains, whole_ref, small_ref = refs
    for mask, piece in enumerate(pieces):
        for whole_at, piece_at in column_places(meta[0], mask, lines):
            whole_ref[:, whole_at] = widen(piece[:, piece_at])
    small = sum(widen(piece[:, piece.shape[1] - WIDE :]) for piece in pieces)
    lane = lax.broadcasted_iota(jnp.int32, small.shape, 1)
    gain = as_column(widen(gains[...])[0:1, :])
    gain_grad = jnp.sum(whole_ref[...] * widen(weights[...]), axis=1, keepdims=True)
    small_ref[...] = jnp.where(lane == FIRST_GAIN, gain_grad / gain, small)


def join_columns(spot, pieces, weights, gains):
    rows, wide = pieces[0].shape
    columns = wide - WIDE
    return pl.pallas_call(
        functools.partial(join_body, HEADS // SPOTS),
        out_shape=[
            jax.ShapeDtypeStruct((rows, columns * SPOTS), jnp.float32),
            jax.ShapeDtypeStruct((rows, WIDE), jnp.float32),
        ],
        in_specs=[SCALARS] + [full_spec(rows, wide)] * SPOTS
        + [full_spec(*weights.shape), full_spec(*gains.shape)],
        out_specs=[full_spec(rows, columns * SPOTS), full_spec(rows, WIDE)],
        compiler_params=params(60),
        name="join_columns",
    )(spot.reshape(1), *pieces, weights, gains)


def expert_body(index, cap, experts, blocks, meta, *refs):
    row_refs, grad_refs, weights = refs[:blocks], refs[blocks : 2 * blocks], refs[2 * blocks :][:4]
    refs = refs[2 * blocks + 4 + 6 :]
    saves, out_parts, row_parts = refs[:6], refs[6 : 6 + blocks], refs[6 + blocks :][:blocks]
    rows_v, grads_v, in_v, out_v, x_v, dy_v, m_v, du_v, part_v, back_v, sem, done = refs[
        6 + 2 * blocks :
    ]
    bf, f32 = jnp.bfloat16, jnp.float32
    count, width, half = rows_v.shape[1], grads_v.shape[2], out_v.shape[1]
    expert = meta[0]

    def fetch(ref, place, n):
        copy = pltpu.make_async_copy(ref, place, sem.at[n])
        copy.start()
        return copy

    fetch_rows = [fetch(ref, rows_v.at[j], j) for j, ref in enumerate(row_refs)]
    fetch_in = [fetch(weights[h], in_v.at[h], blocks + h) for h in range(2)]
    fetch_out = [fetch(weights[2 + h], out_v.at[h], blocks + 2 + h) for h in range(2)]
    fetch_grads = [fetch(ref, grads_v.at[j], blocks + 4 + j) for j, ref in enumerate(grad_refs)]
    leaving = []

    def leave(place, ref):
        leaving.append(pltpu.make_async_copy(place, ref, done.at[len(leaving)]))
        leaving[-1].start()

    def save(place, n):
        leave(place, saves[n].at[pl.ds(index * cap, blocks * cap)])

    lane8 = lax.broadcasted_iota(jnp.int32, (8, WIDE), 1)
    row8 = lax.broadcasted_iota(jnp.int32, (8, WIDE), 0)
    picker = (
        jnp.where((row8 == 0) & (lane8 == expert), 1.0, 0.0)
        + jnp.where((row8 == 1) & (lane8 == experts + expert), 1.0, 0.0)
        + jnp.where((row8 == 1) & (lane8 == 2 * experts + expert), 1.0, 0.0)
    ).astype(bf)
    lanes = lax.broadcasted_iota(jnp.int32, (count, WIDE), 1)
    slots_down = lax.broadcasted_iota(jnp.int32, (cap, count), 0)
    slots_along = lax.broadcasted_iota(jnp.int32, (count, cap), 1)
    gather, scatter, gates = [], [], []
    slots = [slice(j * cap, (j + 1) * cap) for j in range(blocks)]
    for j in range(blocks):
        fetch_rows[j].wait()
        extra = rows_v[j, :, width:]
        info = dot_last(picker, extra)
        chosen = slots_down == info[0:1].astype(jnp.int32)
        gates.append(jnp.sum(jnp.where(chosen, info[1:2], 0.0), axis=1, keepdims=True))
        gather.append(jnp.where(chosen, 1.0, 0.0).astype(bf))
        slot = jnp.sum(
            jnp.where(lanes == expert, widen(extra), 0.0), axis=1, keepdims=True
        ).astype(jnp.int32)
        scatter.append(jnp.where(slots_along == slot, 1.0, 0.0).astype(bf))
        x_v[slots[j], :] = product(gather[j], rows_v[j, :, :width]).astype(bf)
    gate = jnp.concatenate(gates, axis=0)
    save(x_v, 0)
    x = x_v[...]
    inner = []
    for h in range(2):
        fetch_in[h].wait()
        u = product(x, in_v[h])
        gate_part, up_part = u[:, :half], u[:, half:]
        sigmoid = 1.0 / (1.0 + jnp.exp(-gate_part))
        silu = gate_part * sigmoid
        inner.append((gate_part, up_part, sigmoid, silu))
        m_v[h] = (silu * up_part).astype(bf)
        save(m_v.at[h], 2 + h)
    for copy in fetch_out:
        copy.wait()
    y = product(m_v[0], out_v[0]) + product(m_v[1], out_v[1])
    for copy in fetch_grads:
        copy.wait()
    g = jnp.concatenate([product(gather[j], grads_v[j]) for j in range(blocks)], axis=0)
    dgate = jnp.sum(g * y, axis=1, keepdims=True)
    z = (gate * y).astype(bf)
    dy_v[...] = (gate * g).astype(bf)
    save(dy_v, 1)
    for j in range(blocks):
        part_v[j] = product(scatter[j], z[slots[j]]).astype(bf)
        leave(part_v.at[j], out_parts[j])
    dy = dy_v[...]
    for h in range(2):
        gate_part, up_part, sigmoid, silu = inner[h]
        dm = dot_last(dy, out_v[h])
        slope = sigmoid * (1.0 + gate_part * (1.0 - sigmoid))
        du_v[h, :, :half] = (dm * up_part * slope).astype(bf)
        du_v[h, :, half:] = (dm * silu).astype(bf)
        save(du_v.at[h], 4 + h)
    drows = (dot_last(du_v[0], in_v[0]) + dot_last(du_v[1], in_v[1])).astype(bf)
    upper = widen(dgate.astype(bf))
    lane_m = lax.broadcasted_iota(jnp.int32, (blocks * cap, WIDE), 1)
    pair = jnp.where(
        lane_m == 2 * expert, upper, jnp.where(lane_m == 2 * expert + 1, dgate - upper, 0.0)
    ).astype(bf)
    for j in range(blocks):
        back_v[j, :, :width] = product(scatter[j], drows[slots[j]]).astype(bf)
        back_v[j, :, width:] = product(scatter[j], pair[slots[j]]).astype(bf)
        leave(back_v.at[j], row_parts[j])
    for copy in leaving:
        copy.wait()


def expert_blocks(meta, rows, grads, weights, saved, index, total, cap, experts):
    blocks = len(rows)
    count, wide = rows[0].shape
    width, half = grads[0].shape[1], weights[2].shape[0]
    bf = jnp.bfloat16
    used = blocks * cap

    def shape(*dims):
        return jax.ShapeDtypeStruct(dims, bf)

    aliases = {2 * blocks + 5 + t: t for t in range(6)}
    if saved is None:
        saved, aliases = [jnp.zeros((16, WIDE), bf)] * 6, {}
    save_columns = (width, width, half, half, 2 * half, 2 * half)
    results = pl.pallas_call(
        functools.partial(expert_body, index, cap, experts, blocks),
        out_shape=[shape(total * cap, columns) for columns in save_columns]
        + [shape(count, width)] * blocks
        + [shape(count, wide)] * blocks,
        in_specs=[SCALARS] + [ANYWHERE] * (2 * blocks + 10),
        out_specs=[ANYWHERE] * (6 + 2 * blocks),
        scratch_shapes=[
            pltpu.VMEM((blocks, count, wide), bf),
            pltpu.VMEM((blocks, count, width), bf),
            pltpu.VMEM((2, width, 2 * half), bf),
            pltpu.VMEM((2, half, width), bf),
            pltpu.VMEM((used, width), bf),
            pltpu.VMEM((used, width), bf),
            pltpu.VMEM((2, used, half), bf),
            pltpu.VMEM((2, used, 2 * half), bf),
            pltpu.VMEM((blocks, count, width), bf),
            pltpu.VMEM((blocks, count, wide), bf),
            pltpu.SemaphoreType.DMA((2 * blocks + 4,)),
            pltpu.SemaphoreType.DMA((6 + 2 * blocks,)),
        ],
        input_output_aliases=aliases,
        compiler_params=params(60),
        cost_estimate=cost(blocks * 38 * 10**8, 30 << 20, 2 * used * half),
        name="expert_blocks",
    )(meta, *rows, *grads, *weights, *saved)
    return results[:6], results[6 : 6 + blocks], results[6 + blocks :]


def eye(count):
    return lax.broadcasted_iota(jnp.int32, (count, count), 0) == lax.broadcasted_iota(
        jnp.int32, (count, count), 1
    )


def as_column(row):
    return jnp.sum(jnp.where(eye(row.shape[1]), row, 0.0), axis=1, keepdims=True)


def as_row(column):
    return jnp.sum(jnp.where(eye(column.shape[0]), column, 0.0), axis=0, keepdims=True)


def rolled(value):
    return pltpu.roll(value, HEAD_DIM // 2, 1)


def root_of(total):
    return lax.rsqrt(total / D + EPSILON)


def weights_of(query, key, start):
    count = query.shape[0]
    rows = lax.broadcasted_iota(jnp.int32, (count, count), 0)
    columns = lax.broadcasted_iota(jnp.int32, (count, count), 1)
    allowed = (columns <= rows) & (columns >= start.astype(jnp.int32))
    scores = jnp.where(allowed, dot_last(query, key) * HEAD_DIM ** (-0.5), MASKED)
    exponent = jnp.exp(scores - jnp.max(scores, axis=1, keepdims=True))
    return exponent / jnp.sum(exponent, axis=1, keepdims=True)


def spans(mine):
    return [slice(h, h + HEAD_DIM) for h in range(0, mine, HEAD_DIM)]


def project_body(planes, own_rows, meta, *refs):
    blocks, own, other = refs[:SPOTS], refs[SPOTS : SPOTS + planes], refs[SPOTS + planes :][:planes]
    proj_ref, a_ref, in_ref, sums_ref, small_ref, gains_ref = refs[SPOTS + 2 * planes :][:6]
    x_v, a_v, in_v, proj_v, sem, in_sem, done = refs[SPOTS + 2 * planes + 6 :]
    spot, core = meta[0], meta[1]
    count = x_v.shape[1]
    mine = proj_v.shape[1] // 3
    fetch_x = [pltpu.make_async_copy(ref, x_v.at[j], sem.at[j]) for j, ref in enumerate(blocks)]
    for copy in fetch_x:
        copy.start()
    fetch_in = []
    for k in range(planes):
        for mask in range(SPOTS):
            chunk = meta[2 + k] * PLANE + (spot ^ mask) * 2
            for n, (refs_k, c) in enumerate(((own, core), (other, 1 - core))):
                at = pl.multiple_of((chunk + c) * own_rows, own_rows)
                fetch_in.append(
                    pltpu.make_async_copy(
                        refs_k[k].at[mask],
                        in_v.at[pl.ds(at, own_rows)],
                        in_sem.at[(k * SPOTS + mask) * 2 + n],
                    )
                )
                fetch_in[-1].start()
    roots = []
    for j in range(SPOTS):
        fetch_x[j].wait()
        x = widen(x_v[j])
        roots.append(lax.rsqrt(jnp.mean(x * x, axis=1, keepdims=True) + EPSILON))
    for copy in fetch_in:
        copy.wait()
    leaving = [pltpu.make_async_copy(in_v, in_ref, done.at[0])]
    leaving[0].start()
    turn_by = lax.broadcasted_iota(jnp.int32, (small_ref.shape[0], WIDE), 0) == (
        lax.broadcasted_iota(jnp.int32, (small_ref.shape[0], WIDE), 1)
    )
    small = dot_last(jnp.where(turn_by, 1.0, 0.0).astype(jnp.bfloat16), in_v[:, 3 * mine :])
    small_ref[...] = small
    for line in range(mine // HEAD_DIM):
        at = pl.multiple_of((line * SPOTS + spot) * HEAD_DIM, HEAD_DIM)
        for n in range(2):
            gains_ref[n : n + 1, line * HEAD_DIM : (line + 1) * HEAD_DIM] = small_ref[
                FIRST_GAIN + 1 + n : FIRST_GAIN + 2 + n, pl.ds(at, HEAD_DIM)
            ]
    gain = small[FIRST_GAIN : FIRST_GAIN + 1, :]
    for j in range(SPOTS):
        a_v[j * count : (j + 1) * count, :] = (widen(x_v[j]) * roots[j] * gain).astype(jnp.bfloat16)
    leaving.append(pltpu.make_async_copy(a_v, a_ref, done.at[1]))
    leaving[1].start()
    for n in range(3):
        part = slice(n * mine, (n + 1) * mine)
        value = product(a_v[...], in_v[:, part])
        proj_v[:, part] = value
        leaving.append(
            pltpu.make_async_copy(proj_v.at[:, part], proj_ref.at[:, part], done.at[2 + n])
        )
        leaving[-1].start()
        if n < 2:
            squares = jnp.sum(value * value, axis=1, keepdims=True)
            for j in range(SPOTS):
                sums_ref[n, j : j + 1, :] = as_row(squares[j * count : (j + 1) * count])
    for copy in leaving:
        copy.wait()


def project(moves, blocks, own, other):
    planes, own_rows, wide = len(own), own[0].shape[1], own[0].shape[2]
    width = wide - WIDE
    count, depth = blocks[0].shape
    bf, f32 = jnp.bfloat16, jnp.float32
    rows = SPOTS * count
    meta = jnp.concatenate([jnp.stack([moves.spot, moves.core_id]), moves.planes_back])
    shape = jax.ShapeDtypeStruct
    return pl.pallas_call(
        functools.partial(project_body, planes, own_rows),
        out_shape=[
            shape((rows, width), f32),
            shape((rows, depth), bf),
            shape((depth, wide), bf),
            shape((2, SPOTS, count), f32),
            shape((32, depth), f32),
            shape((2, width // 3), f32),
        ],
        in_specs=[SCALARS] + [ANYWHERE] * (SPOTS + 2 * planes),
        out_specs=[ANYWHERE] * 3
        + [full_spec(2, SPOTS, count), full_spec(32, depth), full_spec(2, width // 3)],
        scratch_shapes=[
            pltpu.VMEM((SPOTS, count, depth), bf),
            pltpu.VMEM((rows, depth), bf),
            pltpu.VMEM((depth, wide), bf),
            pltpu.VMEM((rows, width), f32),
            pltpu.SemaphoreType.DMA((SPOTS,)),
            pltpu.SemaphoreType.DMA((2 * SPOTS * planes,)),
            pltpu.SemaphoreType.DMA((5,)),
        ],
        compiler_params=params(60),
        cost_estimate=cost(5 * 10**9, 20 << 20),
        name="project",
    )(meta.astype(jnp.int32), *blocks, *own, *other)


def by_block(count, width):
    return [pl.BlockSpec((count, width), lambda i: (0, 0))] * SPOTS


def put_by_block(step, refs, value):
    for n, ref in enumerate(refs):

        @pl.when(step == n)
        def _(ref=ref):
            ref[...] = value


def forward_body(planes, own_rows, meta, totals, starts, gains, proj_ref, cos_ref, sin_ref, *refs):
    own, other = refs[:planes], refs[planes : 2 * planes]
    q_ref, k_ref, v_ref, o_ref, out_w, *parts = refs[2 * planes :][: 5 + SPOTS]
    sem = refs[-1]
    step = pl.program_id(0)
    bf = jnp.bfloat16
    mine = q_ref.shape[1]
    fetches = []
    for k in range(planes):
        for n, (refs_k, c) in enumerate(((own, meta[1]), (other, 1 - meta[1]))):
            at = pl.multiple_of((meta[2 + k] * 2 + c) * own_rows, own_rows)
            fetches.append(
                pltpu.make_async_copy(
                    refs_k[k], out_w.at[pl.ds(at, own_rows)], sem.at[2 * k + n]
                )
            )

    @pl.when(step == 0)
    def _():
        for copy in fetches:
            copy.start()

    query_root = root_of(as_column(totals[0, pl.ds(step, 1), :]))
    key_root = root_of(as_column(totals[1, pl.ds(step, 1), :]))
    start = as_column(starts[pl.ds(step, 1), :])
    cos, sin = cos_ref[...], sin_ref[...]
    for own_span in spans(mine):
        at = own_span.start
        query = proj_ref[:, at : at + HEAD_DIM] * query_root * gains[0:1, own_span]
        key = proj_ref[:, mine + at : mine + at + HEAD_DIM] * key_root * gains[1:2, own_span]
        value = proj_ref[:, 2 * mine + at : 2 * mine + at + HEAD_DIM].astype(bf)
        query = (query * cos + rolled(query) * sin).astype(bf)
        key = (key * cos + rolled(key) * sin).astype(bf)
        weights = weights_of(query, key, start).astype(bf)
        q_ref[:, own_span] = query
        k_ref[:, own_span] = key
        v_ref[:, own_span] = value
        o_ref[:, own_span] = product(weights, value).astype(bf)

    @pl.when(step == 0)
    def _():
        for copy in fetches:
            copy.wait()

    put_by_block(step, parts, product(o_ref[...], out_w[...]).astype(bf))


def block_spec(count, columns):
    return pl.BlockSpec((count, columns), lambda i: (i, 0))


def attend_forward(moves, totals, starts, gains, projected, cos_all, sin_all, own, other):
    planes, own_rows = len(own), own[0].shape[0]
    rows, mine = projected.shape[0], gains.shape[1]
    count = rows // SPOTS
    bf = jnp.bfloat16
    meta = jnp.concatenate([jnp.stack([moves.spot, moves.core_id]), moves.planes_back])
    return pl.pallas_call(
        functools.partial(forward_body, planes, own_rows),
        grid=(SPOTS,),
        out_shape=[jax.ShapeDtypeStruct((rows, mine), bf)] * 4
        + [jax.ShapeDtypeStruct((mine, D), bf)]
        + [jax.ShapeDtypeStruct((count, D), bf)] * SPOTS,
        in_specs=[
            SCALARS,
            full_spec(*totals.shape),
            full_spec(*starts.shape),
            full_spec(*gains.shape),
            block_spec(count, 3 * mine),
            block_spec(count, HEAD_DIM),
            block_spec(count, HEAD_DIM),
        ]
        + [ANYWHERE] * (2 * planes),
        out_specs=[block_spec(count, mine)] * 4 + [full_spec(mine, D)] + by_block(count, D),
        scratch_shapes=[pltpu.SemaphoreType.DMA((2 * planes,))],
        compiler_params=params(40),
        cost_estimate=cost(5 * 10**9, 20 << 20),
        name="attend_forward",
    )(meta.astype(jnp.int32), totals, starts, gains, projected, cos_all, sin_all, *own, *other)


def backward_body(
    meta, totals, starts, gains, proj_ref, cos_ref, sin_ref, q_ref, k_ref, v_ref, o_ref, out_w, *refs
):
    blocks = refs[:SPOTS]
    dq_ref, dk_ref, dv_ref, sums_ref, own_grad, other_grad, gain_grad = refs[SPOTS : SPOTS + 7]
    grads_v, o_v, total_v, sem = refs[SPOTS + 7 :]
    step = pl.program_id(0)
    bf = jnp.bfloat16
    mine = q_ref.shape[1]

    @pl.when(step == 0)
    def _():
        for n in range(SPOTS):
            pltpu.make_async_copy(blocks[n], grads_v.at[n], sem.at[n]).start()
        gain_grad[...] = jnp.zeros_like(gain_grad)

    pltpu.make_async_copy(blocks[0], grads_v.at[step], sem.at[step]).wait()
    grads = grads_v[step]
    count = grads.shape[0]
    o_v[pl.ds(pl.multiple_of(step * count, 64), count), :] = o_ref[...]
    do = dot_last(grads, out_w[...]).astype(bf)
    roots = [root_of(as_column(totals[n, pl.ds(step, 1), :])) for n in range(2)]
    start = as_column(starts[pl.ds(step, 1), :])
    cos, sin = cos_ref[...], sin_ref[...]
    sums = [0.0, 0.0]
    for own in spans(mine):
        query, key, value = q_ref[:, own], k_ref[:, own], v_ref[:, own]
        weights = weights_of(query, key, start)
        dv_ref[:, own] = dot_first(weights.astype(bf), do[:, own]).astype(bf)
        dweights = dot_last(do[:, own], value)
        inner = jnp.sum(weights * dweights, axis=1, keepdims=True)
        dscores = (weights * (dweights - inner)).astype(bf)
        for n, (grad, ref) in enumerate(
            ((product(dscores, key), dq_ref), (dot_first(dscores, query), dk_ref))
        ):
            grad = grad * HEAD_DIM ** (-0.5)
            grad = grad * cos - rolled(grad) * sin
            ref[:, own] = grad
            at = n * mine + own.start
            raw = grad * proj_ref[:, at : at + HEAD_DIM]
            sums[n] += jnp.sum(raw * gains[n : n + 1, own], axis=1, keepdims=True)
            line = pl.multiple_of((own.start // HEAD_DIM * SPOTS + meta[0]) * HEAD_DIM, HEAD_DIM)
            gain_grad[n : n + 1, pl.ds(line, HEAD_DIM)] += jnp.sum(
                raw * roots[n], axis=0, keepdims=True
            )
    for n in range(2):
        sums_ref[n, pl.ds(step, 1), :] = as_row(sums[n])

    @pl.when(step == SPOTS - 1)
    def _():
        planes, own_rows = own_grad.shape[:2]
        total = sum(
            dot_first(o_v[j * count : (j + 1) * count, :], grads_v[j]) for j in range(SPOTS)
        )
        total_v[...] = total.astype(bf)
        for k in range(planes):
            for ref, c in ((own_grad, meta[1]), (other_grad, 1 - meta[1])):
                at = pl.multiple_of((meta[2 + k] * 2 + c) * own_rows, own_rows)
                ref[k] = total_v[pl.ds(at, own_rows), :]


def attend_backward(
    moves, totals, starts, gains, projected, cos_all, sin_all, heads, out_full, blocks
):
    rows, mine = projected.shape[0], gains.shape[1]
    count = rows // SPOTS
    planes = moves.planes
    own_rows = mine // (2 * planes)
    bf, f32 = jnp.bfloat16, jnp.float32
    meta = jnp.concatenate([jnp.stack([moves.spot, moves.core_id]), moves.planes_back])
    shape = jax.ShapeDtypeStruct
    return pl.pallas_call(
        backward_body,
        grid=(SPOTS,),
        out_shape=[
            shape((rows, mine), f32),
            shape((rows, mine), f32),
            shape((rows, mine), bf),
            shape((2, SPOTS, count), f32),
            shape((planes, own_rows, D), bf),
            shape((planes, own_rows, D), bf),
            shape((2, D), f32),
        ],
        in_specs=[
            SCALARS,
            full_spec(*totals.shape),
            full_spec(*starts.shape),
            full_spec(*gains.shape),
            block_spec(count, 3 * mine),
            block_spec(count, HEAD_DIM),
            block_spec(count, HEAD_DIM),
        ]
        + [block_spec(count, mine)] * 4
        + [full_spec(*out_full.shape)]
        + [ANYWHERE] * SPOTS,
        out_specs=[block_spec(count, mine)] * 3
        + [full_spec(2, SPOTS, count)]
        + [full_spec(planes, own_rows, D)] * 2
        + [full_spec(2, D)],
        scratch_shapes=[
            pltpu.VMEM((SPOTS, count, D), bf),
            pltpu.VMEM((rows, mine), bf),
            pltpu.VMEM((mine, D), bf),
            pltpu.SemaphoreType.DMA((SPOTS,)),
        ],
        compiler_params=params(48),
        cost_estimate=cost(7 * 10**9, 25 << 20),
        name="attend_backward",
    )(
        meta.astype(jnp.int32),
        totals,
        starts,
        gains,
        projected,
        cos_all,
        sin_all,
        *heads,
        out_full,
        *blocks,
    )


def project_back_body(
    planes,
    own_rows,
    meta,
    totals,
    dots,
    gains,
    router_grad,
    small_rows,
    gain_grads,
    second_grad,
    proj_ref,
    dq_ref,
    dk_ref,
    dv_ref,
    a_ref,
    *refs,
):
    dp_ref, own, other, rest = refs[0], refs[1 : 1 + planes], refs[1 + planes], refs[2 + planes]
    a_v, own_v, other_v, riding_v, small, sem, done = refs[3 + planes :]
    bf = jnp.bfloat16
    rows, mine = dv_ref.shape
    count = rows // SPOTS
    fetch = pltpu.make_async_copy(a_ref, a_v, sem.at[0])
    fetch.start()
    for n, ref in enumerate((dq_ref, dk_ref)):
        columns = slice(n * mine, (n + 1) * mine)
        for j in range(SPOTS):
            block = slice(j * count, (j + 1) * count)
            root = root_of(as_column(totals[n, j : j + 1, :]))
            inner = as_column(dots[n, j : j + 1, :])
            grad = root * gains[n : n + 1, :] * ref[block, :]
            grad = grad - proj_ref[block, columns] * (root * root * root * inner / D)
            dp_ref[block, columns] = grad.astype(bf)
    dp_ref[:, 2 * mine :] = dv_ref[...]
    small[...] = jnp.zeros_like(small)
    small[:FIRST_GAIN, :] = router_grad[...]
    small[FIRST_GAIN : FIRST_GAIN + 1, :] = small_rows[FIRST_GAIN : FIRST_GAIN + 1, :]
    small[FIRST_GAIN + 1 : FIRST_GAIN + 3, :] = gain_grads[...]
    small[FIRST_GAIN + 3 : SMALL, :] = second_grad[...]
    turn_by = lax.broadcasted_iota(jnp.int32, (small.shape[0], WIDE), 0) == (
        lax.broadcasted_iota(jnp.int32, (small.shape[0], WIDE), 1)
    )
    riding_v[...] = dot_first(small[...].astype(bf), jnp.where(turn_by, 1.0, 0.0).astype(bf))
    fetch.wait()
    leaving = []
    span = PLANE * own_rows
    for k in [*range(1, planes), 0]:
        plane = meta[2 + k]
        first_row = pl.multiple_of(plane * span, span)
        grads = dot_first(a_v[:, pl.ds(first_row, span)], dp_ref[...])
        for spot in range(SPOTS):
            for c in range(2):
                at = (spot * 2 + c) * own_rows
                grad = grads[at : at + own_rows, :]
                rows_at = pl.ds(pl.multiple_of(first_row + at, own_rows), own_rows)
                riding = riding_v[rows_at, :].astype(bf)

                def put(place, grad=grad, riding=riding):
                    place[:, : 3 * mine] = grad.astype(bf)
                    place[:, 3 * mine :] = riding

                @pl.when(meta[1] == c)
                def _():
                    put(own_v.at[k, spot ^ meta[0]])

                @pl.when(meta[1] != c)
                def _():
                    put(other_v.at[k, spot ^ meta[0]])

        target = other if k == 1 else rest.at[(k - 2) % planes]
        for place, ref in ((own_v, own[k]), (other_v, target)):
            leaving.append(pltpu.make_async_copy(place.at[k], ref, done.at[len(leaving)]))
            leaving[-1].start()
    for copy in leaving:
        copy.wait()


def project_back(moves, totals, dots, gains, small, projected, dq, dk, dv, normed_all):
    rows, mine = dv.shape
    planes = moves.planes
    own_rows = D // (planes * PLANE)
    bf = jnp.bfloat16
    meta = jnp.concatenate([jnp.stack([moves.spot, moves.core_id]), moves.planes_back])
    pieces = (SPOTS, own_rows, 3 * mine + WIDE)
    inputs = (totals, dots, gains, *small, projected, dq, dk, dv)
    return pl.pallas_call(
        functools.partial(project_back_body, planes, own_rows),
        out_shape=[jax.ShapeDtypeStruct((rows, 3 * mine), bf)]
        + [jax.ShapeDtypeStruct(pieces, bf)] * (planes + 1)
        + [jax.ShapeDtypeStruct((planes - 1, *pieces), bf)],
        in_specs=[SCALARS] + [full_spec(*item.shape) for item in inputs] + [ANYWHERE],
        out_specs=[full_spec(rows, 3 * mine)] + [ANYWHERE] * (planes + 2),
        scratch_shapes=[
            pltpu.VMEM((rows, D), bf),
            pltpu.VMEM((planes, *pieces), bf),
            pltpu.VMEM((planes, *pieces), bf),
            pltpu.VMEM((D, WIDE), jnp.float32),
            pltpu.VMEM((32, D), jnp.float32),
            pltpu.SemaphoreType.DMA((2,)),
            pltpu.SemaphoreType.DMA((2 * planes,)),
        ],
        compiler_params=params(60),
        cost_estimate=cost(5 * 10**9, 30 << 20),
        name="project_back",
    )(meta.astype(jnp.int32), *inputs, normed_all)


def rows_back_body(dp_ref, in_w, *parts):
    value = dot_last(dp_ref[...], in_w[:, : dp_ref.shape[1]]).astype(jnp.bfloat16)
    put_by_block(pl.program_id(0), parts, value)


def rows_back(projected_grad, in_full):
    rows, columns = projected_grad.shape
    count = rows // SPOTS
    return pl.pallas_call(
        rows_back_body,
        grid=(SPOTS,),
        out_shape=[jax.ShapeDtypeStruct((count, D), jnp.bfloat16)] * SPOTS,
        in_specs=[block_spec(count, columns), full_spec(*in_full.shape)],
        out_specs=by_block(count, D),
        compiler_params=params(40),
        cost_estimate=cost(5 * 10**9, 12 << 20),
        name="rows_back",
    )(projected_grad, in_full)


def route_body(tokens, home, back, near, match, rank, small, residual_ref, rows_ref, probs_ref):
    bf = jnp.bfloat16
    residual = widen(tokens[...]) + (widen(home[...]) + widen(back[...]) + widen(near[...]))
    residual_ref[...] = residual
    root = lax.rsqrt(jnp.mean(residual * residual, axis=1, keepdims=True) + EPSILON)
    normed = (residual * root * small[FIRST_GAIN + 3 : FIRST_GAIN + 4, :]).astype(bf)
    rows_ref[:, :D] = normed
    experts = match.shape[1]
    logits = dot_last(normed, small[:experts, :].astype(bf))
    exponent = jnp.exp(logits - jnp.max(logits, axis=1, keepdims=True))
    probs = exponent / jnp.sum(exponent, axis=1, keepdims=True)
    chosen = probs * match[...]
    total = jnp.sum(chosen, axis=1, keepdims=True)
    gates = chosen / total
    upper = widen(gates.astype(bf))
    behind = 0.0
    for n, part in enumerate((rank[...], upper.astype(bf), (gates - upper).astype(bf))):
        places = lax.broadcasted_iota(jnp.int32, (experts, WIDE), 0) + n * experts == (
            lax.broadcasted_iota(jnp.int32, (experts, WIDE), 1)
        )
        behind += product(part, jnp.where(places, 1.0, 0.0).astype(bf))
    rows_ref[:, D:] = behind.astype(bf)
    probs_ref[0] = probs
    probs_ref[1] = gates
    probs_ref[2] = jnp.broadcast_to(total, probs.shape)


def route(tokens, home, back, near, match, rank, small):
    count, width = tokens.shape
    experts = match.shape[1]
    inputs = (tokens, home, back, near, match, rank, small)
    shape = jax.ShapeDtypeStruct
    return pl.pallas_call(
        route_body,
        out_shape=[
            shape((count, width), jnp.float32),
            shape((count, width + WIDE), jnp.bfloat16),
            shape((3, count, experts), jnp.float32),
        ],
        in_specs=[full_spec(*item.shape) for item in inputs],
        out_specs=[
            full_spec(count, width),
            full_spec(count, width + WIDE),
            full_spec(3, count, experts),
        ],
        compiler_params=params(40),
        cost_estimate=cost(10**8, 8 << 20),
        name="route",
    )(*inputs)


def route_back_body(total, home, back, near, match, probs_ref, small, residual, upstream, *results):
    grad_ref, branch_ref, router_ref, gain_ref = results
    bf = jnp.bfloat16
    rows = widen(total[...]) + (widen(home[...]) + widen(back[...]) + widen(near[...]))
    experts = match.shape[1]
    probs, gates, gate_total = probs_ref[0], probs_ref[1], probs_ref[2]
    pairs = lax.broadcasted_iota(jnp.int32, (WIDE, experts), 0) // 2 == (
        lax.broadcasted_iota(jnp.int32, (WIDE, experts), 1)
    )
    gate_grad = product(rows[:, D:].astype(bf), jnp.where(pairs, 1.0, 0.0).astype(bf))
    inner = jnp.sum(gate_grad * gates, axis=1, keepdims=True)
    chosen_grad = match[...] * (gate_grad - inner) / gate_total
    inner = jnp.sum(chosen_grad * probs, axis=1, keepdims=True)
    logit_grad = (probs * (chosen_grad - inner)).astype(bf)
    normed_grad = rows[:, :D] + product(logit_grad, small[:experts, :].astype(bf))
    gain = small[FIRST_GAIN + 3 : FIRST_GAIN + 4, :]
    value = residual[...]
    root = lax.rsqrt(jnp.mean(value * value, axis=1, keepdims=True) + EPSILON)
    normed = (value * root * gain).astype(bf)
    router_ref[...] = dot_first(logit_grad, normed)
    scaled = normed_grad * value
    gain_ref[...] = jnp.sum(scaled * root, axis=0, keepdims=True)
    inner = jnp.mean(scaled * gain, axis=1, keepdims=True)
    grad = widen(upstream[...]) + root * gain * normed_grad - value * (root * root * root * inner)
    grad_ref[...] = grad
    branch_ref[...] = grad.astype(bf)


def route_back(total, home, back, near, match, probs, small, residual, upstream):
    count, width = residual.shape
    experts = match.shape[1]
    inputs = (total, home, back, near, match, probs, small, residual, upstream)
    shape = jax.ShapeDtypeStruct
    return pl.pallas_call(
        route_back_body,
        out_shape=[
            shape((count, width), jnp.float32),
            shape((count, width), jnp.bfloat16),
            shape((experts, width), jnp.float32),
            shape((1, width), jnp.float32),
        ],
        in_specs=[full_spec(*item.shape) for item in inputs],
        out_specs=[
            full_spec(count, width),
            full_spec(count, width),
            full_spec(experts, width),
            full_spec(1, width),
        ],
        compiler_params=params(40),
        cost_estimate=cost(10**8, 10 << 20),
        name="route_back",
    )(*inputs)


def shards_dense(
    tokens,
    cotangent,
    norm_gains,
    attention_in,
    attention_out,
    router_weight,
    expert_in,
    expert_out,
    routes,
    lengths,
):
    row_count = tokens.shape[0]
    devices_count = lax.axis_size("fsdp")
    moves = Moves(devices_count)
    planes, core, spot = moves.planes, moves.core_id, moves.spot
    ring, first, second, cores = moves.ring, moves.first, moves.second, moves.core
    experts = devices_count // 2
    choose = routes.shape[1]
    capacity = 4 * row_count * choose // (3 * experts)
    bf, f32 = jnp.bfloat16, jnp.float32
    own_rows = attention_in.shape[0]
    lines = HEADS // SPOTS
    mine = lines * HEAD_DIM

    def low(value):
        return value.astype(bf)

    pieces = split_columns(spot, attention_in, router_weight, norm_gains, lengths)
    traded = [pieces[0]] + [send(pieces[m], moves.spots[m]) for m in range(1, SPOTS)]
    own_1 = send(cotangent, ring)
    tokens_then, traded, own_1 = tie(tokens, traded, own_1)

    in_own = [jnp.stack(traded)]
    in_own.append(send(in_own[0], ring))
    in_other = [send(in_own[0], cores)]
    near_x = send(tokens_then, first)
    near_0 = send(cotangent, first)
    in_own, in_other, near_x = tie(in_own, in_other, near_x)

    in_own.append(send(in_own[1], ring))
    in_other.append(send(in_own[1], cores))
    blocks_x = [tokens, near_x, send(tokens, second), send(near_x, second)]
    in_own, in_other, blocks_x, near_0 = tie(in_own, in_other, blocks_x, near_0)

    in_own.append(send(in_own[2], ring))
    in_other.append(send(in_own[2], cores))
    out_own = [attention_out, send(attention_out, ring)]
    out_other = [send(attention_out, cores)]
    grads = {(0, 0): [cotangent, near_0], (1, 0): [own_1, send(own_1, first)]}
    columns = 3 * mine
    lengths_all = jnp.stack([piece[: lengths.shape[1], columns + SMALL] for piece in traded])
    lengths_all = jnp.where(core == 0, lengths_all, lengths_all[jnp.asarray([0, 2, 1, 3])])
    places = jnp.arange(row_count, dtype=jnp.int32)
    _, position = jax.vmap(lambda item: layout(item, row_count))(lengths_all.astype(jnp.int32))
    starts = (places[None] - position).astype(f32)
    cos_half, sin_half = (table[:, 0] for table in tables(position.reshape(-1)))
    cos_all = jnp.concatenate([cos_half, cos_half], axis=1)
    sin_all = jnp.concatenate([-sin_half, sin_half], axis=1)

    expert_ids = jnp.arange(experts, dtype=jnp.int32)
    match = jnp.sum((routes[:, :, None] == expert_ids[None, None, :]).astype(f32), axis=1)
    before = (places[:, None] > places[None, :]).astype(bf)
    rank = jnp.where(match > 0, product(before, match.astype(bf)), -1.0).astype(bf)
    in_own, in_other, out_other, grads[1, 0], starts, cos_all, sin_all, rank = tie(
        in_own, in_other, out_other, grads[1, 0], starts, cos_all, sin_all, rank
    )

    in_other.append(send(in_own[3], cores))
    in_other, out_own = tie(in_other, out_own)
    out_own.append(send(out_own[1], ring))
    out_other.append(send(out_own[1], cores))
    grads[0, 1] = [send(item, second) for item in grads[0, 0]]
    projected, normed_all, in_full, sums, small_rows, gains = project(
        moves, blocks_x, in_own, in_other
    )
    sums, out_own, out_other, grads = tie(sums, out_own, out_other, grads)
    out_own.append(send(out_own[2], ring))
    out_other.append(send(out_own[2], cores))
    sums = plane_step(moves, by_spot(moves, sums), 1)
    sums, own_1 = tie(sums, own_1)
    totals = by_spot(moves, plane_step(moves, sums, 2))
    totals, out_own, out_other = tie(totals, out_own, out_other)
    out_other.append(send(out_own[3], cores))
    totals, out_other, grads, own_1 = tie(totals, out_other, grads, own_1)

    own_2 = send(own_1, ring)
    grads[1, 1] = [send(item, second) for item in grads[1, 0]]
    weights = [expert_in[0], send(expert_in[0], cores), expert_out[0], send(expert_out[0], cores)]
    attention = (moves, totals, starts, gains, projected, cos_all, sin_all)
    results = attend_forward(*attention, out_own, out_other)
    heads, out_full, parts = results[:4], results[4], results[5:]
    parts, weights, own_2, grads = tie(parts, weights, own_2, grads)

    def cross(parts):
        return [send(parts[2], second), send(parts[3], second)]

    def gather_near(parts, backs):
        near = low(widen(parts[1]) + widen(backs[1]))
        return widen(parts[0]) + widen(backs[0]), send(near, first)

    backs = cross(parts)
    own_3 = send(own_2, ring)
    backs, parts, near_1 = tie(backs, parts, grads[1, 0][1])
    near = send(low(widen(parts[1]) + widen(backs[1])), first)
    near_2 = send(near_1, ring)
    near, own_3 = tie(near, own_3)
    grads[2, 0] = [own_2, near_2]
    residual, rows, probs = route(tokens, parts[0], backs[0], near, match, rank, small_rows)
    rows, near_2 = tie(rows, near_2)

    meta = (moves.device // 2).reshape(1).astype(jnp.int32)
    saved, done = None, 0
    row_parts, out_parts = {}, {}

    def run_expert(group, which, blocks):
        nonlocal saved, done
        saved, outs, backs = expert_blocks(
            meta,
            blocks,
            grads[group, which],
            weights,
            saved,
            done,
            planes * SPOTS,
            capacity,
            experts,
        )
        done += len(blocks)
        out_parts.setdefault(group, []).extend(outs)
        row_parts.setdefault(group, []).extend(backs)

    row_near = send(rows, first)
    row_1 = send(rows, ring)
    rows, row_near = tie(rows, row_near)

    near_row_1 = send(row_near, ring)
    across = [send(rows, second), send(row_near, second)]
    run_expert(0, 0, [rows, row_near])
    saved, across, row_1 = tie(saved, across, row_1)

    row_2 = send(row_1, ring)
    across_row_1 = send(row_1, second)
    across_2 = send(own_2, second)
    near_3 = send(near_2, ring)
    run_expert(0, 1, across)
    saved, near_row_1, across_row_1, across_2 = tie(saved, near_row_1, across_row_1, across_2)

    near_row_2 = send(near_row_1, ring)
    across = [across_row_1, send(near_row_1, second)]
    grads[2, 0], grads[2, 1] = [own_2, near_2], [across_2, send(near_2, second)]
    run_expert(1, 0, [row_1, near_row_1])
    saved, across, row_2, grads[2, 1] = tie(saved, across, row_2, grads[2, 1])

    row_3 = send(row_2, ring)
    across_row_2 = send(row_2, second)
    across_3 = send(own_3, second)
    run_expert(1, 1, across)
    saved, near_row_2, across_row_2, across_3 = tie(saved, near_row_2, across_row_2, across_3)

    near_row_3 = send(near_row_2, ring)
    across = [across_row_2, send(near_row_2, second)]
    backs_1 = cross(row_parts[1])
    run_expert(2, 0, [row_2, near_row_2])
    saved, across, row_3, near_3 = tie(saved, across, row_3, near_3)

    grads[3, 0] = [own_3, near_3]
    across_row_3 = send(row_3, second)
    grads[3, 1] = [across_3, send(near_3, second)]
    run_expert(2, 1, across)
    saved, near_row_3, across_row_3, backs_1 = tie(saved, near_row_3, across_row_3, backs_1)

    across = [across_row_3, send(near_row_3, second)]
    run_expert(3, 0, [row_3, near_row_3])
    saved, across, grads[3, 1], row_parts = tie(saved, across, grads[3, 1], row_parts)

    pair = [send(low(widen(row_parts[1][n]) + widen(backs_1[n])), ring) for n in range(2)]
    backs_2 = cross(row_parts[2])
    run_expert(3, 1, across)
    saved, pair, backs_2 = tie(saved, pair, backs_2)

    near = send(low(widen(pair[1]) + widen(row_parts[2][1]) + widen(backs_2[1])), first)
    home = widen(pair[0]) + (widen(row_parts[2][0]) + widen(backs_2[0]))
    backs_3 = cross(row_parts[3])
    x_rows, dy_rows, m_own, m_other, du_own, du_other = saved
    in_theirs = dot_first(x_rows, du_other)
    home, near, backs_3, in_theirs, row_parts[0] = tie(
        home, near, backs_3, in_theirs, row_parts[0]
    )

    total = send(low(home + widen(near)), ring)
    home, near = gather_near(row_parts[3], backs_3)
    in_theirs = send(in_theirs, cores)
    backs_0 = cross(row_parts[0])
    out_theirs = dot_first(m_other, dy_rows)
    total, home, near, out_theirs = tie(total, home, near, out_theirs)

    total = send(low(widen(total) + (home + widen(near))), ring)
    _, near_0 = gather_near(row_parts[0], backs_0)
    out_theirs = send(out_theirs, cores)
    out_backs = {1: cross(out_parts[1])}
    total, near_0 = tie(total, near_0)
    residual_grad, branch_grad, router_grad, second_gain_grad = route_back(
        total, row_parts[0][0], backs_0[0], near_0, match, probs, small_rows, residual, cotangent
    )
    branch_near = send(branch_grad, first)
    branch_grad, branch_near, out_parts = tie(branch_grad, branch_near, out_parts)

    branch_blocks = [
        branch_grad,
        branch_near,
        send(branch_grad, second),
        send(branch_near, second),
    ]
    out_pair = [
        send(low(widen(out_parts[1][n]) + widen(out_backs[1][n])), ring) for n in range(2)
    ]
    expert_out_grad = dot_first(m_own, dy_rows) + out_theirs
    branch_blocks, expert_out_grad, out_parts = tie(branch_blocks, expert_out_grad, out_parts)

    out_backs[2] = cross(out_parts[2])
    dq, dk, dv, dots, own_grad, other_grad, gain_grads = attend_backward(
        *attention, heads, out_full, branch_blocks
    )
    dots, out_backs, out_parts, out_pair, other_grad = tie(
        dots, out_backs, out_parts, out_pair, other_grad
    )

    other_grad = send(other_grad, cores)
    out_near = send(
        low(widen(out_pair[1]) + widen(out_parts[2][1]) + widen(out_backs[2][1])), first
    )
    dots = plane_step(moves, by_spot(moves, dots), 1)
    dots, other_grad = tie(dots, other_grad)

    def out_sum(step):
        return widen(own_grad[step]) + widen(other_grad[step])

    out_share = send(low(out_sum(1)), ring)
    dots = by_spot(moves, plane_step(moves, dots, 2))
    dots, out_share, out_near, out_parts, out_pair = tie(
        dots, out_share, out_near, out_parts, out_pair
    )
    out_total = low(
        widen(out_pair[0])
        + (widen(out_parts[2][0]) + widen(out_backs[2][0]))
        + widen(out_near)
    )
    out_total = send(out_total, ring)
    out_backs[3] = cross(out_parts[3])
    small = (router_grad, small_rows, gain_grads, second_gain_grad)
    projected_grad, *in_grads = project_back(
        moves, totals, dots, gains, small, projected, dq, dk, dv, normed_all
    )
    in_grads, projected_grad, out_share, out_parts, out_total, out_backs[3] = tie(
        in_grads, projected_grad, out_share, out_parts, out_total, out_backs[3]
    )

    *in_grads, others, others_rest = in_grads
    others = send(others, cores)
    projected_grad, in_full, others = tie(projected_grad, in_full, others)
    in_total = send(low(widen(in_grads[1]) + widen(others)), ring)
    others_rest = send(others_rest, cores)
    out_share = send(low(widen(out_share) + out_sum(2)), ring)
    out_backs[0] = cross(out_parts[0])
    parts = rows_back(projected_grad, in_full)
    in_total, others_rest, parts, x_rows, out_share, out_parts, out_backs = tie(
        in_total, others_rest, parts, x_rows, out_share, out_parts, out_backs
    )

    in_total = send(low(widen(in_total) + (widen(in_grads[2]) + widen(others_rest[0]))), ring)
    backs = cross(parts)
    expert_in_grad = dot_first(x_rows, du_own) + in_theirs
    in_total, backs, expert_in_grad, out_parts, out_share = tie(
        in_total, backs, expert_in_grad, out_parts, out_share
    )

    in_total = send(low(widen(in_total) + (widen(in_grads[3]) + widen(others_rest[1]))), ring)
    home, near = gather_near(parts, backs)
    out_home_3, out_near_3 = gather_near(out_parts[3], out_backs[3])
    out_share = send(low(widen(out_share) + out_sum(3)), ring)
    out_home, out_near = gather_near(out_parts[0], out_backs[0])
    in_total, home, near, out_home_3, out_near_3, out_share = tie(
        in_total, home, near, out_home_3, out_near_3, out_share
    )

    in_total = low(widen(in_total) + (widen(in_grads[0]) + widen(others_rest[2])))
    traded = [in_total[0]] + [send(in_total[m], moves.spots[m]) for m in range(1, SPOTS)]
    out_total = send(low(widen(out_total) + (out_home_3 + widen(out_near_3))), ring)
    out_share = widen(out_share) + out_sum(0)
    _, first_back = jax.vjp(
        lambda value: root_norm(value, small_rows[FIRST_GAIN]), widen(tokens)
    )
    (input_norm_grad,) = first_back(home + widen(near))
    input_grad = residual_grad + input_norm_grad
    traded, input_grad, out_share, out_home, out_near = tie(
        traded, input_grad, out_share, out_home, out_near
    )
    in_share, small_share = join_columns(spot, traded, attention_in, norm_gains)
    out_total, in_share, out_near = tie(out_total, in_share, out_near)
    output = low(residual + (widen(out_total) + (out_home + widen(out_near))))
    return (
        output,
        input_grad,
        small_share[:, FIRST_GAIN:SMALL].T,
        in_share,
        out_share,
        small_share[:, :FIRST_GAIN],
        expert_in_grad[None],
        expert_out_grad[None],
    )


def shards(*arguments):
    routes = arguments[8]
    experts = lax.axis_size("fsdp") // 2
    if 2 * routes.shape[1] >= experts and HEADS == experts:
        return shards_dense(*arguments)
    return shards_routed(*arguments)


def solution(mesh):
    in_specs = (
        P("fsdp", None),
        P("fsdp", None),
        P(None, "fsdp"),
        P("fsdp", None),
        P("fsdp", None),
        P("fsdp", None),
        P("fsdp", None, None),
        P("fsdp", None, None),
        P("fsdp", None),
        P("fsdp", None),
    )
    out_specs = (
        P("fsdp", None),
        P("fsdp", None),
        P(None, "fsdp"),
        P("fsdp", None),
        P("fsdp", None),
        P("fsdp", None),
        P("fsdp", None, None),
        P("fsdp", None, None),
    )
    return jax.shard_map(shards, mesh=mesh, in_specs=in_specs, out_specs=out_specs, check_vma=False)
```
